32 devices in a mesh: dp: 16 (over z, x, core), tensor: 2 (over y).
Axes of the slice: x: 2, y: 2, z: 4, core: 2. Of those that a mesh axis runs over, the one named last changes fastest.
Arguments:
- tokens: bfloat16 [8192, 2048], P('dp'), may hold values from -6 to 6
- positions: int32 [8192], P('dp'), may hold values from 0 to 2046, as said below
- attn_gain: bfloat16 [2048], P('dp'), may hold values from 0.099609375 to 1.8984375
- w_query: bfloat16 [2048, 2048], P('dp', 'tensor'), may hold values from -0.125 to 0.125
- w_key: bfloat16 [2048, 2048], P('dp', 'tensor'), may hold values from -0.125 to 0.125
- w_value: bfloat16 [2048, 2048], P('dp', 'tensor'), may hold values from -0.125 to 0.125
- w_out: bfloat16 [2048, 2048], P('tensor', 'dp'), may hold values from -1 to 1
- ffn_gain: bfloat16 [2048], P('dp'), may hold values from 0.099609375 to 1.8984375
- w_gate: bfloat16 [2048, 5504], P('dp', 'tensor'), may hold values from -0.125 to 0.125
- w_up: bfloat16 [2048, 5504], P('dp', 'tensor'), may hold values from -0.125 to 0.125
- w_down: bfloat16 [5504, 2048], P('tensor', 'dp'), may hold values from -0.078125 to 0.078125
- cotangent: bfloat16 [8192, 2048], P('dp'), may hold values from -6 to 6
Outputs:
- layer_out: bfloat16 [8192, 2048], P('dp')
- tokens_grad: float32 [8192, 2048], P('dp')
- attn_gain_grad: float32 [2048], P('dp')
- w_query_grad: float32 [2048, 2048], P('dp', 'tensor')
- w_key_grad: float32 [2048, 2048], P('dp', 'tensor')
- w_value_grad: float32 [2048, 2048], P('dp', 'tensor')
- w_out_grad: float32 [2048, 2048], P('tensor', 'dp')
- ffn_gain_grad: float32 [2048], P('dp')
- w_gate_grad: float32 [2048, 5504], P('dp', 'tensor')
- w_up_grad: float32 [2048, 5504], P('dp', 'tensor')
- w_down_grad: float32 [5504, 2048], P('tensor', 'dp')
The draws below stay inside these ranges and needn't reach their ends.
Inputs may be any that keep to these rules, and one draw needn't show every extreme that they name: positions is 0 where a document of the packed stream begins and one more than the previous token's elsewhere; documents hold 1 to 2047 tokens.
All inputs are finite; a program needn't handle non-finite values.
Results may differ from the reference program's by a relative error of at most 0.014.
Values may be sent and summed in bfloat16 or wider, within the bound.
A program may use at most 256 MiB of HBM per device.

```python
import jax
import jax.numpy as jnp
from jax import lax

D = 2048
H = 16
E = 128
FF = 5504
WINDOW = 1024
HD = 2048
HALF_DOC = 1024
TOKENS = 8192


def draw_positions(key, part):
    key = jax.random.fold_in(key, 7)
    cell_count = TOKENS // HALF_DOC
    offsets = jax.random.randint(key, (cell_count,), 0, HALF_DOC, dtype=jnp.int32)
    offsets = offsets.at[0].set(0).at[1].set(HALF_DOC - 1)
    token_index = jnp.arange(TOKENS, dtype=jnp.int32)
    cell_index = token_index // HALF_DOC
    inside = token_index % HALF_DOC
    own_offset = offsets[cell_index]
    prior_offset = offsets[jnp.maximum(cell_index - 1, 0)]
    earlier = inside < own_offset
    starts = jnp.where(earlier, (cell_index - 1) * HALF_DOC + prior_offset, cell_index * HALF_DOC + own_offset)
    return token_index - starts


def raised(array, stream_key, source, target, shards_of, factor):
    owner, partner = [(jnp.arange(array.shape[dim]) // (array.shape[dim] // shards_of)).reshape([-1 if axis == dim else 1 for axis in range(array.ndim)]) for dim in (source, target)]
    chosen = jax.random.permutation(stream_key, shards_of)[partner]
    strong = (owner == chosen) | (owner == (partner + shards_of // 2) % shards_of)
    return jnp.where(strong, factor * array, array)


def shard_levels(key, dims, split, least, top_value):
    factor_of = 1.0
    for position, parts in split:
        heights = jax.random.uniform(jax.random.fold_in(jax.random.fold_in(key, 6), position), (parts,), jnp.float32, least / len(split), top_value / len(split))
        factor_of = factor_of * jnp.repeat(jnp.exp(heights), dims[position] // parts).reshape((-1,) + (1,) * (len(dims) - 1 - position))
    return factor_of


def bell_draw(key, extent, width, limit, pieces=(), kind=jnp.bfloat16):
    values = width * jax.random.normal(key, extent, jnp.float32)
    if pieces:
        values = values * shard_levels(key, extent, pieces, -0.22, 0.18)
    return jnp.clip(values, -limit, limit).astype(kind)


def heavy_noise(stream_key, dims, spread, reach, split, heavy, kind=jnp.bfloat16):
    values = spread * jax.random.normal(stream_key, dims, jnp.float32)
    if split:
        values = values * shard_levels(stream_key, dims, split, -0.22, 0.18)
    return jnp.clip(raised(values, jax.random.fold_in(stream_key, 3), *heavy), -reach, reach).astype(kind)


def setup_inputs(seed: int = 0) -> dict:
    keys = jax.random.split(jax.random.key(seed), 13)
    return {
        "tokens": bell_draw(keys[0], (TOKENS, D), 1.0, 6.0, ((0, 16),)),
        "positions": draw_positions(jax.random.fold_in(keys[12], 71), 0),
        "attn_gain": jnp.clip(1.0 + 0.18 * jax.random.normal(keys[2], (D,), jnp.float32), 0.099609375, 1.8984375).astype(jnp.bfloat16),
        "w_query": bell_draw(keys[3], (D, HD), D ** -0.5, 0.125, ((0, 16), (1, 2))),
        "w_key": bell_draw(keys[4], (D, HD), D ** -0.5, 0.125, ((0, 16), (1, 2))),
        "w_value": bell_draw(keys[5], (D, HD), D ** -0.5, 0.125, ((0, 16), (1, 2))),
        "w_out": bell_draw(keys[6], (HD, D), (HD // 64) ** -0.5, 1.0, ((0, 2), (1, 16))),
        "ffn_gain": jnp.clip(1.0 + 0.18 * jax.random.normal(keys[7], (D,), jnp.float32), 0.099609375, 1.8984375).astype(jnp.bfloat16),
        "w_gate": bell_draw(keys[8], (D, FF), D ** -0.5, 0.125, ((0, 16), (1, 2))),
        "w_up": bell_draw(keys[9], (D, FF), D ** -0.5, 0.125, ((0, 16), (1, 2))),
        "w_down": bell_draw(keys[10], (FF, D), FF ** -0.5, 0.078125, ((0, 2), (1, 16))),
        "cotangent": heavy_noise(keys[11], (TOKENS, D), 1.0, 6.0, ((0, 16),), (0, 1, 16, 2.0)),
    }


EPS = 1e-06
THETA = 10000.0

@jax.custom_vjp
def low(v):
    return lax.optimization_barrier(v.astype(jnp.bfloat16)).astype(jnp.float32)

@jax.custom_vjp
def low_back(v):
    return v

def low_keep(v):
    return (low(v), None)

def low_pass(kept, grad):
    return (grad,)

def back_keep(v):
    return (v, None)

def back_low(kept, grad):
    return (low(grad),)
low.defvjp(low_keep, low_pass)
low_back.defvjp(back_keep, back_low)

def rms_scale(matrix, gain):
    mean_square = lax.optimization_barrier(jnp.mean(matrix * matrix, axis=-1, keepdims=True))
    return matrix * lax.rsqrt(mean_square + EPS) * gain

def rotary(matrix, places, head_size):
    half_size = head_size // 2
    frequency = THETA ** (-(jnp.arange(half_size, dtype=jnp.float32) * 2.0 / head_size))
    angles = places[:, None, None] * frequency[None, None, :]
    cosine = jnp.cos(angles)
    sine_part = jnp.sin(angles)
    shaped = matrix.reshape(matrix.shape[0], -1, head_size)
    first_half = shaped[..., :half_size]
    second_half = shaped[..., half_size:]
    turned = jnp.concatenate([first_half * cosine - second_half * sine_part, second_half * cosine + first_half * sine_part], axis=-1)
    return turned.reshape(matrix.shape)

def product(left, right):
    return jnp.dot(left, right, precision=lax.Precision.HIGHEST, preferred_element_type=jnp.float32)

def attend(query_rot, key_rot, value_rot, positions):
    blocks = TOKENS // WINDOW
    padding = jnp.zeros((WINDOW, HD), jnp.float32)
    keys_padded = jnp.concatenate([padding, key_rot], axis=0)
    values_padded = jnp.concatenate([padding, value_rot], axis=0)
    query_index = jnp.arange(WINDOW, dtype=jnp.int32)[:, None] + WINDOW
    key_index = jnp.arange(2 * WINDOW, dtype=jnp.int32)[None, :]
    scale_factor = E ** (-0.5)

    def one_block(block_index):
        start_row = block_index * WINDOW
        queries = lax.dynamic_slice_in_dim(query_rot, start_row, WINDOW, 0).reshape(WINDOW, H, E)
        keys_here = lax.dynamic_slice_in_dim(keys_padded, start_row, 2 * WINDOW, 0).reshape(2 * WINDOW, H, E)
        values_here = lax.dynamic_slice_in_dim(values_padded, start_row, 2 * WINDOW, 0).reshape(2 * WINDOW, H, E)
        places_here = lax.dynamic_slice_in_dim(positions, start_row, WINDOW, 0)
        allowed = (key_index <= query_index) & (key_index > query_index - WINDOW) & (key_index >= query_index - places_here[:, None])
        scores = low_back(jnp.einsum('qhe,khe->hqk', queries, keys_here, precision=lax.Precision.HIGHEST) * scale_factor)
        scores = jnp.where(allowed[None], scores, -1e+30)
        largest = lax.optimization_barrier(jnp.max(scores, axis=-1, keepdims=True))
        shifted = jnp.exp(scores - largest)
        probs = low(shifted / lax.optimization_barrier(jnp.sum(shifted, axis=-1, keepdims=True)))
        mixed = jnp.einsum('hqk,khe->qhe', probs, values_here, precision=lax.Precision.HIGHEST)
        return mixed.reshape(WINDOW, HD)
    mixed_all = lax.map(jax.checkpoint(one_block), jnp.arange(blocks, dtype=jnp.int32))
    return mixed_all.reshape(TOKENS, HD)

def reference(tokens, positions, attn_gain, w_query, w_key, w_value, w_out, ffn_gain, w_gate, w_up, w_down, cotangent):
    places = positions.astype(jnp.float32)

    def forward(rows, gain_attn, query_proj, key_proj, value_proj, out_proj, gain_ffn, gate_proj, up_proj, down_proj):
        normed_attn = low(rms_scale(rows, gain_attn))
        query_rot = low(rotary(low_back(product(normed_attn, query_proj)), places, E))
        key_rot = low(rotary(low_back(product(normed_attn, key_proj)), places, E))
        value_rot = low_back(low(product(normed_attn, value_proj)))
        mixed = low_back(low(attend(query_rot, key_rot, value_rot, positions)))
        hidden = rows + low_back(product(mixed, out_proj))
        normed_ffn = low(rms_scale(hidden, gain_ffn))
        gate_lin = low_back(product(normed_ffn, gate_proj))
        up_lin = low_back(product(normed_ffn, up_proj))
        activated = low(jax.nn.silu(gate_lin) * up_lin)
        return hidden + low_back(product(activated, down_proj))
    result, pullback = jax.vjp(forward, tokens.astype(jnp.float32), attn_gain.astype(jnp.float32), w_query.astype(jnp.float32), w_key.astype(jnp.float32), w_value.astype(jnp.float32), w_out.astype(jnp.float32), ffn_gain.astype(jnp.float32), w_gate.astype(jnp.float32), w_up.astype(jnp.float32), w_down.astype(jnp.float32))
    grads = pullback(cotangent.astype(jnp.float32))
    return (result.astype(jnp.bfloat16), grads[0], grads[1], grads[2], grads[3], grads[4], grads[5], grads[6], grads[7], grads[8], grads[9])
```

```python
import functools

import jax
import jax.numpy as jnp
from jax import lax
from jax.experimental import pallas as pl
from jax.experimental.pallas import tpu as pltpu
from jax.sharding import PartitionSpec as P

E = 128
WINDOW = 1024
EPS = 1e-06
THETA = 10000.0
LOG2E = 1.4426950408889634
MESH = pl.DeviceIdType.MESH
BF = jnp.bfloat16
F32 = jnp.float32
QB = 256
KB = WINDOW + QB
TILE = 256
VMEM = 56 * 1024 * 1024


def whole_spec(shape):
    return pl.BlockSpec(shape, lambda i: (0,) * len(shape))


def cost(flops, nbytes, special=0):
    return pl.CostEstimate(flops=flops, bytes_accessed=nbytes, transcendentals=special)


def ring_chip(place, chips):
    place = lax.rem(place + 2 * chips, chips)
    late = place // (chips // 2)
    return (1 - late) * 2 * place + late * (2 * (chips - 1 - place) + 1)


def ring_place(chip, chips):
    column = lax.rem(chip, 2)
    row = chip // 2
    return (1 - column) * row + column * (chips - 1 - row)


def ring_route(chips, step):
    order = [2 * q if q < chips // 2 else 2 * (chips - 1 - q) + 1 for q in range(chips)]
    return [
        (order[q] * 2 + core, order[(q + step) % chips] * 2 + core)
        for q in range(chips)
        for core in range(2)
    ]


def swap_route(devices):
    return [(i, i ^ 1) for i in range(devices)]


def gather_kernel(devices, chunks, count, *refs):
    ins = refs[:count]
    outs = refs[count : 2 * count]
    local_sem, a_send, a_recv, b_send, b_recv, c_send, c_recv = refs[2 * count :]
    chips = devices // 2
    me = lax.axis_index("dp")
    side = lax.axis_index("tensor")
    core = lax.rem(me, 2)
    place = ring_place(me // 2, chips)

    def device(q):
        return ring_chip(q, chips) * 2 + core

    right = device(place + 1)
    left = device(place - 1)
    partner = me + 1 - 2 * core
    barrier = pltpu.get_barrier_semaphore()
    for other in (right, left, partner):
        pl.semaphore_signal(barrier, inc=1, device_id=(other, side), device_id_type=MESH)
    pl.semaphore_wait(barrier, 3)

    pieces = []
    for index, parts in enumerate(chunks):
        width = ins[index].shape[1] // parts
        for part in range(parts):
            pieces.append((index, part * width, width))
    hops = chips - 1

    def view(ref, row, half, piece, rows):
        index, column, width = piece
        start = row * rows + half * (rows // 2)
        if not isinstance(start, int):
            start = pl.multiple_of(start, 16)
        return ref.at[pl.ds(start, rows // 2), pl.ds(column, width)]

    def remote(source, target, send, recv, other):
        copy = pltpu.make_async_remote_copy(
            src_ref=source,
            dst_ref=target,
            send_sem=send,
            recv_sem=recv,
            device_id=(other, side),
            device_id_type=MESH,
        )
        copy.start()
        return copy

    local = []
    for index in range(count):
        rows = ins[index].shape[0]
        copy = pltpu.make_async_copy(
            ins[index], outs[index].at[pl.ds(pl.multiple_of(me * rows, 16), rows)], local_sem.at[index]
        )
        copy.start()
        local.append(copy)
    forward, partner_copies = {}, []
    for number, piece in enumerate(pieces):
        ref, out = ins[piece[0]], outs[piece[0]]
        rows = ref.shape[0]
        forward[number, 0] = (
            remote(view(ref, 0, 0, piece, rows), view(out, me, 0, piece, rows), a_send.at[number, 0], a_recv.at[number, 0], right),
            remote(view(ref, 0, 1, piece, rows), view(out, me, 1, piece, rows), b_send.at[number, 0], b_recv.at[number, 0], left),
        )
    for number, piece in enumerate(pieces):
        ref, out = ins[piece[0]], outs[piece[0]]
        rows = ref.shape[0]
        for half in range(2):
            partner_copies.append(
                remote(view(ref, 0, half, piece, rows), view(out, me, half, piece, rows), c_send.at[number, 0, half], c_recv.at[number, 0, half], partner)
            )
    for hop in range(hops):
        for number, piece in enumerate(pieces):
            out = outs[piece[0]]
            rows = ins[piece[0]].shape[0]
            came = forward[number, hop]
            sent = []
            for half in range(2):
                came[half].wait_recv()
                owner = device(place - 1 - hop if half == 0 else place + 1 + hop)
                block = view(out, owner, half, piece, rows)
                send, recv = (a_send, a_recv) if half == 0 else (b_send, b_recv)
                if hop < hops - 1:
                    sent.append(
                        remote(block, block, send.at[number, hop + 1], recv.at[number, hop + 1], right if half == 0 else left)
                    )
                partner_copies.append(
                    remote(block, block, c_send.at[number, hop + 1, half], c_recv.at[number, hop + 1, half], partner)
                )
            if sent:
                forward[number, hop + 1] = tuple(sent)
    for copy in local:
        copy.wait()
    for pair in forward.values():
        for copy in pair:
            copy.wait_send()
    for copy in partner_copies:
        copy.wait()


def ring_gather(arrays, chunks, identity):
    devices = lax.axis_size("dp")
    hops = devices // 2 - 1
    pieces = sum(chunks)
    dma = pltpu.SemaphoreType.DMA
    any_space = pl.BlockSpec(memory_space=pl.ANY)
    return pl.pallas_call(
        functools.partial(gather_kernel, devices, chunks, len(arrays)),
        out_shape=[jax.ShapeDtypeStruct((a.shape[0] * devices, a.shape[1]), a.dtype) for a in arrays],
        in_specs=[any_space] * len(arrays),
        out_specs=[any_space] * len(arrays),
        scratch_shapes=[
            dma((len(arrays),)),
            dma((pieces, hops)),
            dma((pieces, hops)),
            dma((pieces, hops)),
            dma((pieces, hops)),
            dma((pieces, hops + 1, 2)),
            dma((pieces, hops + 1, 2)),
        ],
        compiler_params=pltpu.CompilerParams(collective_id=identity, has_side_effects=True),
        name="ring_gather",
    )(*arrays)


def ring_scatter(own_rows):
    devices = lax.axis_size("dp")
    chips = devices // 2
    me = lax.axis_index("dp")
    core = me % 2
    place = ring_place(me // 2, chips)
    rows = own_rows.shape[0] // devices
    width = own_rows.shape[1]
    split = own_rows.reshape(chips, 2, rows, width)
    given = lax.dynamic_slice(split, (0, 1 - core, 0, 0), (chips, 1, rows, width))[:, 0]
    taken = lax.ppermute(given, "dp", swap_route(devices))
    half_rows = rows // 2

    def term(at, half):
        chip = ring_chip(at, chips)
        mine = lax.dynamic_slice(split, (chip, core, half * half_rows, 0), (1, 1, half_rows, width))[0, 0]
        other = lax.dynamic_slice(taken, (chip, half * half_rows, 0), (1, half_rows, width))[0]
        return mine.astype(F32) + other.astype(F32)

    to_right, to_left = term(place - 1, 0).astype(BF), term(place + 1, 1).astype(BF)
    for step in range(chips - 1):
        to_right = lax.ppermute(to_right, "dp", ring_route(chips, 1))
        to_left = lax.ppermute(to_left, "dp", ring_route(chips, -1))
        to_right = to_right.astype(F32) + term(place - 2 - step, 0)
        to_left = to_left.astype(F32) + term(place + 2 + step, 1)
        if step < chips - 2:
            to_right, to_left = to_right.astype(BF), to_left.astype(BF)
    return jnp.concatenate([to_right, to_left], axis=0)


def dot_nn(a, b):
    return jnp.dot(a, b, preferred_element_type=F32)


def dot_nt(a, b):
    return lax.dot_general(a, b, (((1,), (1,)), ((), ())), preferred_element_type=F32)


def matmul_nn(x, w, first, count, name):
    m, k = x.shape

    def kernel(x_ref, w_ref, o_ref):
        o_ref[...] = dot_nn(x_ref[...], w_ref[...]).astype(BF)

    return pl.pallas_call(
        kernel,
        grid=(count,),
        out_shape=jax.ShapeDtypeStruct((m, count * TILE), BF),
        in_specs=[whole_spec((m, k)), pl.BlockSpec((k, TILE), lambda i: (0, i + first))],
        out_specs=pl.BlockSpec((m, TILE), lambda i: (0, i)),
        compiler_params=pltpu.CompilerParams(vmem_limit_bytes=VMEM),
        cost_estimate=cost(2 * m * k * count * TILE, 2 * (m * k + (m + k) * count * TILE)),
        name=name,
    )(x, w)


def matmul_nt(pairs, name):
    m = pairs[0][0].shape[0]
    n = pairs[0][1].shape[0]
    amount = len(pairs)

    def kernel(*refs):
        total = None
        for index in range(amount):
            part = dot_nt(refs[2 * index][...], refs[2 * index + 1][...])
            total = part if total is None else total + part
        refs[-1][...] = total.astype(BF)

    specs, operands, width = [], [], 0
    for x, w, where in pairs:
        specs.append(whole_spec(x.shape))
        specs.append(pl.BlockSpec((TILE, x.shape[1]), functools.partial(lambda where, i: (i, where), where)))
        operands += [x, w]
        width += x.shape[1]
    return pl.pallas_call(
        kernel,
        grid=(n // TILE,),
        out_shape=jax.ShapeDtypeStruct((m, n), BF),
        in_specs=specs,
        out_specs=pl.BlockSpec((m, TILE), lambda i: (0, i)),
        compiler_params=pltpu.CompilerParams(vmem_limit_bytes=VMEM),
        cost_estimate=cost(2 * m * n * width, 2 * (m * width + n * width + m * n)),
        name=name,
    )(*operands)


def turned(block, cosine, sine, back):
    other = pltpu.roll(block, E // 2, 1)
    if back:
        return block * cosine - other * sine
    return block * cosine + other * sine


def project(x, w, cosine, sine, heads):
    m, k = x.shape
    per = TILE // E
    steps = 3 * heads // per
    rotated = 2 * heads // per

    def kernel(x_ref, w_ref, c_ref, s_ref, o_ref):
        step = pl.program_id(0)
        made = dot_nn(x_ref[...], w_ref[...])

        @pl.when(step < rotated)
        def _():
            for part in range(per):
                piece = slice(part * E, (part + 1) * E)
                o_ref[:, piece] = turned(made[:, piece], c_ref[...], s_ref[...], False).astype(BF)

        @pl.when(step >= rotated)
        def _():
            o_ref[...] = made.astype(BF)

    return pl.pallas_call(
        kernel,
        grid=(steps,),
        out_shape=jax.ShapeDtypeStruct((m, steps * TILE), BF),
        in_specs=[
            whole_spec((m, k)),
            pl.BlockSpec((k, TILE), lambda i: (0, i)),
            whole_spec((m, E)),
            whole_spec((m, E)),
        ],
        out_specs=pl.BlockSpec((m, TILE), lambda i: (0, i)),
        compiler_params=pltpu.CompilerParams(vmem_limit_bytes=VMEM),
        cost_estimate=cost(2 * m * k * steps * TILE, 2 * (m * k + (m + k) * steps * TILE)),
        name="project",
    )(x, w, cosine, sine)


def attend(qkv, near, far, places, heads):
    m = qkv.shape[0]
    blocks = m // QB
    factor = E ** (-0.5) * LOG2E

    def kernel(q_ref, k0, v0, k1, v1, k2, v2, p_ref, o_ref, probs_ref, bias):
        @pl.when(pl.program_id(0) == 0)
        def _():
            for block in range(blocks):
                key = lax.broadcasted_iota(jnp.int32, (KB, QB), 0) + block * QB
                query = lax.broadcasted_iota(jnp.int32, (KB, QB), 1) + block * QB
                place = p_ref[:, block * QB : (block + 1) * QB]
                allowed = (key <= query + WINDOW) & (key > query) & (key >= query + WINDOW - place)
                bias[block] = jnp.where(allowed, 0.0, -1e30)

        keys = jnp.concatenate([k2[...], k1[...], k0[...]], axis=0)
        values = jnp.concatenate([v2[...], v1[...], v0[...]], axis=0)
        values_t = values.T
        for block in range(blocks):
            span = slice(block * QB, block * QB + KB)
            scores = dot_nt(keys[span], q_ref[block * QB : (block + 1) * QB, :]) * factor + bias[block]
            largest = jnp.max(scores, axis=0, keepdims=True)
            grown = jnp.exp2(scores - largest)
            inverse = 1.0 / jnp.sum(grown, axis=0, keepdims=True)
            probs = (grown * inverse).astype(BF)
            probs_ref[0, block] = probs
            mixed_t = dot_nn(values_t[:, span], probs)
            o_ref[block * QB : (block + 1) * QB, :] = mixed_t.T.astype(BF)

    def head(offset):
        return pl.BlockSpec((m, E), lambda i: (0, i + offset))

    return pl.pallas_call(
        kernel,
        grid=(heads,),
        out_shape=[
            jax.ShapeDtypeStruct((m, heads * E), BF),
            jax.ShapeDtypeStruct((heads, blocks, KB, QB), BF),
        ],
        in_specs=[head(0), head(heads), head(2 * heads), head(0), head(heads), head(0), head(heads), whole_spec((1, m))],
        out_specs=[head(0), pl.BlockSpec((1, blocks, KB, QB), lambda i: (i, 0, 0, 0))],
        scratch_shapes=[pltpu.VMEM((blocks, KB, QB), F32)],
        compiler_params=pltpu.CompilerParams(vmem_limit_bytes=VMEM),
        cost_estimate=cost(4 * heads * m * KB * E * 2, 2 * heads * m * KB, heads * m * KB),
        name="attend",
    )(qkv, qkv, qkv, near, near, far, far, places)


def attend_back(qkv, near, far, probs, d_mixed, cosine, sine, heads):
    m = qkv.shape[0]
    blocks = m // QB
    factor = E ** (-0.5)
    reach = WINDOW + m

    def kernel(q_ref, k0, v0, k1, v1, k2, v2, p_ref, g_ref, c_ref, s_ref, dq_ref, dk0, dv0, dk1, dv1, dk2, dv2, keys_sum, values_sum):
        keys = jnp.concatenate([k2[...], k1[...], k0[...]], axis=0)
        values = jnp.concatenate([v2[...], v1[...], v0[...]], axis=0)
        keys_t = keys.T
        keys_sum[...] = jnp.zeros_like(keys_sum)
        values_sum[...] = jnp.zeros_like(values_sum)
        for block in range(blocks):
            span = slice(block * QB, block * QB + KB)
            here = slice(block * QB, (block + 1) * QB)
            low = p_ref[0, block]
            grad = g_ref[here, :]
            d_probs = dot_nt(values[span], grad)
            weighted = low.astype(F32) * d_probs
            total = jnp.sum(weighted, axis=0, keepdims=True)
            d_scores = (weighted - low.astype(F32) * total).astype(BF)
            values_sum[span, :] += dot_nn(low, grad)
            keys_sum[span, :] += dot_nn(d_scores, q_ref[here, :])
            d_query = dot_nn(keys_t[:, span], d_scores).T * factor
            dq_ref[here, :] = turned(d_query, c_ref[here, :], s_ref[here, :], True).astype(BF)
        for index, (dk, dv) in enumerate(((dk2, dv2), (dk1, dv1), (dk0, dv0))):
            rows = slice(index * m, (index + 1) * m)
            dk[...] = (keys_sum[rows, :] * factor).astype(BF)
            dv[...] = values_sum[rows, :].astype(BF)

    def head(offset):
        return pl.BlockSpec((m, E), lambda i: (0, i + offset))

    low = jax.ShapeDtypeStruct((m, heads * E), BF)
    return pl.pallas_call(
        kernel,
        grid=(heads,),
        out_shape=[low] * 7,
        in_specs=[
            head(0), head(heads), head(2 * heads), head(0), head(heads), head(0), head(heads),
            pl.BlockSpec((1, blocks, KB, QB), lambda i: (i, 0, 0, 0)),
            head(0),
            whole_spec((m, E)),
            whole_spec((m, E)),
        ],
        out_specs=[head(0)] * 7,
        scratch_shapes=[pltpu.VMEM((reach, E), F32), pltpu.VMEM((reach, E), F32)],
        compiler_params=pltpu.CompilerParams(vmem_limit_bytes=VMEM),
        cost_estimate=cost(8 * heads * m * KB * E * 2, 2 * heads * m * KB),
        name="attend_back",
    )(qkv, qkv, qkv, near, near, far, far, probs, d_mixed, cosine, sine)


def feed(x, dy, w, tiles):
    m, k = x.shape

    def kernel(x_ref, dy_ref, g_ref, u_ref, d_ref, act_ref, dg_ref, du_ref):
        gate = dot_nn(x_ref[...], g_ref[...])
        up = dot_nn(x_ref[...], u_ref[...])
        d_act = dot_nn(dy_ref[...], d_ref[...])
        soft = 1.0 / (1.0 + jnp.exp(-gate))
        silu = gate * soft
        act_ref[...] = (silu * up).astype(BF)
        dg_ref[...] = (d_act * up * (soft * (1.0 + gate * (1.0 - soft)))).astype(BF)
        du_ref[...] = (d_act * silu).astype(BF)

    tile = pl.BlockSpec((m, TILE), lambda i: (0, i))
    return pl.pallas_call(
        kernel,
        grid=(tiles,),
        out_shape=[jax.ShapeDtypeStruct((m, tiles * TILE), BF)] * 3,
        in_specs=[
            whole_spec((m, k)),
            whole_spec((m, k)),
            pl.BlockSpec((k, TILE), lambda i: (0, i)),
            pl.BlockSpec((k, TILE), lambda i: (0, i + tiles)),
            pl.BlockSpec((k, TILE), lambda i: (0, i + 2 * tiles)),
        ],
        out_specs=[tile] * 3,
        compiler_params=pltpu.CompilerParams(vmem_limit_bytes=VMEM),
        cost_estimate=cost(6 * m * k * tiles * TILE, 6 * (m + k) * tiles * TILE, m * tiles * TILE),
        name="feed",
    )(x, dy, w, w, w)


def norm_root(rows):
    return lax.rsqrt(jnp.mean(rows * rows, axis=-1, keepdims=True) + EPS)


def norm_back(rows, root, gain, grad):
    pushed = grad * gain
    inner = jnp.mean(pushed * rows, axis=-1, keepdims=True)
    d_rows = root * pushed - rows * (root * root * root * inner)
    return d_rows, jnp.sum(grad * rows * root, axis=0)


def pair_sum(part, route):
    return part.astype(F32) + lax.ppermute(part, "tensor", route).astype(F32)


def shards(tokens, positions, attn_gain, w_query, w_key, w_value, w_out, ffn_gain, w_gate, w_up, w_down, cotangent):
    devices = lax.axis_size("dp")
    core = lax.axis_index("dp") % 2
    sides = lax.axis_size("tensor")
    flip = [(i, (i + 1) % sides) for i in range(sides)]
    span = tokens.shape[0]
    own_rows = w_query.shape[0]
    width = tokens.shape[1]
    head_columns = w_query.shape[1]
    heads = head_columns // E
    hidden_units = w_gate.shape[1]
    tiles = (hidden_units + TILE - 1) // TILE
    padded = tiles * TILE

    attn_pack = jnp.concatenate([w_query, w_key, w_value, w_out.T], axis=1)
    lanes = max(128, own_rows)
    gains = jnp.zeros((32, lanes), BF).at[0, :own_rows].set(attn_gain).at[16, :own_rows].set(ffn_gain)
    w_attn, all_gains = ring_gather((attn_pack, gains), (2, 1), 0)

    def wide(matrix):
        return jnp.pad(matrix, ((0, 0), (0, padded - hidden_units)))

    ffn_pack = jnp.concatenate([wide(w_gate), wide(w_up), wide(w_down.T)], axis=1)
    w_attn, all_gains, ffn_pack = lax.optimization_barrier((w_attn, all_gains, ffn_pack))
    w_ffn = lax.all_gather(ffn_pack, "dp", axis=0, tiled=True)
    all_gains = all_gains.reshape(devices, 32, lanes)
    gain_attn = all_gains[:, 0, :own_rows].reshape(1, width).astype(F32)
    gain_ffn = all_gains[:, 16, :own_rows].reshape(1, width).astype(F32)

    frequency = THETA ** (-(jnp.arange(E // 2, dtype=F32) * 2.0 / E))
    angles = positions.astype(F32)[:, None] * frequency[None, :]
    cosine_half, sine_half = jnp.cos(angles), jnp.sin(angles)
    cosine = jnp.concatenate([cosine_half, cosine_half], axis=1)
    sine = jnp.concatenate([-sine_half, sine_half], axis=1)

    rows = tokens.astype(F32)
    root_attn = norm_root(rows)
    normed_attn = (rows * root_attn * gain_attn).astype(BF)
    qkv = project(normed_attn, w_attn, cosine, sine, heads)
    own_kv = qkv[:, head_columns:]
    far = lax.ppermute(own_kv, "dp", [(i - 2, i) for i in range(2, devices)])
    near = lax.ppermute(jnp.where(core == 0, own_kv, far), "dp", swap_route(devices))
    mixed, probs = attend(qkv, near, far, positions[None, :], heads)
    hidden = rows + pair_sum(matmul_nt([(mixed, w_attn, 3)], "out_project"), flip)

    root_ffn = norm_root(hidden)
    normed_ffn = (hidden * root_ffn * gain_ffn).astype(BF)
    activated, d_gate, d_up = feed(normed_ffn, cotangent, w_ffn, tiles)
    down_grad = ring_scatter(matmul_nn(cotangent.T, activated, 0, tiles, "down_grad"))
    normed_ffn_t = normed_ffn.T
    gate_grad = ring_scatter(matmul_nn(normed_ffn_t, d_gate, 0, tiles, "gate_grad"))
    up_grad = ring_scatter(matmul_nn(normed_ffn_t, d_up, 0, tiles, "up_grad"))
    d_normed_ffn = pair_sum(matmul_nt([(d_gate, w_ffn, 0), (d_up, w_ffn, 1)], "ffn_back"), flip)
    d_hidden_norm, gain_ffn_grad = norm_back(hidden, root_ffn, gain_ffn, d_normed_ffn)
    d_hidden = cotangent.astype(F32) + d_hidden_norm
    d_hidden_low = d_hidden.astype(BF)
    layer_out = (hidden + pair_sum(matmul_nt([(activated, w_ffn, 2)], "down_project"), flip)).astype(BF)

    d_mixed = matmul_nn(d_hidden_low, w_attn, 3 * head_columns // TILE, head_columns // TILE, "out_back")
    out_part = matmul_nn(d_hidden_low.T, mixed, 0, head_columns // TILE, "out_grad")
    d_query, dk0, dv0, dk1, dv1, dk2, dv2 = attend_back(qkv, near, far, probs, d_mixed, cosine, sine, heads)
    near_sum = lax.ppermute(jnp.concatenate([dk1, dv1], axis=1), "dp", swap_route(devices)).astype(F32)
    far_part = jnp.concatenate([dk2, dv2], axis=1)
    far_part = (far_part.astype(F32) + jnp.where(core == 1, near_sum, 0.0)).astype(BF)
    far_sum = lax.ppermute(far_part, "dp", [(i, i - 2) for i in range(2, devices)]).astype(F32)
    d_kv = jnp.concatenate([dk0, dv0], axis=1).astype(F32) + jnp.where(core == 0, near_sum, 0.0) + far_sum
    d_key = d_kv[:, :head_columns].reshape(span, heads, E)
    d_key = d_key * cosine[:, None, :] - jnp.roll(d_key, E // 2, axis=2) * sine[:, None, :]
    d_qkv = jnp.concatenate([d_query, d_key.reshape(span, head_columns).astype(BF), d_kv[:, head_columns:].astype(BF)], axis=1)
    normed_attn_t = normed_attn.T
    qkv_part = matmul_nn(normed_attn_t, d_qkv, 0, 3 * head_columns // TILE, "qkv_grad")
    attn_grads = ring_scatter(jnp.concatenate([qkv_part, out_part], axis=1))
    d_normed_attn = pair_sum(matmul_nt([(d_qkv, w_attn, 0)], "qkv_back"), flip)
    d_rows, gain_attn_grad = norm_back(rows, root_attn, gain_attn, d_normed_attn)
    tokens_grad = d_hidden + d_rows
    gain_sums = lax.psum_scatter(
        jnp.stack([gain_attn_grad.reshape(devices, own_rows), gain_ffn_grad.reshape(devices, own_rows)], axis=1),
        "dp", scatter_dimension=0, tiled=False,
    )
    return (
        layer_out,
        tokens_grad,
        gain_sums[0],
        attn_grads[:, :head_columns],
        attn_grads[:, head_columns : 2 * head_columns],
        attn_grads[:, 2 * head_columns : 3 * head_columns],
        attn_grads[:, 3 * head_columns :].T,
        gain_sums[1],
        gate_grad[:, :hidden_units],
        up_grad[:, :hidden_units],
        down_grad[:, :hidden_units].T,
    )


def solution(mesh):
    by_rows, by_both, turned_both, line = P("dp", None), P("dp", "tensor"), P("tensor", "dp"), P("dp")
    return jax.shard_map(
        shards,
        mesh=mesh,
        in_specs=(by_rows, line, line, by_both, by_both, by_both, turned_both, line, by_both, by_both, turned_both, by_rows),
        out_specs=(by_rows, by_rows, line, by_both, by_both, by_both, turned_both, line, by_both, by_both, turned_both),
        check_vma=False,
    )
```

```python
import functools

import jax
import jax.numpy as jnp
from jax import lax
from jax.experimental import pallas as pl
from jax.experimental.pallas import tpu as pltpu
from jax.sharding import PartitionSpec as P

E = 128
WINDOW = 1024
EPS = 1e-06
THETA = 10000.0
LOG2E = 1.4426950408889634
MESH = pl.DeviceIdType.MESH
BF = jnp.bfloat16
F32 = jnp.float32
QB = 256
KB = WINDOW + QB
TILE = 256
VMEM = 56 * 1024 * 1024


def whole_spec(shape):
    return pl.BlockSpec(shape, lambda i: (0,) * len(shape))


def cost(flops, nbytes, special=0):
    return pl.CostEstimate(flops=flops, bytes_accessed=nbytes, transcendentals=special)


def ring_chip(place, chips):
    place = lax.rem(place + 2 * chips, chips)
    late = place // (chips // 2)
    return (1 - late) * 2 * place + late * (2 * (chips - 1 - place) + 1)


def ring_place(chip, chips):
    column = lax.rem(chip, 2)
    row = chip // 2
    return (1 - column) * row + column * (chips - 1 - row)


def swap_route(devices):
    return [(i, i ^ 1) for i in range(devices)]


def gather_kernel(devices, chunks, count, *refs):
    ins = refs[:count]
    outs = refs[count : 2 * count]
    local_sem, a_send, a_recv, b_send, b_recv, c_send, c_recv = refs[2 * count :]
    chips = devices // 2
    me = lax.axis_index("dp")
    side = lax.axis_index("tensor")
    core = lax.rem(me, 2)
    place = ring_place(me // 2, chips)

    def device(q):
        return ring_chip(q, chips) * 2 + core

    right = device(place + 1)
    left = device(place - 1)
    partner = me + 1 - 2 * core
    barrier = pltpu.get_barrier_semaphore()
    for other in (right, left, partner):
        pl.semaphore_signal(barrier, inc=1, device_id=(other, side), device_id_type=MESH)
    pl.semaphore_wait(barrier, 3)

    pieces = []
    for index, parts in enumerate(chunks):
        width = ins[index].shape[1] // parts
        for part in range(parts):
            pieces.append((index, part * width, width))
    hops = chips - 1

    def view(ref, row, half, piece, rows):
        index, column, width = piece
        start = row * rows + half * (rows // 2)
        if not isinstance(start, int):
            start = pl.multiple_of(start, 16)
        return ref.at[pl.ds(start, rows // 2), pl.ds(column, width)]

    def remote(source, target, send, recv, other):
        copy = pltpu.make_async_remote_copy(
            src_ref=source,
            dst_ref=target,
            send_sem=send,
            recv_sem=recv,
            device_id=(other, side),
            device_id_type=MESH,
        )
        copy.start()
        return copy

    local = []
    for index in range(count):
        rows = ins[index].shape[0]
        copy = pltpu.make_async_copy(
            ins[index], outs[index].at[pl.ds(pl.multiple_of(me * rows, 16), rows)], local_sem.at[index]
        )
        copy.start()
        local.append(copy)
    forward, partner_copies = {}, []
    for number, piece in enumerate(pieces):
        ref, out = ins[piece[0]], outs[piece[0]]
        rows = ref.shape[0]
        forward[number, 0] = (
            remote(view(ref, 0, 0, piece, rows), view(out, me, 0, piece, rows), a_send.at[number, 0], a_recv.at[number, 0], right),
            remote(view(ref, 0, 1, piece, rows), view(out, me, 1, piece, rows), b_send.at[number, 0], b_recv.at[number, 0], left),
        )
    for number, piece in enumerate(pieces):
        ref, out = ins[piece[0]], outs[piece[0]]
        rows = ref.shape[0]
        for half in range(2):
            partner_copies.append(
                remote(view(ref, 0, half, piece, rows), view(out, me, half, piece, rows), c_send.at[number, 0, half], c_recv.at[number, 0, half], partner)
            )
    for hop in range(hops):
        for number, piece in enumerate(pieces):
            out = outs[piece[0]]
            rows = ins[piece[0]].shape[0]
            came = forward[number, hop]
            sent = []
            for half in range(2):
                came[half].wait_recv()
                owner = device(place - 1 - hop if half == 0 else place + 1 + hop)
                block = view(out, owner, half, piece, rows)
                send, recv = (a_send, a_recv) if half == 0 else (b_send, b_recv)
                if hop < hops - 1:
                    sent.append(
                        remote(block, block, send.at[number, hop + 1], recv.at[number, hop + 1], right if half == 0 else left)
                    )
                partner_copies.append(
                    remote(block, block, c_send.at[number, hop + 1, half], c_recv.at[number, hop + 1, half], partner)
                )
            if sent:
                forward[number, hop + 1] = tuple(sent)
    for copy in local:
        copy.wait()
    for pair in forward.values():
        for copy in pair:
            copy.wait_send()
    for copy in partner_copies:
        copy.wait()


def ring_gather(arrays, chunks, identity):
    devices = lax.axis_size("dp")
    hops = devices // 2 - 1
    pieces = sum(chunks)
    dma = pltpu.SemaphoreType.DMA
    any_space = pl.BlockSpec(memory_space=pl.ANY)
    return pl.pallas_call(
        functools.partial(gather_kernel, devices, chunks, len(arrays)),
        out_shape=[jax.ShapeDtypeStruct((a.shape[0] * devices, a.shape[1]), a.dtype) for a in arrays],
        in_specs=[any_space] * len(arrays),
        out_specs=[any_space] * len(arrays),
        scratch_shapes=[
            dma((len(arrays),)),
            dma((pieces, hops)),
            dma((pieces, hops)),
            dma((pieces, hops)),
            dma((pieces, hops)),
            dma((pieces, hops + 1, 2)),
            dma((pieces, hops + 1, 2)),
        ],
        compiler_params=pltpu.CompilerParams(collective_id=identity, has_side_effects=True),
        name="ring_gather",
    )(*arrays)


class Ring:
    def __init__(self, devices, sources, outs, scratch):
        self.devices, self.chips = devices, devices // 2
        self.sources, self.outs = sources, outs
        count = len(sources)
        self.mine, self.taken, self.inbox = scratch[0 : 3 * count : 3], scratch[1 : 3 * count : 3], scratch[2 : 3 * count : 3]
        self.own_sem, self.give_sem, self.take_sem, self.send_sem, self.recv_sem = scratch[3 * count :]
        self.me = lax.axis_index("dp")
        self.side = lax.axis_index("tensor")
        self.core = lax.rem(self.me, 2)
        self.place = ring_place(self.me // 2, self.chips)
        self.partner = self.me + 1 - 2 * self.core
        self.next = (
            ring_chip(self.place + 1, self.chips) * 2 + self.core,
            ring_chip(self.place - 1, self.chips) * 2 + self.core,
        )

    @staticmethod
    def scratch(devices, shapes):
        chips, count = devices // 2, len(shapes)
        dma = pltpu.SemaphoreType.DMA
        buffers = []
        for rows, width in shapes:
            buffers += [pltpu.VMEM((amount, 2, rows // 2, width), BF) for amount in (chips, chips, chips - 1)]
        return buffers + [dma((count, amount, 2)) for amount in (chips, chips, chips, chips - 1, chips - 1)]

    def barrier(self, others=()):
        semaphore = pltpu.get_barrier_semaphore()
        everyone = [(self.next[0], self.side), (self.next[1], self.side), (self.partner, self.side), *others]
        for other in everyone:
            pl.semaphore_signal(semaphore, inc=1, device_id=other, device_id_type=MESH)
        pl.semaphore_wait(semaphore, len(everyone))

    def term(self, index, stage, half, core):
        at = self.place - 1 - stage if half == 0 else self.place + 1 + stage
        size = self.mine[index].shape[2]
        return self.sources[index].at[ring_chip(at, self.chips) * 2 + core, pl.ds(half * size, size), :]

    def own(self, index, stage, half):
        return pltpu.make_async_copy(
            self.term(index, stage, half, self.core), self.mine[index].at[stage, half], self.own_sem.at[index, stage, half]
        )

    def given(self, index, stage, half):
        return pltpu.make_async_remote_copy(
            src_ref=self.term(index, stage, half, 1 - self.core),
            dst_ref=self.taken[index].at[stage, half],
            send_sem=self.give_sem.at[index, stage, half],
            recv_sem=self.take_sem.at[index, stage, half],
            device_id=(self.partner, self.side),
            device_id_type=MESH,
        )

    def hop(self, index, stage, half, first):
        source = self.mine[index].at[0, half] if first else self.inbox[index].at[stage - 1, half]
        return pltpu.make_async_remote_copy(
            src_ref=source,
            dst_ref=self.inbox[index].at[stage, half],
            send_sem=self.send_sem.at[index, stage, half],
            recv_sem=self.recv_sem.at[index, stage, half],
            device_id=(self.next[half], self.side),
            device_id_type=MESH,
        )

    def each(self):
        return [(index, half) for index in range(len(self.sources)) for half in range(2)]

    def begin(self):
        def step(stage, carry):
            for index, half in self.each():
                self.given(index, stage, half).start()
                self.own(index, stage, half).start()
            return carry

        lax.fori_loop(0, self.chips, step, 0)

    def chip_term(self, index, stage, half):
        self.own(index, stage, half).wait()
        self.given(index, stage, half).wait_recv()
        return self.mine[index][stage, half].astype(F32) + self.taken[index][stage, half].astype(F32)

    def stage(self, stage):
        last = self.chips - 1

        @pl.when(stage == 0)
        def _():
            for index, half in self.each():
                self.mine[index][0, half] = self.chip_term(index, 0, half).astype(BF)
                self.hop(index, 0, half, True).start()

        @pl.when((stage > 0) & (stage < last))
        def _():
            for index, half in self.each():
                self.hop(index, stage - 1, half, True).wait_recv()
                came = self.inbox[index][stage - 1, half].astype(F32)
                self.inbox[index][stage - 1, half] = (came + self.chip_term(index, stage, half)).astype(BF)
                self.hop(index, stage, half, False).start()

        @pl.when(stage == last)
        def _():
            for index, half in self.each():
                self.hop(index, last - 1, half, True).wait_recv()
                came = self.inbox[index][last - 1, half].astype(F32)
                size = came.shape[0]
                total = came + self.chip_term(index, last, half)
                out = self.outs[index]
                out[half * size : (half + 1) * size, :] = total[:, : out.shape[1]]

    def pace(self, step, first, total):
        def done(at):
            return jnp.maximum(at - first, 0) * self.chips // (total - first)

        def one(stage, carry):
            self.stage(stage)
            return carry

        lax.fori_loop(done(step), done(step + 1), one, 0)

    def finish(self):
        for index, half in self.each():
            self.hop(index, 0, half, True).wait_send()

        def sent(stage, carry):
            for index, half in self.each():
                self.hop(index, stage, half, False).wait_send()
            return carry

        lax.fori_loop(1, self.chips - 1, sent, 0)

        def gave(stage, carry):
            for index, half in self.each():
                self.given(index, stage, half).wait_send()
            return carry

        lax.fori_loop(0, self.chips, gave, 0)


def dot_nn(a, b):
    return jnp.dot(a, b, preferred_element_type=F32)


def dot_nt(a, b):
    return lax.dot_general(a, b, (((1,), (1,)), ((), ())), preferred_element_type=F32)


def matmul_nn(x, w, first, count, name):
    m, k = x.shape

    def kernel(x_ref, w_ref, o_ref):
        o_ref[...] = dot_nn(x_ref[...], w_ref[...]).astype(BF)

    return pl.pallas_call(
        kernel,
        grid=(count,),
        out_shape=jax.ShapeDtypeStruct((m, count * TILE), BF),
        in_specs=[whole_spec((m, k)), pl.BlockSpec((k, TILE), lambda i: (0, i + first))],
        out_specs=pl.BlockSpec((m, TILE), lambda i: (0, i)),
        compiler_params=pltpu.CompilerParams(vmem_limit_bytes=VMEM),
        cost_estimate=cost(2 * m * k * count * TILE, 2 * (m * k + (m + k) * count * TILE)),
        name=name,
    )(x, w)


def matmul_nt(pairs, name):
    m = pairs[0][0].shape[0]
    n = pairs[0][1].shape[0]
    amount = len(pairs)

    def kernel(*refs):
        total = None
        for index in range(amount):
            part = dot_nt(refs[2 * index][...], refs[2 * index + 1][...])
            total = part if total is None else total + part
        refs[-1][...] = total.astype(BF)

    specs, operands, width = [], [], 0
    for x, w, where in pairs:
        specs.append(whole_spec(x.shape))
        specs.append(pl.BlockSpec((TILE, x.shape[1]), functools.partial(lambda where, i: (i, where), where)))
        operands += [x, w]
        width += x.shape[1]
    return pl.pallas_call(
        kernel,
        grid=(n // TILE,),
        out_shape=jax.ShapeDtypeStruct((m, n), BF),
        in_specs=specs,
        out_specs=pl.BlockSpec((m, TILE), lambda i: (0, i)),
        compiler_params=pltpu.CompilerParams(vmem_limit_bytes=VMEM),
        cost_estimate=cost(2 * m * n * width, 2 * (m * width + n * width + m * n)),
        name=name,
    )(*operands)


def turned(block, cosine, sine, back):
    other = pltpu.roll(block, E // 2, 1)
    if back:
        return block * cosine - other * sine
    return block * cosine + other * sine


def project(x, w, cosine, sine, heads):
    m, k = x.shape
    per = TILE // E
    steps = 3 * heads // per
    rotated = 2 * heads // per

    def kernel(x_ref, w_ref, c_ref, s_ref, o_ref):
        step = pl.program_id(0)
        made = dot_nn(x_ref[...], w_ref[...])

        @pl.when(step < rotated)
        def _():
            for part in range(per):
                piece = slice(part * E, (part + 1) * E)
                o_ref[:, piece] = turned(made[:, piece], c_ref[...], s_ref[...], False).astype(BF)

        @pl.when(step >= rotated)
        def _():
            o_ref[...] = made.astype(BF)

    return pl.pallas_call(
        kernel,
        grid=(steps,),
        out_shape=jax.ShapeDtypeStruct((m, steps * TILE), BF),
        in_specs=[
            whole_spec((m, k)),
            pl.BlockSpec((k, TILE), lambda i: (0, i)),
            whole_spec((m, E)),
            whole_spec((m, E)),
        ],
        out_specs=pl.BlockSpec((m, TILE), lambda i: (0, i)),
        compiler_params=pltpu.CompilerParams(vmem_limit_bytes=VMEM),
        cost_estimate=cost(2 * m * k * steps * TILE, 2 * (m * k + (m + k) * steps * TILE)),
        name="project",
    )(x, w, cosine, sine)


def attend(qkv, near, far, places, heads):
    m = qkv.shape[0]
    blocks = m // QB
    factor = E ** (-0.5) * LOG2E

    def kernel(q_ref, k0, v0, k1, v1, k2, v2, p_ref, o_ref, probs_ref, bias):
        @pl.when(pl.program_id(0) == 0)
        def _():
            for block in range(blocks):
                key = lax.broadcasted_iota(jnp.int32, (KB, QB), 0) + block * QB
                query = lax.broadcasted_iota(jnp.int32, (KB, QB), 1) + block * QB
                place = p_ref[:, block * QB : (block + 1) * QB]
                allowed = (key <= query + WINDOW) & (key > query) & (key >= query + WINDOW - place)
                bias[block] = jnp.where(allowed, 0.0, -1e30)

        keys = jnp.concatenate([k2[...], k1[...], k0[...]], axis=0)
        values = jnp.concatenate([v2[...], v1[...], v0[...]], axis=0)
        values_t = values.T
        for block in range(blocks):
            span = slice(block * QB, block * QB + KB)
            scores = dot_nt(keys[span], q_ref[block * QB : (block + 1) * QB, :]) * factor + bias[block]
            largest = jnp.max(scores, axis=0, keepdims=True)
            grown = jnp.exp2(scores - largest)
            inverse = 1.0 / jnp.sum(grown, axis=0, keepdims=True)
            probs = (grown * inverse).astype(BF)
            probs_ref[0, block] = probs
            mixed_t = dot_nn(values_t[:, span], probs)
            o_ref[block * QB : (block + 1) * QB, :] = mixed_t.T.astype(BF)

    def head(offset):
        return pl.BlockSpec((m, E), lambda i: (0, i + offset))

    return pl.pallas_call(
        kernel,
        grid=(heads,),
        out_shape=[
            jax.ShapeDtypeStruct((m, heads * E), BF),
            jax.ShapeDtypeStruct((heads, blocks, KB, QB), BF),
        ],
        in_specs=[head(0), head(heads), head(2 * heads), head(0), head(heads), head(0), head(heads), whole_spec((1, m))],
        out_specs=[head(0), pl.BlockSpec((1, blocks, KB, QB), lambda i: (i, 0, 0, 0))],
        scratch_shapes=[pltpu.VMEM((blocks, KB, QB), F32)],
        compiler_params=pltpu.CompilerParams(vmem_limit_bytes=VMEM),
        cost_estimate=cost(4 * heads * m * KB * E * 2, 2 * heads * m * KB, heads * m * KB),
        name="attend",
    )(qkv, qkv, qkv, near, near, far, far, places)


def single(shape):
    return pl.BlockSpec(shape, lambda i: (0,) * len(shape), pipeline_mode=pl.Buffered(1))


def attend_back(qkv, near, far, probs, mixed, w_attn, d_hidden, d_hidden_t, cosine, sine, ring_source, heads, out_width, identity):
    m, width = d_hidden.shape
    devices, rows, ring_width = ring_source.shape[1:]
    blocks = m // QB
    factor = E ** (-0.5)
    reach = WINDOW + m
    columns = heads * E

    def kernel(q_ref, k0, v0, k1, v1, k2, v2, p_ref, x_ref, w_ref, g_ref, gt_ref, c_ref, s_ref, source, d_ref, out_ref, sum_ref, keys_sum, values_sum, near_out, near_in, far_out, far_in, kept, near_send, near_recv, far_send, far_recv, *scratch):
        head = pl.program_id(0)
        ring = Ring(devices, [source.at[0]], [sum_ref], scratch)
        me, side, core = ring.me, ring.side, ring.core

        @pl.when(head == 0)
        def _():
            ring.barrier(((lax.rem(me + 2, devices), side), (lax.rem(me + devices - 2, devices), side)))
            ring.begin()

        def near_copy(which):
            return pltpu.make_async_remote_copy(
                src_ref=near_out.at[which], dst_ref=near_in.at[which], send_sem=near_send.at[which], recv_sem=near_recv.at[which],
                device_id=(ring.partner, side), device_id_type=MESH,
            )

        def far_copy(which):
            return pltpu.make_async_remote_copy(
                src_ref=far_out.at[which], dst_ref=far_in.at[which], send_sem=far_send.at[which], recv_sem=far_recv.at[which],
                device_id=(lax.rem(me + devices - 2, devices), side), device_id_type=MESH,
            )

        grad_all = dot_nn(g_ref[...], w_ref[...]).astype(BF)
        out_ref[...] = dot_nn(gt_ref[...], x_ref[...]).astype(BF)
        keys = jnp.concatenate([k2[...], k1[...], k0[...]], axis=0)
        values = jnp.concatenate([v2[...], v1[...], v0[...]], axis=0)
        keys_t = keys.T
        keys_sum[...] = jnp.zeros_like(keys_sum)
        values_sum[...] = jnp.zeros_like(values_sum)
        for block in range(blocks):
            span = slice(block * QB, block * QB + KB)
            here = slice(block * QB, (block + 1) * QB)
            low = p_ref[0, block]
            grad = grad_all[here, :]
            d_probs = dot_nt(values[span], grad)
            weighted = low.astype(F32) * d_probs
            total = jnp.sum(weighted, axis=0, keepdims=True)
            d_scores = (weighted - low.astype(F32) * total).astype(BF)
            values_sum[span, :] += dot_nn(low, grad)
            keys_sum[span, :] += dot_nn(d_scores, q_ref[here, :])
            d_query = dot_nn(keys_t[:, span], d_scores).T * factor
            d_ref[here, pl.ds(pl.multiple_of(head * E, E), E)] = turned(d_query, c_ref[here, :], s_ref[here, :], True).astype(BF)
        for which, (total, scale) in enumerate(((keys_sum, factor), (values_sum, 1.0))):
            far_out[head, which] = (total[:m, :] * scale).astype(BF)
            near_out[head, which] = (total[m : 2 * m, :] * scale).astype(BF)
            kept[head, which] = total[2 * m :, :] * scale
        near_copy(head).start()

        def settle(which):
            near_copy(which).wait_recv()
            came = near_in[which].astype(F32)
            share = core.astype(F32)
            far_out[which] = (far_out[which].astype(F32) + came * share).astype(BF)
            kept[which] = kept[which] + came * (1.0 - share)

            @pl.when(me >= 2)
            def _():
                far_copy(which).start()

        def close(which):
            @pl.when(me < devices - 2)
            def _():
                far_copy(which).wait_recv()
                kept[which] = kept[which] + far_in[which].astype(F32)

            d_key = turned(kept[which, 0], c_ref[...], s_ref[...], True).astype(BF)
            d_ref[:, pl.ds(pl.multiple_of((heads + which) * E, E), E)] = d_key
            d_ref[:, pl.ds(pl.multiple_of((2 * heads + which) * E, E), E)] = kept[which, 1].astype(BF)
            near_copy(which).wait_send()

            @pl.when(me >= 2)
            def _():
                far_copy(which).wait_send()

        @pl.when(head > 0)
        def _():
            settle(head - 1)

        @pl.when(head == heads - 1)
        def _():
            settle(head)

        ring.pace(head, 0, heads)

        @pl.when(head == heads - 1)
        def _():
            def one(which, carry):
                close(which)
                return carry

            lax.fori_loop(0, heads, one, 0)
            ring.finish()

    def head_spec(offset):
        return pl.BlockSpec((m, E), lambda i: (0, i + offset))

    dma = pltpu.SemaphoreType.DMA
    pieces = (heads, 2, m, E)
    return pl.pallas_call(
        kernel,
        grid=(heads,),
        out_shape=[
            jax.ShapeDtypeStruct((m, 3 * columns), BF),
            jax.ShapeDtypeStruct((width, columns), BF),
            jax.ShapeDtypeStruct((rows, out_width), F32),
        ],
        in_specs=[
            head_spec(0), head_spec(heads), head_spec(2 * heads), head_spec(0), head_spec(heads), head_spec(0), head_spec(heads),
            pl.BlockSpec((1, blocks, KB, QB), lambda i: (i, 0, 0, 0)),
            head_spec(0),
            pl.BlockSpec((width, E), lambda i: (0, i + 3 * heads)),
            single((m, width)),
            single((width, m)),
            single((m, E)),
            single((m, E)),
            pl.BlockSpec(memory_space=pl.ANY),
        ],
        out_specs=[single((m, 3 * columns)), pl.BlockSpec((width, E), lambda i: (0, i)), single((rows, out_width))],
        scratch_shapes=[
            pltpu.VMEM((reach, E), F32), pltpu.VMEM((reach, E), F32),
            pltpu.VMEM(pieces, BF), pltpu.VMEM(pieces, BF), pltpu.VMEM(pieces, BF), pltpu.VMEM(pieces, BF), pltpu.VMEM(pieces, F32),
            dma((heads,)), dma((heads,)), dma((heads,)), dma((heads,)),
            *Ring.scratch(devices, [(rows, ring_width)]),
        ],
        compiler_params=pltpu.CompilerParams(vmem_limit_bytes=VMEM, collective_id=identity, has_side_effects=True),
        cost_estimate=cost(8 * heads * m * KB * E * 2, 2 * heads * m * KB),
        name="attend_back",
    )(qkv, qkv, qkv, near, near, far, far, probs, mixed, w_attn, d_hidden, d_hidden_t, cosine, sine, ring_source)


def back_pass(x_t, d_out, weights, extra, ring_sources, out_widths, identity, name):
    amount, m, columns = d_out.shape
    width = x_t.shape[0]
    devices = lax.axis_size("dp")
    sides = lax.axis_size("tensor")
    tiles = width // TILE
    per = columns // TILE
    total = tiles + amount * per
    ring_shapes = [(source.shape[-2], source.shape[-1]) for source, _ in ring_sources]
    count = len(ring_sources)

    def kernel(*refs):
        refs = list(refs)

        def take(number):
            taken = refs[:number]
            del refs[:number]
            return taken

        xt_ref, tile_ref, d_ref = take(3)
        w_refs = take(amount)
        extra_refs = take(2) if extra else None
        sources = [ref if lead is None else ref.at[lead] for ref, (_, lead) in zip(take(count), ring_sources)]
        grad_ref, back_ref = take(2)
        extra_out = take(1)[0] if extra else None
        sums = take(count)
        sent, got, y_send, y_recv = take(4)
        ring = Ring(devices, sources, sums, refs)
        other = (ring.me, lax.rem(ring.side + 1, sides))
        step = pl.program_id(0)

        def across(which):
            return pltpu.make_async_remote_copy(
                src_ref=sent.at[which], dst_ref=got.at[which], send_sem=y_send.at[which], recv_sem=y_recv.at[which],
                device_id=other, device_id_type=MESH,
            )

        @pl.when(step == 0)
        def _():
            ring.barrier((other,))
            ring.begin()

        @pl.when(step < tiles)
        def _():
            part = None
            for index in range(amount):
                made = dot_nt(d_ref[index], w_refs[index][...])
                part = made if part is None else part + made
            sent[step] = part.astype(BF)
            across(step).start()
            if extra:
                extra_out[...] = dot_nt(extra_refs[0][...], extra_refs[1][...]).astype(BF)

        @pl.when(step >= tiles)
        def _():
            grad_ref[0] = dot_nn(xt_ref[...], tile_ref[0]).astype(BF)

        ring.pace(step, 0, total)

        @pl.when(step == total - 1)
        def _():
            for which in range(tiles):
                across(which).wait()
                back_ref[:, which * TILE : (which + 1) * TILE] = sent[which].astype(F32) + got[which].astype(F32)
            ring.finish()

    def late(i):
        return jnp.maximum(i - tiles, 0)

    def early(i):
        return jnp.minimum(i, tiles - 1)

    specs = [
        single((width, m)),
        pl.BlockSpec((1, m, TILE), lambda i: (late(i) // per, 0, late(i) % per)),
        single((amount, m, columns)),
    ]
    operands = [x_t, d_out, d_out]
    for index in range(amount):
        specs.append(pl.BlockSpec((TILE, columns), functools.partial(lambda where, i: (early(i), where), index)))
        operands.append(weights)
    out_specs = [pl.BlockSpec((1, width, TILE), lambda i: (late(i) // per, 0, late(i) % per)), single((m, width))]
    out_shape = [jax.ShapeDtypeStruct((amount, width, columns), BF), jax.ShapeDtypeStruct((m, width), F32)]
    if extra:
        x, w, where = extra
        specs += [single(x.shape), pl.BlockSpec((TILE, x.shape[1]), lambda i: (early(i), where))]
        operands += [x, w]
        out_specs.append(pl.BlockSpec((m, TILE), lambda i: (0, early(i))))
        out_shape.append(jax.ShapeDtypeStruct((m, width), BF))
    specs += [pl.BlockSpec(memory_space=pl.ANY)] * count
    operands += [source for source, _ in ring_sources]
    for (rows, _), out_width in zip(ring_shapes, out_widths):
        out_specs.append(single((rows, out_width)))
        out_shape.append(jax.ShapeDtypeStruct((rows, out_width), F32))
    dma = pltpu.SemaphoreType.DMA
    return pl.pallas_call(
        kernel,
        grid=(total,),
        out_shape=out_shape,
        in_specs=specs,
        out_specs=out_specs,
        scratch_shapes=[
            pltpu.VMEM((tiles, m, TILE), BF),
            pltpu.VMEM((tiles, m, TILE), BF),
            dma((tiles,)),
            dma((tiles,)),
            *Ring.scratch(devices, ring_shapes),
        ],
        compiler_params=pltpu.CompilerParams(vmem_limit_bytes=VMEM, collective_id=identity, has_side_effects=True),
        cost_estimate=cost(4 * m * width * amount * columns, 6 * width * amount * columns),
        name=name,
    )(*operands)


def ring_only(ring_sources, out_widths, identity):
    devices = lax.axis_size("dp")
    shapes = [source.shape[1:] for source in ring_sources]
    count = len(shapes)

    def kernel(*refs):
        ring = Ring(devices, list(refs[:count]), list(refs[count : 2 * count]), refs[2 * count :])
        ring.barrier()
        ring.begin()

        def one(stage, carry):
            ring.stage(stage)
            return carry

        lax.fori_loop(0, ring.chips, one, 0)
        ring.finish()

    return pl.pallas_call(
        kernel,
        out_shape=[jax.ShapeDtypeStruct((rows, out_width), F32) for (rows, _), out_width in zip(shapes, out_widths)],
        in_specs=[pl.BlockSpec(memory_space=pl.ANY)] * count,
        out_specs=[pl.BlockSpec(memory_space=pltpu.VMEM)] * count,
        scratch_shapes=Ring.scratch(devices, shapes),
        compiler_params=pltpu.CompilerParams(vmem_limit_bytes=VMEM, collective_id=identity, has_side_effects=True),
        name="ring_sum",
    )(*ring_sources)


def feed(x, dy, w, tiles):
    m, k = x.shape

    def kernel(x_ref, dy_ref, g_ref, u_ref, d_ref, act_ref, both_ref):
        gate = dot_nn(x_ref[...], g_ref[...])
        up = dot_nn(x_ref[...], u_ref[...])
        d_act = dot_nn(dy_ref[...], d_ref[...])
        soft = 1.0 / (1.0 + jnp.exp(-gate))
        silu = gate * soft
        act_ref[...] = (silu * up).astype(BF)
        both_ref[0] = (d_act * up * (soft * (1.0 + gate * (1.0 - soft)))).astype(BF)
        both_ref[1] = (d_act * silu).astype(BF)

    tile = pl.BlockSpec((m, TILE), lambda i: (0, i))
    return pl.pallas_call(
        kernel,
        grid=(tiles,),
        out_shape=[jax.ShapeDtypeStruct((m, tiles * TILE), BF), jax.ShapeDtypeStruct((2, m, tiles * TILE), BF)],
        in_specs=[
            whole_spec((m, k)),
            whole_spec((m, k)),
            pl.BlockSpec((k, TILE), lambda i: (0, i)),
            pl.BlockSpec((k, TILE), lambda i: (0, i + tiles)),
            pl.BlockSpec((k, TILE), lambda i: (0, i + 2 * tiles)),
        ],
        out_specs=[tile, pl.BlockSpec((2, m, TILE), lambda i: (0, 0, i))],
        compiler_params=pltpu.CompilerParams(vmem_limit_bytes=VMEM),
        cost_estimate=cost(6 * m * k * tiles * TILE, 6 * (m + k) * tiles * TILE, m * tiles * TILE),
        name="feed",
    )(x, dy, w, w, w)


def norm_root(rows):
    return lax.rsqrt(jnp.mean(rows * rows, axis=-1, keepdims=True) + EPS)


def norm_back(rows, root, gain, grad):
    pushed = grad * gain
    inner = jnp.mean(pushed * rows, axis=-1, keepdims=True)
    d_rows = root * pushed - rows * (root * root * root * inner)
    return d_rows, jnp.sum(grad * rows * root, axis=0)


def pair_sum(part, route):
    return part.astype(F32) + lax.ppermute(part, "tensor", route).astype(F32)


def shards(tokens, positions, attn_gain, w_query, w_key, w_value, w_out, ffn_gain, w_gate, w_up, w_down, cotangent):
    devices = lax.axis_size("dp")
    core = lax.axis_index("dp") % 2
    sides = lax.axis_size("tensor")
    flip = [(i, (i + 1) % sides) for i in range(sides)]
    span = tokens.shape[0]
    own_rows = w_query.shape[0]
    width = tokens.shape[1]
    head_columns = w_query.shape[1]
    heads = head_columns // E
    hidden_units = w_gate.shape[1]
    tiles = (hidden_units + TILE - 1) // TILE
    padded = tiles * TILE

    attn_pack = jnp.concatenate([w_query, w_key, w_value, w_out.T], axis=1)
    lanes = max(128, own_rows)
    gains = jnp.zeros((32, lanes), BF).at[0, :own_rows].set(attn_gain).at[16, :own_rows].set(ffn_gain)
    w_attn, all_gains = ring_gather((attn_pack, gains), (2, 1), 0)

    def wide(matrix):
        return jnp.pad(matrix, ((0, 0), (0, padded - hidden_units)))

    ffn_pack = jnp.concatenate([wide(w_gate), wide(w_up), wide(w_down.T)], axis=1)
    w_attn, all_gains, ffn_pack = lax.optimization_barrier((w_attn, all_gains, ffn_pack))
    w_ffn = lax.all_gather(ffn_pack, "dp", axis=0, tiled=True)
    all_gains = all_gains.reshape(devices, 32, lanes)
    gain_attn = all_gains[:, 0, :own_rows].reshape(1, width).astype(F32)
    gain_ffn = all_gains[:, 16, :own_rows].reshape(1, width).astype(F32)

    frequency = THETA ** (-(jnp.arange(E // 2, dtype=F32) * 2.0 / E))
    angles = positions.astype(F32)[:, None] * frequency[None, :]
    cosine_half, sine_half = jnp.cos(angles), jnp.sin(angles)
    cosine = jnp.concatenate([cosine_half, cosine_half], axis=1)
    sine = jnp.concatenate([-sine_half, sine_half], axis=1)

    rows = tokens.astype(F32)
    root_attn = norm_root(rows)
    normed_attn = (rows * root_attn * gain_attn).astype(BF)
    qkv = project(normed_attn, w_attn, cosine, sine, heads)
    own_kv = qkv[:, head_columns:]
    far = lax.ppermute(own_kv, "dp", [(i - 2, i) for i in range(2, devices)])
    near = lax.ppermute(jnp.where(core == 0, own_kv, far), "dp", swap_route(devices))
    mixed, probs = attend(qkv, near, far, positions[None, :], heads)
    hidden = rows + pair_sum(matmul_nt([(mixed, w_attn, 3)], "out_project"), flip)

    root_ffn = norm_root(hidden)
    normed_ffn = (hidden * root_ffn * gain_ffn).astype(BF)
    activated, d_both = feed(normed_ffn, cotangent, w_ffn, tiles)
    down_part = matmul_nn(cotangent.T, activated, 0, tiles, "down_grad").reshape(devices, own_rows, padded)
    both_part, d_normed_ffn, ffn_part, down_grad = back_pass(
        normed_ffn.T, d_both, w_ffn, (activated, w_ffn, 2), [(down_part, None)], [hidden_units], 1, "ffn_back"
    )
    both_part = both_part.reshape(2, devices, own_rows, padded)
    layer_out = (hidden + pair_sum(ffn_part, flip)).astype(BF)
    d_hidden_norm, gain_ffn_grad = norm_back(hidden, root_ffn, gain_ffn, d_normed_ffn)
    d_hidden = cotangent.astype(F32) + d_hidden_norm
    d_hidden_low = d_hidden.astype(BF)

    d_qkv, out_part, gate_grad = attend_back(
        qkv, near, far, probs, mixed, w_attn, d_hidden_low, d_hidden_low.T, cosine, sine, both_part, heads, hidden_units, 2
    )
    qkv_part, d_normed_attn, up_grad, out_grad = back_pass(
        normed_attn.T, d_qkv[None], w_attn, None,
        [(both_part, 1), (out_part.reshape(devices, own_rows, head_columns), None)], [hidden_units, head_columns], 3, "qkv_back",
    )
    d_rows, gain_attn_grad = norm_back(rows, root_attn, gain_attn, d_normed_attn)
    tokens_grad = d_hidden + d_rows
    gain_part = jnp.zeros((devices, 32, lanes), BF)
    gain_part = gain_part.at[:, 0, :own_rows].set(gain_attn_grad.reshape(devices, own_rows).astype(BF))
    gain_part = gain_part.at[:, 16, :own_rows].set(gain_ffn_grad.reshape(devices, own_rows).astype(BF))
    qkv_grad, gain_grads = ring_only(
        [qkv_part.reshape(devices, own_rows, 3 * head_columns), gain_part], [3 * head_columns, lanes], 4
    )
    return (
        layer_out,
        tokens_grad,
        gain_grads[0, :own_rows],
        qkv_grad[:, :head_columns],
        qkv_grad[:, head_columns : 2 * head_columns],
        qkv_grad[:, 2 * head_columns :],
        out_grad.T,
        gain_grads[16, :own_rows],
        gate_grad,
        up_grad,
        down_grad.T,
    )


def solution(mesh):
    by_rows, by_both, turned_both, line = P("dp", None), P("dp", "tensor"), P("tensor", "dp"), P("dp")
    return jax.shard_map(
        shards,
        mesh=mesh,
        in_specs=(by_rows, line, line, by_both, by_both, by_both, turned_both, line, by_both, by_both, turned_both, by_rows),
        out_specs=(by_rows, by_rows, line, by_both, by_both, by_both, turned_both, line, by_both, by_both, turned_both),
        check_vma=False,
    )
```

```python
import functools

import jax
import jax.numpy as jnp
from jax import lax
from jax.experimental import pallas as pl
from jax.experimental.pallas import tpu as pltpu
from jax.sharding import PartitionSpec as P

E = 128
WINDOW = 1024
EPS = 1e-06
THETA = 10000.0
LOG2E = 1.4426950408889634
MESH = pl.DeviceIdType.MESH
BF = jnp.bfloat16
F32 = jnp.float32
QB = 256
KB = WINDOW + QB
TILE = 256
ROWS = 128
VMEM = 56 * 1024 * 1024


def whole_spec(shape):
    return pl.BlockSpec(shape, lambda i: (0,) * len(shape))


def cost(flops, nbytes, special=0):
    return pl.CostEstimate(flops=flops, bytes_accessed=nbytes, transcendentals=special)


def ring_chip(place, chips):
    place = lax.rem(place + 2 * chips, chips)
    late = place // (chips // 2)
    return (1 - late) * 2 * place + late * (2 * (chips - 1 - place) + 1)


def ring_place(chip, chips):
    column = lax.rem(chip, 2)
    row = chip // 2
    return (1 - column) * row + column * (chips - 1 - row)


def swap_route(devices):
    return [(i, i ^ 1) for i in range(devices)]


def gather_kernel(devices, chunks, count, *refs):
    ins = refs[:count]
    outs = refs[count : 2 * count]
    local_sem, a_send, a_recv, b_send, b_recv, c_send, c_recv = refs[2 * count :]
    chips = devices // 2
    me = lax.axis_index("dp")
    side = lax.axis_index("tensor")
    core = lax.rem(me, 2)
    place = ring_place(me // 2, chips)

    def device(q):
        return ring_chip(q, chips) * 2 + core

    right = device(place + 1)
    left = device(place - 1)
    partner = me + 1 - 2 * core
    barrier = pltpu.get_barrier_semaphore()
    for other in (right, left, partner):
        pl.semaphore_signal(barrier, inc=1, device_id=(other, side), device_id_type=MESH)
    pl.semaphore_wait(barrier, 3)

    pieces = []
    for index, parts in enumerate(chunks):
        width = ins[index].shape[1] // parts
        for part in range(parts):
            pieces.append((index, part * width, width))
    hops = chips - 1

    def view(ref, row, half, piece, rows):
        index, column, width = piece
        start = row * rows + half * (rows // 2)
        if not isinstance(start, int):
            start = pl.multiple_of(start, 16)
        return ref.at[pl.ds(start, rows // 2), pl.ds(column, width)]

    def remote(source, target, send, recv, other):
        copy = pltpu.make_async_remote_copy(
            src_ref=source,
            dst_ref=target,
            send_sem=send,
            recv_sem=recv,
            device_id=(other, side),
            device_id_type=MESH,
        )
        copy.start()
        return copy

    local = []
    for index in range(count):
        rows = ins[index].shape[0]
        copy = pltpu.make_async_copy(
            ins[index], outs[index].at[pl.ds(pl.multiple_of(me * rows, 16), rows)], local_sem.at[index]
        )
        copy.start()
        local.append(copy)
    forward, partner_copies = {}, []
    for number, piece in enumerate(pieces):
        ref, out = ins[piece[0]], outs[piece[0]]
        rows = ref.shape[0]
        forward[number, 0] = (
            remote(view(ref, 0, 0, piece, rows), view(out, me, 0, piece, rows), a_send.at[number, 0], a_recv.at[number, 0], right),
            remote(view(ref, 0, 1, piece, rows), view(out, me, 1, piece, rows), b_send.at[number, 0], b_recv.at[number, 0], left),
        )
    for number, piece in enumerate(pieces):
        ref, out = ins[piece[0]], outs[piece[0]]
        rows = ref.shape[0]
        for half in range(2):
            partner_copies.append(
                remote(view(ref, 0, half, piece, rows), view(out, me, half, piece, rows), c_send.at[number, 0, half], c_recv.at[number, 0, half], partner)
            )
    for hop in range(hops):
        for number, piece in enumerate(pieces):
            out = outs[piece[0]]
            rows = ins[piece[0]].shape[0]
            came = forward[number, hop]
            sent = []
            for half in range(2):
                came[half].wait_recv()
                owner = device(place - 1 - hop if half == 0 else place + 1 + hop)
                block = view(out, owner, half, piece, rows)
                send, recv = (a_send, a_recv) if half == 0 else (b_send, b_recv)
                if hop < hops - 1:
                    sent.append(
                        remote(block, block, send.at[number, hop + 1], recv.at[number, hop + 1], right if half == 0 else left)
                    )
                partner_copies.append(
                    remote(block, block, c_send.at[number, hop + 1, half], c_recv.at[number, hop + 1, half], partner)
                )
            if sent:
                forward[number, hop + 1] = tuple(sent)
    for copy in local:
        copy.wait()
    for pair in forward.values():
        for copy in pair:
            copy.wait_send()
    for copy in partner_copies:
        copy.wait()


def ring_gather(arrays, chunks, identity):
    devices = lax.axis_size("dp")
    hops = devices // 2 - 1
    pieces = sum(chunks)
    dma = pltpu.SemaphoreType.DMA
    any_space = pl.BlockSpec(memory_space=pl.ANY)
    return pl.pallas_call(
        functools.partial(gather_kernel, devices, chunks, len(arrays)),
        out_shape=[jax.ShapeDtypeStruct((a.shape[0] * devices, a.shape[1]), a.dtype) for a in arrays],
        in_specs=[any_space] * len(arrays),
        out_specs=[any_space] * len(arrays),
        scratch_shapes=[
            dma((len(arrays),)),
            dma((pieces, hops)),
            dma((pieces, hops)),
            dma((pieces, hops)),
            dma((pieces, hops)),
            dma((pieces, hops + 1, 2)),
            dma((pieces, hops + 1, 2)),
        ],
        compiler_params=pltpu.CompilerParams(collective_id=identity, has_side_effects=True),
        name="ring_gather",
    )(*arrays)


class Ring:
    AHEAD = 3

    def __init__(self, devices, terms, goals, groups, scratch):
        self.devices, self.chips = devices, devices // 2
        self.terms, self.goals, self.groups = terms, goals, groups
        count = len(terms)
        self.mine, self.taken, self.inbox = scratch[0 : 3 * count : 3], scratch[1 : 3 * count : 3], scratch[2 : 3 * count : 3]
        self.own_sem, self.give_sem, self.take_sem, self.send_sem, self.recv_sem = scratch[3 * count : 3 * count + 5]
        self.me = lax.axis_index("dp")
        self.side = lax.axis_index("tensor")
        self.core = lax.rem(self.me, 2)
        self.place = ring_place(self.me // 2, self.chips)
        self.partner = self.me + 1 - 2 * self.core
        self.next = (
            ring_chip(self.place + 1, self.chips) * 2 + self.core,
            ring_chip(self.place - 1, self.chips) * 2 + self.core,
        )
        self.events = self.chips * len(groups)

    @staticmethod
    def scratch(devices, shapes):
        chips, count = devices // 2, len(shapes)
        dma = pltpu.SemaphoreType.DMA
        buffers = []
        for rows, width in shapes:
            buffers += [pltpu.VMEM((amount, 2, rows // 2, width), BF) for amount in (chips, chips, chips - 1)]
        return buffers + [dma((count, amount, 2)) for amount in (chips, chips, chips, chips - 1, chips - 1)]

    def barrier(self, others=()):
        semaphore = pltpu.get_barrier_semaphore()
        everyone = [(self.next[0], self.side), (self.next[1], self.side), (self.partner, self.side), *others]
        for other in everyone:
            pl.semaphore_signal(semaphore, inc=1, device_id=other, device_id_type=MESH)
        pl.semaphore_wait(semaphore, len(everyone))

    def block(self, index, stage, half, core):
        at = self.place - 1 - stage if half == 0 else self.place + 1 + stage
        size = self.mine[index].shape[2]
        source, column, width = self.terms[index]
        return source.at[ring_chip(at, self.chips) * 2 + core, pl.ds(half * size, size), pl.ds(column, width)]

    def own(self, index, stage, half):
        return pltpu.make_async_copy(
            self.block(index, stage, half, self.core), self.mine[index].at[stage, half], self.own_sem.at[index, stage, half]
        )

    def given(self, index, stage, half):
        return pltpu.make_async_remote_copy(
            src_ref=self.block(index, stage, half, 1 - self.core),
            dst_ref=self.taken[index].at[stage, half],
            send_sem=self.give_sem.at[index, stage, half],
            recv_sem=self.take_sem.at[index, stage, half],
            device_id=(self.partner, self.side),
            device_id_type=MESH,
        )

    def hop(self, index, stage, half, first):
        source = self.mine[index].at[0, half] if first else self.inbox[index].at[stage - 1, half]
        return pltpu.make_async_remote_copy(
            src_ref=source,
            dst_ref=self.inbox[index].at[stage, half],
            send_sem=self.send_sem.at[index, stage, half],
            recv_sem=self.recv_sem.at[index, stage, half],
            device_id=(self.next[half], self.side),
            device_id_type=MESH,
        )

    def each(self, group=None):
        members = range(len(self.terms)) if group is None else self.groups[group]
        return [(index, half) for index in members for half in range(2)]

    def fetch(self, stage, group):
        for index, half in self.each(group):
            self.given(index, stage, half).start()
            self.own(index, stage, half).start()

    def begin(self):
        for stage in range(min(self.AHEAD, self.chips)):
            for group in range(len(self.groups)):
                self.fetch(stage, group)

    def chip_term(self, index, stage, half):
        self.own(index, stage, half).wait()
        self.given(index, stage, half).wait_recv()
        return self.mine[index][stage, half].astype(F32) + self.taken[index][stage, half].astype(F32)

    def stage(self, stage, group):
        last = self.chips - 1

        @pl.when(stage == 0)
        def _():
            for index, half in self.each(group):
                self.mine[index][0, half] = self.chip_term(index, 0, half).astype(BF)
                self.hop(index, 0, half, True).start()

        @pl.when((stage > 0) & (stage < last))
        def _():
            for index, half in self.each(group):
                self.hop(index, stage - 1, half, True).wait_recv()
                came = self.inbox[index][stage - 1, half].astype(F32)
                self.inbox[index][stage - 1, half] = (came + self.chip_term(index, stage, half)).astype(BF)
                self.hop(index, stage, half, False).start()

        @pl.when(stage + self.AHEAD < self.chips)
        def _():
            self.fetch(stage + self.AHEAD, group)

        @pl.when(stage == last)
        def _():
            for index, half in self.each(group):
                self.hop(index, last - 1, half, True).wait_recv()
                came = self.inbox[index][last - 1, half].astype(F32)
                size = came.shape[0]
                total = came + self.chip_term(index, last, half)
                goal, column = self.goals[index]
                width = min(goal.shape[1] - column, total.shape[1])
                goal[half * size : (half + 1) * size, column : column + width] = total[:, :width]

    def run(self, first, stop):
        count = len(self.groups)

        def one(event, carry):
            for group in range(count):
                if count == 1:
                    self.stage(event, 0)
                else:
                    pl.when(lax.rem(event, count) == group)(functools.partial(self.stage, event // count, group))
            return carry

        lax.fori_loop(first, stop, one, 0)

    def pace(self, step, costs):
        whole = sum(steps * each for steps, each in costs)

        def done(at):
            spent, before = 0, 0
            for steps, each in costs:
                spent = spent + jnp.minimum(jnp.maximum(at - before, 0), steps) * each
                before += steps
            return spent * self.events // whole

        self.run(done(step), done(step + 1))

    def finish(self):
        for index, half in self.each():
            self.hop(index, 0, half, True).wait_send()

        def sent(stage, carry):
            for index, half in self.each():
                self.hop(index, stage, half, False).wait_send()
            return carry

        lax.fori_loop(1, self.chips - 1, sent, 0)

        def gave(stage, carry):
            for index, half in self.each():
                self.given(index, stage, half).wait_send()
            return carry

        lax.fori_loop(0, self.chips, gave, 0)


def dot_nn(a, b):
    return jnp.dot(a, b, preferred_element_type=F32)


def dot_nt(a, b):
    return lax.dot_general(a, b, (((1,), (1,)), ((), ())), preferred_element_type=F32)


def matmul_nn(x, w, first, count, name):
    m, k = x.shape

    def kernel(x_ref, w_ref, o_ref):
        o_ref[...] = dot_nn(x_ref[...], w_ref[...]).astype(BF)

    return pl.pallas_call(
        kernel,
        grid=(count,),
        out_shape=jax.ShapeDtypeStruct((m, count * TILE), BF),
        in_specs=[whole_spec((m, k)), pl.BlockSpec((k, TILE), lambda i: (0, i + first))],
        out_specs=pl.BlockSpec((m, TILE), lambda i: (0, i)),
        compiler_params=pltpu.CompilerParams(vmem_limit_bytes=VMEM),
        cost_estimate=cost(2 * m * k * count * TILE, 2 * (m * k + (m + k) * count * TILE)),
        name=name,
    )(x, w)


def matmul_nt(pairs, name):
    m = pairs[0][0].shape[0]
    n = pairs[0][1].shape[0]
    amount = len(pairs)

    def kernel(*refs):
        total = None
        for index in range(amount):
            part = dot_nt(refs[2 * index][...], refs[2 * index + 1][...])
            total = part if total is None else total + part
        refs[-1][...] = total.astype(BF)

    specs, operands, width = [], [], 0
    for x, w, where in pairs:
        specs.append(whole_spec(x.shape))
        specs.append(pl.BlockSpec((TILE, x.shape[1]), functools.partial(lambda where, i: (i, where), where)))
        operands += [x, w]
        width += x.shape[1]
    return pl.pallas_call(
        kernel,
        grid=(n // TILE,),
        out_shape=jax.ShapeDtypeStruct((m, n), BF),
        in_specs=specs,
        out_specs=pl.BlockSpec((m, TILE), lambda i: (0, i)),
        compiler_params=pltpu.CompilerParams(vmem_limit_bytes=VMEM),
        cost_estimate=cost(2 * m * n * width, 2 * (m * width + n * width + m * n)),
        name=name,
    )(*operands)


def turned(block, cosine, sine, back):
    other = pltpu.roll(block, E // 2, 1)
    if back:
        return block * cosine - other * sine
    return block * cosine + other * sine


def project(x, w, cosine, sine, heads):
    m, k = x.shape
    per = TILE // E
    steps = 3 * heads // per
    rotated = 2 * heads // per

    def kernel(x_ref, w_ref, c_ref, s_ref, q_ref, kv_ref):
        step = pl.program_id(0)
        made = dot_nn(x_ref[...], w_ref[...])

        def rotate_to(ref):
            for part in range(per):
                piece = slice(part * E, (part + 1) * E)
                ref[:, piece] = turned(made[:, piece], c_ref[...], s_ref[...], False).astype(BF)

        @pl.when(step < rotated // 2)
        def _():
            rotate_to(q_ref)

        @pl.when((step >= rotated // 2) & (step < rotated))
        def _():
            rotate_to(kv_ref)

        @pl.when(step >= rotated)
        def _():
            kv_ref[...] = made.astype(BF)

    return pl.pallas_call(
        kernel,
        grid=(steps,),
        out_shape=[jax.ShapeDtypeStruct((m, heads * E), BF), jax.ShapeDtypeStruct((m, 2 * heads * E), BF)],
        in_specs=[
            whole_spec((m, k)),
            pl.BlockSpec((k, TILE), lambda i: (0, i)),
            whole_spec((m, E)),
            whole_spec((m, E)),
        ],
        out_specs=[
            pl.BlockSpec((m, TILE), lambda i: (0, jnp.minimum(i, rotated // 2 - 1))),
            pl.BlockSpec((m, TILE), lambda i: (0, jnp.maximum(i - rotated // 2, 0))),
        ],
        compiler_params=pltpu.CompilerParams(vmem_limit_bytes=VMEM),
        cost_estimate=cost(2 * m * k * steps * TILE, 2 * (m * k + (m + k) * steps * TILE)),
        name="project",
    )(x, w, cosine, sine)


def attend(query, own, near, far, places, heads):
    m = query.shape[0]
    blocks = m // QB
    factor = E ** (-0.5) * LOG2E

    def kernel(q_ref, k0, v0, k1, v1, k2, v2, p_ref, o_ref, probs_ref, bias):
        @pl.when(pl.program_id(0) == 0)
        def _():
            for block in range(blocks):
                key = lax.broadcasted_iota(jnp.int32, (KB, QB), 0) + block * QB
                query = lax.broadcasted_iota(jnp.int32, (KB, QB), 1) + block * QB
                place = p_ref[:, block * QB : (block + 1) * QB]
                allowed = (key <= query + WINDOW) & (key > query) & (key >= query + WINDOW - place)
                bias[block] = jnp.where(allowed, 0.0, -1e30)

        keys = jnp.concatenate([k2[...], k1[...], k0[...]], axis=0)
        values = jnp.concatenate([v2[...], v1[...], v0[...]], axis=0)
        values_t = values.T
        for block in range(blocks):
            span = slice(block * QB, block * QB + KB)
            scores = dot_nt(keys[span], q_ref[block * QB : (block + 1) * QB, :]) * factor + bias[block]
            largest = jnp.max(scores, axis=0, keepdims=True)
            grown = jnp.exp2(scores - largest)
            inverse = 1.0 / jnp.sum(grown, axis=0, keepdims=True)
            probs = (grown * inverse).astype(BF)
            probs_ref[0, block] = probs
            mixed_t = dot_nn(values_t[:, span], probs)
            o_ref[block * QB : (block + 1) * QB, :] = mixed_t.T.astype(BF)

    def head(offset):
        return pl.BlockSpec((m, E), lambda i: (0, i + offset))

    return pl.pallas_call(
        kernel,
        grid=(heads,),
        out_shape=[
            jax.ShapeDtypeStruct((m, heads * E), BF),
            jax.ShapeDtypeStruct((heads, blocks, KB, QB), BF),
        ],
        in_specs=[head(0), head(0), head(heads), head(0), head(heads), head(0), head(heads), whole_spec((1, m))],
        out_specs=[head(0), pl.BlockSpec((1, blocks, KB, QB), lambda i: (i, 0, 0, 0))],
        scratch_shapes=[pltpu.VMEM((blocks, KB, QB), F32)],
        compiler_params=pltpu.CompilerParams(vmem_limit_bytes=VMEM),
        cost_estimate=cost(4 * heads * m * KB * E * 2, 2 * heads * m * KB, heads * m * KB),
        name="attend",
    )(query, own, own, near, near, far, far, places)


def single(shape):
    return pl.BlockSpec(shape, lambda i: (0,) * len(shape), pipeline_mode=pl.Buffered(1))


def attend_back(query, own, near, far, probs, mixed, w_attn, d_hidden, d_hidden_t, cosine, sine, flip, ring_source, heads, out_width, identity):
    m, width = d_hidden.shape
    devices, rows, ring_width = ring_source.shape[1:]
    blocks = m // QB
    factor = E ** (-0.5)
    reach = WINDOW + m
    columns = heads * E

    def kernel(q_ref, k0, v0, k1, v1, k2, v2, p_ref, x_ref, w_ref, g_ref, gt_ref, c_ref, s_ref, flip_ref, source, d_ref, out_ref, sum_ref, flipped_ref, keys_sum, values_sum, near_out, near_in, far_out, far_in, kept, near_send, near_recv, far_send, far_recv, *scratch):
        head = pl.program_id(0)
        half = ring_width // 2
        ring = Ring(devices, [(source.at[0], 0, half), (source.at[0], half, half)], [(sum_ref, 0), (sum_ref, half)], [[0], [1]], scratch)
        me, side, core = ring.me, ring.side, ring.core

        @pl.when(head == 0)
        def _():
            ring.barrier(((lax.rem(me + 2, devices), side), (lax.rem(me + devices - 2, devices), side)))
            ring.begin()

        def near_copy(which):
            return pltpu.make_async_remote_copy(
                src_ref=near_out.at[which], dst_ref=near_in.at[which], send_sem=near_send.at[which], recv_sem=near_recv.at[which],
                device_id=(ring.partner, side), device_id_type=MESH,
            )

        def far_copy(which):
            return pltpu.make_async_remote_copy(
                src_ref=far_out.at[which], dst_ref=far_in.at[which], send_sem=far_send.at[which], recv_sem=far_recv.at[which],
                device_id=(lax.rem(me + devices - 2, devices), side), device_id_type=MESH,
            )

        grad_all = dot_nn(g_ref[...], w_ref[...]).astype(BF)
        out_ref[...] = dot_nn(gt_ref[...], x_ref[...]).astype(BF)
        keys = jnp.concatenate([k2[...], k1[...], k0[...]], axis=0)
        values = jnp.concatenate([v2[...], v1[...], v0[...]], axis=0)
        keys_t = keys.T
        keys_sum[...] = jnp.zeros_like(keys_sum)
        values_sum[...] = jnp.zeros_like(values_sum)
        for block in range(blocks):
            span = slice(block * QB, block * QB + KB)
            here = slice(block * QB, (block + 1) * QB)
            low = p_ref[0, block]
            grad = grad_all[here, :]
            d_probs = dot_nt(values[span], grad)
            weighted = low.astype(F32) * d_probs
            total = jnp.sum(weighted, axis=0, keepdims=True)
            d_scores = (weighted - low.astype(F32) * total).astype(BF)
            values_sum[span, :] += dot_nn(low, grad)
            keys_sum[span, :] += dot_nn(d_scores, q_ref[here, :])
            d_query = dot_nn(keys_t[:, span], d_scores).T * factor
            d_ref[here, pl.ds(pl.multiple_of(head * E, E), E)] = turned(d_query, c_ref[here, :], s_ref[here, :], True).astype(BF)
            if block == 0:
                ring.pace(2 * head, [(2 * heads, 1)])
        for which, (total, scale) in enumerate(((keys_sum, factor), (values_sum, 1.0))):
            far_out[head, which] = (total[:m, :] * scale).astype(BF)
            near_out[head, which] = (total[m : 2 * m, :] * scale).astype(BF)
            kept[head, which] = total[2 * m :, :] * scale
        near_copy(head).start()

        def settle(which):
            near_copy(which).wait_recv()
            came = near_in[which].astype(F32)
            share = core.astype(F32)
            far_out[which] = (far_out[which].astype(F32) + came * share).astype(BF)
            kept[which] = kept[which] + came * (1.0 - share)

            @pl.when(me >= 2)
            def _():
                far_copy(which).start()

        def close(which):
            @pl.when(me < devices - 2)
            def _():
                far_copy(which).wait_recv()
                kept[which] = kept[which] + far_in[which].astype(F32)

            d_key = turned(kept[which, 0], c_ref[...], s_ref[...], True).astype(BF)
            d_ref[:, pl.ds(pl.multiple_of((heads + which) * E, E), E)] = d_key
            d_ref[:, pl.ds(pl.multiple_of((2 * heads + which) * E, E), E)] = kept[which, 1].astype(BF)
            near_copy(which).wait_send()

            @pl.when(me >= 2)
            def _():
                far_copy(which).wait_send()

        @pl.when(head > 0)
        def _():
            settle(head - 1)

        @pl.when(head == heads - 1)
        def _():
            settle(head)

        ring.pace(2 * head + 1, [(2 * heads, 1)])

        @pl.when(head == 1)
        def _():
            flipped_ref[...] = flip_ref[...].T[: flipped_ref.shape[0]]

        @pl.when(head == heads - 1)
        def _():
            def one(which, carry):
                close(which)
                return carry

            lax.fori_loop(0, heads, one, 0)
            ring.finish()

    def head_spec(offset):
        return pl.BlockSpec((m, E), lambda i: (0, i + offset))

    dma = pltpu.SemaphoreType.DMA
    pieces = (heads, 2, m, E)
    return pl.pallas_call(
        kernel,
        grid=(heads,),
        out_shape=[
            jax.ShapeDtypeStruct((m, 3 * columns), BF),
            jax.ShapeDtypeStruct((width, columns), BF),
            jax.ShapeDtypeStruct((rows, out_width), F32),
            jax.ShapeDtypeStruct((out_width, rows), F32),
        ],
        in_specs=[
            head_spec(0), head_spec(0), head_spec(heads), head_spec(0), head_spec(heads), head_spec(0), head_spec(heads),
            pl.BlockSpec((1, blocks, KB, QB), lambda i: (i, 0, 0, 0)),
            head_spec(0),
            pl.BlockSpec((width, E), lambda i: (0, i + 3 * heads)),
            single((m, width)),
            single((width, m)),
            single((m, E)),
            single((m, E)),
            single(flip.shape),
            pl.BlockSpec(memory_space=pl.ANY),
        ],
        out_specs=[
            single((m, 3 * columns)),
            pl.BlockSpec((width, E), lambda i: (0, i)),
            single((rows, out_width)),
            single((out_width, rows)),
        ],
        scratch_shapes=[
            pltpu.VMEM((reach, E), F32), pltpu.VMEM((reach, E), F32),
            pltpu.VMEM(pieces, BF), pltpu.VMEM(pieces, BF), pltpu.VMEM(pieces, BF), pltpu.VMEM(pieces, BF), pltpu.VMEM(pieces, F32),
            dma((heads,)), dma((heads,)), dma((heads,)), dma((heads,)),
            *Ring.scratch(devices, [(rows, ring_width // 2)] * 2),
        ],
        compiler_params=pltpu.CompilerParams(vmem_limit_bytes=VMEM, collective_id=identity, has_side_effects=True),
        cost_estimate=cost(8 * heads * m * KB * E * 2, 2 * heads * m * KB),
        name="attend_back",
    )(query, own, own, near, near, far, far, probs, mixed, w_attn, d_hidden, d_hidden_t, cosine, sine, flip, ring_source)


def back_pass(x_t, d_out, weights, extra, ring_sources, out_widths, costs, identity, name):
    amount, m, columns = d_out.shape
    width = x_t.shape[0]
    devices = lax.axis_size("dp")
    sides = lax.axis_size("tensor")
    tiles = width // TILE
    per = columns // TILE
    total = tiles + amount * per
    count = len(ring_sources)
    shapes = [(source.shape[-2], source.shape[-1] // pieces) for source, _, pieces in ring_sources for _ in range(pieces)]
    groups = [[index] for index in range(len(shapes))]

    def kernel(*refs):
        refs = list(refs)

        def take(number):
            taken = refs[:number]
            del refs[:number]
            return taken

        xt_ref, tile_ref, d_ref = take(3)
        w_refs = take(amount)
        extra_refs = take(2) if extra else None
        sources = [ref if lead is None else ref.at[lead] for ref, (_, lead, _) in zip(take(count), ring_sources)]
        grad_ref, back_ref = take(2)
        extra_out = take(1)[0] if extra else None
        sums = take(count)
        sent, got, y_send, y_recv = take(4)
        terms, goals = [], []
        for source, goal, (array, _, pieces) in zip(sources, sums, ring_sources):
            piece = array.shape[-1] // pieces
            terms += [(source, number * piece, piece) for number in range(pieces)]
            goals += [(goal, number * piece) for number in range(pieces)]
        ring = Ring(devices, terms, goals, groups, refs)
        other = (ring.me, lax.rem(ring.side + 1, sides))
        step = pl.program_id(0)

        def across(which):
            return pltpu.make_async_remote_copy(
                src_ref=sent.at[which], dst_ref=got.at[which], send_sem=y_send.at[which], recv_sem=y_recv.at[which],
                device_id=other, device_id_type=MESH,
            )

        @pl.when(step == 0)
        def _():
            ring.barrier((other,))
            ring.begin()

        @pl.when(step < tiles)
        def _():
            part = None
            for index in range(amount):
                made = dot_nt(d_ref[index], w_refs[index][...])
                part = made if part is None else part + made
            sent[step] = part.astype(BF)
            across(step).start()
            if extra:
                extra_out[...] = dot_nt(extra_refs[0][...], extra_refs[1][...]).astype(BF)

        @pl.when(step >= tiles)
        def _():
            grad_ref[0] = dot_nn(xt_ref[...], tile_ref[0]).astype(BF)

        ring.pace(step, [(tiles, costs[0]), (amount * per, costs[1])])

        @pl.when(step == total - 1)
        def _():
            for which in range(tiles):
                across(which).wait()
                back_ref[:, which * TILE : (which + 1) * TILE] = sent[which].astype(F32) + got[which].astype(F32)
            ring.finish()

    def late(i):
        return jnp.maximum(i - tiles, 0)

    def early(i):
        return jnp.minimum(i, tiles - 1)

    specs = [
        single((width, m)),
        pl.BlockSpec((1, m, TILE), lambda i: (late(i) // per, 0, late(i) % per)),
        single((amount, m, columns)),
    ]
    operands = [x_t, d_out, d_out]
    for index in range(amount):
        specs.append(pl.BlockSpec((TILE, columns), functools.partial(lambda where, i: (early(i), where), index)))
        operands.append(weights)
    out_specs = [pl.BlockSpec((1, width, TILE), lambda i: (late(i) // per, 0, late(i) % per)), single((m, width))]
    out_shape = [jax.ShapeDtypeStruct((amount, width, columns), BF), jax.ShapeDtypeStruct((m, width), F32)]
    if extra:
        x, w, where = extra
        specs += [single(x.shape), pl.BlockSpec((TILE, x.shape[1]), lambda i: (early(i), where))]
        operands += [x, w]
        out_specs.append(pl.BlockSpec((m, TILE), lambda i: (0, early(i))))
        out_shape.append(jax.ShapeDtypeStruct((m, width), BF))
    specs += [pl.BlockSpec(memory_space=pl.ANY)] * count
    operands += [source for source, _, _ in ring_sources]
    for (source, _, _), out_width in zip(ring_sources, out_widths):
        rows = source.shape[-2]
        out_specs.append(single((rows, out_width)))
        out_shape.append(jax.ShapeDtypeStruct((rows, out_width), F32))
    dma = pltpu.SemaphoreType.DMA
    return pl.pallas_call(
        kernel,
        grid=(total,),
        out_shape=out_shape,
        in_specs=specs,
        out_specs=out_specs,
        scratch_shapes=[
            pltpu.VMEM((tiles, m, TILE), BF),
            pltpu.VMEM((tiles, m, TILE), BF),
            dma((tiles,)),
            dma((tiles,)),
            *Ring.scratch(devices, shapes),
        ],
        compiler_params=pltpu.CompilerParams(vmem_limit_bytes=VMEM, collective_id=identity, has_side_effects=True),
        cost_estimate=cost(4 * m * width * amount * columns, 6 * width * amount * columns),
        name=name,
    )(*operands)


def root_of(rows):
    return lax.rsqrt(jnp.mean(rows * rows, axis=-1, keepdims=True) + EPS)


def norm_grad(rows, gain, grad):
    root = root_of(rows)
    pushed = grad * gain
    inner = jnp.mean(pushed * rows, axis=-1, keepdims=True)
    return root * pushed - rows * (root * root * root * inner), jnp.sum(grad * rows * root, axis=0, keepdims=True)


def first_norm(tokens, gain):
    m, width = tokens.shape

    def kernel(x_ref, g_ref, o_ref, t_ref):
        rows = x_ref[...].astype(F32)
        normed = (rows * root_of(rows) * g_ref[...]).astype(BF)
        o_ref[...] = normed
        t_ref[...] = normed.T

    rows_spec = pl.BlockSpec((ROWS, width), lambda i: (i, 0))
    return pl.pallas_call(
        kernel,
        grid=(m // ROWS,),
        out_shape=[jax.ShapeDtypeStruct((m, width), BF), jax.ShapeDtypeStruct((width, m), BF)],
        in_specs=[rows_spec, whole_spec((1, width))],
        out_specs=[rows_spec, pl.BlockSpec((width, ROWS), lambda i: (0, i))],
        compiler_params=pltpu.CompilerParams(vmem_limit_bytes=VMEM),
        cost_estimate=cost(8 * m * width, 6 * m * width),
        name="first_norm",
    )(tokens, gain)


def out_norm(mixed, w_attn, place, tokens, gain, identity):
    m, columns = mixed.shape
    width = tokens.shape[1]
    steps = m // ROWS
    sides = lax.axis_size("tensor")

    def kernel(x_ref, w_ref, r_ref, g_ref, hidden_ref, normed_ref, turned_ref, sent, got, send, recv):
        step = pl.program_id(0)
        other = (lax.axis_index("dp"), lax.rem(lax.axis_index("tensor") + 1, sides))

        @pl.when(step == 0)
        def _():
            semaphore = pltpu.get_barrier_semaphore()
            pl.semaphore_signal(semaphore, inc=1, device_id=other, device_id_type=MESH)
            pl.semaphore_wait(semaphore, 1)

        def across(which):
            return pltpu.make_async_remote_copy(
                src_ref=sent.at[which], dst_ref=got.at[which], send_sem=send.at[which], recv_sem=recv.at[which],
                device_id=other, device_id_type=MESH,
            )

        @pl.when(step < steps)
        def _():
            sent[step] = dot_nt(x_ref[...], w_ref[...]).astype(BF)
            across(step).start()

        @pl.when(step >= steps)
        def _():
            which = step - steps
            across(which).wait()
            hidden = r_ref[...].astype(F32) + (sent[which].astype(F32) + got[which].astype(F32))
            normed = (hidden * root_of(hidden) * g_ref[...]).astype(BF)
            hidden_ref[...] = hidden
            normed_ref[...] = normed
            turned_ref[...] = normed.T

    def late(i):
        return jnp.maximum(i - steps, 0)

    late_rows = pl.BlockSpec((ROWS, width), lambda i: (late(i), 0))
    dma = pltpu.SemaphoreType.DMA
    return pl.pallas_call(
        kernel,
        grid=(2 * steps,),
        out_shape=[
            jax.ShapeDtypeStruct((m, width), F32),
            jax.ShapeDtypeStruct((m, width), BF),
            jax.ShapeDtypeStruct((width, m), BF),
        ],
        in_specs=[
            pl.BlockSpec((ROWS, columns), lambda i: (jnp.minimum(i, steps - 1), 0)),
            pl.BlockSpec((width, columns), lambda i: (0, place), pipeline_mode=pl.Buffered(1)),
            late_rows,
            single((1, width)),
        ],
        out_specs=[late_rows, late_rows, pl.BlockSpec((width, ROWS), lambda i: (0, late(i)))],
        scratch_shapes=[pltpu.VMEM((steps, ROWS, width), BF), pltpu.VMEM((steps, ROWS, width), BF), dma((steps,)), dma((steps,))],
        compiler_params=pltpu.CompilerParams(vmem_limit_bytes=VMEM, collective_id=identity, has_side_effects=True),
        cost_estimate=cost(2 * m * width * columns, 12 * m * width),
        name="out_norm",
    )(mixed, w_attn, tokens, gain)


def hidden_grad(hidden, gain, grad, cotangent):
    m, width = hidden.shape

    def kernel(h_ref, g_ref, d_ref, y_ref, o_ref, low_ref, turned_ref, gain_ref):
        change, gain_part = norm_grad(h_ref[...], g_ref[...], d_ref[...])
        total = y_ref[...].astype(F32) + change
        low = total.astype(BF)
        o_ref[...] = total
        low_ref[...] = low
        turned_ref[...] = low.T

        @pl.when(pl.program_id(0) == 0)
        def _():
            gain_ref[...] = gain_part

        @pl.when(pl.program_id(0) > 0)
        def _():
            gain_ref[...] += gain_part

    rows_spec = pl.BlockSpec((ROWS, width), lambda i: (i, 0))
    return pl.pallas_call(
        kernel,
        grid=(m // ROWS,),
        out_shape=[
            jax.ShapeDtypeStruct((m, width), F32),
            jax.ShapeDtypeStruct((m, width), BF),
            jax.ShapeDtypeStruct((width, m), BF),
            jax.ShapeDtypeStruct((1, width), F32),
        ],
        in_specs=[rows_spec, whole_spec((1, width)), rows_spec, rows_spec],
        out_specs=[rows_spec, rows_spec, pl.BlockSpec((width, ROWS), lambda i: (0, i)), whole_spec((1, width))],
        compiler_params=pltpu.CompilerParams(vmem_limit_bytes=VMEM),
        cost_estimate=cost(16 * m * width, 18 * m * width),
        name="hidden_grad",
    )(hidden, gain, grad, cotangent)


def last_pass(tokens, gain, grad, d_hidden, hidden, ffn_part, ffn_other, gain_ffn_grad, flip, qkv_part, lanes, identity):
    m, width = tokens.shape
    devices, rows, all_columns = qkv_part.shape
    columns = all_columns // 3
    chips = devices // 2
    size = ROWS // 2
    steps = m // size
    total = steps + chips
    names = 3

    def kernel(x_ref, g_ref, dn_ref, dh_ref, h_ref, p_ref, o_ref, gf_ref, flip_ref, source, grad_ref, layer_ref, flipped_ref, q_ref, k_ref, v_ref, gains_ref, gain_sum, gain_source, *scratch):
        step = pl.program_id(0)
        ring = Ring(
            devices, [(source, number * columns, columns) for number in range(names)], [(q_ref, 0), (k_ref, 0), (v_ref, 0)],
            [[0], [1], [2]], scratch[: 3 * names + 5],
        )
        gain_ring = Ring(devices, [(gain_source, 0, lanes)], [(gains_ref, 0)], [[0]], scratch[3 * names + 5 :])

        @pl.when(step == 0)
        def _():
            ring.barrier()
            ring.begin()

        @pl.when(step < steps)
        def _():
            change, gain_part = norm_grad(x_ref[...].astype(F32), g_ref[...], dn_ref[...])
            grad_ref[...] = dh_ref[...] + change
            layer_ref[...] = (h_ref[...] + (p_ref[...].astype(F32) + o_ref[...].astype(F32))).astype(BF)

            @pl.when(step == 0)
            def _():
                gain_sum[...] = gain_part
                flipped_ref[...] = flip_ref[...].T

            @pl.when(step > 0)
            def _():
                gain_sum[...] += gain_part

        @pl.when(step == steps - 1)
        def _():
            gain_source[...] = jnp.zeros_like(gain_source)
            for device in range(devices):
                span = slice(device * rows, (device + 1) * rows)
                gain_source[device, :16, :rows] = jnp.broadcast_to(gain_sum[:, span], (16, rows)).astype(BF)
                gain_source[device, 16:, :rows] = jnp.broadcast_to(gf_ref[:, span], (16, rows)).astype(BF)
            gain_ring.begin()

        ring.pace(step, [(steps, 3), (chips, 4)])

        @pl.when(step >= steps)
        def _():
            gain_ring.run(step - steps, step - steps + 1)

        @pl.when(step == total - 1)
        def _():
            ring.finish()
            gain_ring.finish()

    def early(i):
        return jnp.minimum(i, steps - 1)

    rows_spec = pl.BlockSpec((size, width), lambda i: (early(i), 0))
    sums = jax.ShapeDtypeStruct((rows, columns), F32)
    return pl.pallas_call(
        kernel,
        grid=(total,),
        out_shape=[
            jax.ShapeDtypeStruct((m, width), F32),
            jax.ShapeDtypeStruct((m, width), BF),
            jax.ShapeDtypeStruct((flip.shape[1], flip.shape[0]), F32),
            sums, sums, sums,
            jax.ShapeDtypeStruct((32, lanes), F32),
        ],
        in_specs=[
            rows_spec, single((1, width)), rows_spec, rows_spec, rows_spec, rows_spec, rows_spec, single((1, width)),
            single(flip.shape), pl.BlockSpec(memory_space=pl.ANY),
        ],
        out_specs=[
            rows_spec, rows_spec, single((flip.shape[1], flip.shape[0])),
            single(sums.shape), single(sums.shape), single(sums.shape), single((32, lanes)),
        ],
        scratch_shapes=[
            pltpu.VMEM((1, width), F32),
            pltpu.VMEM((devices, 32, lanes), BF),
            *Ring.scratch(devices, [(rows, columns)] * names),
            *Ring.scratch(devices, [(32, lanes)]),
        ],
        compiler_params=pltpu.CompilerParams(vmem_limit_bytes=VMEM, collective_id=identity, has_side_effects=True),
        cost_estimate=cost(20 * m * width, 24 * m * width),
        name="last_pass",
    )(tokens, gain, grad, d_hidden, hidden, ffn_part, ffn_other, gain_ffn_grad, flip, qkv_part)


def feed(x, dy, w, tiles):
    m, k = x.shape

    def kernel(x_ref, dy_ref, g_ref, u_ref, d_ref, act_ref, both_ref):
        gate = dot_nn(x_ref[...], g_ref[...])
        up = dot_nn(x_ref[...], u_ref[...])
        d_act = dot_nn(dy_ref[...], d_ref[...])
        soft = 1.0 / (1.0 + jnp.exp(-gate))
        silu = gate * soft
        act_ref[...] = (silu * up).astype(BF)
        both_ref[0] = (d_act * up * (soft * (1.0 + gate * (1.0 - soft)))).astype(BF)
        both_ref[1] = (d_act * silu).astype(BF)

    tile = pl.BlockSpec((m, TILE), lambda i: (0, i))
    return pl.pallas_call(
        kernel,
        grid=(tiles,),
        out_shape=[jax.ShapeDtypeStruct((m, tiles * TILE), BF), jax.ShapeDtypeStruct((2, m, tiles * TILE), BF)],
        in_specs=[
            whole_spec((m, k)),
            whole_spec((m, k)),
            pl.BlockSpec((k, TILE), lambda i: (0, i)),
            pl.BlockSpec((k, TILE), lambda i: (0, i + tiles)),
            pl.BlockSpec((k, TILE), lambda i: (0, i + 2 * tiles)),
        ],
        out_specs=[tile, pl.BlockSpec((2, m, TILE), lambda i: (0, 0, i))],
        compiler_params=pltpu.CompilerParams(vmem_limit_bytes=VMEM),
        cost_estimate=cost(6 * m * k * tiles * TILE, 6 * (m + k) * tiles * TILE, m * tiles * TILE),
        name="feed",
    )(x, dy, w, w, w)


def shards(tokens, positions, attn_gain, w_query, w_key, w_value, w_out, ffn_gain, w_gate, w_up, w_down, cotangent):
    devices = lax.axis_size("dp")
    core = lax.axis_index("dp") % 2
    sides = lax.axis_size("tensor")
    flip = [(i, (i + 1) % sides) for i in range(sides)]
    span = tokens.shape[0]
    own_rows = w_query.shape[0]
    width = tokens.shape[1]
    head_columns = w_query.shape[1]
    heads = head_columns // E
    hidden_units = w_gate.shape[1]
    tiles = (hidden_units + TILE - 1) // TILE
    padded = tiles * TILE

    attn_pack = jnp.concatenate([w_query, w_key, w_value, w_out.T], axis=1)
    lanes = max(128, own_rows)
    gains = jnp.zeros((32, lanes), BF).at[0, :own_rows].set(attn_gain).at[16, :own_rows].set(ffn_gain)
    w_attn, all_gains = ring_gather((attn_pack, gains), (2, 1), 0)

    def wide(matrix):
        return jnp.pad(matrix, ((0, 0), (0, padded - hidden_units)))

    ffn_pack = jnp.concatenate([wide(w_gate), wide(w_up), wide(w_down.T)], axis=1)
    w_attn, all_gains, ffn_pack = lax.optimization_barrier((w_attn, all_gains, ffn_pack))
    w_ffn = lax.all_gather(ffn_pack, "dp", axis=0, tiled=True)
    all_gains = all_gains.reshape(devices, 32, lanes)
    gain_attn = all_gains[:, 0, :own_rows].reshape(1, width).astype(F32)
    gain_ffn = all_gains[:, 16, :own_rows].reshape(1, width).astype(F32)

    frequency = THETA ** (-(jnp.arange(E // 2, dtype=F32) * 2.0 / E))
    angles = positions.astype(F32)[:, None] * frequency[None, :]
    cosine_half, sine_half = jnp.cos(angles), jnp.sin(angles)
    cosine = jnp.concatenate([cosine_half, cosine_half], axis=1)
    sine = jnp.concatenate([-sine_half, sine_half], axis=1)

    normed_attn, normed_attn_t = first_norm(tokens, gain_attn)
    query, own_kv = project(normed_attn, w_attn, cosine, sine, heads)
    far = lax.ppermute(own_kv, "dp", [(i - 2, i) for i in range(2, devices)])
    near = lax.ppermute(jnp.where(core == 0, own_kv, far), "dp", swap_route(devices))
    mixed, probs = attend(query, own_kv, near, far, positions[None, :], heads)
    hidden, normed_ffn, normed_ffn_t = out_norm(mixed, w_attn, 3, tokens, gain_ffn, 5)

    activated, d_both = feed(normed_ffn, cotangent, w_ffn, tiles)
    down_part = matmul_nn(cotangent.T, activated, 0, tiles, "down_grad").reshape(devices, own_rows, padded)
    both_part, d_normed_ffn, ffn_part, down_grad = back_pass(
        normed_ffn_t, d_both, w_ffn, (activated, w_ffn, 2), [(down_part, None, 2)], [padded], (13, 4), 1, "ffn_back"
    )
    both_part = both_part.reshape(2, devices, own_rows, padded)
    ffn_other = lax.ppermute(ffn_part, "tensor", flip)
    d_hidden, d_hidden_low, d_hidden_t, gain_ffn_grad = hidden_grad(hidden, gain_ffn, d_normed_ffn, cotangent)

    d_qkv, out_part, gate_grad, w_down_grad = attend_back(
        query, own_kv, near, far, probs, mixed, w_attn, d_hidden_low, d_hidden_t, cosine, sine, down_grad, both_part, heads, hidden_units, 2
    )
    qkv_part, d_normed_attn, up_grad, out_grad = back_pass(
        normed_attn_t, d_qkv[None], w_attn, None,
        [(both_part, 1, 2), (out_part.reshape(devices, own_rows, head_columns), None, 1)], [hidden_units, head_columns], (4, 3), 3, "qkv_back",
    )
    tokens_grad, layer_out, w_out_grad, query_grad, key_grad, value_grad, gain_grads = last_pass(
        tokens, gain_attn, d_normed_attn, d_hidden, hidden, ffn_part, ffn_other, gain_ffn_grad, out_grad,
        qkv_part.reshape(devices, own_rows, 3 * head_columns), lanes, 4,
    )
    return (
        layer_out,
        tokens_grad,
        gain_grads[0, :own_rows],
        query_grad,
        key_grad,
        value_grad,
        w_out_grad,
        gain_grads[16, :own_rows],
        gate_grad,
        up_grad,
        w_down_grad,
    )


def solution(mesh):
    by_rows, by_both, turned_both, line = P("dp", None), P("dp", "tensor"), P("tensor", "dp"), P("dp")
    return jax.shard_map(
        shards,
        mesh=mesh,
        in_specs=(by_rows, line, line, by_both, by_both, by_both, turned_both, line, by_both, by_both, turned_both, by_rows),
        out_specs=(by_rows, by_rows, line, by_both, by_both, by_both, turned_both, line, by_both, by_both, turned_both),
        check_vma=False,
    )
```

```python
import functools

import jax
import jax.numpy as jnp
from jax import lax
from jax.experimental import pallas as pl
from jax.experimental.pallas import tpu as pltpu
from jax.sharding import PartitionSpec as P

E = 128
WINDOW = 1024
EPS = 1e-06
THETA = 10000.0
LOG2E = 1.4426950408889634
MESH = pl.DeviceIdType.MESH
BF = jnp.bfloat16
F32 = jnp.float32
QB = 256
KB = WINDOW + QB
TILE = 256
ROWS = 128
VMEM = 56 * 1024 * 1024


def whole_spec(shape):
    return pl.BlockSpec(shape, lambda i: (0,) * len(shape))


def single(shape):
    return pl.BlockSpec(shape, lambda i: (0,) * len(shape), pipeline_mode=pl.Buffered(1))


def cost(flops, nbytes, special=0):
    return pl.CostEstimate(flops=flops, bytes_accessed=nbytes, transcendentals=special)


def ring_chip(place, chips):
    place = lax.rem(place + 2 * chips, chips)
    late = place // (chips // 2)
    return (1 - late) * 2 * place + late * (2 * (chips - 1 - place) + 1)


def ring_place(chip, chips):
    column = lax.rem(chip, 2)
    row = chip // 2
    return (1 - column) * row + column * (chips - 1 - row)


def gather_kernel(devices, chunks, count, *refs):
    ins, tokens = refs[:count], refs[count]
    outs, near, far = refs[count + 1 : 2 * count + 1], refs[2 * count + 1], refs[2 * count + 2]
    local_sem, a_send, a_recv, b_send, b_recv, c_send, c_recv, far_send, far_recv, near_send, near_recv = refs[2 * count + 3 :]
    chips = devices // 2
    me = lax.axis_index("dp")
    side = lax.axis_index("tensor")
    core = lax.rem(me, 2)
    place = ring_place(me // 2, chips)

    def device(q):
        return ring_chip(q, chips) * 2 + core

    right = device(place + 1)
    left = device(place - 1)
    partner = me + 1 - 2 * core
    across = lax.rem(side + 1, lax.axis_size("tensor"))
    later, before = lax.rem(me + 2, devices), lax.rem(me + devices - 2, devices)
    barrier = pltpu.get_barrier_semaphore()
    for other in ((right, side), (left, side), (partner, side), (me, across), (later, side), (before, side)):
        pl.semaphore_signal(barrier, inc=1, device_id=other, device_id_type=MESH)
    pl.semaphore_wait(barrier, 6)

    pieces = []
    for index, parts in enumerate(chunks):
        width = ins[index].shape[1] // parts
        for part in range(parts):
            pieces.append((index, part * width, width))
    hops = chips - 1

    def view(ref, row, half, piece, rows):
        index, column, width = piece
        start = row * rows + half * (rows // 2)
        if not isinstance(start, int):
            start = pl.multiple_of(start, 16)
        return ref.at[pl.ds(start, rows // 2), pl.ds(column, width)]

    def described(source, target, send, recv, other):
        return pltpu.make_async_remote_copy(
            src_ref=source, dst_ref=target, send_sem=send, recv_sem=recv, device_id=other, device_id_type=MESH
        )

    def remote(source, target, send, recv, other):
        copy = described(source, target, send, recv, (other, side))
        copy.start()
        return copy

    span = tokens.shape[0] // 2

    def half_rows(ref, which):
        return ref.at[pl.ds(pl.multiple_of(which * span, span), span)]

    far_copy = described(half_rows(tokens, side), half_rows(far, side), far_send.at[0], far_recv.at[0], (later, side))
    cross_copy = described(half_rows(far, side), half_rows(far, side), far_send.at[1], far_recv.at[1], (me, across))
    own_near = [described(half_rows(tokens, which), half_rows(near, which), near_send.at[which], near_recv.at[which], (partner, side)) for which in range(2)]
    far_near = [described(half_rows(far, which), half_rows(near, which), near_send.at[slot], near_recv.at[slot], (partner, side)) for slot, which in enumerate((side, across))]

    @pl.when(me < devices - 2)
    def _():
        far_copy.start()

    @pl.when(core == 0)
    def _():
        for copy in own_near:
            copy.start()

    def pass_on(slot):
        @pl.when(me >= 2)
        def _():
            if slot == 0:
                far_copy.wait_recv()
                cross_copy.start()
            else:
                cross_copy.wait_recv()

            @pl.when(core == 1)
            def _():
                far_near[slot].start()

    local = []
    for index in range(count):
        rows = ins[index].shape[0]
        copy = pltpu.make_async_copy(
            ins[index], outs[index].at[pl.ds(pl.multiple_of(me * rows, 16), rows)], local_sem.at[index]
        )
        copy.start()
        local.append(copy)
    forward, partner_copies = {}, []
    for number, piece in enumerate(pieces):
        ref, out = ins[piece[0]], outs[piece[0]]
        rows = ref.shape[0]
        forward[number, 0] = (
            remote(view(ref, 0, 0, piece, rows), view(out, me, 0, piece, rows), a_send.at[number, 0], a_recv.at[number, 0], right),
            remote(view(ref, 0, 1, piece, rows), view(out, me, 1, piece, rows), b_send.at[number, 0], b_recv.at[number, 0], left),
        )
    for number, piece in enumerate(pieces):
        ref, out = ins[piece[0]], outs[piece[0]]
        rows = ref.shape[0]
        for half in range(2):
            partner_copies.append(
                remote(view(ref, 0, half, piece, rows), view(out, me, half, piece, rows), c_send.at[number, 0, half], c_recv.at[number, 0, half], partner)
            )
    for hop in range(hops):
        for number, piece in enumerate(pieces):
            out = outs[piece[0]]
            rows = ins[piece[0]].shape[0]
            came = forward[number, hop]
            sent = []
            for half in range(2):
                came[half].wait_recv()
                owner = device(place - 1 - hop if half == 0 else place + 1 + hop)
                block = view(out, owner, half, piece, rows)
                send, recv = (a_send, a_recv) if half == 0 else (b_send, b_recv)
                if hop < hops - 1:
                    sent.append(
                        remote(block, block, send.at[number, hop + 1], recv.at[number, hop + 1], right if half == 0 else left)
                    )
                partner_copies.append(
                    remote(block, block, c_send.at[number, hop + 1, half], c_recv.at[number, hop + 1, half], partner)
                )
            if sent:
                forward[number, hop + 1] = tuple(sent)
        if hop == hops // 2:
            pass_on(0)
        if hop == hops - 2:
            pass_on(1)
    for copy in local:
        copy.wait()
    for pair in forward.values():
        for copy in pair:
            copy.wait_send()
    for copy in partner_copies:
        copy.wait()

    @pl.when(me < devices - 2)
    def _():
        far_copy.wait_send()

    @pl.when(me >= 2)
    def _():
        cross_copy.wait_send()

        @pl.when(core == 1)
        def _():
            for copy in far_near:
                copy.wait_send()

    @pl.when(core == 0)
    def _():
        for copy in own_near:
            copy.wait_send()

    @pl.when((core == 1) | (me >= 2))
    def _():
        for copy in own_near:
            copy.wait_recv()


def ring_gather(arrays, chunks, tokens, identity):
    devices = lax.axis_size("dp")
    hops = devices // 2 - 1
    pieces = sum(chunks)
    dma = pltpu.SemaphoreType.DMA
    any_space = pl.BlockSpec(memory_space=pl.ANY)
    return pl.pallas_call(
        functools.partial(gather_kernel, devices, chunks, len(arrays)),
        out_shape=[jax.ShapeDtypeStruct((a.shape[0] * devices, a.shape[1]), a.dtype) for a in arrays]
        + [jax.ShapeDtypeStruct(tokens.shape, tokens.dtype)] * 2,
        in_specs=[any_space] * (len(arrays) + 1),
        out_specs=[any_space] * (len(arrays) + 2),
        scratch_shapes=[
            dma((len(arrays),)),
            dma((pieces, hops)),
            dma((pieces, hops)),
            dma((pieces, hops)),
            dma((pieces, hops)),
            dma((pieces, hops + 1, 2)),
            dma((pieces, hops + 1, 2)),
            dma((2,)),
            dma((2,)),
            dma((2,)),
            dma((2,)),
        ],
        compiler_params=pltpu.CompilerParams(collective_id=identity, has_side_effects=True),
        name="ring_gather",
    )(*arrays, tokens)


class Ring:
    AHEAD = 3

    def __init__(self, devices, terms, goals, groups, scratch):
        self.devices, self.chips = devices, devices // 2
        self.terms, self.goals, self.groups = terms, goals, groups
        count = len(terms)
        self.mine, self.taken, self.inbox = scratch[0 : 3 * count : 3], scratch[1 : 3 * count : 3], scratch[2 : 3 * count : 3]
        self.own_sem, self.give_sem, self.take_sem, self.send_sem, self.recv_sem = scratch[3 * count : 3 * count + 5]
        self.me = lax.axis_index("dp")
        self.side = lax.axis_index("tensor")
        self.core = lax.rem(self.me, 2)
        self.place = ring_place(self.me // 2, self.chips)
        self.partner = self.me + 1 - 2 * self.core
        self.next = (
            ring_chip(self.place + 1, self.chips) * 2 + self.core,
            ring_chip(self.place - 1, self.chips) * 2 + self.core,
        )
        self.events = self.chips * len(groups)

    @staticmethod
    def scratch(devices, shapes):
        chips, count = devices // 2, len(shapes)
        dma = pltpu.SemaphoreType.DMA
        buffers = []
        for rows, width in shapes:
            buffers += [pltpu.VMEM((amount, 2, rows // 2, width), BF) for amount in (chips, chips, chips - 1)]
        return buffers + [dma((count, amount, 2)) for amount in (chips, chips, chips, chips - 1, chips - 1)]

    def barrier(self, others=()):
        semaphore = pltpu.get_barrier_semaphore()
        everyone = [(self.next[0], self.side), (self.next[1], self.side), (self.partner, self.side), *others]
        for other in everyone:
            pl.semaphore_signal(semaphore, inc=1, device_id=other, device_id_type=MESH)
        pl.semaphore_wait(semaphore, len(everyone))

    def block(self, index, stage, half, core):
        at = self.place - 1 - stage if half == 0 else self.place + 1 + stage
        size = self.mine[index].shape[2]
        source, column, width = self.terms[index]
        return source.at[ring_chip(at, self.chips) * 2 + core, pl.ds(half * size, size), pl.ds(column, width)]

    def own(self, index, stage, half):
        return pltpu.make_async_copy(
            self.block(index, stage, half, self.core), self.mine[index].at[stage, half], self.own_sem.at[index, stage, half]
        )

    def given(self, index, stage, half):
        return pltpu.make_async_remote_copy(
            src_ref=self.block(index, stage, half, 1 - self.core),
            dst_ref=self.taken[index].at[stage, half],
            send_sem=self.give_sem.at[index, stage, half],
            recv_sem=self.take_sem.at[index, stage, half],
            device_id=(self.partner, self.side),
            device_id_type=MESH,
        )

    def hop(self, index, stage, half, first):
        source = self.mine[index].at[0, half] if first else self.inbox[index].at[stage - 1, half]
        return pltpu.make_async_remote_copy(
            src_ref=source,
            dst_ref=self.inbox[index].at[stage, half],
            send_sem=self.send_sem.at[index, stage, half],
            recv_sem=self.recv_sem.at[index, stage, half],
            device_id=(self.next[half], self.side),
            device_id_type=MESH,
        )

    def each(self, group=None):
        members = range(len(self.terms)) if group is None else self.groups[group]
        return [(index, half) for index in members for half in range(2)]

    def fetch(self, stage, group):
        for index, half in self.each(group):
            self.given(index, stage, half).start()
            self.own(index, stage, half).start()

    def begin(self):
        for stage in range(min(self.AHEAD, self.chips)):
            for group in range(len(self.groups)):
                self.fetch(stage, group)

    def chip_term(self, index, stage, half):
        self.own(index, stage, half).wait()
        self.given(index, stage, half).wait_recv()
        return self.mine[index][stage, half].astype(F32) + self.taken[index][stage, half].astype(F32)

    def stage(self, stage, group):
        last = self.chips - 1

        @pl.when(stage == 0)
        def _():
            for index, half in self.each(group):
                self.mine[index][0, half] = self.chip_term(index, 0, half).astype(BF)
                self.hop(index, 0, half, True).start()

        @pl.when((stage > 0) & (stage < last))
        def _():
            for index, half in self.each(group):
                self.hop(index, stage - 1, half, True).wait_recv()
                came = self.inbox[index][stage - 1, half].astype(F32)
                self.inbox[index][stage - 1, half] = (came + self.chip_term(index, stage, half)).astype(BF)
                self.hop(index, stage, half, False).start()

        @pl.when(stage + self.AHEAD < self.chips)
        def _():
            self.fetch(stage + self.AHEAD, group)

        @pl.when(stage == last)
        def _():
            for index, half in self.each(group):
                self.hop(index, last - 1, half, True).wait_recv()
                came = self.inbox[index][last - 1, half].astype(F32)
                size = came.shape[0]
                total = came + self.chip_term(index, last, half)
                goal, column = self.goals[index]
                width = min(goal.shape[1] - column, total.shape[1])
                goal[half * size : (half + 1) * size, column : column + width] = total[:, :width]

    def run(self, first, stop):
        count = len(self.groups)

        def one(event, carry):
            for group in range(count):
                if count == 1:
                    self.stage(event, 0)
                else:
                    pl.when(lax.rem(event, count) == group)(functools.partial(self.stage, event // count, group))
            return carry

        lax.fori_loop(first, stop, one, 0)

    def pace(self, step, costs):
        whole = sum(steps * each for steps, each in costs)

        def done(at):
            spent, before = 0, 0
            for steps, each in costs:
                spent = spent + jnp.minimum(jnp.maximum(at - before, 0), steps) * each
                before += steps
            return spent * self.events // whole

        self.run(done(step), done(step + 1))

    def finish(self):
        for index, half in self.each():
            self.hop(index, 0, half, True).wait_send()

        def sent(stage, carry):
            for index, half in self.each():
                self.hop(index, stage, half, False).wait_send()
            return carry

        lax.fori_loop(1, self.chips - 1, sent, 0)

        def gave(stage, carry):
            for index, half in self.each():
                self.given(index, stage, half).wait_send()
            return carry

        lax.fori_loop(0, self.chips, gave, 0)


def dot_nn(a, b):
    return jnp.dot(a, b, preferred_element_type=F32)


def dot_nt(a, b):
    return lax.dot_general(a, b, (((1,), (1,)), ((), ())), preferred_element_type=F32)


def matmul_nn(x, w, first, count, name):
    m, k = x.shape

    def kernel(x_ref, w_ref, o_ref):
        o_ref[...] = dot_nn(x_ref[...], w_ref[...]).astype(BF)

    return pl.pallas_call(
        kernel,
        grid=(count,),
        out_shape=jax.ShapeDtypeStruct((m, count * TILE), BF),
        in_specs=[whole_spec((m, k)), pl.BlockSpec((k, TILE), lambda i: (0, i + first))],
        out_specs=pl.BlockSpec((m, TILE), lambda i: (0, i)),
        compiler_params=pltpu.CompilerParams(vmem_limit_bytes=VMEM),
        cost_estimate=cost(2 * m * k * count * TILE, 2 * (m * k + (m + k) * count * TILE)),
        name=name,
    )(x, w)


def turned(block, cosine, sine, back):
    other = pltpu.roll(block, E // 2, 1)
    if back:
        return block * cosine - other * sine
    return block * cosine + other * sine


def project(x, w, cosine, sine, own, heads):
    m, k = x.shape
    per = TILE // E
    some = heads // per

    def kernel(x_ref, w_ref, c_ref, s_ref, q_ref, kv_ref):
        step = pl.program_id(0)

        def rotate_to(ref, made, rows):
            for part in range(per):
                piece = slice(part * E, (part + 1) * E)
                ref[:, piece] = turned(made[:, piece], c_ref[rows, :], s_ref[rows, :], False).astype(BF)

        @pl.when(step < some)
        def _():
            rows = slice(m - own, m)
            rotate_to(q_ref, dot_nn(x_ref[rows, :], w_ref[...]), rows)

        @pl.when((step >= some) & (step < 2 * some))
        def _():
            rotate_to(kv_ref, dot_nn(x_ref[...], w_ref[...]), slice(0, m))

        @pl.when(step >= 2 * some)
        def _():
            kv_ref[...] = dot_nn(x_ref[...], w_ref[...]).astype(BF)

    return pl.pallas_call(
        kernel,
        grid=(3 * some,),
        out_shape=[jax.ShapeDtypeStruct((own, heads * E), BF), jax.ShapeDtypeStruct((m, 2 * heads * E), BF)],
        in_specs=[single((m, k)), pl.BlockSpec((k, TILE), lambda i: (0, i)), single((m, E)), single((m, E))],
        out_specs=[
            pl.BlockSpec((own, TILE), lambda i: (0, jnp.minimum(i, some - 1))),
            pl.BlockSpec((m, TILE), lambda i: (0, jnp.maximum(i - some, 0))),
        ],
        compiler_params=pltpu.CompilerParams(vmem_limit_bytes=VMEM),
        cost_estimate=cost(2 * (own + 2 * m) * k * heads * E, 2 * (m * k + 3 * (m + k) * heads * E)),
        name="project",
    )(x, w, cosine, sine)


def attend(query, kv, places, heads):
    m = query.shape[0]
    blocks = m // QB
    factor = E ** (-0.5) * LOG2E

    def kernel(q_ref, k_ref, v_ref, p_ref, o_ref, probs_ref, bias):
        @pl.when(pl.program_id(0) == 0)
        def _():
            for block in range(blocks):
                key = lax.broadcasted_iota(jnp.int32, (KB, QB), 0) + block * QB
                query = lax.broadcasted_iota(jnp.int32, (KB, QB), 1) + block * QB
                place = p_ref[:, block * QB : (block + 1) * QB]
                allowed = (key <= query + WINDOW) & (key > query) & (key >= query + WINDOW - place)
                bias[block] = jnp.where(allowed, 0.0, -1e30)

        values_t = v_ref[...].T
        for block in range(blocks):
            span = slice(block * QB, block * QB + KB)
            scores = dot_nt(k_ref[span, :], q_ref[block * QB : (block + 1) * QB, :]) * factor + bias[block]
            largest = jnp.max(scores, axis=0, keepdims=True)
            grown = jnp.exp2(scores - largest)
            inverse = 1.0 / jnp.sum(grown, axis=0, keepdims=True)
            probs = (grown * inverse).astype(BF)
            probs_ref[0, block] = probs
            mixed_t = dot_nn(values_t[:, span], probs)
            o_ref[block * QB : (block + 1) * QB, :] = mixed_t.T.astype(BF)

    head = pl.BlockSpec((m, E), lambda i: (0, i))
    reach = kv.shape[0]

    return pl.pallas_call(
        kernel,
        grid=(heads,),
        out_shape=[
            jax.ShapeDtypeStruct((m, heads * E), BF),
            jax.ShapeDtypeStruct((heads, blocks, KB, QB), BF),
        ],
        in_specs=[
            head,
            pl.BlockSpec((reach, E), lambda i: (0, i)),
            pl.BlockSpec((reach, E), lambda i: (0, i + heads)),
            whole_spec((1, m)),
        ],
        out_specs=[head, pl.BlockSpec((1, blocks, KB, QB), lambda i: (i, 0, 0, 0))],
        scratch_shapes=[pltpu.VMEM((blocks, KB, QB), F32)],
        compiler_params=pltpu.CompilerParams(vmem_limit_bytes=VMEM),
        cost_estimate=cost(4 * heads * m * KB * E * 2, 2 * heads * m * KB, heads * m * KB),
        name="attend",
    )(query, kv, kv, places)


def attend_back(query, kv, probs, mixed, w_attn, d_hidden, d_hidden_t, cosine, sine, flip, ring_source, heads, out_width, identity):
    m, width = d_hidden.shape
    devices, rows, ring_width = ring_source.shape[1:]
    blocks = m // QB
    factor = E ** (-0.5)
    reach = WINDOW + m
    columns = heads * E

    def kernel(q_ref, k_ref, v_ref, p_ref, x_ref, w_ref, g_ref, gt_ref, c_ref, s_ref, flip_ref, source, d_ref, out_ref, sum_ref, flipped_ref, keys_sum, values_sum, near_out, near_in, far_out, far_in, kept, near_send, near_recv, far_send, far_recv, *scratch):
        head = pl.program_id(0)
        half = ring_width // 2
        ring = Ring(devices, [(source.at[0], 0, half), (source.at[0], half, half)], [(sum_ref, 0), (sum_ref, half)], [[0], [1]], scratch)
        me, side, core = ring.me, ring.side, ring.core

        @pl.when(head == 0)
        def _():
            ring.barrier(((lax.rem(me + 2, devices), side), (lax.rem(me + devices - 2, devices), side)))
            ring.begin()

        def near_copy(which):
            return pltpu.make_async_remote_copy(
                src_ref=near_out.at[which], dst_ref=near_in.at[which], send_sem=near_send.at[which], recv_sem=near_recv.at[which],
                device_id=(ring.partner, side), device_id_type=MESH,
            )

        def far_copy(which):
            return pltpu.make_async_remote_copy(
                src_ref=far_out.at[which], dst_ref=far_in.at[which], send_sem=far_send.at[which], recv_sem=far_recv.at[which],
                device_id=(lax.rem(me + devices - 2, devices), side), device_id_type=MESH,
            )

        grad_all = dot_nn(g_ref[...], w_ref[...]).astype(BF)
        out_ref[...] = dot_nn(gt_ref[...], x_ref[...]).astype(BF)
        keys_t = k_ref[...].T
        keys_sum[...] = jnp.zeros_like(keys_sum)
        values_sum[...] = jnp.zeros_like(values_sum)
        for block in range(blocks):
            span = slice(block * QB, block * QB + KB)
            here = slice(block * QB, (block + 1) * QB)
            low = p_ref[0, block]
            grad = grad_all[here, :]
            d_probs = dot_nt(v_ref[span, :], grad)
            weighted = low.astype(F32) * d_probs
            total = jnp.sum(weighted, axis=0, keepdims=True)
            d_scores = (weighted - low.astype(F32) * total).astype(BF)
            values_sum[span, :] += dot_nn(low, grad)
            keys_sum[span, :] += dot_nn(d_scores, q_ref[here, :])
            d_query = dot_nn(keys_t[:, span], d_scores).T * factor
            d_ref[here, pl.ds(pl.multiple_of(head * E, E), E)] = turned(d_query, c_ref[here, :], s_ref[here, :], True).astype(BF)
            if block == 0:
                ring.pace(2 * head, [(2 * heads, 1)])
        for which, (total, scale) in enumerate(((keys_sum, factor), (values_sum, 1.0))):
            far_out[head, which] = (total[:m, :] * scale).astype(BF)
            near_out[head, which] = (total[m : 2 * m, :] * scale).astype(BF)
            kept[head, which] = total[2 * m :, :] * scale
        near_copy(head).start()

        def settle(which):
            near_copy(which).wait_recv()
            came = near_in[which].astype(F32)
            share = core.astype(F32)
            far_out[which] = (far_out[which].astype(F32) + came * share).astype(BF)
            kept[which] = kept[which] + came * (1.0 - share)

            @pl.when(me >= 2)
            def _():
                far_copy(which).start()

        def close(which):
            @pl.when(me < devices - 2)
            def _():
                far_copy(which).wait_recv()
                kept[which] = kept[which] + far_in[which].astype(F32)

            d_key = turned(kept[which, 0], c_ref[...], s_ref[...], True).astype(BF)
            d_ref[:, pl.ds(pl.multiple_of((heads + which) * E, E), E)] = d_key
            d_ref[:, pl.ds(pl.multiple_of((2 * heads + which) * E, E), E)] = kept[which, 1].astype(BF)
            near_copy(which).wait_send()

            @pl.when(me >= 2)
            def _():
                far_copy(which).wait_send()

        @pl.when(head > 0)
        def _():
            settle(head - 1)

        @pl.when(head == heads - 1)
        def _():
            settle(head)

        ring.pace(2 * head + 1, [(2 * heads, 1)])

        @pl.when(head == 1)
        def _():
            flipped_ref[...] = flip_ref[...].T[: flipped_ref.shape[0]]

        @pl.when(head == heads - 1)
        def _():
            def one(which, carry):
                close(which)
                return carry

            lax.fori_loop(0, heads, one, 0)
            ring.finish()

    def head_spec(offset):
        return pl.BlockSpec((m, E), lambda i: (0, i + offset))

    dma = pltpu.SemaphoreType.DMA
    pieces = (heads, 2, m, E)
    return pl.pallas_call(
        kernel,
        grid=(heads,),
        out_shape=[
            jax.ShapeDtypeStruct((m, 3 * columns), BF),
            jax.ShapeDtypeStruct((width, columns), BF),
            jax.ShapeDtypeStruct((rows, out_width), F32),
            jax.ShapeDtypeStruct((out_width, rows), F32),
        ],
        in_specs=[
            head_spec(0),
            pl.BlockSpec((reach, E), lambda i: (0, i)),
            pl.BlockSpec((reach, E), lambda i: (0, i + heads)),
            pl.BlockSpec((1, blocks, KB, QB), lambda i: (i, 0, 0, 0)),
            head_spec(0),
            pl.BlockSpec((width, E), lambda i: (0, i + 3 * heads)),
            single((m, width)),
            single((width, m)),
            single((m, E)),
            single((m, E)),
            single(flip.shape),
            pl.BlockSpec(memory_space=pl.ANY),
        ],
        out_specs=[
            single((m, 3 * columns)),
            pl.BlockSpec((width, E), lambda i: (0, i)),
            single((rows, out_width)),
            single((out_width, rows)),
        ],
        scratch_shapes=[
            pltpu.VMEM((reach, E), F32), pltpu.VMEM((reach, E), F32),
            pltpu.VMEM(pieces, BF), pltpu.VMEM(pieces, BF), pltpu.VMEM(pieces, BF), pltpu.VMEM(pieces, BF), pltpu.VMEM(pieces, F32),
            dma((heads,)), dma((heads,)), dma((heads,)), dma((heads,)),
            *Ring.scratch(devices, [(rows, ring_width // 2)] * 2),
        ],
        compiler_params=pltpu.CompilerParams(vmem_limit_bytes=VMEM, collective_id=identity, has_side_effects=True),
        cost_estimate=cost(8 * heads * m * KB * E * 2, 2 * heads * m * KB),
        name="attend_back",
    )(query, kv, kv, probs, mixed, w_attn, d_hidden, d_hidden_t, cosine, sine, flip, ring_source)


def back_pass(x_t, d_out, weights, ring_sources, out_widths, costs, identity, name):
    amount, m, columns = d_out.shape
    width = x_t.shape[0]
    devices = lax.axis_size("dp")
    sides = lax.axis_size("tensor")
    tiles = width // TILE
    per = columns // TILE
    total = tiles + amount * per
    count = len(ring_sources)
    shapes = [(source.shape[-2], source.shape[-1] // pieces) for source, _, pieces in ring_sources for _ in range(pieces)]
    groups = [[index] for index in range(len(shapes))]

    def kernel(*refs):
        refs = list(refs)

        def take(number):
            taken = refs[:number]
            del refs[:number]
            return taken

        xt_ref, tile_ref, d_ref = take(3)
        w_refs = take(amount)
        sources = [ref if lead is None else ref.at[lead] for ref, (_, lead, _) in zip(take(count), ring_sources)]
        grad_ref, back_ref = take(2)
        sums = take(count)
        sent, got, y_send, y_recv = take(4)
        terms, goals = [], []
        for source, goal, (array, _, pieces) in zip(sources, sums, ring_sources):
            piece = array.shape[-1] // pieces
            terms += [(source, number * piece, piece) for number in range(pieces)]
            goals += [(goal, number * piece) for number in range(pieces)]
        ring = Ring(devices, terms, goals, groups, refs)
        other = (ring.me, lax.rem(ring.side + 1, sides))
        step = pl.program_id(0)

        def across(which):
            return pltpu.make_async_remote_copy(
                src_ref=sent.at[which], dst_ref=got.at[which], send_sem=y_send.at[which], recv_sem=y_recv.at[which],
                device_id=other, device_id_type=MESH,
            )

        @pl.when(step == 0)
        def _():
            ring.barrier((other,))
            ring.begin()

        @pl.when(step < tiles)
        def _():
            part = None
            for index in range(amount):
                made = dot_nt(d_ref[index], w_refs[index][...])
                part = made if part is None else part + made
            sent[step] = part.astype(BF)
            across(step).start()

        @pl.when(step >= tiles)
        def _():
            grad_ref[0] = dot_nn(xt_ref[...], tile_ref[0]).astype(BF)

        ring.pace(step, [(tiles, costs[0]), (amount * per, costs[1])])

        @pl.when(step == total - 1)
        def _():
            for which in range(tiles):
                across(which).wait()
                back_ref[:, which * TILE : (which + 1) * TILE] = sent[which].astype(F32) + got[which].astype(F32)
            ring.finish()

    def late(i):
        return jnp.maximum(i - tiles, 0)

    def early(i):
        return jnp.minimum(i, tiles - 1)

    specs = [
        single((width, m)),
        pl.BlockSpec((1, m, TILE), lambda i: (late(i) // per, 0, late(i) % per)),
        single((amount, m, columns)),
    ]
    operands = [x_t, d_out, d_out]
    for index in range(amount):
        specs.append(pl.BlockSpec((TILE, columns), functools.partial(lambda where, i: (early(i), where), index)))
        operands.append(weights)
    out_specs = [pl.BlockSpec((1, width, TILE), lambda i: (late(i) // per, 0, late(i) % per)), single((m, width))]
    out_shape = [jax.ShapeDtypeStruct((amount, width, columns), BF), jax.ShapeDtypeStruct((m, width), F32)]
    specs += [pl.BlockSpec(memory_space=pl.ANY)] * count
    operands += [source for source, _, _ in ring_sources]
    for (source, _, _), out_width in zip(ring_sources, out_widths):
        rows = source.shape[-2]
        out_specs.append(single((rows, out_width)))
        out_shape.append(jax.ShapeDtypeStruct((rows, out_width), F32))
    dma = pltpu.SemaphoreType.DMA
    return pl.pallas_call(
        kernel,
        grid=(total,),
        out_shape=out_shape,
        in_specs=specs,
        out_specs=out_specs,
        scratch_shapes=[
            pltpu.VMEM((tiles, m, TILE), BF),
            pltpu.VMEM((tiles, m, TILE), BF),
            dma((tiles,)),
            dma((tiles,)),
            *Ring.scratch(devices, shapes),
        ],
        compiler_params=pltpu.CompilerParams(vmem_limit_bytes=VMEM, collective_id=identity, has_side_effects=True),
        cost_estimate=cost(4 * m * width * amount * columns, 6 * width * amount * columns),
        name=name,
    )(*operands)


def root_of(rows):
    return lax.rsqrt(jnp.mean(rows * rows, axis=-1, keepdims=True) + EPS)


def norm_grad(rows, gain, grad):
    root = root_of(rows)
    pushed = grad * gain
    inner = jnp.mean(pushed * rows, axis=-1, keepdims=True)
    return root * pushed - rows * (root * root * root * inner), jnp.sum(grad * rows * root, axis=0, keepdims=True)


def first_norm(far, near, tokens, gain):
    m, width = tokens.shape
    steps = m // ROWS

    def kernel(far_ref, near_ref, x_ref, g_ref, o_ref, t_ref):
        step = pl.program_id(0)
        me = lax.axis_index("dp")

        def normed(ref):
            rows = ref[...].astype(F32)
            return (rows * root_of(rows) * g_ref[...]).astype(BF)

        def earlier(ref, there):
            @pl.when(there)
            def _():
                o_ref[...] = normed(ref)

            @pl.when(jnp.logical_not(there))
            def _():
                o_ref[...] = jnp.zeros_like(o_ref)

        @pl.when(step < steps)
        def _():
            earlier(far_ref, me >= 2)

        @pl.when((step >= steps) & (step < 2 * steps))
        def _():
            earlier(near_ref, me >= 1)

        @pl.when(step >= 2 * steps)
        def _():
            made = normed(x_ref)
            o_ref[...] = made
            t_ref[...] = made.T

    def part(which):
        return pl.BlockSpec((ROWS, width), lambda i: (jnp.clip(i - which * steps, 0, steps - 1), 0))

    return pl.pallas_call(
        kernel,
        grid=(3 * steps,),
        out_shape=[jax.ShapeDtypeStruct((3 * m, width), BF), jax.ShapeDtypeStruct((width, m), BF)],
        in_specs=[part(0), part(1), part(2), whole_spec((1, width))],
        out_specs=[
            pl.BlockSpec((ROWS, width), lambda i: (i, 0)),
            pl.BlockSpec((width, ROWS), lambda i: (0, jnp.maximum(i - 2 * steps, 0))),
        ],
        compiler_params=pltpu.CompilerParams(vmem_limit_bytes=VMEM),
        cost_estimate=cost(24 * m * width, 14 * m * width),
        name="first_norm",
    )(far, near, tokens, gain)


def out_norm(mixed, w_attn, place, tokens, gain, identity):
    m, columns = mixed.shape
    width = tokens.shape[1]
    steps = m // ROWS
    sides = lax.axis_size("tensor")

    def kernel(x_ref, w_ref, r_ref, g_ref, hidden_ref, normed_ref, turned_ref, sent, got, send, recv):
        step = pl.program_id(0)
        other = (lax.axis_index("dp"), lax.rem(lax.axis_index("tensor") + 1, sides))

        @pl.when(step == 0)
        def _():
            semaphore = pltpu.get_barrier_semaphore()
            pl.semaphore_signal(semaphore, inc=1, device_id=other, device_id_type=MESH)
            pl.semaphore_wait(semaphore, 1)

        def across(which):
            return pltpu.make_async_remote_copy(
                src_ref=sent.at[which], dst_ref=got.at[which], send_sem=send.at[which], recv_sem=recv.at[which],
                device_id=other, device_id_type=MESH,
            )

        @pl.when(step < steps)
        def _():
            sent[step] = dot_nt(x_ref[...], w_ref[...]).astype(BF)
            across(step).start()

        @pl.when(step >= steps)
        def _():
            which = step - steps
            across(which).wait()
            hidden = r_ref[...].astype(F32) + (sent[which].astype(F32) + got[which].astype(F32))
            normed = (hidden * root_of(hidden) * g_ref[...]).astype(BF)
            hidden_ref[...] = hidden
            normed_ref[...] = normed
            turned_ref[...] = normed.T

    def late(i):
        return jnp.maximum(i - steps, 0)

    late_rows = pl.BlockSpec((ROWS, width), lambda i: (late(i), 0))
    dma = pltpu.SemaphoreType.DMA
    return pl.pallas_call(
        kernel,
        grid=(2 * steps,),
        out_shape=[
            jax.ShapeDtypeStruct((m, width), F32),
            jax.ShapeDtypeStruct((m, width), BF),
            jax.ShapeDtypeStruct((width, m), BF),
        ],
        in_specs=[
            pl.BlockSpec((ROWS, columns), lambda i: (jnp.minimum(i, steps - 1), 0)),
            pl.BlockSpec((width, columns), lambda i: (0, place), pipeline_mode=pl.Buffered(1)),
            late_rows,
            single((1, width)),
        ],
        out_specs=[late_rows, late_rows, pl.BlockSpec((width, ROWS), lambda i: (0, late(i)))],
        scratch_shapes=[pltpu.VMEM((steps, ROWS, width), BF), pltpu.VMEM((steps, ROWS, width), BF), dma((steps,)), dma((steps,))],
        compiler_params=pltpu.CompilerParams(vmem_limit_bytes=VMEM, collective_id=identity, has_side_effects=True),
        cost_estimate=cost(2 * m * width * columns, 12 * m * width),
        name="out_norm",
    )(mixed, w_attn, tokens, gain)


def hidden_grad(hidden, gain, grad, cotangent):
    m, width = hidden.shape

    def kernel(h_ref, g_ref, d_ref, y_ref, o_ref, low_ref, turned_ref, gain_ref):
        change, gain_part = norm_grad(h_ref[...], g_ref[...], d_ref[...])
        total = y_ref[...].astype(F32) + change
        low = total.astype(BF)
        o_ref[...] = total
        low_ref[...] = low
        turned_ref[...] = low.T

        @pl.when(pl.program_id(0) == 0)
        def _():
            gain_ref[...] = gain_part

        @pl.when(pl.program_id(0) > 0)
        def _():
            gain_ref[...] += gain_part

    rows_spec = pl.BlockSpec((ROWS, width), lambda i: (i, 0))
    return pl.pallas_call(
        kernel,
        grid=(m // ROWS,),
        out_shape=[
            jax.ShapeDtypeStruct((m, width), F32),
            jax.ShapeDtypeStruct((m, width), BF),
            jax.ShapeDtypeStruct((width, m), BF),
            jax.ShapeDtypeStruct((1, width), F32),
        ],
        in_specs=[rows_spec, whole_spec((1, width)), rows_spec, rows_spec],
        out_specs=[rows_spec, rows_spec, pl.BlockSpec((width, ROWS), lambda i: (0, i)), whole_spec((1, width))],
        compiler_params=pltpu.CompilerParams(vmem_limit_bytes=VMEM),
        cost_estimate=cost(16 * m * width, 18 * m * width),
        name="hidden_grad",
    )(hidden, gain, grad, cotangent)


def last_pass(tokens, gain, grad, d_hidden, hidden, activated, w_ffn, gain_ffn_grad, flip, qkv_part, lanes, identity):
    m, width = tokens.shape
    devices, rows, all_columns = qkv_part.shape
    columns = all_columns // 3
    chips = devices // 2
    size = ROWS // 2
    steps = m // size
    total = steps + chips
    names = 3
    tiles = width // TILE
    units = activated.shape[1]
    sides = lax.axis_size("tensor")
    assert tiles == steps and chips >= tiles

    def kernel(x_ref, g_ref, dn_ref, dh_ref, h_ref, a_ref, w_ref, gf_ref, flip_ref, source, grad_ref, layer_ref, flipped_ref, q_ref, k_ref, v_ref, gains_ref, gain_sum, gain_source, sent, got, y_send, y_recv, *scratch):
        step = pl.program_id(0)
        ring = Ring(
            devices, [(source, number * columns, columns) for number in range(names)], [(q_ref, 0), (k_ref, 0), (v_ref, 0)],
            [[0], [1], [2]], scratch[: 3 * names + 5],
        )
        gain_ring = Ring(devices, [(gain_source, 0, lanes)], [(gains_ref, 0)], [[0]], scratch[3 * names + 5 :])
        other = (ring.me, lax.rem(ring.side + 1, sides))

        def across(which):
            return pltpu.make_async_remote_copy(
                src_ref=sent.at[which], dst_ref=got.at[which], send_sem=y_send.at[which], recv_sem=y_recv.at[which],
                device_id=other, device_id_type=MESH,
            )

        @pl.when(step == 0)
        def _():
            ring.barrier((other,))
            ring.begin()

        @pl.when(step < tiles)
        def _():
            sent[step] = dot_nt(a_ref[...], w_ref[...]).astype(BF)
            across(step).start()

        @pl.when(step < steps)
        def _():
            change, gain_part = norm_grad(x_ref[...].astype(F32), g_ref[...], dn_ref[...])
            grad_ref[...] = dh_ref[...] + change

            @pl.when(step == 0)
            def _():
                gain_sum[...] = gain_part
                flipped_ref[...] = flip_ref[...].T

            @pl.when(step > 0)
            def _():
                gain_sum[...] += gain_part

        @pl.when(step == steps - 1)
        def _():
            gain_source[...] = jnp.zeros_like(gain_source)
            for device in range(devices):
                span = slice(device * rows, (device + 1) * rows)
                gain_source[device, :16, :rows] = jnp.broadcast_to(gain_sum[:, span], (16, rows)).astype(BF)
                gain_source[device, 16:, :rows] = jnp.broadcast_to(gf_ref[:, span], (16, rows)).astype(BF)
            gain_ring.begin()

        ring.pace(step, [(steps, 3), (chips, 5)])

        @pl.when(step >= steps)
        def _():
            gain_ring.run(step - steps, step - steps + 1)

        @pl.when((step >= steps) & (step < steps + tiles))
        def _():
            which = step - steps
            across(which).wait()
            layer_ref[...] = (h_ref[...] + (sent[which].astype(F32) + got[which].astype(F32))).astype(BF)

        @pl.when(step == total - 1)
        def _():
            ring.finish()
            gain_ring.finish()

    def early(i):
        return jnp.minimum(i, steps - 1)

    rows_spec = pl.BlockSpec((size, width), lambda i: (early(i), 0))
    tile_spec = pl.BlockSpec((m, TILE), lambda i: (0, jnp.clip(i - steps, 0, tiles - 1)))
    dma = pltpu.SemaphoreType.DMA
    sums = jax.ShapeDtypeStruct((rows, columns), F32)
    return pl.pallas_call(
        kernel,
        grid=(total,),
        out_shape=[
            jax.ShapeDtypeStruct((m, width), F32),
            jax.ShapeDtypeStruct((m, width), BF),
            jax.ShapeDtypeStruct((flip.shape[1], flip.shape[0]), F32),
            sums, sums, sums,
            jax.ShapeDtypeStruct((32, lanes), F32),
        ],
        in_specs=[
            rows_spec, single((1, width)), rows_spec, rows_spec, tile_spec, single((m, units)),
            pl.BlockSpec((TILE, units), lambda i: (early(i), 2)), single((1, width)),
            single(flip.shape), pl.BlockSpec(memory_space=pl.ANY),
        ],
        out_specs=[
            rows_spec, tile_spec, single((flip.shape[1], flip.shape[0])),
            single(sums.shape), single(sums.shape), single(sums.shape), single((32, lanes)),
        ],
        scratch_shapes=[
            pltpu.VMEM((1, width), F32),
            pltpu.VMEM((devices, 32, lanes), BF),
            pltpu.VMEM((tiles, m, TILE), BF),
            pltpu.VMEM((tiles, m, TILE), BF),
            dma((tiles,)),
            dma((tiles,)),
            *Ring.scratch(devices, [(rows, columns)] * names),
            *Ring.scratch(devices, [(32, lanes)]),
        ],
        compiler_params=pltpu.CompilerParams(vmem_limit_bytes=VMEM, collective_id=identity, has_side_effects=True),
        cost_estimate=cost(20 * m * width, 24 * m * width),
        name="last_pass",
    )(tokens, gain, grad, d_hidden, hidden, activated, w_ffn, gain_ffn_grad, flip, qkv_part)


def feed(x, dy, w, tiles):
    m, k = x.shape

    def kernel(x_ref, dy_ref, g_ref, u_ref, d_ref, act_ref, both_ref):
        gate = dot_nn(x_ref[...], g_ref[...])
        up = dot_nn(x_ref[...], u_ref[...])
        d_act = dot_nn(dy_ref[...], d_ref[...])
        soft = 1.0 / (1.0 + jnp.exp(-gate))
        silu = gate * soft
        act_ref[...] = (silu * up).astype(BF)
        both_ref[0] = (d_act * up * (soft * (1.0 + gate * (1.0 - soft)))).astype(BF)
        both_ref[1] = (d_act * silu).astype(BF)

    tile = pl.BlockSpec((m, TILE), lambda i: (0, i))
    return pl.pallas_call(
        kernel,
        grid=(tiles,),
        out_shape=[jax.ShapeDtypeStruct((m, tiles * TILE), BF), jax.ShapeDtypeStruct((2, m, tiles * TILE), BF)],
        in_specs=[
            whole_spec((m, k)),
            whole_spec((m, k)),
            pl.BlockSpec((k, TILE), lambda i: (0, i)),
            pl.BlockSpec((k, TILE), lambda i: (0, i + tiles)),
            pl.BlockSpec((k, TILE), lambda i: (0, i + 2 * tiles)),
        ],
        out_specs=[tile, pl.BlockSpec((2, m, TILE), lambda i: (0, 0, i))],
        compiler_params=pltpu.CompilerParams(vmem_limit_bytes=VMEM),
        cost_estimate=cost(6 * m * k * tiles * TILE, 6 * (m + k) * tiles * TILE, m * tiles * TILE),
        name="feed",
    )(x, dy, w, w, w)


def shards(tokens, positions, attn_gain, w_query, w_key, w_value, w_out, ffn_gain, w_gate, w_up, w_down, cotangent):
    devices = lax.axis_size("dp")
    span = tokens.shape[0]
    assert 2 * span == WINDOW
    own_rows = w_query.shape[0]
    width = tokens.shape[1]
    head_columns = w_query.shape[1]
    heads = head_columns // E
    hidden_units = w_gate.shape[1]
    tiles = (hidden_units + TILE - 1) // TILE
    padded = tiles * TILE

    attn_pack = jnp.concatenate([w_query, w_key, w_value, w_out.T], axis=1)
    lanes = max(128, own_rows)
    gains = jnp.zeros((32, lanes), BF).at[0, :own_rows].set(attn_gain).at[16, :own_rows].set(ffn_gain)
    w_attn, all_gains, near, far = ring_gather((attn_pack, gains), (2, 1), tokens, 0)

    def wide(matrix):
        return jnp.pad(matrix, ((0, 0), (0, padded - hidden_units)))

    ffn_pack = jnp.concatenate([wide(w_gate), wide(w_up), wide(w_down.T)], axis=1)
    w_attn, all_gains, ffn_pack = lax.optimization_barrier((w_attn, all_gains, ffn_pack))
    w_ffn = lax.all_gather(ffn_pack, "dp", axis=0, tiled=True)
    all_gains = all_gains.reshape(devices, 32, lanes)
    gain_attn = all_gains[:, 0, :own_rows].reshape(1, width).astype(F32)
    gain_ffn = all_gains[:, 16, :own_rows].reshape(1, width).astype(F32)

    frequency = THETA ** (-(jnp.arange(E // 2, dtype=F32) * 2.0 / E))
    earlier = positions[0] - WINDOW + jnp.arange(WINDOW, dtype=jnp.int32)
    angles = jnp.concatenate([earlier, positions]).astype(F32)[:, None] * frequency[None, :]
    cosine_half, sine_half = jnp.cos(angles), jnp.sin(angles)
    cosine = jnp.concatenate([cosine_half, cosine_half], axis=1)
    sine = jnp.concatenate([-sine_half, sine_half], axis=1)

    normed_attn, normed_attn_t = first_norm(far, near, tokens, gain_attn)
    query, kv = project(normed_attn, w_attn, cosine, sine, span, heads)
    mixed, probs = attend(query, kv, positions[None, :], heads)
    cosine, sine = cosine[WINDOW:], sine[WINDOW:]
    hidden, normed_ffn, normed_ffn_t = out_norm(mixed, w_attn, 3, tokens, gain_ffn, 5)

    activated, d_both = feed(normed_ffn, cotangent, w_ffn, tiles)
    down_part = matmul_nn(cotangent.T, activated, 0, tiles, "down_grad").reshape(devices, own_rows, padded)
    both_part, d_normed_ffn, down_grad = back_pass(
        normed_ffn_t, d_both, w_ffn, [(down_part, None, 2)], [padded], (2, 1), 1, "ffn_back"
    )
    both_part = both_part.reshape(2, devices, own_rows, padded)
    d_hidden, d_hidden_low, d_hidden_t, gain_ffn_grad = hidden_grad(hidden, gain_ffn, d_normed_ffn, cotangent)

    d_qkv, out_part, gate_grad, w_down_grad = attend_back(
        query, kv, probs, mixed, w_attn, d_hidden_low, d_hidden_t, cosine, sine, down_grad, both_part, heads, hidden_units, 2
    )
    qkv_part, d_normed_attn, up_grad, out_grad = back_pass(
        normed_attn_t, d_qkv[None], w_attn,
        [(both_part, 1, 2), (out_part.reshape(devices, own_rows, head_columns), None, 1)], [hidden_units, head_columns], (4, 3), 3, "qkv_back",
    )
    tokens_grad, layer_out, w_out_grad, query_grad, key_grad, value_grad, gain_grads = last_pass(
        tokens, gain_attn, d_normed_attn, d_hidden, hidden, activated, w_ffn, gain_ffn_grad, out_grad,
        qkv_part.reshape(devices, own_rows, 3 * head_columns), lanes, 4,
    )
    return (
        layer_out,
        tokens_grad,
        gain_grads[0, :own_rows],
        query_grad,
        key_grad,
        value_grad,
        w_out_grad,
        gain_grads[16, :own_rows],
        gate_grad,
        up_grad,
        w_down_grad,
    )


def solution(mesh):
    by_rows, by_both, turned_both, line = P("dp", None), P("dp", "tensor"), P("tensor", "dp"), P("dp")
    return jax.shard_map(
        shards,
        mesh=mesh,
        in_specs=(by_rows, line, line, by_both, by_both, by_both, turned_both, line, by_both, by_both, turned_both, by_rows),
        out_specs=(by_rows, by_rows, line, by_both, by_both, by_both, turned_both, line, by_both, by_both, turned_both),
        check_vma=False,
    )
```

```python
import functools

import jax
import jax.numpy as jnp
from jax import lax
from jax.experimental import pallas as pl
from jax.experimental.pallas import tpu as pltpu
from jax.sharding import PartitionSpec as P

E = 128
WINDOW = 1024
EPS = 1e-06
THETA = 10000.0
LOG2E = 1.4426950408889634
MESH = pl.DeviceIdType.MESH
BF = jnp.bfloat16
F32 = jnp.float32
QB = 256
KB = WINDOW + QB
TILE = 256
ROWS = 128
LATE = 2
VMEM = 59 * 1024 * 1024


def whole_spec(shape):
    return pl.BlockSpec(shape, lambda i: (0,) * len(shape))


def single(shape):
    return pl.BlockSpec(shape, lambda i: (0,) * len(shape), pipeline_mode=pl.Buffered(1))


def cost(flops, nbytes, special=0):
    return pl.CostEstimate(flops=flops, bytes_accessed=nbytes, transcendentals=special)


def ring_chip(place, chips):
    place = lax.rem(place + 2 * chips, chips)
    late = place // (chips // 2)
    return (1 - late) * 2 * place + late * (2 * (chips - 1 - place) + 1)


def ring_place(chip, chips):
    column = lax.rem(chip, 2)
    row = chip // 2
    return (1 - column) * row + column * (chips - 1 - row)


def gather_kernel(devices, chunks, count, *refs):
    ins, tokens = refs[:count], refs[count]
    outs, near, far = refs[count + 1 : 2 * count + 1], refs[2 * count + 1], refs[2 * count + 2]
    local_sem, a_send, a_recv, b_send, b_recv, c_send, c_recv, far_send, far_recv, near_send, near_recv = refs[2 * count + 3 :]
    chips = devices // 2
    me = lax.axis_index("dp")
    side = lax.axis_index("tensor")
    core = lax.rem(me, 2)
    place = ring_place(me // 2, chips)

    def device(q):
        return ring_chip(q, chips) * 2 + core

    right = device(place + 1)
    left = device(place - 1)
    partner = me + 1 - 2 * core
    across = lax.rem(side + 1, lax.axis_size("tensor"))
    later, before = lax.rem(me + 2, devices), lax.rem(me + devices - 2, devices)
    barrier = pltpu.get_barrier_semaphore()
    for other in ((right, side), (left, side), (partner, side), (me, across), (later, side), (before, side)):
        pl.semaphore_signal(barrier, inc=1, device_id=other, device_id_type=MESH)
    pl.semaphore_wait(barrier, 6)

    pieces = []
    for index, parts in enumerate(chunks):
        width = ins[index].shape[1] // parts
        for part in range(parts):
            pieces.append((index, part * width, width))
    hops = chips - 1

    def view(ref, row, half, piece, rows):
        index, column, width = piece
        start = row * rows + half * (rows // 2)
        if not isinstance(start, int):
            start = pl.multiple_of(start, 16)
        return ref.at[pl.ds(start, rows // 2), pl.ds(column, width)]

    def described(source, target, send, recv, other):
        return pltpu.make_async_remote_copy(
            src_ref=source, dst_ref=target, send_sem=send, recv_sem=recv, device_id=other, device_id_type=MESH
        )

    def remote(source, target, send, recv, other):
        copy = described(source, target, send, recv, (other, side))
        copy.start()
        return copy

    span = tokens.shape[0] // 2

    def half_rows(ref, which):
        return ref.at[pl.ds(pl.multiple_of(which * span, span), span)]

    far_copy = described(half_rows(tokens, side), half_rows(far, side), far_send.at[0], far_recv.at[0], (later, side))
    cross_copy = described(half_rows(far, side), half_rows(far, side), far_send.at[1], far_recv.at[1], (me, across))
    own_near = [described(half_rows(tokens, which), half_rows(near, which), near_send.at[which], near_recv.at[which], (partner, side)) for which in range(2)]
    far_near = [described(half_rows(far, which), half_rows(near, which), near_send.at[slot], near_recv.at[slot], (partner, side)) for slot, which in enumerate((side, across))]

    @pl.when(me < devices - 2)
    def _():
        far_copy.start()

    @pl.when(core == 0)
    def _():
        for copy in own_near:
            copy.start()

    def pass_on(slot):
        @pl.when(me >= 2)
        def _():
            if slot == 0:
                far_copy.wait_recv()
                cross_copy.start()
            else:
                cross_copy.wait_recv()

            @pl.when(core == 1)
            def _():
                far_near[slot].start()

    local = []
    for index in range(count):
        rows = ins[index].shape[0]
        copy = pltpu.make_async_copy(
            ins[index], outs[index].at[pl.ds(pl.multiple_of(me * rows, 16), rows)], local_sem.at[index]
        )
        copy.start()
        local.append(copy)
    forward, partner_copies = {}, []
    for number, piece in enumerate(pieces):
        ref, out = ins[piece[0]], outs[piece[0]]
        rows = ref.shape[0]
        forward[number, 0] = (
            remote(view(ref, 0, 0, piece, rows), view(out, me, 0, piece, rows), a_send.at[number, 0], a_recv.at[number, 0], right),
            remote(view(ref, 0, 1, piece, rows), view(out, me, 1, piece, rows), b_send.at[number, 0], b_recv.at[number, 0], left),
        )
    for number, piece in enumerate(pieces):
        ref, out = ins[piece[0]], outs[piece[0]]
        rows = ref.shape[0]
        for half in range(2):
            partner_copies.append(
                remote(view(ref, 0, half, piece, rows), view(out, me, half, piece, rows), c_send.at[number, 0, half], c_recv.at[number, 0, half], partner)
            )
    for hop in range(hops):
        for number, piece in enumerate(pieces):
            out = outs[piece[0]]
            rows = ins[piece[0]].shape[0]
            came = forward[number, hop]
            sent = []
            for half in range(2):
                came[half].wait_recv()
                owner = device(place - 1 - hop if half == 0 else place + 1 + hop)
                block = view(out, owner, half, piece, rows)
                send, recv = (a_send, a_recv) if half == 0 else (b_send, b_recv)
                if hop < hops - 1:
                    sent.append(
                        remote(block, block, send.at[number, hop + 1], recv.at[number, hop + 1], right if half == 0 else left)
                    )
                partner_copies.append(
                    remote(block, block, c_send.at[number, hop + 1, half], c_recv.at[number, hop + 1, half], partner)
                )
            if sent:
                forward[number, hop + 1] = tuple(sent)
        if hop == hops // 2:
            pass_on(0)
        if hop == hops - 2:
            pass_on(1)
    for copy in local:
        copy.wait()
    for pair in forward.values():
        for copy in pair:
            copy.wait_send()
    for copy in partner_copies:
        copy.wait()

    @pl.when(me < devices - 2)
    def _():
        far_copy.wait_send()

    @pl.when(me >= 2)
    def _():
        cross_copy.wait_send()

        @pl.when(core == 1)
        def _():
            for copy in far_near:
                copy.wait_send()

    @pl.when(core == 0)
    def _():
        for copy in own_near:
            copy.wait_send()

    @pl.when((core == 1) | (me >= 2))
    def _():
        for copy in own_near:
            copy.wait_recv()


def ring_gather(arrays, chunks, tokens, identity):
    devices = lax.axis_size("dp")
    hops = devices // 2 - 1
    pieces = sum(chunks)
    dma = pltpu.SemaphoreType.DMA
    any_space = pl.BlockSpec(memory_space=pl.ANY)
    return pl.pallas_call(
        functools.partial(gather_kernel, devices, chunks, len(arrays)),
        out_shape=[jax.ShapeDtypeStruct((a.shape[0] * devices, a.shape[1]), a.dtype) for a in arrays]
        + [jax.ShapeDtypeStruct(tokens.shape, tokens.dtype)] * 2,
        in_specs=[any_space] * (len(arrays) + 1),
        out_specs=[any_space] * (len(arrays) + 2),
        scratch_shapes=[
            dma((len(arrays),)),
            dma((pieces, hops)),
            dma((pieces, hops)),
            dma((pieces, hops)),
            dma((pieces, hops)),
            dma((pieces, hops + 1, 2)),
            dma((pieces, hops + 1, 2)),
            dma((2,)),
            dma((2,)),
            dma((2,)),
            dma((2,)),
        ],
        compiler_params=pltpu.CompilerParams(collective_id=identity, has_side_effects=True),
        name="ring_gather",
    )(*arrays, tokens)


class Spread:
    def __init__(self, devices, pieces, scratch):
        self.devices, self.chips, self.pieces = devices, devices // 2, pieces
        self.local_sem, self.send_sem, self.recv_sem, self.give_sem, self.take_sem = scratch
        self.me = lax.axis_index("dp")
        self.side = lax.axis_index("tensor")
        self.core = lax.rem(self.me, 2)
        self.place = ring_place(self.me // 2, self.chips)
        self.partner = self.me + 1 - 2 * self.core
        self.next = (
            ring_chip(self.place + 1, self.chips) * 2 + self.core,
            ring_chip(self.place - 1, self.chips) * 2 + self.core,
        )
        self.events = (self.chips - 1) * len(pieces)

    @staticmethod
    def scratch(devices, count):
        dma = pltpu.SemaphoreType.DMA
        chips = devices // 2
        return [dma((count,))] + [dma((count, amount, 2)) for amount in (chips - 1, chips - 1, chips, chips)]

    def barrier(self):
        semaphore = pltpu.get_barrier_semaphore()
        for other in (*self.next, self.partner):
            pl.semaphore_signal(semaphore, inc=1, device_id=(other, self.side), device_id_type=MESH)
        pl.semaphore_wait(semaphore, 3)

    def block(self, index, stage, half):
        source, whole, column, width = self.pieces[index]
        rows = source.shape[0]
        owner = ring_chip(self.place - stage if half == 0 else self.place + stage, self.chips) * 2 + self.core
        return whole.at[pl.ds(pl.multiple_of(owner * rows + half * (rows // 2), 16), rows // 2), pl.ds(column, width)]

    def first(self, index, half):
        source, _, column, width = self.pieces[index]
        rows = source.shape[0]
        return source.at[pl.ds(half * (rows // 2), rows // 2), pl.ds(column, width)]

    def local(self, index):
        source, whole, column, width = self.pieces[index]
        rows = source.shape[0]
        span = pl.ds(pl.multiple_of(self.me * rows, 16), rows)
        return pltpu.make_async_copy(
            source.at[:, pl.ds(column, width)], whole.at[span, pl.ds(column, width)], self.local_sem.at[index]
        )

    def copy(self, index, stage, half, start, across):
        block = self.block(index, stage, half)
        send, recv = (self.give_sem, self.take_sem) if across else (self.send_sem, self.recv_sem)
        return pltpu.make_async_remote_copy(
            src_ref=self.first(index, half) if start else block,
            dst_ref=block,
            send_sem=send.at[index, stage, half],
            recv_sem=recv.at[index, stage, half],
            device_id=(self.partner if across else self.next[half], self.side),
            device_id_type=MESH,
        )

    def each(self):
        return [(index, half) for index in range(len(self.pieces)) for half in range(2)]

    def begin(self):
        for index, half in self.each():
            self.copy(index, 0, half, True, False).start()
        for index, half in self.each():
            self.copy(index, 0, half, True, True).start()
        for index in range(len(self.pieces)):
            self.local(index).start()

    def stage(self, stage, index):
        for half in range(2):
            self.copy(index, stage - 1, half, False, False).wait_recv()

            @pl.when(stage < self.chips - 1)
            def _():
                self.copy(index, stage, half, False, False).start()

            self.copy(index, stage, half, False, True).start()

    def pace(self, step, total):
        count = len(self.pieces)

        def one(event, carry):
            for index in range(count):
                pl.when(lax.rem(event, count) == index)(functools.partial(self.stage, event // count + 1, index))
            return carry

        lax.fori_loop(step * self.events // total, (step + 1) * self.events // total, one, 0)

    def finish(self):
        for index in range(len(self.pieces)):
            self.local(index).wait()
        for index, half in self.each():
            self.copy(index, 0, half, True, False).wait_send()
            self.copy(index, 0, half, True, True).wait()

        def sent(stage, carry):
            for index, half in self.each():
                self.copy(index, stage, half, False, False).wait_send()
            return carry

        lax.fori_loop(1, self.chips - 1, sent, 0)

        def gave(stage, carry):
            for index, half in self.each():
                self.copy(index, stage, half, False, True).wait()
            return carry

        lax.fori_loop(1, self.chips, gave, 0)


class Ring:
    AHEAD = 3

    def __init__(self, devices, terms, goals, groups, scratch):
        self.devices, self.chips = devices, devices // 2
        self.terms, self.goals, self.groups = terms, goals, groups
        count = len(terms)
        self.mine, self.taken, self.inbox = scratch[0 : 3 * count : 3], scratch[1 : 3 * count : 3], scratch[2 : 3 * count : 3]
        self.own_sem, self.give_sem, self.take_sem, self.send_sem, self.recv_sem = scratch[3 * count : 3 * count + 5]
        self.me = lax.axis_index("dp")
        self.side = lax.axis_index("tensor")
        self.core = lax.rem(self.me, 2)
        self.place = ring_place(self.me // 2, self.chips)
        self.partner = self.me + 1 - 2 * self.core
        self.next = (
            ring_chip(self.place + 1, self.chips) * 2 + self.core,
            ring_chip(self.place - 1, self.chips) * 2 + self.core,
        )
        self.events = self.chips * len(groups)

    @staticmethod
    def scratch(devices, shapes):
        chips, count = devices // 2, len(shapes)
        dma = pltpu.SemaphoreType.DMA
        buffers = []
        for rows, width in shapes:
            buffers += [pltpu.VMEM((amount, 2, rows // 2, width), BF) for amount in (chips, chips, chips - 1)]
        return buffers + [dma((count, amount, 2)) for amount in (chips, chips, chips, chips - 1, chips - 1)]

    def barrier(self, others=()):
        semaphore = pltpu.get_barrier_semaphore()
        everyone = [(self.next[0], self.side), (self.next[1], self.side), (self.partner, self.side), *others]
        for other in everyone:
            pl.semaphore_signal(semaphore, inc=1, device_id=other, device_id_type=MESH)
        pl.semaphore_wait(semaphore, len(everyone))

    def block(self, index, stage, half, core):
        at = self.place - 1 - stage if half == 0 else self.place + 1 + stage
        size = self.mine[index].shape[2]
        source, column, width = self.terms[index]
        return source.at[ring_chip(at, self.chips) * 2 + core, pl.ds(half * size, size), pl.ds(column, width)]

    def own(self, index, stage, half):
        return pltpu.make_async_copy(
            self.block(index, stage, half, self.core), self.mine[index].at[stage, half], self.own_sem.at[index, stage, half]
        )

    def given(self, index, stage, half):
        return pltpu.make_async_remote_copy(
            src_ref=self.block(index, stage, half, 1 - self.core),
            dst_ref=self.taken[index].at[stage, half],
            send_sem=self.give_sem.at[index, stage, half],
            recv_sem=self.take_sem.at[index, stage, half],
            device_id=(self.partner, self.side),
            device_id_type=MESH,
        )

    def hop(self, index, stage, half, first):
        source = self.mine[index].at[0, half] if first else self.inbox[index].at[stage - 1, half]
        return pltpu.make_async_remote_copy(
            src_ref=source,
            dst_ref=self.inbox[index].at[stage, half],
            send_sem=self.send_sem.at[index, stage, half],
            recv_sem=self.recv_sem.at[index, stage, half],
            device_id=(self.next[half], self.side),
            device_id_type=MESH,
        )

    def each(self, group=None):
        members = range(len(self.terms)) if group is None else self.groups[group]
        return [(index, half) for index in members for half in range(2)]

    def fetch(self, stage, group):
        for index, half in self.each(group):
            self.given(index, stage, half).start()
            self.own(index, stage, half).start()

    def begin(self):
        for stage in range(min(self.AHEAD, self.chips)):
            for group in range(len(self.groups)):
                self.fetch(stage, group)

    def chip_term(self, index, stage, half):
        self.own(index, stage, half).wait()
        self.given(index, stage, half).wait_recv()
        return self.mine[index][stage, half].astype(F32) + self.taken[index][stage, half].astype(F32)

    def stage(self, stage, group):
        last = self.chips - 1

        @pl.when(stage == 0)
        def _():
            for index, half in self.each(group):
                self.mine[index][0, half] = self.chip_term(index, 0, half).astype(BF)
                self.hop(index, 0, half, True).start()

        @pl.when((stage > 0) & (stage < last))
        def _():
            for index, half in self.each(group):
                self.hop(index, stage - 1, half, True).wait_recv()
                came = self.inbox[index][stage - 1, half].astype(F32)
                self.inbox[index][stage - 1, half] = (came + self.chip_term(index, stage, half)).astype(BF)
                self.hop(index, stage, half, False).start()

        @pl.when(stage + self.AHEAD < self.chips)
        def _():
            self.fetch(stage + self.AHEAD, group)

        @pl.when(stage == last)
        def _():
            for index, half in self.each(group):
                self.hop(index, last - 1, half, True).wait_recv()
                came = self.inbox[index][last - 1, half].astype(F32)
                size = came.shape[0]
                total = came + self.chip_term(index, last, half)
                goal, column = self.goals[index]
                width = min(goal.shape[1] - column, total.shape[1])
                goal[half * size : (half + 1) * size, column : column + width] = total[:, :width]

    def run(self, first, stop):
        count = len(self.groups)

        def one(event, carry):
            for group in range(count):
                if count == 1:
                    self.stage(event, 0)
                else:
                    pl.when(lax.rem(event, count) == group)(functools.partial(self.stage, event // count, group))
            return carry

        lax.fori_loop(first, stop, one, 0)

    def pace(self, step, costs):
        whole = sum(steps * each for steps, each in costs)

        def done(at):
            spent, before = 0, 0
            for steps, each in costs:
                spent = spent + jnp.minimum(jnp.maximum(at - before, 0), steps) * each
                before += steps
            return spent * self.events // whole

        self.run(done(step), done(step + 1))

    def finish(self):
        for index, half in self.each():
            self.hop(index, 0, half, True).wait_send()

        def sent(stage, carry):
            for index, half in self.each():
                self.hop(index, stage, half, False).wait_send()
            return carry

        lax.fori_loop(1, self.chips - 1, sent, 0)

        def gave(stage, carry):
            for index, half in self.each():
                self.given(index, stage, half).wait_send()
            return carry

        lax.fori_loop(0, self.chips, gave, 0)


def dot_nn(a, b):
    return jnp.dot(a, b, preferred_element_type=F32)


def dot_nt(a, b):
    return lax.dot_general(a, b, (((1,), (1,)), ((), ())), preferred_element_type=F32)


def turned(block, cosine, sine, back):
    other = pltpu.roll(block, E // 2, 1)
    if back:
        return block * cosine - other * sine
    return block * cosine + other * sine


def project(x, w, cosine, sine, own, heads):
    m, k = x.shape
    per = TILE // E
    some = heads // per

    def kernel(x_ref, w_ref, c_ref, s_ref, q_ref, kv_ref):
        step = pl.program_id(0)

        def rotate_to(ref, made, rows):
            for part in range(per):
                piece = slice(part * E, (part + 1) * E)
                ref[:, piece] = turned(made[:, piece], c_ref[rows, :], s_ref[rows, :], False).astype(BF)

        @pl.when(step < some)
        def _():
            rows = slice(m - own, m)
            rotate_to(q_ref, dot_nn(x_ref[rows, :], w_ref[...]), rows)

        @pl.when((step >= some) & (step < 2 * some))
        def _():
            rotate_to(kv_ref, dot_nn(x_ref[...], w_ref[...]), slice(0, m))

        @pl.when(step >= 2 * some)
        def _():
            kv_ref[...] = dot_nn(x_ref[...], w_ref[...]).astype(BF)

    return pl.pallas_call(
        kernel,
        grid=(3 * some,),
        out_shape=[jax.ShapeDtypeStruct((own, heads * E), BF), jax.ShapeDtypeStruct((m, 2 * heads * E), BF)],
        in_specs=[single((m, k)), pl.BlockSpec((k, TILE), lambda i: (0, i)), single((m, E)), single((m, E))],
        out_specs=[
            pl.BlockSpec((own, TILE), lambda i: (0, jnp.minimum(i, some - 1))),
            pl.BlockSpec((m, TILE), lambda i: (0, jnp.maximum(i - some, 0))),
        ],
        compiler_params=pltpu.CompilerParams(vmem_limit_bytes=VMEM),
        cost_estimate=cost(2 * (own + 2 * m) * k * heads * E, 2 * (m * k + 3 * (m + k) * heads * E)),
        name="project",
    )(x, w, cosine, sine)


def attend(query, kv, places, heads):
    m = query.shape[0]
    blocks = m // QB
    factor = E ** (-0.5) * LOG2E

    def kernel(q_ref, k_ref, v_ref, p_ref, o_ref, probs_ref, bias):
        @pl.when(pl.program_id(0) == 0)
        def _():
            for block in range(blocks):
                key = lax.broadcasted_iota(jnp.int32, (KB, QB), 0) + block * QB
                query = lax.broadcasted_iota(jnp.int32, (KB, QB), 1) + block * QB
                place = p_ref[:, block * QB : (block + 1) * QB]
                allowed = (key <= query + WINDOW) & (key > query) & (key >= query + WINDOW - place)
                bias[block] = jnp.where(allowed, 0.0, -1e30)

        values_t = v_ref[...].T
        for block in range(blocks):
            span = slice(block * QB, block * QB + KB)
            scores = dot_nt(k_ref[span, :], q_ref[block * QB : (block + 1) * QB, :]) * factor + bias[block]
            largest = jnp.max(scores, axis=0, keepdims=True)
            grown = jnp.exp2(scores - largest)
            inverse = 1.0 / jnp.sum(grown, axis=0, keepdims=True)
            probs = (grown * inverse).astype(BF)
            probs_ref[0, block] = probs
            mixed_t = dot_nn(values_t[:, span], probs)
            o_ref[block * QB : (block + 1) * QB, :] = mixed_t.T.astype(BF)

    head = pl.BlockSpec((m, E), lambda i: (0, i))
    reach = kv.shape[0]

    return pl.pallas_call(
        kernel,
        grid=(heads,),
        out_shape=[
            jax.ShapeDtypeStruct((m, heads * E), BF),
            jax.ShapeDtypeStruct((heads, blocks, KB, QB), BF),
        ],
        in_specs=[
            head,
            pl.BlockSpec((reach, E), lambda i: (0, i)),
            pl.BlockSpec((reach, E), lambda i: (0, i + heads)),
            whole_spec((1, m)),
        ],
        out_specs=[head, pl.BlockSpec((1, blocks, KB, QB), lambda i: (i, 0, 0, 0))],
        scratch_shapes=[pltpu.VMEM((blocks, KB, QB), F32)],
        compiler_params=pltpu.CompilerParams(vmem_limit_bytes=VMEM),
        cost_estimate=cost(4 * heads * m * KB * E * 2, 2 * heads * m * KB, heads * m * KB),
        name="attend",
    )(query, kv, kv, places)


def attend_back(query, kv, probs, mixed, w_attn, hidden, gain, d_normed, cotangent, cosine, sine, flip, ring_source, heads, out_width, identity):
    m, width = hidden.shape
    firsts = m // ROWS
    devices, rows, ring_width = ring_source.shape[1:]
    blocks = m // QB
    factor = E ** (-0.5)
    reach = WINDOW + m
    columns = heads * E

    def kernel(q_ref, k_ref, v_ref, p_ref, x_ref, w_ref, h_ref, gain_ref, dn_ref, y_ref, c_ref, s_ref, flip_ref, source, d_ref, out_ref, sum_ref, flipped_ref, dh_ref, gain_out, g_ref, gt_ref, keys_sum, values_sum, near_out, near_in, far_out, far_in, kept, near_send, near_recv, far_send, far_recv, *scratch):
        step = pl.program_id(0)
        half = ring_width // 2
        ring = Ring(devices, [(source.at[0], 0, half), (source.at[0], half, half)], [(sum_ref, 0), (sum_ref, half)], [[0], [1]], scratch)
        me, side, core = ring.me, ring.side, ring.core

        @pl.when(step == 0)
        def _():
            ring.barrier(((lax.rem(me + 2, devices), side), (lax.rem(me + devices - 2, devices), side)))
            ring.begin()

        def near_copy(which):
            return pltpu.make_async_remote_copy(
                src_ref=near_out.at[which], dst_ref=near_in.at[which], send_sem=near_send.at[which], recv_sem=near_recv.at[which],
                device_id=(ring.partner, side), device_id_type=MESH,
            )

        def far_copy(which):
            return pltpu.make_async_remote_copy(
                src_ref=far_out.at[which], dst_ref=far_in.at[which], send_sem=far_send.at[which], recv_sem=far_recv.at[which],
                device_id=(lax.rem(me + devices - 2, devices), side), device_id_type=MESH,
            )

        turns = [(firsts + 2 * heads, 1)]

        @pl.when(step < firsts)
        def _():
            change, gain_part = norm_grad(h_ref[...], gain_ref[...], dn_ref[...])
            total = y_ref[...].astype(F32) + change
            low = total.astype(BF)
            dh_ref[...] = total
            here = pl.ds(pl.multiple_of(step * ROWS, ROWS), ROWS)
            g_ref[here, :] = low
            gt_ref[:, here] = low.T

            @pl.when(step == 0)
            def _():
                gain_out[...] = gain_part

            @pl.when(step > 0)
            def _():
                gain_out[...] += gain_part

            ring.pace(step, turns)

        @pl.when(step >= firsts)
        def _():
            head = step - firsts
            grad_all = dot_nn(g_ref[...], w_ref[...]).astype(BF)
            out_ref[...] = dot_nn(gt_ref[...], x_ref[...]).astype(BF)
            keys_t = k_ref[...].T
            keys_sum[...] = jnp.zeros_like(keys_sum)
            values_sum[...] = jnp.zeros_like(values_sum)
            for block in range(blocks):
                span = slice(block * QB, block * QB + KB)
                here = slice(block * QB, (block + 1) * QB)
                low = p_ref[0, block]
                grad = grad_all[here, :]
                d_probs = dot_nt(v_ref[span, :], grad)
                weighted = low.astype(F32) * d_probs
                total = jnp.sum(weighted, axis=0, keepdims=True)
                d_scores = (weighted - low.astype(F32) * total).astype(BF)
                values_sum[span, :] += dot_nn(low, grad)
                keys_sum[span, :] += dot_nn(d_scores, q_ref[here, :])
                d_query = dot_nn(keys_t[:, span], d_scores).T * factor
                d_ref[here, pl.ds(pl.multiple_of(head * E, E), E)] = turned(d_query, c_ref[here, :], s_ref[here, :], True).astype(BF)
                if block == 0:
                    ring.pace(firsts + 2 * head, turns)
            for which, (total, scale) in enumerate(((keys_sum, factor), (values_sum, 1.0))):
                far_out[head, which] = (total[:m, :] * scale).astype(BF)
                near_out[head, which] = (total[m : 2 * m, :] * scale).astype(BF)
                kept[head, which] = total[2 * m :, :] * scale
            near_copy(head).start()

            def settle(which):
                near_copy(which).wait_recv()
                came = near_in[which].astype(F32)
                share = core.astype(F32)
                far_out[which] = (far_out[which].astype(F32) + came * share).astype(BF)
                kept[which] = kept[which] + came * (1.0 - share)

                @pl.when(me >= 2)
                def _():
                    far_copy(which).start()

            def close(which):
                @pl.when(me < devices - 2)
                def _():
                    far_copy(which).wait_recv()
                    kept[which] = kept[which] + far_in[which].astype(F32)

                d_key = turned(kept[which, 0], c_ref[...], s_ref[...], True).astype(BF)
                d_ref[:, pl.ds(pl.multiple_of((heads + which) * E, E), E)] = d_key
                d_ref[:, pl.ds(pl.multiple_of((2 * heads + which) * E, E), E)] = kept[which, 1].astype(BF)
                near_copy(which).wait_send()

                @pl.when(me >= 2)
                def _():
                    far_copy(which).wait_send()

            @pl.when(head > 0)
            def _():
                settle(head - 1)

            @pl.when(head == heads - 1)
            def _():
                settle(head)

            ring.pace(firsts + 2 * head + 1, turns)

            @pl.when(head == 1)
            def _():
                flipped_ref[...] = flip_ref[...].T[: flipped_ref.shape[0]]

            @pl.when(head == heads - 1)
            def _():
                def one(which, carry):
                    close(which)
                    return carry

                lax.fori_loop(0, heads, one, 0)
                ring.finish()

    def at(i):
        return jnp.maximum(i - firsts, 0)

    head_spec = pl.BlockSpec((m, E), lambda i: (0, at(i)))
    rows_spec = pl.BlockSpec((ROWS, width), lambda i: (jnp.minimum(i, firsts - 1), 0))
    dma = pltpu.SemaphoreType.DMA
    pieces = (heads, 2, m, E)
    return pl.pallas_call(
        kernel,
        grid=(firsts + heads,),
        out_shape=[
            jax.ShapeDtypeStruct((m, 3 * columns), BF),
            jax.ShapeDtypeStruct((width, columns), BF),
            jax.ShapeDtypeStruct((rows, out_width), F32),
            jax.ShapeDtypeStruct((out_width, rows), F32),
            jax.ShapeDtypeStruct((m, width), F32),
            jax.ShapeDtypeStruct((1, width), F32),
        ],
        in_specs=[
            head_spec,
            pl.BlockSpec((reach, E), lambda i: (0, at(i))),
            pl.BlockSpec((reach, E), lambda i: (0, at(i) + heads)),
            pl.BlockSpec((1, blocks, KB, QB), lambda i: (at(i), 0, 0, 0)),
            head_spec,
            pl.BlockSpec((width, E), lambda i: (0, at(i) + 3 * heads)),
            rows_spec,
            single((1, width)),
            rows_spec,
            rows_spec,
            single((m, E)),
            single((m, E)),
            single(flip.shape),
            pl.BlockSpec(memory_space=pl.ANY),
        ],
        out_specs=[
            single((m, 3 * columns)),
            pl.BlockSpec((width, E), lambda i: (0, at(i))),
            single((rows, out_width)),
            single((out_width, rows)),
            rows_spec,
            single((1, width)),
        ],
        scratch_shapes=[
            pltpu.VMEM((m, width), BF), pltpu.VMEM((width, m), BF),
            pltpu.VMEM((reach, E), F32), pltpu.VMEM((reach, E), F32),
            pltpu.VMEM(pieces, BF), pltpu.VMEM(pieces, BF), pltpu.VMEM(pieces, BF), pltpu.VMEM(pieces, BF), pltpu.VMEM(pieces, F32),
            dma((heads,)), dma((heads,)), dma((heads,)), dma((heads,)),
            *Ring.scratch(devices, [(rows, ring_width // 2)] * 2),
        ],
        compiler_params=pltpu.CompilerParams(vmem_limit_bytes=VMEM, collective_id=identity, has_side_effects=True),
        cost_estimate=cost(8 * heads * m * KB * E * 2, 2 * heads * m * KB),
        name="attend_back",
    )(query, kv, kv, probs, mixed, w_attn, hidden, gain, d_normed, cotangent, cosine, sine, flip, ring_source)


def back_pass(x_t, d_out, weights, ring_sources, out_widths, costs, identity, name):
    amount, m, columns = d_out.shape
    width = x_t.shape[0]
    devices = lax.axis_size("dp")
    sides = lax.axis_size("tensor")
    tiles = width // TILE
    per = columns // TILE
    total = tiles + amount * per
    count = len(ring_sources)
    shapes = [(source.shape[-2], source.shape[-1] // pieces) for source, _, pieces in ring_sources for _ in range(pieces)]
    groups = [[index] for index in range(len(shapes))]

    def kernel(*refs):
        refs = list(refs)

        def take(number):
            taken = refs[:number]
            del refs[:number]
            return taken

        xt_ref, tile_ref, d_ref = take(3)
        w_refs = [take(amount) for _ in weights]
        sources = [ref if lead is None else ref.at[lead] for ref, (_, lead, _) in zip(take(count), ring_sources)]
        grad_ref, back_ref = take(2)
        sums = take(count)
        sent, got, y_send, y_recv = take(4)
        terms, goals = [], []
        for source, goal, (array, _, pieces) in zip(sources, sums, ring_sources):
            piece = array.shape[-1] // pieces
            terms += [(source, number * piece, piece) for number in range(pieces)]
            goals += [(goal, number * piece) for number in range(pieces)]
        ring = Ring(devices, terms, goals, groups, refs)
        other = (ring.me, lax.rem(ring.side + 1, sides))
        step = pl.program_id(0)

        def across(which):
            return pltpu.make_async_remote_copy(
                src_ref=sent.at[which], dst_ref=got.at[which], send_sem=y_send.at[which], recv_sem=y_recv.at[which],
                device_id=other, device_id_type=MESH,
            )

        @pl.when(step == 0)
        def _():
            ring.barrier((other,))
            ring.begin()

        @pl.when(step < tiles)
        def _():
            part = None
            for index in range(amount):
                column = 0
                for (_, several), blocks in zip(weights, w_refs):
                    made = dot_nt(d_ref[index, :, column : column + several], blocks[index][...])
                    part = made if part is None else part + made
                    column += several
            sent[step] = part.astype(BF)
            across(step).start()

        @pl.when(step >= tiles)
        def _():
            grad_ref[0] = dot_nn(xt_ref[...], tile_ref[0]).astype(BF)

        ring.pace(step, [(tiles, costs[0]), (amount * per, costs[1])])

        @pl.when(step == total - 1)
        def _():
            for which in range(tiles):
                across(which).wait()
                back_ref[:, which * TILE : (which + 1) * TILE] = sent[which].astype(F32) + got[which].astype(F32)
            ring.finish()

    def late(i):
        return jnp.maximum(i - tiles, 0)

    def early(i):
        return jnp.minimum(i, tiles - 1)

    specs = [
        single((width, m)),
        pl.BlockSpec((1, m, TILE), lambda i: (late(i) // per, 0, late(i) % per)),
        single((amount, m, columns)),
    ]
    operands = [x_t, d_out, d_out]
    for array, several in weights:
        for index in range(amount):
            specs.append(pl.BlockSpec((TILE, several), functools.partial(lambda where, i: (early(i), where), index)))
            operands.append(array)
    out_specs = [pl.BlockSpec((1, width, TILE), lambda i: (late(i) // per, 0, late(i) % per)), single((m, width))]
    out_shape = [jax.ShapeDtypeStruct((amount, width, columns), BF), jax.ShapeDtypeStruct((m, width), F32)]
    specs += [pl.BlockSpec(memory_space=pl.ANY)] * count
    operands += [source for source, _, _ in ring_sources]
    for (source, _, _), out_width in zip(ring_sources, out_widths):
        rows = source.shape[-2]
        out_specs.append(single((rows, out_width)))
        out_shape.append(jax.ShapeDtypeStruct((rows, out_width), F32))
    dma = pltpu.SemaphoreType.DMA
    return pl.pallas_call(
        kernel,
        grid=(total,),
        out_shape=out_shape,
        in_specs=specs,
        out_specs=out_specs,
        scratch_shapes=[
            pltpu.VMEM((tiles, m, TILE), BF),
            pltpu.VMEM((tiles, m, TILE), BF),
            dma((tiles,)),
            dma((tiles,)),
            *Ring.scratch(devices, shapes),
        ],
        compiler_params=pltpu.CompilerParams(vmem_limit_bytes=VMEM, collective_id=identity, has_side_effects=True),
        cost_estimate=cost(4 * m * width * amount * columns, 6 * width * amount * columns),
        name=name,
    )(*operands)


def root_of(rows):
    return lax.rsqrt(jnp.mean(rows * rows, axis=-1, keepdims=True) + EPS)


def norm_grad(rows, gain, grad):
    root = root_of(rows)
    pushed = grad * gain
    inner = jnp.mean(pushed * rows, axis=-1, keepdims=True)
    return root * pushed - rows * (root * root * root * inner), jnp.sum(grad * rows * root, axis=0, keepdims=True)


def first_norm(far, near, tokens, gain):
    m, width = tokens.shape
    steps = m // ROWS

    def kernel(far_ref, near_ref, x_ref, g_ref, o_ref, t_ref):
        step = pl.program_id(0)
        me = lax.axis_index("dp")

        def normed(ref):
            rows = ref[...].astype(F32)
            return (rows * root_of(rows) * g_ref[...]).astype(BF)

        def earlier(ref, there):
            @pl.when(there)
            def _():
                o_ref[...] = normed(ref)

            @pl.when(jnp.logical_not(there))
            def _():
                o_ref[...] = jnp.zeros_like(o_ref)

        @pl.when(step < steps)
        def _():
            earlier(far_ref, me >= 2)

        @pl.when((step >= steps) & (step < 2 * steps))
        def _():
            earlier(near_ref, me >= 1)

        @pl.when(step >= 2 * steps)
        def _():
            made = normed(x_ref)
            o_ref[...] = made
            t_ref[...] = made.T

    def part(which):
        return pl.BlockSpec((ROWS, width), lambda i: (jnp.clip(i - which * steps, 0, steps - 1), 0))

    return pl.pallas_call(
        kernel,
        grid=(3 * steps,),
        out_shape=[jax.ShapeDtypeStruct((3 * m, width), BF), jax.ShapeDtypeStruct((width, m), BF)],
        in_specs=[part(0), part(1), part(2), whole_spec((1, width))],
        out_specs=[
            pl.BlockSpec((ROWS, width), lambda i: (i, 0)),
            pl.BlockSpec((width, ROWS), lambda i: (0, jnp.maximum(i - 2 * steps, 0))),
        ],
        compiler_params=pltpu.CompilerParams(vmem_limit_bytes=VMEM),
        cost_estimate=cost(24 * m * width, 14 * m * width),
        name="first_norm",
    )(far, near, tokens, gain)


def out_norm(mixed, w_attn, place, tokens, gain, identity):
    m, columns = mixed.shape
    width = tokens.shape[1]
    steps = m // ROWS
    sides = lax.axis_size("tensor")

    def kernel(x_ref, w_ref, r_ref, g_ref, hidden_ref, normed_ref, turned_ref, sent, got, send, recv):
        step = pl.program_id(0)
        other = (lax.axis_index("dp"), lax.rem(lax.axis_index("tensor") + 1, sides))

        @pl.when(step == 0)
        def _():
            semaphore = pltpu.get_barrier_semaphore()
            pl.semaphore_signal(semaphore, inc=1, device_id=other, device_id_type=MESH)
            pl.semaphore_wait(semaphore, 1)

        def across(which):
            return pltpu.make_async_remote_copy(
                src_ref=sent.at[which], dst_ref=got.at[which], send_sem=send.at[which], recv_sem=recv.at[which],
                device_id=other, device_id_type=MESH,
            )

        @pl.when(step < steps)
        def _():
            sent[step] = dot_nt(x_ref[...], w_ref[...]).astype(BF)
            across(step).start()

        @pl.when(step >= steps)
        def _():
            which = step - steps
            across(which).wait()
            hidden = r_ref[...].astype(F32) + (sent[which].astype(F32) + got[which].astype(F32))
            normed = (hidden * root_of(hidden) * g_ref[...]).astype(BF)
            hidden_ref[...] = hidden
            normed_ref[...] = normed
            turned_ref[...] = normed.T

    def late(i):
        return jnp.maximum(i - steps, 0)

    late_rows = pl.BlockSpec((ROWS, width), lambda i: (late(i), 0))
    dma = pltpu.SemaphoreType.DMA
    return pl.pallas_call(
        kernel,
        grid=(2 * steps,),
        out_shape=[
            jax.ShapeDtypeStruct((m, width), F32),
            jax.ShapeDtypeStruct((m, width), BF),
            jax.ShapeDtypeStruct((width, m), BF),
        ],
        in_specs=[
            pl.BlockSpec((ROWS, columns), lambda i: (jnp.minimum(i, steps - 1), 0)),
            pl.BlockSpec((width, columns), lambda i: (0, place), pipeline_mode=pl.Buffered(1)),
            late_rows,
            single((1, width)),
        ],
        out_specs=[late_rows, late_rows, pl.BlockSpec((width, ROWS), lambda i: (0, late(i)))],
        scratch_shapes=[pltpu.VMEM((steps, ROWS, width), BF), pltpu.VMEM((steps, ROWS, width), BF), dma((steps,)), dma((steps,))],
        compiler_params=pltpu.CompilerParams(vmem_limit_bytes=VMEM, collective_id=identity, has_side_effects=True),
        cost_estimate=cost(2 * m * width * columns, 12 * m * width),
        name="out_norm",
    )(mixed, w_attn, tokens, gain)


def last_pass(tokens, gain, grad, d_hidden, hidden, activated, w_ffn, rest, gain_ffn_grad, flip, qkv_part, lanes, identity):
    m, width = tokens.shape
    devices, rows, all_columns = qkv_part.shape
    columns = all_columns // 3
    chips = devices // 2
    size = ROWS // 2
    steps = m // size
    total = steps + chips
    names = 3
    tiles = width // TILE
    units = activated.shape[1]
    sides = lax.axis_size("tensor")
    assert tiles == steps and chips >= tiles

    some = w_ffn.shape[1] // 3

    def kernel(x_ref, g_ref, dn_ref, dh_ref, h_ref, a_ref, w_ref, rest_ref, gf_ref, flip_ref, source, grad_ref, layer_ref, flipped_ref, q_ref, k_ref, v_ref, gains_ref, gain_sum, gain_source, sent, got, y_send, y_recv, *scratch):
        step = pl.program_id(0)
        ring = Ring(
            devices, [(source, number * columns, columns) for number in range(names)], [(q_ref, 0), (k_ref, 0), (v_ref, 0)],
            [[0], [1], [2]], scratch[: 3 * names + 5],
        )
        gain_ring = Ring(devices, [(gain_source, 0, lanes)], [(gains_ref, 0)], [[0]], scratch[3 * names + 5 :])
        other = (ring.me, lax.rem(ring.side + 1, sides))

        def across(which):
            return pltpu.make_async_remote_copy(
                src_ref=sent.at[which], dst_ref=got.at[which], send_sem=y_send.at[which], recv_sem=y_recv.at[which],
                device_id=other, device_id_type=MESH,
            )

        @pl.when(step == 0)
        def _():
            ring.barrier((other,))
            ring.begin()

        @pl.when(step < tiles)
        def _():
            sent[step] = (dot_nt(a_ref[:, :some], w_ref[...]) + dot_nt(a_ref[:, some:], rest_ref[...])).astype(BF)
            across(step).start()

        @pl.when(step < steps)
        def _():
            change, gain_part = norm_grad(x_ref[...].astype(F32), g_ref[...], dn_ref[...])
            grad_ref[...] = dh_ref[...] + change

            @pl.when(step == 0)
            def _():
                gain_sum[...] = gain_part
                flipped_ref[...] = flip_ref[...].T

            @pl.when(step > 0)
            def _():
                gain_sum[...] += gain_part

        @pl.when(step == steps - 1)
        def _():
            gain_source[...] = jnp.zeros_like(gain_source)
            for device in range(devices):
                span = slice(device * rows, (device + 1) * rows)
                gain_source[device, :16, :rows] = jnp.broadcast_to(gain_sum[:, span], (16, rows)).astype(BF)
                gain_source[device, 16:, :rows] = jnp.broadcast_to(gf_ref[:, span], (16, rows)).astype(BF)
            gain_ring.begin()

        ring.pace(step, [(steps, 3), (chips, 5)])

        @pl.when(step >= steps)
        def _():
            gain_ring.run(step - steps, step - steps + 1)

        @pl.when((step >= steps) & (step < steps + tiles))
        def _():
            which = step - steps
            across(which).wait()
            layer_ref[...] = (h_ref[...] + (sent[which].astype(F32) + got[which].astype(F32))).astype(BF)

        @pl.when(step == total - 1)
        def _():
            ring.finish()
            gain_ring.finish()

    def early(i):
        return jnp.minimum(i, steps - 1)

    rows_spec = pl.BlockSpec((size, width), lambda i: (early(i), 0))
    tile_spec = pl.BlockSpec((m, TILE), lambda i: (0, jnp.clip(i - steps, 0, tiles - 1)))
    dma = pltpu.SemaphoreType.DMA
    sums = jax.ShapeDtypeStruct((rows, columns), F32)
    return pl.pallas_call(
        kernel,
        grid=(total,),
        out_shape=[
            jax.ShapeDtypeStruct((m, width), F32),
            jax.ShapeDtypeStruct((m, width), BF),
            jax.ShapeDtypeStruct((flip.shape[1], flip.shape[0]), F32),
            sums, sums, sums,
            jax.ShapeDtypeStruct((32, lanes), F32),
        ],
        in_specs=[
            rows_spec, single((1, width)), rows_spec, rows_spec, tile_spec, single((m, units)),
            pl.BlockSpec((TILE, some), lambda i: (early(i), 2)), pl.BlockSpec((TILE, units - some), lambda i: (early(i), 2)), single((1, width)),
            single(flip.shape), pl.BlockSpec(memory_space=pl.ANY),
        ],
        out_specs=[
            rows_spec, tile_spec, single((flip.shape[1], flip.shape[0])),
            single(sums.shape), single(sums.shape), single(sums.shape), single((32, lanes)),
        ],
        scratch_shapes=[
            pltpu.VMEM((1, width), F32),
            pltpu.VMEM((devices, 32, lanes), BF),
            pltpu.VMEM((tiles, m, TILE), BF),
            pltpu.VMEM((tiles, m, TILE), BF),
            dma((tiles,)),
            dma((tiles,)),
            *Ring.scratch(devices, [(rows, columns)] * names),
            *Ring.scratch(devices, [(32, lanes)]),
        ],
        compiler_params=pltpu.CompilerParams(vmem_limit_bytes=VMEM, collective_id=identity, has_side_effects=True),
        cost_estimate=cost(20 * m * width, 24 * m * width),
        name="last_pass",
    )(tokens, gain, grad, d_hidden, hidden, activated, w_ffn, rest, gain_ffn_grad, flip, qkv_part)


def feed_tile(x_ref, dy_ref, dyt_ref, g_ref, u_ref, d_ref, act_ref, both_ref, down_ref):
    gate = dot_nn(x_ref[...], g_ref[...])
    up = dot_nn(x_ref[...], u_ref[...])
    d_act = dot_nn(dy_ref[...], d_ref[...])
    soft = 1.0 / (1.0 + jnp.exp(-gate))
    silu = gate * soft
    act = (silu * up).astype(BF)
    act_ref[...] = act
    both_ref[0] = (d_act * up * (soft * (1.0 + gate * (1.0 - soft)))).astype(BF)
    both_ref[1] = (d_act * silu).astype(BF)
    down_ref[...] = dot_nn(dyt_ref[...], act).astype(BF)


def feed(x, dy, dy_t, w, block, tiles, identity):
    m, k = x.shape
    early = tiles - LATE
    devices = lax.axis_size("dp")
    width = block.shape[1] // 2

    def kernel(x_ref, dy_ref, dyt_ref, g_ref, u_ref, d_ref, block_ref, act_ref, both_ref, down_ref, rest_ref, *scratch):
        step = pl.program_id(0)
        spread = Spread(devices, [(block_ref, rest_ref, 0, width), (block_ref, rest_ref, width, width)], scratch)

        @pl.when(step == 0)
        def _():
            spread.barrier()
            spread.begin()

        feed_tile(x_ref, dy_ref, dyt_ref, g_ref, u_ref, d_ref, act_ref, both_ref, down_ref)
        spread.pace(step, early)

        @pl.when(step == early - 1)
        def _():
            spread.finish()

    any_space = pl.BlockSpec(memory_space=pl.ANY)
    return pl.pallas_call(
        kernel,
        grid=(early,),
        out_shape=[
            jax.ShapeDtypeStruct((m, tiles * TILE), BF),
            jax.ShapeDtypeStruct((2, m, tiles * TILE), BF),
            jax.ShapeDtypeStruct((k, tiles * TILE), BF),
            jax.ShapeDtypeStruct((k, block.shape[1]), BF),
        ],
        in_specs=[
            single((m, k)),
            single((m, k)),
            single((k, m)),
            pl.BlockSpec((k, TILE), lambda i: (0, i)),
            pl.BlockSpec((k, TILE), lambda i: (0, i + early)),
            pl.BlockSpec((k, TILE), lambda i: (0, i + 2 * early)),
            any_space,
        ],
        out_specs=[
            pl.BlockSpec((m, TILE), lambda i: (0, i)),
            pl.BlockSpec((2, m, TILE), lambda i: (0, 0, i)),
            pl.BlockSpec((k, TILE), lambda i: (0, i)),
            any_space,
        ],
        scratch_shapes=Spread.scratch(devices, 2),
        compiler_params=pltpu.CompilerParams(vmem_limit_bytes=VMEM, collective_id=identity, has_side_effects=True),
        cost_estimate=cost(8 * m * k * early * TILE, 8 * (m + k) * early * TILE, m * early * TILE),
        name="feed",
    )(x, dy, dy_t, w, w, w, block)


def feed_rest(x, dy, dy_t, rest, activated, d_both, down_part):
    m, k = x.shape
    tiles = activated.shape[1] // TILE
    early = tiles - LATE

    def kernel(x_ref, dy_ref, dyt_ref, g_ref, u_ref, d_ref, act_in, both_in, down_in, act_ref, both_ref, down_ref):
        feed_tile(x_ref, dy_ref, dyt_ref, g_ref, u_ref, d_ref, act_ref, both_ref, down_ref)

    any_space = pl.BlockSpec(memory_space=pl.ANY)
    return pl.pallas_call(
        kernel,
        grid=(LATE,),
        out_shape=[jax.ShapeDtypeStruct(a.shape, BF) for a in (activated, d_both, down_part)],
        in_specs=[
            single((m, k)),
            single((m, k)),
            single((k, m)),
            pl.BlockSpec((k, TILE), lambda i: (0, i)),
            pl.BlockSpec((k, TILE), lambda i: (0, i + LATE)),
            pl.BlockSpec((k, TILE), lambda i: (0, i + 2 * LATE)),
            any_space, any_space, any_space,
        ],
        out_specs=[
            pl.BlockSpec((m, TILE), lambda i: (0, i + early)),
            pl.BlockSpec((2, m, TILE), lambda i: (0, 0, i + early)),
            pl.BlockSpec((k, TILE), lambda i: (0, i + early)),
        ],
        input_output_aliases={6: 0, 7: 1, 8: 2},
        compiler_params=pltpu.CompilerParams(vmem_limit_bytes=VMEM),
        cost_estimate=cost(8 * m * k * LATE * TILE, 8 * (m + k) * LATE * TILE, m * LATE * TILE),
        name="feed_rest",
    )(x, dy, dy_t, rest, rest, rest, activated, d_both, down_part)


def shards(tokens, positions, attn_gain, w_query, w_key, w_value, w_out, ffn_gain, w_gate, w_up, w_down, cotangent):
    devices = lax.axis_size("dp")
    span = tokens.shape[0]
    assert 2 * span == WINDOW
    own_rows = w_query.shape[0]
    width = tokens.shape[1]
    head_columns = w_query.shape[1]
    heads = head_columns // E
    hidden_units = w_gate.shape[1]
    tiles = (hidden_units + TILE - 1) // TILE
    padded = tiles * TILE

    attn_pack = jnp.concatenate([w_query, w_key, w_value, w_out.T], axis=1)
    lanes = max(128, own_rows)
    gains = jnp.zeros((32, lanes), BF).at[0, :own_rows].set(attn_gain).at[16, :own_rows].set(ffn_gain)
    w_attn, all_gains, near, far = ring_gather((attn_pack, gains), (2, 1), tokens, 0)

    def wide(matrix):
        return jnp.pad(matrix, ((0, 0), (0, padded - hidden_units)))

    ffn_parts = [wide(w_gate), wide(w_up), wide(w_down.T)]
    some = padded - LATE * TILE
    ffn_pack = jnp.concatenate([part[:, :some] for part in ffn_parts], axis=1)
    rest_pack = jnp.concatenate([part[:, some:] for part in ffn_parts], axis=1)
    w_attn, all_gains, ffn_pack = lax.optimization_barrier((w_attn, all_gains, ffn_pack))
    w_ffn = lax.all_gather(ffn_pack, "dp", axis=0, tiled=True)
    all_gains = all_gains.reshape(devices, 32, lanes)
    gain_attn = all_gains[:, 0, :own_rows].reshape(1, width).astype(F32)
    gain_ffn = all_gains[:, 16, :own_rows].reshape(1, width).astype(F32)

    frequency = THETA ** (-(jnp.arange(E // 2, dtype=F32) * 2.0 / E))
    earlier = positions[0] - WINDOW + jnp.arange(WINDOW, dtype=jnp.int32)
    angles = jnp.concatenate([earlier, positions]).astype(F32)[:, None] * frequency[None, :]
    cosine_half, sine_half = jnp.cos(angles), jnp.sin(angles)
    cosine = jnp.concatenate([cosine_half, cosine_half], axis=1)
    sine = jnp.concatenate([-sine_half, sine_half], axis=1)

    normed_attn, normed_attn_t = first_norm(far, near, tokens, gain_attn)
    query, kv = project(normed_attn, w_attn, cosine, sine, span, heads)
    mixed, probs = attend(query, kv, positions[None, :], heads)
    cosine, sine = cosine[WINDOW:], sine[WINDOW:]
    hidden, normed_ffn, normed_ffn_t = out_norm(mixed, w_attn, 3, tokens, gain_ffn, 5)

    cotangent_t = cotangent.T
    activated, d_both, down_part, rest = feed(normed_ffn, cotangent, cotangent_t, w_ffn, rest_pack, tiles, 6)
    activated, d_both, down_part = feed_rest(normed_ffn, cotangent, cotangent_t, rest, activated, d_both, down_part)
    both_part, d_normed_ffn, down_grad = back_pass(
        normed_ffn_t, d_both, [(w_ffn, some), (rest, padded - some)], [(down_part.reshape(devices, own_rows, padded), None, 2)], [padded],
        (2, 1), 1, "ffn_back",
    )
    both_part = both_part.reshape(2, devices, own_rows, padded)

    d_qkv, out_part, gate_grad, w_down_grad, d_hidden, gain_ffn_grad = attend_back(
        query, kv, probs, mixed, w_attn, hidden, gain_ffn, d_normed_ffn, cotangent, cosine, sine, down_grad, both_part, heads, hidden_units, 2
    )
    qkv_part, d_normed_attn, up_grad, out_grad = back_pass(
        normed_attn_t, d_qkv[None], [(w_attn, 3 * head_columns)],
        [(both_part, 1, 2), (out_part.reshape(devices, own_rows, head_columns), None, 1)], [hidden_units, head_columns], (4, 3), 3, "qkv_back",
    )
    tokens_grad, layer_out, w_out_grad, query_grad, key_grad, value_grad, gain_grads = last_pass(
        tokens, gain_attn, d_normed_attn, d_hidden, hidden, activated, w_ffn, rest, gain_ffn_grad, out_grad,
        qkv_part.reshape(devices, own_rows, 3 * head_columns), lanes, 4,
    )
    return (
        layer_out,
        tokens_grad,
        gain_grads[0, :own_rows],
        query_grad,
        key_grad,
        value_grad,
        w_out_grad,
        gain_grads[16, :own_rows],
        gate_grad,
        up_grad,
        w_down_grad,
    )


def solution(mesh):
    by_rows, by_both, turned_both, line = P("dp", None), P("dp", "tensor"), P("tensor", "dp"), P("dp")
    return jax.shard_map(
        shards,
        mesh=mesh,
        in_specs=(by_rows, line, line, by_both, by_both, by_both, turned_both, line, by_both, by_both, turned_both, by_rows),
        out_specs=(by_rows, by_rows, line, by_both, by_both, by_both, turned_both, line, by_both, by_both, turned_both),
        check_vma=False,
    )
```

```python
import functools

import jax
import jax.numpy as jnp
from jax import lax
from jax.experimental import pallas as pl
from jax.experimental.pallas import tpu as pltpu
from jax.sharding import PartitionSpec as P

E = 128
WINDOW = 1024
EPS = 1e-06
THETA = 10000.0
LOG2E = 1.4426950408889634
MESH = pl.DeviceIdType.MESH
BF = jnp.bfloat16
F32 = jnp.float32
QB = 256
KB = WINDOW + QB
TILE = 256
ROWS = 128
LATE = 3
VMEM = 59 * 1024 * 1024


def whole_spec(shape):
    return pl.BlockSpec(shape, lambda i: (0,) * len(shape))


def single(shape):
    return pl.BlockSpec(shape, lambda i: (0,) * len(shape), pipeline_mode=pl.Buffered(1))


def cost(flops, nbytes, special=0):
    return pl.CostEstimate(flops=flops, bytes_accessed=nbytes, transcendentals=special)


def ring_chip(place, chips):
    place = lax.rem(place + 2 * chips, chips)
    late = place // (chips // 2)
    return (1 - late) * 2 * place + late * (2 * (chips - 1 - place) + 1)


def ring_place(chip, chips):
    column = lax.rem(chip, 2)
    row = chip // 2
    return (1 - column) * row + column * (chips - 1 - row)


def gather_kernel(devices, chunks, count, *refs):
    ins, tokens = refs[:count], refs[count]
    outs, near, far = refs[count + 1 : 2 * count + 1], refs[2 * count + 1], refs[2 * count + 2]
    local_sem, a_send, a_recv, b_send, b_recv, c_send, c_recv, far_send, far_recv, near_send, near_recv = refs[2 * count + 3 :]
    chips = devices // 2
    me = lax.axis_index("dp")
    side = lax.axis_index("tensor")
    core = lax.rem(me, 2)
    place = ring_place(me // 2, chips)

    def device(q):
        return ring_chip(q, chips) * 2 + core

    right = device(place + 1)
    left = device(place - 1)
    partner = me + 1 - 2 * core
    across = lax.rem(side + 1, lax.axis_size("tensor"))
    later, before = lax.rem(me + 2, devices), lax.rem(me + devices - 2, devices)
    barrier = pltpu.get_barrier_semaphore()
    for other in ((right, side), (left, side), (partner, side), (me, across), (later, side), (before, side)):
        pl.semaphore_signal(barrier, inc=1, device_id=other, device_id_type=MESH)
    pl.semaphore_wait(barrier, 6)

    pieces = []
    for index, parts in enumerate(chunks):
        width = ins[index].shape[1] // parts
        for part in range(parts):
            pieces.append((index, part * width, width))
    hops = chips - 1

    def view(ref, row, half, piece, rows):
        index, column, width = piece
        start = row * rows + half * (rows // 2)
        if not isinstance(start, int):
            start = pl.multiple_of(start, 16)
        return ref.at[pl.ds(start, rows // 2), pl.ds(column, width)]

    def described(source, target, send, recv, other):
        return pltpu.make_async_remote_copy(
            src_ref=source, dst_ref=target, send_sem=send, recv_sem=recv, device_id=other, device_id_type=MESH
        )

    def remote(source, target, send, recv, other):
        copy = described(source, target, send, recv, (other, side))
        copy.start()
        return copy

    span = tokens.shape[0] // 2

    def half_rows(ref, which):
        return ref.at[pl.ds(pl.multiple_of(which * span, span), span)]

    far_copy = described(half_rows(tokens, side), half_rows(far, side), far_send.at[0], far_recv.at[0], (later, side))
    cross_copy = described(half_rows(far, side), half_rows(far, side), far_send.at[1], far_recv.at[1], (me, across))
    own_near = [described(half_rows(tokens, which), half_rows(near, which), near_send.at[which], near_recv.at[which], (partner, side)) for which in range(2)]
    far_near = [described(half_rows(far, which), half_rows(near, which), near_send.at[slot], near_recv.at[slot], (partner, side)) for slot, which in enumerate((side, across))]

    @pl.when(me < devices - 2)
    def _():
        far_copy.start()

    @pl.when(core == 0)
    def _():
        for copy in own_near:
            copy.start()

    def pass_on(slot):
        @pl.when(me >= 2)
        def _():
            if slot == 0:
                far_copy.wait_recv()
                cross_copy.start()
            else:
                cross_copy.wait_recv()

            @pl.when(core == 1)
            def _():
                far_near[slot].start()

    local = []
    for index in range(count):
        rows = ins[index].shape[0]
        copy = pltpu.make_async_copy(
            ins[index], outs[index].at[pl.ds(pl.multiple_of(me * rows, 16), rows)], local_sem.at[index]
        )
        copy.start()
        local.append(copy)
    forward, partner_copies = {}, []
    for number, piece in enumerate(pieces):
        ref, out = ins[piece[0]], outs[piece[0]]
        rows = ref.shape[0]
        forward[number, 0] = (
            remote(view(ref, 0, 0, piece, rows), view(out, me, 0, piece, rows), a_send.at[number, 0], a_recv.at[number, 0], right),
            remote(view(ref, 0, 1, piece, rows), view(out, me, 1, piece, rows), b_send.at[number, 0], b_recv.at[number, 0], left),
        )
    for number, piece in enumerate(pieces):
        ref, out = ins[piece[0]], outs[piece[0]]
        rows = ref.shape[0]
        for half in range(2):
            partner_copies.append(
                remote(view(ref, 0, half, piece, rows), view(out, me, half, piece, rows), c_send.at[number, 0, half], c_recv.at[number, 0, half], partner)
            )
    for hop in range(hops):
        for number, piece in enumerate(pieces):
            out = outs[piece[0]]
            rows = ins[piece[0]].shape[0]
            came = forward[number, hop]
            sent = []
            for half in range(2):
                came[half].wait_recv()
                owner = device(place - 1 - hop if half == 0 else place + 1 + hop)
                block = view(out, owner, half, piece, rows)
                send, recv = (a_send, a_recv) if half == 0 else (b_send, b_recv)
                if hop < hops - 1:
                    sent.append(
                        remote(block, block, send.at[number, hop + 1], recv.at[number, hop + 1], right if half == 0 else left)
                    )
                partner_copies.append(
                    remote(block, block, c_send.at[number, hop + 1, half], c_recv.at[number, hop + 1, half], partner)
                )
            if sent:
                forward[number, hop + 1] = tuple(sent)
        if hop == hops // 2:
            pass_on(0)
        if hop == hops - 2:
            pass_on(1)
    for copy in local:
        copy.wait()
    for pair in forward.values():
        for copy in pair:
            copy.wait_send()
    for copy in partner_copies:
        copy.wait()

    @pl.when(me < devices - 2)
    def _():
        far_copy.wait_send()

    @pl.when(me >= 2)
    def _():
        cross_copy.wait_send()

        @pl.when(core == 1)
        def _():
            for copy in far_near:
                copy.wait_send()

    @pl.when(core == 0)
    def _():
        for copy in own_near:
            copy.wait_send()

    @pl.when((core == 1) | (me >= 2))
    def _():
        for copy in own_near:
            copy.wait_recv()


def ring_gather(arrays, chunks, tokens, identity):
    devices = lax.axis_size("dp")
    hops = devices // 2 - 1
    pieces = sum(chunks)
    dma = pltpu.SemaphoreType.DMA
    any_space = pl.BlockSpec(memory_space=pl.ANY)
    return pl.pallas_call(
        functools.partial(gather_kernel, devices, chunks, len(arrays)),
        out_shape=[jax.ShapeDtypeStruct((a.shape[0] * devices, a.shape[1]), a.dtype) for a in arrays]
        + [jax.ShapeDtypeStruct(tokens.shape, tokens.dtype)] * 2,
        in_specs=[any_space] * (len(arrays) + 1),
        out_specs=[any_space] * (len(arrays) + 2),
        scratch_shapes=[
            dma((len(arrays),)),
            dma((pieces, hops)),
            dma((pieces, hops)),
            dma((pieces, hops)),
            dma((pieces, hops)),
            dma((pieces, hops + 1, 2)),
            dma((pieces, hops + 1, 2)),
            dma((2,)),
            dma((2,)),
            dma((2,)),
            dma((2,)),
        ],
        compiler_params=pltpu.CompilerParams(collective_id=identity, has_side_effects=True),
        name="ring_gather",
    )(*arrays, tokens)


class Spread:
    def __init__(self, devices, pieces, scratch):
        self.devices, self.chips, self.pieces = devices, devices // 2, pieces
        self.local_sem, self.send_sem, self.recv_sem, self.give_sem, self.take_sem = scratch
        self.me = lax.axis_index("dp")
        self.side = lax.axis_index("tensor")
        self.core = lax.rem(self.me, 2)
        self.place = ring_place(self.me // 2, self.chips)
        self.partner = self.me + 1 - 2 * self.core
        self.next = (
            ring_chip(self.place + 1, self.chips) * 2 + self.core,
            ring_chip(self.place - 1, self.chips) * 2 + self.core,
        )
        self.events = (self.chips - 1) * len(pieces)

    @staticmethod
    def scratch(devices, count):
        dma = pltpu.SemaphoreType.DMA
        chips = devices // 2
        return [dma((count,))] + [dma((count, amount, 2)) for amount in (chips - 1, chips - 1, chips, chips)]

    def barrier(self):
        semaphore = pltpu.get_barrier_semaphore()
        for other in (*self.next, self.partner):
            pl.semaphore_signal(semaphore, inc=1, device_id=(other, self.side), device_id_type=MESH)
        pl.semaphore_wait(semaphore, 3)

    def block(self, index, stage, half):
        source, whole, column, width = self.pieces[index]
        rows = source.shape[0]
        owner = ring_chip(self.place - stage if half == 0 else self.place + stage, self.chips) * 2 + self.core
        return whole.at[pl.ds(pl.multiple_of(owner * rows + half * (rows // 2), 16), rows // 2), pl.ds(column, width)]

    def first(self, index, half):
        source, _, column, width = self.pieces[index]
        rows = source.shape[0]
        return source.at[pl.ds(half * (rows // 2), rows // 2), pl.ds(column, width)]

    def local(self, index):
        source, whole, column, width = self.pieces[index]
        rows = source.shape[0]
        span = pl.ds(pl.multiple_of(self.me * rows, 16), rows)
        return pltpu.make_async_copy(
            source.at[:, pl.ds(column, width)], whole.at[span, pl.ds(column, width)], self.local_sem.at[index]
        )

    def copy(self, index, stage, half, start, across):
        block = self.block(index, stage, half)
        send, recv = (self.give_sem, self.take_sem) if across else (self.send_sem, self.recv_sem)
        return pltpu.make_async_remote_copy(
            src_ref=self.first(index, half) if start else block,
            dst_ref=block,
            send_sem=send.at[index, stage, half],
            recv_sem=recv.at[index, stage, half],
            device_id=(self.partner if across else self.next[half], self.side),
            device_id_type=MESH,
        )

    def each(self):
        return [(index, half) for index in range(len(self.pieces)) for half in range(2)]

    def begin(self):
        for index, half in self.each():
            self.copy(index, 0, half, True, False).start()
        for index, half in self.each():
            self.copy(index, 0, half, True, True).start()
        for index in range(len(self.pieces)):
            self.local(index).start()

    def stage(self, stage, index):
        for half in range(2):
            self.copy(index, stage - 1, half, False, False).wait_recv()

            @pl.when(stage < self.chips - 1)
            def _():
                self.copy(index, stage, half, False, False).start()

            self.copy(index, stage, half, False, True).start()

    def pace(self, step, total):
        count = len(self.pieces)

        def one(event, carry):
            for index in range(count):
                pl.when(lax.rem(event, count) == index)(functools.partial(self.stage, event // count + 1, index))
            return carry

        lax.fori_loop(step * self.events // total, (step + 1) * self.events // total, one, 0)

    def finish(self):
        for index in range(len(self.pieces)):
            self.local(index).wait()
        for index, half in self.each():
            self.copy(index, 0, half, True, False).wait_send()
            self.copy(index, 0, half, True, True).wait()

        def sent(stage, carry):
            for index, half in self.each():
                self.copy(index, stage, half, False, False).wait_send()
            return carry

        lax.fori_loop(1, self.chips - 1, sent, 0)

        def gave(stage, carry):
            for index, half in self.each():
                self.copy(index, stage, half, False, True).wait()
            return carry

        lax.fori_loop(1, self.chips, gave, 0)


class Ring:
    AHEAD = 3

    def __init__(self, devices, terms, goals, groups, scratch):
        self.devices, self.chips = devices, devices // 2
        self.terms, self.goals, self.groups = terms, goals, groups
        count = len(terms)
        self.mine, self.taken, self.inbox = scratch[0 : 3 * count : 3], scratch[1 : 3 * count : 3], scratch[2 : 3 * count : 3]
        self.own_sem, self.give_sem, self.take_sem, self.send_sem, self.recv_sem = scratch[3 * count : 3 * count + 5]
        self.me = lax.axis_index("dp")
        self.side = lax.axis_index("tensor")
        self.core = lax.rem(self.me, 2)
        self.place = ring_place(self.me // 2, self.chips)
        self.partner = self.me + 1 - 2 * self.core
        self.next = (
            ring_chip(self.place + 1, self.chips) * 2 + self.core,
            ring_chip(self.place - 1, self.chips) * 2 + self.core,
        )
        self.events = (self.chips - 1) * len(groups)

    @staticmethod
    def scratch(devices, shapes):
        chips, count = devices // 2, len(shapes)
        dma = pltpu.SemaphoreType.DMA
        buffers = []
        for rows, width in shapes:
            buffers += [pltpu.VMEM((amount, 2, rows // 2, width), BF) for amount in (chips, chips, chips - 1)]
        return buffers + [dma((count, amount, 2)) for amount in (chips, chips, chips, chips - 1, chips - 1)]

    def barrier(self, others=()):
        semaphore = pltpu.get_barrier_semaphore()
        everyone = [(self.next[0], self.side), (self.next[1], self.side), (self.partner, self.side), *others]
        for other in everyone:
            pl.semaphore_signal(semaphore, inc=1, device_id=other, device_id_type=MESH)
        pl.semaphore_wait(semaphore, len(everyone))

    def block(self, index, stage, half, core):
        at = self.place - 1 - stage if half == 0 else self.place + 1 + stage
        size = self.mine[index].shape[2]
        source, column, width = self.terms[index]
        return source.at[ring_chip(at, self.chips) * 2 + core, pl.ds(half * size, size), pl.ds(column, width)]

    def own(self, index, stage, half):
        return pltpu.make_async_copy(
            self.block(index, stage, half, self.core), self.mine[index].at[stage, half], self.own_sem.at[index, stage, half]
        )

    def given(self, index, stage, half):
        return pltpu.make_async_remote_copy(
            src_ref=self.block(index, stage, half, 1 - self.core),
            dst_ref=self.taken[index].at[stage, half],
            send_sem=self.give_sem.at[index, stage, half],
            recv_sem=self.take_sem.at[index, stage, half],
            device_id=(self.partner, self.side),
            device_id_type=MESH,
        )

    def hop(self, index, stage, half, first):
        source = self.mine[index].at[0, half] if first else self.inbox[index].at[stage - 1, half]
        return pltpu.make_async_remote_copy(
            src_ref=source,
            dst_ref=self.inbox[index].at[stage, half],
            send_sem=self.send_sem.at[index, stage, half],
            recv_sem=self.recv_sem.at[index, stage, half],
            device_id=(self.next[half], self.side),
            device_id_type=MESH,
        )

    def each(self, group=None):
        members = range(len(self.terms)) if group is None else self.groups[group]
        return [(index, half) for index in members for half in range(2)]

    def fetch(self, stage, group):
        for index, half in self.each(group):
            self.given(index, stage, half).start()
            self.own(index, stage, half).start()

    def begin(self):
        for group in range(len(self.groups)):
            self.fetch(0, group)
        for index, half in self.each():
            self.mine[index][0, half] = self.chip_term(index, 0, half).astype(BF)
            self.hop(index, 0, half, True).start()
        for stage in range(1, self.AHEAD + 1):
            for group in range(len(self.groups)):
                self.fetch(stage, group)

    def chip_term(self, index, stage, half):
        self.own(index, stage, half).wait()
        self.given(index, stage, half).wait_recv()
        return self.mine[index][stage, half].astype(F32) + self.taken[index][stage, half].astype(F32)

    def stage(self, stage, group):
        last = self.chips - 1

        @pl.when(stage < last)
        def _():
            for index, half in self.each(group):
                self.hop(index, stage - 1, half, True).wait_recv()
                came = self.inbox[index][stage - 1, half].astype(F32)
                self.inbox[index][stage - 1, half] = (came + self.chip_term(index, stage, half)).astype(BF)
                self.hop(index, stage, half, False).start()

        @pl.when(stage + self.AHEAD < self.chips)
        def _():
            self.fetch(stage + self.AHEAD, group)

        @pl.when(stage == last)
        def _():
            for index, half in self.each(group):
                self.hop(index, last - 1, half, True).wait_recv()
                came = self.inbox[index][last - 1, half].astype(F32)
                size = came.shape[0]
                total = came + self.chip_term(index, last, half)
                goal, column = self.goals[index]
                width = min(goal.shape[1] - column, total.shape[1])
                goal[half * size : (half + 1) * size, column : column + width] = total[:, :width]

    def run(self, first, stop):
        count = len(self.groups)

        def one(event, carry):
            for group in range(count):
                if count == 1:
                    self.stage(event + 1, 0)
                else:
                    pl.when(lax.rem(event, count) == group)(functools.partial(self.stage, event // count + 1, group))
            return carry

        lax.fori_loop(first, stop, one, 0)

    def pace(self, step, costs):
        whole = sum(steps * each for steps, each in costs)

        def done(at):
            spent, before = 0, 0
            for steps, each in costs:
                spent = spent + jnp.minimum(jnp.maximum(at - before, 0), steps) * each
                before += steps
            return spent * self.events // whole

        self.run(done(step), done(step + 1))

    def finish(self):
        for index, half in self.each():
            self.hop(index, 0, half, True).wait_send()

        def sent(stage, carry):
            for index, half in self.each():
                self.hop(index, stage, half, False).wait_send()
            return carry

        lax.fori_loop(1, self.chips - 1, sent, 0)

        def gave(stage, carry):
            for index, half in self.each():
                self.given(index, stage, half).wait_send()
            return carry

        lax.fori_loop(0, self.chips, gave, 0)


def dot_nn(a, b):
    return jnp.dot(a, b, preferred_element_type=F32)


def dot_nt(a, b):
    return lax.dot_general(a, b, (((1,), (1,)), ((), ())), preferred_element_type=F32)


def turned(block, cosine, sine, back):
    other = pltpu.roll(block, E // 2, 1)
    if back:
        return block * cosine - other * sine
    return block * cosine + other * sine


def project(x, w, cosine, sine, own, heads):
    m, k = x.shape
    per = TILE // E
    some = heads // per

    def kernel(x_ref, w_ref, c_ref, s_ref, q_ref, kv_ref):
        step = pl.program_id(0)

        def rotate_to(ref, made, rows):
            for part in range(per):
                piece = slice(part * E, (part + 1) * E)
                ref[:, piece] = turned(made[:, piece], c_ref[rows, :], s_ref[rows, :], False).astype(BF)

        @pl.when(step < some)
        def _():
            rows = slice(m - own, m)
            rotate_to(q_ref, dot_nn(x_ref[rows, :], w_ref[...]), rows)

        @pl.when((step >= some) & (step < 2 * some))
        def _():
            rotate_to(kv_ref, dot_nn(x_ref[...], w_ref[...]), slice(0, m))

        @pl.when(step >= 2 * some)
        def _():
            kv_ref[...] = dot_nn(x_ref[...], w_ref[...]).astype(BF)

    return pl.pallas_call(
        kernel,
        grid=(3 * some,),
        out_shape=[jax.ShapeDtypeStruct((own, heads * E), BF), jax.ShapeDtypeStruct((m, 2 * heads * E), BF)],
        in_specs=[single((m, k)), pl.BlockSpec((k, TILE), lambda i: (0, i)), single((m, E)), single((m, E))],
        out_specs=[
            pl.BlockSpec((own, TILE), lambda i: (0, jnp.minimum(i, some - 1))),
            pl.BlockSpec((m, TILE), lambda i: (0, jnp.maximum(i - some, 0))),
        ],
        compiler_params=pltpu.CompilerParams(vmem_limit_bytes=VMEM),
        cost_estimate=cost(2 * (own + 2 * m) * k * heads * E, 2 * (m * k + 3 * (m + k) * heads * E)),
        name="project",
    )(x, w, cosine, sine)


def attend(query, kv, places, heads):
    m = query.shape[0]
    blocks = m // QB
    factor = E ** (-0.5) * LOG2E

    def kernel(q_ref, k_ref, v_ref, p_ref, o_ref, probs_ref, bias):
        @pl.when(pl.program_id(0) == 0)
        def _():
            for block in range(blocks):
                key = lax.broadcasted_iota(jnp.int32, (KB, QB), 0) + block * QB
                query = lax.broadcasted_iota(jnp.int32, (KB, QB), 1) + block * QB
                place = p_ref[:, block * QB : (block + 1) * QB]
                allowed = (key <= query + WINDOW) & (key > query) & (key >= query + WINDOW - place)
                bias[block] = jnp.where(allowed, 0.0, -1e30)

        values_t = v_ref[...].T
        for block in range(blocks):
            span = slice(block * QB, block * QB + KB)
            scores = dot_nt(k_ref[span, :], q_ref[block * QB : (block + 1) * QB, :]) * factor + bias[block]
            largest = jnp.max(scores, axis=0, keepdims=True)
            grown = jnp.exp2(scores - largest)
            inverse = 1.0 / jnp.sum(grown, axis=0, keepdims=True)
            probs = (grown * inverse).astype(BF)
            probs_ref[0, block] = probs
            mixed_t = dot_nn(values_t[:, span], probs)
            o_ref[block * QB : (block + 1) * QB, :] = mixed_t.T.astype(BF)

    head = pl.BlockSpec((m, E), lambda i: (0, i))
    reach = kv.shape[0]

    return pl.pallas_call(
        kernel,
        grid=(heads,),
        out_shape=[
            jax.ShapeDtypeStruct((m, heads * E), BF),
            jax.ShapeDtypeStruct((heads, blocks, KB, QB), BF),
        ],
        in_specs=[
            head,
            pl.BlockSpec((reach, E), lambda i: (0, i)),
            pl.BlockSpec((reach, E), lambda i: (0, i + heads)),
            whole_spec((1, m)),
        ],
        out_specs=[head, pl.BlockSpec((1, blocks, KB, QB), lambda i: (i, 0, 0, 0))],
        scratch_shapes=[pltpu.VMEM((blocks, KB, QB), F32)],
        compiler_params=pltpu.CompilerParams(vmem_limit_bytes=VMEM),
        cost_estimate=cost(4 * heads * m * KB * E * 2, 2 * heads * m * KB, heads * m * KB),
        name="attend",
    )(query, kv, kv, places)


def attend_back(query, kv, probs, mixed, w_attn, hidden, gain, d_normed, d_normed_other, cotangent, cosine, sine, flip, ring_source, heads, out_width, identity):
    m, width = hidden.shape
    firsts = m // ROWS
    devices, rows, ring_width = ring_source.shape[1:]
    blocks = m // QB
    factor = E ** (-0.5)
    reach = WINDOW + m
    columns = heads * E

    def kernel(q_ref, k_ref, v_ref, p_ref, x_ref, w_ref, h_ref, gain_ref, dn_ref, do_ref, y_ref, c_ref, s_ref, flip_ref, source, d_ref, out_ref, sum_ref, flipped_ref, dh_ref, gain_out, g_ref, gt_ref, keys_sum, values_sum, near_out, near_in, far_out, far_in, kept, near_send, near_recv, far_send, far_recv, *scratch):
        step = pl.program_id(0)
        half = ring_width // 2
        ring = Ring(devices, [(source.at[0], 0, half), (source.at[0], half, half)], [(sum_ref, 0), (sum_ref, half)], [[0], [1]], scratch)
        me, side, core = ring.me, ring.side, ring.core

        @pl.when(step == 0)
        def _():
            ring.barrier(((lax.rem(me + 2, devices), side), (lax.rem(me + devices - 2, devices), side)))
            ring.begin()

        def near_copy(which):
            return pltpu.make_async_remote_copy(
                src_ref=near_out.at[which], dst_ref=near_in.at[which], send_sem=near_send.at[which], recv_sem=near_recv.at[which],
                device_id=(ring.partner, side), device_id_type=MESH,
            )

        def far_copy(which):
            return pltpu.make_async_remote_copy(
                src_ref=far_out.at[which], dst_ref=far_in.at[which], send_sem=far_send.at[which], recv_sem=far_recv.at[which],
                device_id=(lax.rem(me + devices - 2, devices), side), device_id_type=MESH,
            )

        turns = [(firsts + 2 * heads, 1)]

        @pl.when(step < firsts)
        def _():
            change, gain_part = norm_grad(h_ref[...], gain_ref[...], dn_ref[...].astype(F32) + do_ref[...].astype(F32))
            total = y_ref[...].astype(F32) + change
            low = total.astype(BF)
            dh_ref[...] = total
            here = pl.ds(pl.multiple_of(step * ROWS, ROWS), ROWS)
            g_ref[here, :] = low
            gt_ref[:, here] = low.T

            @pl.when(step == 0)
            def _():
                gain_out[...] = gain_part

            @pl.when(step > 0)
            def _():
                gain_out[...] += gain_part

            ring.pace(step, turns)

        @pl.when(step >= firsts)
        def _():
            head = step - firsts
            grad_all = dot_nn(g_ref[...], w_ref[...]).astype(BF)
            out_ref[...] = dot_nn(gt_ref[...], x_ref[...]).astype(BF)
            keys_t = k_ref[...].T
            keys_sum[...] = jnp.zeros_like(keys_sum)
            values_sum[...] = jnp.zeros_like(values_sum)
            for block in range(blocks):
                span = slice(block * QB, block * QB + KB)
                here = slice(block * QB, (block + 1) * QB)
                low = p_ref[0, block]
                grad = grad_all[here, :]
                d_probs = dot_nt(v_ref[span, :], grad)
                weighted = low.astype(F32) * d_probs
                total = jnp.sum(weighted, axis=0, keepdims=True)
                d_scores = (weighted - low.astype(F32) * total).astype(BF)
                values_sum[span, :] += dot_nn(low, grad)
                keys_sum[span, :] += dot_nn(d_scores, q_ref[here, :])
                d_query = dot_nn(keys_t[:, span], d_scores).T * factor
                d_ref[here, pl.ds(pl.multiple_of(head * E, E), E)] = turned(d_query, c_ref[here, :], s_ref[here, :], True).astype(BF)
                if block == 0:
                    ring.pace(firsts + 2 * head, turns)
            for which, (total, scale) in enumerate(((keys_sum, factor), (values_sum, 1.0))):
                far_out[head, which] = (total[:m, :] * scale).astype(BF)
                near_out[head, which] = (total[m : 2 * m, :] * scale).astype(BF)
                kept[head, which] = total[2 * m :, :] * scale
            near_copy(head).start()

            def settle(which):
                near_copy(which).wait_recv()
                came = near_in[which].astype(F32)
                share = core.astype(F32)
                far_out[which] = (far_out[which].astype(F32) + came * share).astype(BF)
                kept[which] = kept[which] + came * (1.0 - share)

                @pl.when(me >= 2)
                def _():
                    far_copy(which).start()

            def close(which):
                @pl.when(me < devices - 2)
                def _():
                    far_copy(which).wait_recv()
                    kept[which] = kept[which] + far_in[which].astype(F32)

                d_key = turned(kept[which, 0], c_ref[...], s_ref[...], True).astype(BF)
                d_ref[:, pl.ds(pl.multiple_of((heads + which) * E, E), E)] = d_key
                d_ref[:, pl.ds(pl.multiple_of((2 * heads + which) * E, E), E)] = kept[which, 1].astype(BF)
                near_copy(which).wait_send()

                @pl.when(me >= 2)
                def _():
                    far_copy(which).wait_send()

            @pl.when(head > 0)
            def _():
                settle(head - 1)

            @pl.when(head == heads - 1)
            def _():
                settle(head)

            ring.pace(firsts + 2 * head + 1, turns)

            @pl.when(head == 1)
            def _():
                flipped_ref[...] = flip_ref[...].T[: flipped_ref.shape[0]]

            @pl.when(head == heads - 1)
            def _():
                def one(which, carry):
                    close(which)
                    return carry

                lax.fori_loop(0, heads, one, 0)
                ring.finish()

    def at(i):
        return jnp.maximum(i - firsts, 0)

    head_spec = pl.BlockSpec((m, E), lambda i: (0, at(i)))
    rows_spec = pl.BlockSpec((ROWS, width), lambda i: (jnp.minimum(i, firsts - 1), 0))
    dma = pltpu.SemaphoreType.DMA
    pieces = (heads, 2, m, E)
    return pl.pallas_call(
        kernel,
        grid=(firsts + heads,),
        out_shape=[
            jax.ShapeDtypeStruct((m, 3 * columns), BF),
            jax.ShapeDtypeStruct((width, columns), BF),
            jax.ShapeDtypeStruct((rows, out_width), F32),
            jax.ShapeDtypeStruct((out_width, rows), F32),
            jax.ShapeDtypeStruct((m, width), F32),
            jax.ShapeDtypeStruct((1, width), F32),
        ],
        in_specs=[
            head_spec,
            pl.BlockSpec((reach, E), lambda i: (0, at(i))),
            pl.BlockSpec((reach, E), lambda i: (0, at(i) + heads)),
            pl.BlockSpec((1, blocks, KB, QB), lambda i: (at(i), 0, 0, 0)),
            head_spec,
            pl.BlockSpec((width, E), lambda i: (0, at(i) + 3 * heads)),
            rows_spec,
            single((1, width)),
            rows_spec,
            rows_spec,
            rows_spec,
            single((m, E)),
            single((m, E)),
            single(flip.shape),
            pl.BlockSpec(memory_space=pl.ANY),
        ],
        out_specs=[
            single((m, 3 * columns)),
            pl.BlockSpec((width, E), lambda i: (0, at(i))),
            single((rows, out_width)),
            single((out_width, rows)),
            rows_spec,
            single((1, width)),
        ],
        scratch_shapes=[
            pltpu.VMEM((m, width), BF), pltpu.VMEM((width, m), BF),
            pltpu.VMEM((reach, E), F32), pltpu.VMEM((reach, E), F32),
            pltpu.VMEM(pieces, BF), pltpu.VMEM(pieces, BF), pltpu.VMEM(pieces, BF), pltpu.VMEM(pieces, BF), pltpu.VMEM(pieces, F32),
            dma((heads,)), dma((heads,)), dma((heads,)), dma((heads,)),
            *Ring.scratch(devices, [(rows, ring_width // 2)] * 2),
        ],
        compiler_params=pltpu.CompilerParams(vmem_limit_bytes=VMEM, collective_id=identity, has_side_effects=True),
        cost_estimate=cost(8 * heads * m * KB * E * 2, 2 * heads * m * KB),
        name="attend_back",
    )(query, kv, kv, probs, mixed, w_attn, hidden, gain, d_normed, d_normed_other, cotangent, cosine, sine, flip, ring_source)


def back_pass(x_t, d_out, weights, ring_sources, out_widths, costs, identity, name):
    amount, m, columns = d_out.shape
    width = x_t.shape[0]
    devices = lax.axis_size("dp")
    sides = lax.axis_size("tensor")
    tiles = width // TILE
    per = columns // TILE
    total = tiles + amount * per
    count = len(ring_sources)
    shapes = [(source.shape[-2], source.shape[-1] // pieces) for source, _, pieces in ring_sources for _ in range(pieces)]
    groups = [[index] for index in range(len(shapes))]

    def kernel(*refs):
        refs = list(refs)

        def take(number):
            taken = refs[:number]
            del refs[:number]
            return taken

        xt_ref, tile_ref, d_ref = take(3)
        w_refs = [take(amount) for _ in weights]
        sources = [ref if lead is None else ref.at[lead] for ref, (_, lead, _) in zip(take(count), ring_sources)]
        grad_ref, back_ref = take(2)
        sums = take(count)
        sent, got, y_send, y_recv = take(4)
        terms, goals = [], []
        for source, goal, (array, _, pieces) in zip(sources, sums, ring_sources):
            piece = array.shape[-1] // pieces
            terms += [(source, number * piece, piece) for number in range(pieces)]
            goals += [(goal, number * piece) for number in range(pieces)]
        ring = Ring(devices, terms, goals, groups, refs)
        other = (ring.me, lax.rem(ring.side + 1, sides))
        step = pl.program_id(0)

        def across(which):
            return pltpu.make_async_remote_copy(
                src_ref=sent.at[which], dst_ref=got.at[which], send_sem=y_send.at[which], recv_sem=y_recv.at[which],
                device_id=other, device_id_type=MESH,
            )

        @pl.when(step == 0)
        def _():
            ring.barrier((other,))
            ring.begin()

        @pl.when(step < tiles)
        def _():
            part = None
            for index in range(amount):
                column = 0
                for (_, several), blocks in zip(weights, w_refs):
                    made = dot_nt(d_ref[index, :, column : column + several], blocks[index][...])
                    part = made if part is None else part + made
                    column += several
            sent[step] = part.astype(BF)
            across(step).start()

        @pl.when(step >= tiles)
        def _():
            grad_ref[0] = dot_nn(xt_ref[...], tile_ref[0]).astype(BF)

        ring.pace(step, [(tiles, costs[0]), (amount * per, costs[1])])

        @pl.when(step == total - 1)
        def _():
            for which in range(tiles):
                across(which).wait()
                back_ref[:, which * TILE : (which + 1) * TILE] = sent[which].astype(F32) + got[which].astype(F32)
            ring.finish()

    def late(i):
        return jnp.maximum(i - tiles, 0)

    def early(i):
        return jnp.minimum(i, tiles - 1)

    specs = [
        single((width, m)),
        pl.BlockSpec((1, m, TILE), lambda i: (late(i) // per, 0, late(i) % per)),
        single((amount, m, columns)),
    ]
    operands = [x_t, d_out, d_out]
    for array, several in weights:
        for index in range(amount):
            specs.append(pl.BlockSpec((TILE, several), functools.partial(lambda where, i: (early(i), where), index)))
            operands.append(array)
    out_specs = [pl.BlockSpec((1, width, TILE), lambda i: (late(i) // per, 0, late(i) % per)), single((m, width))]
    out_shape = [jax.ShapeDtypeStruct((amount, width, columns), BF), jax.ShapeDtypeStruct((m, width), F32)]
    specs += [pl.BlockSpec(memory_space=pl.ANY)] * count
    operands += [source for source, _, _ in ring_sources]
    for (source, _, _), out_width in zip(ring_sources, out_widths):
        rows = source.shape[-2]
        out_specs.append(single((rows, out_width)))
        out_shape.append(jax.ShapeDtypeStruct((rows, out_width), F32))
    dma = pltpu.SemaphoreType.DMA
    return pl.pallas_call(
        kernel,
        grid=(total,),
        out_shape=out_shape,
        in_specs=specs,
        out_specs=out_specs,
        scratch_shapes=[
            pltpu.VMEM((tiles, m, TILE), BF),
            pltpu.VMEM((tiles, m, TILE), BF),
            dma((tiles,)),
            dma((tiles,)),
            *Ring.scratch(devices, shapes),
        ],
        compiler_params=pltpu.CompilerParams(vmem_limit_bytes=VMEM, collective_id=identity, has_side_effects=True),
        cost_estimate=cost(4 * m * width * amount * columns, 6 * width * amount * columns),
        name=name,
    )(*operands)


def root_of(rows):
    return lax.rsqrt(jnp.mean(rows * rows, axis=-1, keepdims=True) + EPS)


def norm_grad(rows, gain, grad):
    root = root_of(rows)
    pushed = grad * gain
    inner = jnp.mean(pushed * rows, axis=-1, keepdims=True)
    return root * pushed - rows * (root * root * root * inner), jnp.sum(grad * rows * root, axis=0, keepdims=True)


def first_norm(far, near, tokens, gain):
    m, width = tokens.shape
    steps = m // ROWS

    def kernel(far_ref, near_ref, x_ref, g_ref, o_ref, t_ref):
        step = pl.program_id(0)
        me = lax.axis_index("dp")

        def normed(ref):
            rows = ref[...].astype(F32)
            return (rows * root_of(rows) * g_ref[...]).astype(BF)

        def earlier(ref, there):
            @pl.when(there)
            def _():
                o_ref[...] = normed(ref)

            @pl.when(jnp.logical_not(there))
            def _():
                o_ref[...] = jnp.zeros_like(o_ref)

        @pl.when(step < steps)
        def _():
            earlier(far_ref, me >= 2)

        @pl.when((step >= steps) & (step < 2 * steps))
        def _():
            earlier(near_ref, me >= 1)

        @pl.when(step >= 2 * steps)
        def _():
            made = normed(x_ref)
            o_ref[...] = made
            t_ref[...] = made.T

    def part(which):
        return pl.BlockSpec((ROWS, width), lambda i: (jnp.clip(i - which * steps, 0, steps - 1), 0))

    return pl.pallas_call(
        kernel,
        grid=(3 * steps,),
        out_shape=[jax.ShapeDtypeStruct((3 * m, width), BF), jax.ShapeDtypeStruct((width, m), BF)],
        in_specs=[part(0), part(1), part(2), whole_spec((1, width))],
        out_specs=[
            pl.BlockSpec((ROWS, width), lambda i: (i, 0)),
            pl.BlockSpec((width, ROWS), lambda i: (0, jnp.maximum(i - 2 * steps, 0))),
        ],
        compiler_params=pltpu.CompilerParams(vmem_limit_bytes=VMEM),
        cost_estimate=cost(24 * m * width, 14 * m * width),
        name="first_norm",
    )(far, near, tokens, gain)


def out_norm(mixed, w_attn, place, tokens, gain, identity):
    m, columns = mixed.shape
    width = tokens.shape[1]
    steps = m // ROWS
    sides = lax.axis_size("tensor")

    def kernel(x_ref, w_ref, r_ref, g_ref, hidden_ref, normed_ref, turned_ref, sent, got, send, recv):
        step = pl.program_id(0)
        other = (lax.axis_index("dp"), lax.rem(lax.axis_index("tensor") + 1, sides))

        @pl.when(step == 0)
        def _():
            semaphore = pltpu.get_barrier_semaphore()
            pl.semaphore_signal(semaphore, inc=1, device_id=other, device_id_type=MESH)
            pl.semaphore_wait(semaphore, 1)

        def across(which):
            return pltpu.make_async_remote_copy(
                src_ref=sent.at[which], dst_ref=got.at[which], send_sem=send.at[which], recv_sem=recv.at[which],
                device_id=other, device_id_type=MESH,
            )

        @pl.when(step < steps)
        def _():
            sent[step] = dot_nt(x_ref[...], w_ref[...]).astype(BF)
            across(step).start()

        @pl.when(step >= steps)
        def _():
            which = step - steps
            across(which).wait()
            hidden = r_ref[...].astype(F32) + (sent[which].astype(F32) + got[which].astype(F32))
            normed = (hidden * root_of(hidden) * g_ref[...]).astype(BF)
            hidden_ref[...] = hidden
            normed_ref[...] = normed
            turned_ref[...] = normed.T

    def late(i):
        return jnp.maximum(i - steps, 0)

    late_rows = pl.BlockSpec((ROWS, width), lambda i: (late(i), 0))
    dma = pltpu.SemaphoreType.DMA
    return pl.pallas_call(
        kernel,
        grid=(2 * steps,),
        out_shape=[
            jax.ShapeDtypeStruct((m, width), F32),
            jax.ShapeDtypeStruct((m, width), BF),
            jax.ShapeDtypeStruct((width, m), BF),
        ],
        in_specs=[
            pl.BlockSpec((ROWS, columns), lambda i: (jnp.minimum(i, steps - 1), 0)),
            pl.BlockSpec((width, columns), lambda i: (0, place), pipeline_mode=pl.Buffered(1)),
            late_rows,
            single((1, width)),
        ],
        out_specs=[late_rows, late_rows, pl.BlockSpec((width, ROWS), lambda i: (0, late(i)))],
        scratch_shapes=[pltpu.VMEM((steps, ROWS, width), BF), pltpu.VMEM((steps, ROWS, width), BF), dma((steps,)), dma((steps,))],
        compiler_params=pltpu.CompilerParams(vmem_limit_bytes=VMEM, collective_id=identity, has_side_effects=True),
        cost_estimate=cost(2 * m * width * columns, 12 * m * width),
        name="out_norm",
    )(mixed, w_attn, tokens, gain)


def last_pass(tokens, gain, grad, d_hidden, hidden, act_early, act_late, w_ffn, rest, gain_ffn_grad, flip, qkv_part, lanes, identity):
    m, width = tokens.shape
    devices, rows, all_columns = qkv_part.shape
    columns = all_columns // 3
    chips = devices // 2
    size = ROWS // 2
    steps = m // size
    total = steps + chips
    names = 3
    tiles = width // TILE
    some, late = act_early.shape[1], act_late.shape[1]
    sides = lax.axis_size("tensor")
    assert tiles == steps and chips >= tiles

    def kernel(x_ref, g_ref, dn_ref, dh_ref, h_ref, a_ref, al_ref, w_ref, rest_ref, gf_ref, flip_ref, source, grad_ref, layer_ref, flipped_ref, q_ref, k_ref, v_ref, gains_ref, gain_sum, gain_source, sent, got, y_send, y_recv, *scratch):
        step = pl.program_id(0)
        ring = Ring(
            devices, [(source, number * columns, columns) for number in range(names)], [(q_ref, 0), (k_ref, 0), (v_ref, 0)],
            [[0], [1], [2]], scratch[: 3 * names + 5],
        )
        gain_ring = Ring(devices, [(gain_source, 0, lanes)], [(gains_ref, 0)], [[0]], scratch[3 * names + 5 :])
        other = (ring.me, lax.rem(ring.side + 1, sides))

        def across(which):
            return pltpu.make_async_remote_copy(
                src_ref=sent.at[which], dst_ref=got.at[which], send_sem=y_send.at[which], recv_sem=y_recv.at[which],
                device_id=other, device_id_type=MESH,
            )

        @pl.when(step == 0)
        def _():
            ring.barrier((other,))
            ring.begin()

        @pl.when(step < tiles)
        def _():
            sent[step] = (dot_nt(a_ref[...], w_ref[...]) + dot_nt(al_ref[...], rest_ref[...])).astype(BF)
            across(step).start()

        @pl.when(step < steps)
        def _():
            change, gain_part = norm_grad(x_ref[...].astype(F32), g_ref[...], dn_ref[...])
            grad_ref[...] = dh_ref[...] + change

            @pl.when(step == 0)
            def _():
                gain_sum[...] = gain_part
                flipped_ref[...] = flip_ref[...].T

            @pl.when(step > 0)
            def _():
                gain_sum[...] += gain_part

        @pl.when(step == steps - 1)
        def _():
            gain_source[...] = jnp.zeros_like(gain_source)
            for device in range(devices):
                span = slice(device * rows, (device + 1) * rows)
                gain_source[device, :16, :rows] = jnp.broadcast_to(gain_sum[:, span], (16, rows)).astype(BF)
                gain_source[device, 16:, :rows] = jnp.broadcast_to(gf_ref[:, span], (16, rows)).astype(BF)
            gain_ring.begin()

        ring.pace(step, [(steps, 3), (chips, 5)])

        @pl.when(step >= steps)
        def _():
            gain_ring.run(step - steps, jnp.minimum(step - steps + 1, gain_ring.events))

        @pl.when((step >= steps) & (step < steps + tiles))
        def _():
            which = step - steps
            across(which).wait()
            layer_ref[...] = (h_ref[...] + (sent[which].astype(F32) + got[which].astype(F32))).astype(BF)

        @pl.when(step == total - 1)
        def _():
            ring.finish()
            gain_ring.finish()

    def early(i):
        return jnp.minimum(i, steps - 1)

    rows_spec = pl.BlockSpec((size, width), lambda i: (early(i), 0))
    tile_spec = pl.BlockSpec((m, TILE), lambda i: (0, jnp.clip(i - steps, 0, tiles - 1)))
    dma = pltpu.SemaphoreType.DMA
    sums = jax.ShapeDtypeStruct((rows, columns), F32)
    return pl.pallas_call(
        kernel,
        grid=(total,),
        out_shape=[
            jax.ShapeDtypeStruct((m, width), F32),
            jax.ShapeDtypeStruct((m, width), BF),
            jax.ShapeDtypeStruct((flip.shape[1], flip.shape[0]), F32),
            sums, sums, sums,
            jax.ShapeDtypeStruct((32, lanes), F32),
        ],
        in_specs=[
            rows_spec, single((1, width)), rows_spec, rows_spec, tile_spec, single((m, some)), single((m, late)),
            pl.BlockSpec((TILE, some), lambda i: (early(i), 2)), pl.BlockSpec((TILE, late), lambda i: (early(i), 2)), single((1, width)),
            single(flip.shape), pl.BlockSpec(memory_space=pl.ANY),
        ],
        out_specs=[
            rows_spec, tile_spec, single((flip.shape[1], flip.shape[0])),
            single(sums.shape), single(sums.shape), single(sums.shape), single((32, lanes)),
        ],
        scratch_shapes=[
            pltpu.VMEM((1, width), F32),
            pltpu.VMEM((devices, 32, lanes), BF),
            pltpu.VMEM((tiles, m, TILE), BF),
            pltpu.VMEM((tiles, m, TILE), BF),
            dma((tiles,)),
            dma((tiles,)),
            *Ring.scratch(devices, [(rows, columns)] * names),
            *Ring.scratch(devices, [(32, lanes)]),
        ],
        compiler_params=pltpu.CompilerParams(vmem_limit_bytes=VMEM, collective_id=identity, has_side_effects=True),
        cost_estimate=cost(20 * m * width, 24 * m * width),
        name="last_pass",
    )(tokens, gain, grad, d_hidden, hidden, act_early, act_late, w_ffn, rest, gain_ffn_grad, flip, qkv_part)


def feed_tile(x_ref, dy_ref, dyt_ref, g_ref, u_ref, d_ref, act_ref, both_ref, down_ref):
    gate = dot_nn(x_ref[...], g_ref[...])
    up = dot_nn(x_ref[...], u_ref[...])
    d_act = dot_nn(dy_ref[...], d_ref[...])
    soft = 1.0 / (1.0 + jnp.exp(-gate))
    silu = gate * soft
    act = (silu * up).astype(BF)
    act_ref[...] = act
    both_ref[0] = (d_act * up * (soft * (1.0 + gate * (1.0 - soft)))).astype(BF)
    both_ref[1] = (d_act * silu).astype(BF)
    down_ref[...] = dot_nn(dyt_ref[...], act).astype(BF)


def feed(x, dy, dy_t, w, block, tiles, identity):
    m, k = x.shape
    early = tiles - LATE
    devices = lax.axis_size("dp")
    width = block.shape[1] // 2

    def kernel(x_ref, dy_ref, dyt_ref, g_ref, u_ref, d_ref, block_ref, act_ref, both_ref, down_ref, rest_ref, *scratch):
        step = pl.program_id(0)
        spread = Spread(devices, [(block_ref, rest_ref, 0, width), (block_ref, rest_ref, width, width)], scratch)

        @pl.when(step == 0)
        def _():
            spread.barrier()
            spread.begin()

        feed_tile(x_ref, dy_ref, dyt_ref, g_ref, u_ref, d_ref, act_ref, both_ref, down_ref)
        spread.pace(step, early)

        @pl.when(step == early - 1)
        def _():
            spread.finish()

    any_space = pl.BlockSpec(memory_space=pl.ANY)
    return pl.pallas_call(
        kernel,
        grid=(early,),
        out_shape=[
            jax.ShapeDtypeStruct((m, early * TILE), BF),
            jax.ShapeDtypeStruct((2, m, early * TILE), BF),
            jax.ShapeDtypeStruct((k, early * TILE), BF),
            jax.ShapeDtypeStruct((k, block.shape[1]), BF),
        ],
        in_specs=[
            single((m, k)),
            single((m, k)),
            single((k, m)),
            pl.BlockSpec((k, TILE), lambda i: (0, i)),
            pl.BlockSpec((k, TILE), lambda i: (0, i + early)),
            pl.BlockSpec((k, TILE), lambda i: (0, i + 2 * early)),
            any_space,
        ],
        out_specs=[
            pl.BlockSpec((m, TILE), lambda i: (0, i)),
            pl.BlockSpec((2, m, TILE), lambda i: (0, 0, i)),
            pl.BlockSpec((k, TILE), lambda i: (0, i)),
            any_space,
        ],
        scratch_shapes=Spread.scratch(devices, 2),
        compiler_params=pltpu.CompilerParams(vmem_limit_bytes=VMEM, collective_id=identity, has_side_effects=True),
        cost_estimate=cost(8 * m * k * early * TILE, 8 * (m + k) * early * TILE, m * early * TILE),
        name="feed",
    )(x, dy, dy_t, w, w, w, block)


def ffn_back(x, x_t, dy, dy_t, d_early, w_ffn, rest, down_early, identity):
    m, width = x.shape
    devices, rows, some = down_early.shape
    late = LATE * TILE
    padded = some + late
    early_tiles = some // TILE
    tiles = width // TILE
    grads = 2 * (early_tiles + LATE)
    total = LATE + tiles + grads
    sides = lax.axis_size("tensor")
    pieces = [(rows, some // 2)] * 2

    def kernel(x_ref, xt_ref, dy_ref, dyt_ref, rg_ref, ru_ref, rd_ref, d_ref, tile_ref, wg_ref, wu_ref, lg_ref, lu_ref, source, act_ref, grad_ref, sent_ref, got, sum_ref, d_late, down_late, down_tile, both_tile, sent, y_send, y_recv, *scratch):
        step = pl.program_id(0)
        ring = Ring(devices, [(source, 0, some // 2), (source, some // 2, some // 2)], [(sum_ref, 0), (sum_ref, some // 2)], [[0], [1]], scratch[:11])
        late_ring = Ring(devices, [(down_late, 0, late)], [(sum_ref, some)], [[0]], scratch[11:])
        other = (ring.me, lax.rem(ring.side + 1, sides))

        def across(which):
            return pltpu.make_async_remote_copy(
                src_ref=sent.at[which], dst_ref=got.at[:, pl.ds(pl.multiple_of(which * TILE, TILE), TILE)],
                send_sem=y_send.at[which], recv_sem=y_recv.at[which], device_id=other, device_id_type=MESH,
            )

        @pl.when(step == 0)
        def _():
            ring.barrier((other,))
            ring.begin()

        @pl.when(step < LATE)
        def _():
            feed_tile(x_ref, dy_ref, dyt_ref, rg_ref, ru_ref, rd_ref, act_ref, both_tile, down_tile)
            here = pl.ds(pl.multiple_of(step * TILE, TILE), TILE)
            d_late[:, :, here] = both_tile[...]
            down_late[:, :, here] = down_tile[...].reshape(devices, rows, TILE)

        @pl.when(step == LATE - 1)
        def _():
            late_ring.begin()

        @pl.when((step >= LATE) & (step < LATE + tiles))
        def _():
            which = step - LATE
            part = dot_nt(d_ref[0], wg_ref[...]) + dot_nt(d_ref[1], wu_ref[...])
            part += dot_nt(d_late[0], lg_ref[...]) + dot_nt(d_late[1], lu_ref[...])
            low = part.astype(BF)
            sent[which] = low
            sent_ref[...] = low
            across(which).start()

        @pl.when((step >= LATE + tiles) & (step < LATE + tiles + 2 * early_tiles))
        def _():
            grad_ref[0] = dot_nn(xt_ref[...], tile_ref[0]).astype(BF)

        @pl.when(step >= LATE + tiles + 2 * early_tiles)
        def _():
            number = step - (LATE + tiles + 2 * early_tiles)
            here = pl.ds(pl.multiple_of(lax.rem(number, LATE) * TILE, TILE), TILE)
            grad_ref[0] = dot_nn(xt_ref[...], d_late[number // LATE, :, here]).astype(BF)

        ring.pace(step, [(LATE, 12), (tiles, 8), (grads, 4)])
        late_ring.pace(step, [(LATE, 0), (tiles, 8), (grads, 4)])

        @pl.when(step == total - 1)
        def _():
            for which in range(tiles):
                across(which).wait()
            ring.finish()
            late_ring.finish()

    def first(i):
        return jnp.minimum(i, LATE - 1)

    def second(i):
        return jnp.clip(i - LATE, 0, tiles - 1)

    def third(i):
        at = jnp.clip(i - LATE - tiles, 0, 2 * early_tiles - 1)
        return (at // early_tiles, 0, at % early_tiles)

    def grad_at(i):
        at = jnp.maximum(i - LATE - tiles, 0)
        more = jnp.maximum(at - 2 * early_tiles, 0)
        is_late = at // (2 * early_tiles)
        return (
            (1 - is_late) * (at // early_tiles) + is_late * (more // LATE),
            0,
            (1 - is_late) * (at % early_tiles) + is_late * (early_tiles + more % LATE),
        )

    assert LATE <= early_tiles
    any_space = pl.BlockSpec(memory_space=pl.ANY)
    dma = pltpu.SemaphoreType.DMA

    def rest_tile(which):
        return pl.BlockSpec((width, TILE), lambda i: (0, first(i) + which * LATE))

    return pl.pallas_call(
        kernel,
        grid=(total,),
        out_shape=[
            jax.ShapeDtypeStruct((m, late), BF),
            jax.ShapeDtypeStruct((2, width, padded), BF),
            jax.ShapeDtypeStruct((m, width), BF),
            jax.ShapeDtypeStruct((m, width), BF),
            jax.ShapeDtypeStruct((rows, padded), F32),
        ],
        in_specs=[
            single((m, width)), single((width, m)), single((m, width)), single((width, m)),
            rest_tile(0), rest_tile(1), rest_tile(2),
            single((2, m, some)),
            pl.BlockSpec((1, m, TILE), third),
            pl.BlockSpec((TILE, some), lambda i: (second(i), 0)),
            pl.BlockSpec((TILE, some), lambda i: (second(i), 1)),
            pl.BlockSpec((TILE, late), lambda i: (second(i), 0)),
            pl.BlockSpec((TILE, late), lambda i: (second(i), 1)),
            any_space,
        ],
        out_specs=[
            pl.BlockSpec((m, TILE), lambda i: (0, first(i))),
            pl.BlockSpec((1, width, TILE), grad_at),
            pl.BlockSpec((m, TILE), lambda i: (0, second(i))),
            any_space,
            single((rows, padded)),
        ],
        scratch_shapes=[
            pltpu.VMEM((2, m, late), BF),
            pltpu.VMEM((devices, rows, late), BF),
            pltpu.VMEM((width, TILE), BF),
            pltpu.VMEM((2, m, TILE), BF),
            pltpu.VMEM((tiles, m, TILE), BF),
            dma((tiles,)),
            dma((tiles,)),
            *Ring.scratch(devices, pieces),
            *Ring.scratch(devices, [(rows, late)]),
        ],
        compiler_params=pltpu.CompilerParams(vmem_limit_bytes=VMEM, collective_id=identity, has_side_effects=True),
        cost_estimate=cost(8 * m * width * padded + 8 * m * width * late, 10 * width * padded),
        name="ffn_back",
    )(x, x_t, dy, dy_t, rest, rest, rest, d_early, d_early, w_ffn, w_ffn, rest, rest, down_early)


def shards(tokens, positions, attn_gain, w_query, w_key, w_value, w_out, ffn_gain, w_gate, w_up, w_down, cotangent):
    devices = lax.axis_size("dp")
    span = tokens.shape[0]
    assert 2 * span == WINDOW
    own_rows = w_query.shape[0]
    width = tokens.shape[1]
    head_columns = w_query.shape[1]
    heads = head_columns // E
    hidden_units = w_gate.shape[1]
    tiles = (hidden_units + TILE - 1) // TILE
    padded = tiles * TILE

    attn_pack = jnp.concatenate([w_query, w_key, w_value, w_out.T], axis=1)
    lanes = max(128, own_rows)
    gains = jnp.zeros((32, lanes), BF).at[0, :own_rows].set(attn_gain).at[16, :own_rows].set(ffn_gain)
    w_attn, all_gains, near, far = ring_gather((attn_pack, gains), (2, 1), tokens, 0)

    def wide(matrix):
        return jnp.pad(matrix, ((0, 0), (0, padded - hidden_units)))

    ffn_parts = [wide(w_gate), wide(w_up), wide(w_down.T)]
    some = padded - LATE * TILE
    ffn_pack = jnp.concatenate([part[:, :some] for part in ffn_parts], axis=1)
    rest_pack = jnp.concatenate([part[:, some:] for part in ffn_parts], axis=1)
    w_attn, all_gains, ffn_pack = lax.optimization_barrier((w_attn, all_gains, ffn_pack))
    w_ffn = lax.all_gather(ffn_pack, "dp", axis=0, tiled=True)
    all_gains = all_gains.reshape(devices, 32, lanes)
    gain_attn = all_gains[:, 0, :own_rows].reshape(1, width).astype(F32)
    gain_ffn = all_gains[:, 16, :own_rows].reshape(1, width).astype(F32)

    frequency = THETA ** (-(jnp.arange(E // 2, dtype=F32) * 2.0 / E))
    earlier = positions[0] - WINDOW + jnp.arange(WINDOW, dtype=jnp.int32)
    angles = jnp.concatenate([earlier, positions]).astype(F32)[:, None] * frequency[None, :]
    cosine_half, sine_half = jnp.cos(angles), jnp.sin(angles)
    cosine = jnp.concatenate([cosine_half, cosine_half], axis=1)
    sine = jnp.concatenate([-sine_half, sine_half], axis=1)

    normed_attn, normed_attn_t = first_norm(far, near, tokens, gain_attn)
    query, kv = project(normed_attn, w_attn, cosine, sine, span, heads)
    mixed, probs = attend(query, kv, positions[None, :], heads)
    cosine, sine = cosine[WINDOW:], sine[WINDOW:]
    hidden, normed_ffn, normed_ffn_t = out_norm(mixed, w_attn, 3, tokens, gain_ffn, 5)

    cotangent_t = cotangent.T
    act_early, d_early, down_early, rest = feed(normed_ffn, cotangent, cotangent_t, w_ffn, rest_pack, tiles, 6)
    act_late, both_part, d_normed_ffn, d_normed_other, down_grad = ffn_back(
        normed_ffn, normed_ffn_t, cotangent, cotangent_t, d_early, w_ffn, rest, down_early.reshape(devices, own_rows, some), 1
    )
    both_part = both_part.reshape(2, devices, own_rows, padded)

    d_qkv, out_part, gate_grad, w_down_grad, d_hidden, gain_ffn_grad = attend_back(
        query, kv, probs, mixed, w_attn, hidden, gain_ffn, d_normed_ffn, d_normed_other, cotangent, cosine, sine, down_grad, both_part, heads, hidden_units, 2
    )
    qkv_part, d_normed_attn, up_grad, out_grad = back_pass(
        normed_attn_t, d_qkv[None], [(w_attn, 3 * head_columns)],
        [(both_part, 1, 2), (out_part.reshape(devices, own_rows, head_columns), None, 1)], [hidden_units, head_columns], (4, 3), 3, "qkv_back",
    )
    tokens_grad, layer_out, w_out_grad, query_grad, key_grad, value_grad, gain_grads = last_pass(
        tokens, gain_attn, d_normed_attn, d_hidden, hidden, act_early, act_late, w_ffn, rest, gain_ffn_grad, out_grad,
        qkv_part.reshape(devices, own_rows, 3 * head_columns), lanes, 4,
    )
    return (
        layer_out,
        tokens_grad,
        gain_grads[0, :own_rows],
        query_grad,
        key_grad,
        value_grad,
        w_out_grad,
        gain_grads[16, :own_rows],
        gate_grad,
        up_grad,
        w_down_grad,
    )


def solution(mesh):
    by_rows, by_both, turned_both, line = P("dp", None), P("dp", "tensor"), P("tensor", "dp"), P("dp")
    return jax.shard_map(
        shards,
        mesh=mesh,
        in_specs=(by_rows, line, line, by_both, by_both, by_both, turned_both, line, by_both, by_both, turned_both, by_rows),
        out_specs=(by_rows, by_rows, line, by_both, by_both, by_both, turned_both, line, by_both, by_both, turned_both),
        check_vma=False,
    )
```

```python
import functools

import jax
import jax.numpy as jnp
from jax import lax
from jax.experimental import pallas as pl
from jax.experimental.pallas import tpu as pltpu
from jax.sharding import PartitionSpec as P

E = 128
WINDOW = 1024
EPS = 1e-06
THETA = 10000.0
LOG2E = 1.4426950408889634
MESH = pl.DeviceIdType.MESH
BF = jnp.bfloat16
F32 = jnp.float32
QB = 256
KB = WINDOW + QB
TILE = 256
ROWS = 128
LATE = 3
VMEM = 59 * 1024 * 1024


def whole_spec(shape):
    return pl.BlockSpec(shape, lambda i: (0,) * len(shape))


def single(shape):
    return pl.BlockSpec(shape, lambda i: (0,) * len(shape), pipeline_mode=pl.Buffered(1))


def loads(sources, targets, semaphores):
    return [pltpu.make_async_copy(s, t, semaphores.at[i]) for i, (s, t) in enumerate(zip(sources, targets))]


def cost(flops, nbytes, special=0):
    return pl.CostEstimate(flops=flops, bytes_accessed=nbytes, transcendentals=special)


def ring_chip(place, chips):
    place = lax.rem(place + 2 * chips, chips)
    late = place // (chips // 2)
    return (1 - late) * 2 * place + late * (2 * (chips - 1 - place) + 1)


def ring_place(chip, chips):
    column = lax.rem(chip, 2)
    row = chip // 2
    return (1 - column) * row + column * (chips - 1 - row)


def gather_kernel(devices, chunks, count, *refs):
    ins, tokens = refs[:count], refs[count]
    outs, near, far = refs[count + 1 : 2 * count + 1], refs[2 * count + 1], refs[2 * count + 2]
    local_sem, a_send, a_recv, b_send, b_recv, c_send, c_recv, far_send, far_recv, near_send, near_recv = refs[2 * count + 3 :]
    chips = devices // 2
    me = lax.axis_index("dp")
    side = lax.axis_index("tensor")
    core = lax.rem(me, 2)
    place = ring_place(me // 2, chips)

    def device(q):
        return ring_chip(q, chips) * 2 + core

    right = device(place + 1)
    left = device(place - 1)
    partner = me + 1 - 2 * core
    across = lax.rem(side + 1, lax.axis_size("tensor"))
    later, before = lax.rem(me + 2, devices), lax.rem(me + devices - 2, devices)
    barrier = pltpu.get_barrier_semaphore()
    for other in ((right, side), (left, side), (partner, side), (me, across), (later, side), (before, side)):
        pl.semaphore_signal(barrier, inc=1, device_id=other, device_id_type=MESH)
    pl.semaphore_wait(barrier, 6)

    pieces = []
    for index, parts in enumerate(chunks):
        width = ins[index].shape[1] // parts
        for part in range(parts):
            pieces.append((index, part * width, width))
    hops = chips - 1

    def view(ref, row, half, piece, rows):
        index, column, width = piece
        start = row * rows + half * (rows // 2)
        if not isinstance(start, int):
            start = pl.multiple_of(start, 16)
        return ref.at[pl.ds(start, rows // 2), pl.ds(column, width)]

    def described(source, target, send, recv, other):
        return pltpu.make_async_remote_copy(
            src_ref=source, dst_ref=target, send_sem=send, recv_sem=recv, device_id=other, device_id_type=MESH
        )

    def remote(source, target, send, recv, other):
        copy = described(source, target, send, recv, (other, side))
        copy.start()
        return copy

    span = tokens.shape[0] // 2

    def half_rows(ref, which):
        return ref.at[pl.ds(pl.multiple_of(which * span, span), span)]

    far_copy = described(half_rows(tokens, side), half_rows(far, side), far_send.at[0], far_recv.at[0], (later, side))
    cross_copy = described(half_rows(far, side), half_rows(far, side), far_send.at[1], far_recv.at[1], (me, across))
    own_near = [described(half_rows(tokens, which), half_rows(near, which), near_send.at[which], near_recv.at[which], (partner, side)) for which in range(2)]
    far_near = [described(half_rows(far, which), half_rows(near, which), near_send.at[slot], near_recv.at[slot], (partner, side)) for slot, which in enumerate((side, across))]

    @pl.when(me < devices - 2)
    def _():
        far_copy.start()

    @pl.when(core == 0)
    def _():
        for copy in own_near:
            copy.start()

    def pass_on(slot):
        @pl.when(me >= 2)
        def _():
            if slot == 0:
                far_copy.wait_recv()
                cross_copy.start()
            else:
                cross_copy.wait_recv()

            @pl.when(core == 1)
            def _():
                far_near[slot].start()

    local = []
    for index in range(count):
        rows = ins[index].shape[0]
        copy = pltpu.make_async_copy(
            ins[index], outs[index].at[pl.ds(pl.multiple_of(me * rows, 16), rows)], local_sem.at[index]
        )
        copy.start()
        local.append(copy)
    forward, partner_copies = {}, []
    for number, piece in enumerate(pieces):
        ref, out = ins[piece[0]], outs[piece[0]]
        rows = ref.shape[0]
        forward[number, 0] = (
            remote(view(ref, 0, 0, piece, rows), view(out, me, 0, piece, rows), a_send.at[number, 0], a_recv.at[number, 0], right),
            remote(view(ref, 0, 1, piece, rows), view(out, me, 1, piece, rows), b_send.at[number, 0], b_recv.at[number, 0], left),
        )
    for number, piece in enumerate(pieces):
        ref, out = ins[piece[0]], outs[piece[0]]
        rows = ref.shape[0]
        for half in range(2):
            partner_copies.append(
                remote(view(ref, 0, half, piece, rows), view(out, me, half, piece, rows), c_send.at[number, 0, half], c_recv.at[number, 0, half], partner)
            )
    for hop in range(hops):
        for number, piece in enumerate(pieces):
            out = outs[piece[0]]
            rows = ins[piece[0]].shape[0]
            came = forward[number, hop]
            sent = []
            for half in range(2):
                came[half].wait_recv()
                owner = device(place - 1 - hop if half == 0 else place + 1 + hop)
                block = view(out, owner, half, piece, rows)
                send, recv = (a_send, a_recv) if half == 0 else (b_send, b_recv)
                if hop < hops - 1:
                    sent.append(
                        remote(block, block, send.at[number, hop + 1], recv.at[number, hop + 1], right if half == 0 else left)
                    )
                partner_copies.append(
                    remote(block, block, c_send.at[number, hop + 1, half], c_recv.at[number, hop + 1, half], partner)
                )
            if sent:
                forward[number, hop + 1] = tuple(sent)
        if hop == hops // 2:
            pass_on(0)
        if hop == hops - 2:
            pass_on(1)
    for copy in local:
        copy.wait()
    for pair in forward.values():
        for copy in pair:
            copy.wait_send()
    for copy in partner_copies:
        copy.wait()

    @pl.when(me < devices - 2)
    def _():
        far_copy.wait_send()

    @pl.when(me >= 2)
    def _():
        cross_copy.wait_send()

        @pl.when(core == 1)
        def _():
            for copy in far_near:
                copy.wait_send()

    @pl.when(core == 0)
    def _():
        for copy in own_near:
            copy.wait_send()

    @pl.when((core == 1) | (me >= 2))
    def _():
        for copy in own_near:
            copy.wait_recv()


def ring_gather(arrays, chunks, tokens, identity):
    devices = lax.axis_size("dp")
    hops = devices // 2 - 1
    pieces = sum(chunks)
    dma = pltpu.SemaphoreType.DMA
    any_space = pl.BlockSpec(memory_space=pl.ANY)
    return pl.pallas_call(
        functools.partial(gather_kernel, devices, chunks, len(arrays)),
        out_shape=[jax.ShapeDtypeStruct((a.shape[0] * devices, a.shape[1]), a.dtype) for a in arrays]
        + [jax.ShapeDtypeStruct(tokens.shape, tokens.dtype)] * 2,
        in_specs=[any_space] * (len(arrays) + 1),
        out_specs=[any_space] * (len(arrays) + 2),
        scratch_shapes=[
            dma((len(arrays),)),
            dma((pieces, hops)),
            dma((pieces, hops)),
            dma((pieces, hops)),
            dma((pieces, hops)),
            dma((pieces, hops + 1, 2)),
            dma((pieces, hops + 1, 2)),
            dma((2,)),
            dma((2,)),
            dma((2,)),
            dma((2,)),
        ],
        compiler_params=pltpu.CompilerParams(collective_id=identity, has_side_effects=True),
        name="ring_gather",
    )(*arrays, tokens)


class Spread:
    def __init__(self, devices, pieces, scratch):
        self.devices, self.chips, self.pieces = devices, devices // 2, pieces
        self.local_sem, self.send_sem, self.recv_sem, self.give_sem, self.take_sem = scratch
        self.me = lax.axis_index("dp")
        self.side = lax.axis_index("tensor")
        self.core = lax.rem(self.me, 2)
        self.place = ring_place(self.me // 2, self.chips)
        self.partner = self.me + 1 - 2 * self.core
        self.next = (
            ring_chip(self.place + 1, self.chips) * 2 + self.core,
            ring_chip(self.place - 1, self.chips) * 2 + self.core,
        )
        self.events = (self.chips - 1) * len(pieces)

    @staticmethod
    def scratch(devices, count):
        dma = pltpu.SemaphoreType.DMA
        chips = devices // 2
        return [dma((count,))] + [dma((count, amount, 2)) for amount in (chips - 1, chips - 1, chips, chips)]

    def barrier(self):
        semaphore = pltpu.get_barrier_semaphore()
        for other in (*self.next, self.partner):
            pl.semaphore_signal(semaphore, inc=1, device_id=(other, self.side), device_id_type=MESH)
        pl.semaphore_wait(semaphore, 3)

    def block(self, index, stage, half):
        source, whole, column, width = self.pieces[index]
        rows = source.shape[0]
        owner = ring_chip(self.place - stage if half == 0 else self.place + stage, self.chips) * 2 + self.core
        return whole.at[pl.ds(pl.multiple_of(owner * rows + half * (rows // 2), 16), rows // 2), pl.ds(column, width)]

    def first(self, index, half):
        source, _, column, width = self.pieces[index]
        rows = source.shape[0]
        return source.at[pl.ds(half * (rows // 2), rows // 2), pl.ds(column, width)]

    def local(self, index):
        source, whole, column, width = self.pieces[index]
        rows = source.shape[0]
        span = pl.ds(pl.multiple_of(self.me * rows, 16), rows)
        return pltpu.make_async_copy(
            source.at[:, pl.ds(column, width)], whole.at[span, pl.ds(column, width)], self.local_sem.at[index]
        )

    def copy(self, index, stage, half, start, across):
        block = self.block(index, stage, half)
        send, recv = (self.give_sem, self.take_sem) if across else (self.send_sem, self.recv_sem)
        return pltpu.make_async_remote_copy(
            src_ref=self.first(index, half) if start else block,
            dst_ref=block,
            send_sem=send.at[index, stage, half],
            recv_sem=recv.at[index, stage, half],
            device_id=(self.partner if across else self.next[half], self.side),
            device_id_type=MESH,
        )

    def each(self):
        return [(index, half) for index in range(len(self.pieces)) for half in range(2)]

    def begin(self):
        for index, half in self.each():
            self.copy(index, 0, half, True, False).start()
        for index, half in self.each():
            self.copy(index, 0, half, True, True).start()
        for index in range(len(self.pieces)):
            self.local(index).start()

    def stage(self, stage, index):
        for half in range(2):
            self.copy(index, stage - 1, half, False, False).wait_recv()

            @pl.when(stage < self.chips - 1)
            def _():
                self.copy(index, stage, half, False, False).start()

            self.copy(index, stage, half, False, True).start()

    def pace(self, step, total):
        count = len(self.pieces)

        def one(event, carry):
            for index in range(count):
                pl.when(lax.rem(event, count) == index)(functools.partial(self.stage, event // count + 1, index))
            return carry

        lax.fori_loop(step * self.events // total, (step + 1) * self.events // total, one, 0)

    def finish(self):
        for index in range(len(self.pieces)):
            self.local(index).wait()
        for index, half in self.each():
            self.copy(index, 0, half, True, False).wait_send()
            self.copy(index, 0, half, True, True).wait()

        def sent(stage, carry):
            for index, half in self.each():
                self.copy(index, stage, half, False, False).wait_send()
            return carry

        lax.fori_loop(1, self.chips - 1, sent, 0)

        def gave(stage, carry):
            for index, half in self.each():
                self.copy(index, stage, half, False, True).wait()
            return carry

        lax.fori_loop(1, self.chips, gave, 0)


class Ring:
    AHEAD = 3

    def __init__(self, devices, terms, goals, groups, scratch):
        self.devices, self.chips = devices, devices // 2
        self.terms, self.goals, self.groups = terms, goals, groups
        count = len(terms)
        self.mine, self.taken, self.inbox = scratch[0 : 3 * count : 3], scratch[1 : 3 * count : 3], scratch[2 : 3 * count : 3]
        self.own_sem, self.give_sem, self.take_sem, self.send_sem, self.recv_sem = scratch[3 * count : 3 * count + 5]
        self.me = lax.axis_index("dp")
        self.side = lax.axis_index("tensor")
        self.core = lax.rem(self.me, 2)
        self.place = ring_place(self.me // 2, self.chips)
        self.partner = self.me + 1 - 2 * self.core
        self.next = (
            ring_chip(self.place + 1, self.chips) * 2 + self.core,
            ring_chip(self.place - 1, self.chips) * 2 + self.core,
        )
        self.events = (self.chips - 1) * len(groups)

    @staticmethod
    def scratch(devices, shapes):
        chips, count = devices // 2, len(shapes)
        dma = pltpu.SemaphoreType.DMA
        buffers = []
        for rows, width in shapes:
            buffers += [pltpu.VMEM((amount, 2, rows // 2, width), BF) for amount in (chips, chips, chips - 1)]
        return buffers + [dma((count, amount, 2)) for amount in (chips, chips, chips, chips - 1, chips - 1)]

    def barrier(self, others=()):
        semaphore = pltpu.get_barrier_semaphore()
        everyone = [(self.next[0], self.side), (self.next[1], self.side), (self.partner, self.side), *others]
        for other in everyone:
            pl.semaphore_signal(semaphore, inc=1, device_id=other, device_id_type=MESH)
        pl.semaphore_wait(semaphore, len(everyone))

    def block(self, index, stage, half, core):
        at = self.place - 1 - stage if half == 0 else self.place + 1 + stage
        size = self.mine[index].shape[2]
        source, column, width = self.terms[index]
        return source.at[ring_chip(at, self.chips) * 2 + core, pl.ds(half * size, size), pl.ds(column, width)]

    def own(self, index, stage, half):
        return pltpu.make_async_copy(
            self.block(index, stage, half, self.core), self.mine[index].at[stage, half], self.own_sem.at[index, stage, half]
        )

    def given(self, index, stage, half):
        return pltpu.make_async_remote_copy(
            src_ref=self.block(index, stage, half, 1 - self.core),
            dst_ref=self.taken[index].at[stage, half],
            send_sem=self.give_sem.at[index, stage, half],
            recv_sem=self.take_sem.at[index, stage, half],
            device_id=(self.partner, self.side),
            device_id_type=MESH,
        )

    def hop(self, index, stage, half, first):
        source = self.mine[index].at[0, half] if first else self.inbox[index].at[stage - 1, half]
        return pltpu.make_async_remote_copy(
            src_ref=source,
            dst_ref=self.inbox[index].at[stage, half],
            send_sem=self.send_sem.at[index, stage, half],
            recv_sem=self.recv_sem.at[index, stage, half],
            device_id=(self.next[half], self.side),
            device_id_type=MESH,
        )

    def each(self, group=None):
        members = range(len(self.terms)) if group is None else self.groups[group]
        return [(index, half) for index in members for half in range(2)]

    def fetch(self, stage, group):
        for index, half in self.each(group):
            self.given(index, stage, half).start()
            self.own(index, stage, half).start()

    def begin(self):
        for group in range(len(self.groups)):
            self.fetch(0, group)
        for index, half in self.each():
            self.mine[index][0, half] = self.chip_term(index, 0, half).astype(BF)
            self.hop(index, 0, half, True).start()
        for stage in range(1, self.AHEAD + 1):
            for group in range(len(self.groups)):
                self.fetch(stage, group)

    def chip_term(self, index, stage, half):
        self.own(index, stage, half).wait()
        self.given(index, stage, half).wait_recv()
        return self.mine[index][stage, half].astype(F32) + self.taken[index][stage, half].astype(F32)

    def stage(self, stage, group):
        last = self.chips - 1

        @pl.when(stage < last)
        def _():
            for index, half in self.each(group):
                self.hop(index, stage - 1, half, True).wait_recv()
                came = self.inbox[index][stage - 1, half].astype(F32)
                self.inbox[index][stage - 1, half] = (came + self.chip_term(index, stage, half)).astype(BF)
                self.hop(index, stage, half, False).start()

        @pl.when(stage + self.AHEAD < self.chips)
        def _():
            self.fetch(stage + self.AHEAD, group)

        @pl.when(stage == last)
        def _():
            for index, half in self.each(group):
                self.hop(index, last - 1, half, True).wait_recv()
                came = self.inbox[index][last - 1, half].astype(F32)
                size = came.shape[0]
                total = came + self.chip_term(index, last, half)
                goal, column = self.goals[index]
                width = min(goal.shape[1] - column, total.shape[1])
                goal[half * size : (half + 1) * size, column : column + width] = total[:, :width]

    def run(self, first, stop):
        count = len(self.groups)

        def one(event, carry):
            for group in range(count):
                if count == 1:
                    self.stage(event + 1, 0)
                else:
                    pl.when(lax.rem(event, count) == group)(functools.partial(self.stage, event // count + 1, group))
            return carry

        lax.fori_loop(first, stop, one, 0)

    def pace(self, step, costs):
        whole = sum(steps * each for steps, each in costs)

        def done(at):
            spent, before = 0, 0
            for steps, each in costs:
                spent = spent + jnp.minimum(jnp.maximum(at - before, 0), steps) * each
                before += steps
            return spent * self.events // whole

        self.run(done(step), done(step + 1))

    def finish(self):
        for index, half in self.each():
            self.hop(index, 0, half, True).wait_send()

        def sent(stage, carry):
            for index, half in self.each():
                self.hop(index, stage, half, False).wait_send()
            return carry

        lax.fori_loop(1, self.chips - 1, sent, 0)

        def gave(stage, carry):
            for index, half in self.each():
                self.given(index, stage, half).wait_send()
            return carry

        lax.fori_loop(0, self.chips, gave, 0)


def dot_nn(a, b):
    return jnp.dot(a, b, preferred_element_type=F32)


def dot_nt(a, b):
    return lax.dot_general(a, b, (((1,), (1,)), ((), ())), preferred_element_type=F32)


def turned(block, cosine, sine, back):
    other = pltpu.roll(block, E // 2, 1)
    if back:
        return block * cosine - other * sine
    return block * cosine + other * sine


def project(x, w, cosine, sine, own, heads):
    m, k = x.shape
    per = TILE // E
    some = heads // per

    def kernel(x_ref, w_ref, c_ref, s_ref, q_ref, kv_ref):
        step = pl.program_id(0)

        def rotate_to(ref, made, rows):
            for part in range(per):
                piece = slice(part * E, (part + 1) * E)
                ref[:, piece] = turned(made[:, piece], c_ref[rows, :], s_ref[rows, :], False).astype(BF)

        @pl.when(step < some)
        def _():
            rows = slice(m - own, m)
            rotate_to(q_ref, dot_nn(x_ref[rows, :], w_ref[...]), rows)

        @pl.when((step >= some) & (step < 2 * some))
        def _():
            rotate_to(kv_ref, dot_nn(x_ref[...], w_ref[...]), slice(0, m))

        @pl.when(step >= 2 * some)
        def _():
            kv_ref[...] = dot_nn(x_ref[...], w_ref[...]).astype(BF)

    return pl.pallas_call(
        kernel,
        grid=(3 * some,),
        out_shape=[jax.ShapeDtypeStruct((own, heads * E), BF), jax.ShapeDtypeStruct((m, 2 * heads * E), BF)],
        in_specs=[single((m, k)), pl.BlockSpec((k, TILE), lambda i: (0, i)), single((m, E)), single((m, E))],
        out_specs=[
            pl.BlockSpec((own, TILE), lambda i: (0, jnp.minimum(i, some - 1))),
            pl.BlockSpec((m, TILE), lambda i: (0, jnp.maximum(i - some, 0))),
        ],
        compiler_params=pltpu.CompilerParams(vmem_limit_bytes=VMEM),
        cost_estimate=cost(2 * (own + 2 * m) * k * heads * E, 2 * (m * k + 3 * (m + k) * heads * E)),
        name="project",
    )(x, w, cosine, sine)


def attend(query, kv, places, heads):
    m = query.shape[0]
    blocks = m // QB
    factor = E ** (-0.5) * LOG2E

    def kernel(q_ref, k_ref, v_ref, p_ref, o_ref, probs_ref, bias):
        @pl.when(pl.program_id(0) == 0)
        def _():
            for block in range(blocks):
                key = lax.broadcasted_iota(jnp.int32, (KB, QB), 0) + block * QB
                query = lax.broadcasted_iota(jnp.int32, (KB, QB), 1) + block * QB
                place = p_ref[:, block * QB : (block + 1) * QB]
                allowed = (key <= query + WINDOW) & (key > query) & (key >= query + WINDOW - place)
                bias[block] = jnp.where(allowed, 0.0, -1e30)

        values_t = v_ref[...].T
        for block in range(blocks):
            span = slice(block * QB, block * QB + KB)
            scores = dot_nt(k_ref[span, :], q_ref[block * QB : (block + 1) * QB, :]) * factor + bias[block]
            largest = jnp.max(scores, axis=0, keepdims=True)
            grown = jnp.exp2(scores - largest)
            inverse = 1.0 / jnp.sum(grown, axis=0, keepdims=True)
            probs = (grown * inverse).astype(BF)
            probs_ref[0, block] = probs
            mixed_t = dot_nn(values_t[:, span], probs)
            o_ref[block * QB : (block + 1) * QB, :] = mixed_t.T.astype(BF)

    head = pl.BlockSpec((m, E), lambda i: (0, i))
    reach = kv.shape[0]

    return pl.pallas_call(
        kernel,
        grid=(heads,),
        out_shape=[
            jax.ShapeDtypeStruct((m, heads * E), BF),
            jax.ShapeDtypeStruct((heads, blocks, KB, QB), BF),
        ],
        in_specs=[
            head,
            pl.BlockSpec((reach, E), lambda i: (0, i)),
            pl.BlockSpec((reach, E), lambda i: (0, i + heads)),
            whole_spec((1, m)),
        ],
        out_specs=[head, pl.BlockSpec((1, blocks, KB, QB), lambda i: (i, 0, 0, 0))],
        scratch_shapes=[pltpu.VMEM((blocks, KB, QB), F32)],
        compiler_params=pltpu.CompilerParams(vmem_limit_bytes=VMEM),
        cost_estimate=cost(4 * heads * m * KB * E * 2, 2 * heads * m * KB, heads * m * KB),
        name="attend",
    )(query, kv, kv, places)


def attend_back(query, kv, probs, mixed, w_attn, hidden, gain, d_normed, d_normed_other, cotangent, cosine, sine, flip, ring_source, heads, out_width, identity):
    m, width = hidden.shape
    firsts = m // ROWS
    devices, rows, ring_width = ring_source.shape[1:]
    blocks = m // QB
    factor = E ** (-0.5)
    reach = WINDOW + m
    columns = heads * E

    def kernel(q_ref, k_ref, v_ref, p_ref, x_ref, w_ref, h_ref, gain_ref, dn_ref, do_ref, y_ref, c_hbm, s_hbm, flip_hbm, source, dq_ref, dk_ref, dv_ref, out_ref, sum_ref, flipped_ref, dh_ref, gain_out, c_ref, s_ref, flip_ref, load_sem, g_ref, gt_ref, keys_sum, values_sum, *scratch):
        step = pl.program_id(0)
        half = ring_width // 2
        ring = Ring(devices, [(source.at[0], 0, half), (source.at[0], half, half)], [(sum_ref, 0), (sum_ref, half)], [[0], [1]], scratch)
        brought = loads((c_hbm, s_hbm, flip_hbm), (c_ref, s_ref, flip_ref), load_sem)
        turns = [(firsts + 2 * heads, 1)]

        @pl.when(step == 0)
        def _():
            for copy in brought:
                copy.start()
            ring.barrier()
            ring.begin()

        @pl.when(step == firsts)
        def _():
            for copy in brought:
                copy.wait()

        @pl.when(step < firsts)
        def _():
            change, gain_part = norm_grad(h_ref[...], gain_ref[...], dn_ref[...].astype(F32) + do_ref[...].astype(F32))
            total = y_ref[...].astype(F32) + change
            low = total.astype(BF)
            dh_ref[...] = total
            here = pl.ds(pl.multiple_of(step * ROWS, ROWS), ROWS)
            g_ref[here, :] = low
            gt_ref[:, here] = low.T

            @pl.when(step == 0)
            def _():
                gain_out[...] = gain_part

            @pl.when(step > 0)
            def _():
                gain_out[...] += gain_part

            ring.pace(step, turns)

        @pl.when(step >= firsts)
        def _():
            head = step - firsts
            grad_all = dot_nn(g_ref[...], w_ref[...]).astype(BF)
            out_ref[...] = dot_nn(gt_ref[...], x_ref[...]).astype(BF)
            keys_t = k_ref[...].T
            keys_sum[...] = jnp.zeros_like(keys_sum)
            values_sum[...] = jnp.zeros_like(values_sum)
            for block in range(blocks):
                span = slice(block * QB, block * QB + KB)
                here = slice(block * QB, (block + 1) * QB)
                there = slice(WINDOW + block * QB, WINDOW + (block + 1) * QB)
                low = p_ref[0, block]
                grad = grad_all[here, :]
                d_probs = dot_nt(v_ref[span, :], grad)
                weighted = low.astype(F32) * d_probs
                total = jnp.sum(weighted, axis=0, keepdims=True)
                d_scores = (weighted - low.astype(F32) * total).astype(BF)
                values_sum[span, :] += dot_nn(low, grad)
                keys_sum[span, :] += dot_nn(d_scores, q_ref[here, :])
                d_query = dot_nn(keys_t[:, span], d_scores).T * factor
                dq_ref[here, :] = turned(d_query, c_ref[there, :], s_ref[there, :], True).astype(BF)
                if block == 0:
                    ring.pace(firsts + 2 * head, turns)
            dk_ref[...] = turned(keys_sum[...] * factor, c_ref[...], s_ref[...], True).astype(BF)
            dv_ref[...] = values_sum[...].astype(BF)
            ring.pace(firsts + 2 * head + 1, turns)

            @pl.when(head == 1)
            def _():
                flipped_ref[...] = flip_ref[...].T[: flipped_ref.shape[0]]

            @pl.when(head == heads - 1)
            def _():
                ring.finish()

    def at(i):
        return jnp.maximum(i - firsts, 0)

    head_spec = pl.BlockSpec((m, E), lambda i: (0, at(i)))
    long_spec = pl.BlockSpec((reach, E), lambda i: (0, at(i)))
    rows_spec = pl.BlockSpec((ROWS, width), lambda i: (jnp.minimum(i, firsts - 1), 0))
    any_space = pl.BlockSpec(memory_space=pl.ANY)
    return pl.pallas_call(
        kernel,
        grid=(firsts + heads,),
        out_shape=[
            jax.ShapeDtypeStruct((m, columns), BF),
            jax.ShapeDtypeStruct((reach, columns), BF),
            jax.ShapeDtypeStruct((reach, columns), BF),
            jax.ShapeDtypeStruct((width, columns), BF),
            jax.ShapeDtypeStruct((rows, out_width), F32),
            jax.ShapeDtypeStruct((out_width, rows), F32),
            jax.ShapeDtypeStruct((m, width), F32),
            jax.ShapeDtypeStruct((1, width), F32),
        ],
        in_specs=[
            head_spec,
            long_spec,
            pl.BlockSpec((reach, E), lambda i: (0, at(i) + heads)),
            pl.BlockSpec((1, blocks, KB, QB), lambda i: (at(i), 0, 0, 0)),
            head_spec,
            pl.BlockSpec((width, E), lambda i: (0, at(i) + 3 * heads)),
            rows_spec,
            single((1, width)),
            rows_spec,
            rows_spec,
            rows_spec,
            any_space, any_space, any_space, any_space,
        ],
        out_specs=[
            head_spec,
            long_spec,
            long_spec,
            pl.BlockSpec((width, E), lambda i: (0, at(i))),
            single((rows, out_width)),
            single((out_width, rows)),
            rows_spec,
            single((1, width)),
        ],
        scratch_shapes=[
            pltpu.VMEM((reach, E), F32), pltpu.VMEM((reach, E), F32), pltpu.VMEM(flip.shape, F32), pltpu.SemaphoreType.DMA((3,)),
            pltpu.VMEM((m, width), BF), pltpu.VMEM((width, m), BF),
            pltpu.VMEM((reach, E), F32), pltpu.VMEM((reach, E), F32),
            *Ring.scratch(devices, [(rows, ring_width // 2)] * 2),
        ],
        compiler_params=pltpu.CompilerParams(vmem_limit_bytes=VMEM, collective_id=identity, has_side_effects=True),
        cost_estimate=cost(8 * heads * m * KB * E * 2, 2 * heads * m * KB),
        name="attend_back",
    )(query, kv, kv, probs, mixed, w_attn, hidden, gain, d_normed, d_normed_other, cotangent, cosine, sine, flip, ring_source)


def qkv_back(x_t, d_query, d_key, d_value, w_attn, up_part, out_part, out_width, identity):
    width, reach = x_t.shape
    m, columns = d_query.shape
    devices, rows, up_width = up_part.shape[1:]
    tiles = width // TILE
    per = columns // TILE
    total = tiles + 3 * per
    sides = lax.axis_size("tensor")
    half = m // 2
    piece = up_width // 2
    shapes = [(rows, piece), (rows, piece), (rows, columns)]
    assert 3 * per > tiles and reach == 3 * m

    def kernel(xt_hbm, dq_hbm, dk_hbm, dv_hbm, w_ref, up_ref, out_ref, grad_ref, sent_ref, got, add_ref, up_sum, out_sum, xt_ref, dq_ref, dk_ref, dv_ref, load_sem, sent, early, early_in, near_in, far_in, own_send, own_recv, early_send, early_recv, near_send, near_recv, far_send, far_recv, *scratch):
        step = pl.program_id(0)
        source = up_ref.at[1]
        ring = Ring(
            devices, [(source, 0, piece), (source, piece, piece), (out_ref, 0, columns)], [(up_sum, 0), (up_sum, piece), (out_sum, 0)],
            [[0], [1], [2]], scratch,
        )
        me, side = ring.me, ring.side
        across = lax.rem(side + 1, sides)
        later, before = lax.rem(me + 2, devices), lax.rem(me + devices - 2, devices)
        share = ring.core.astype(F32)
        brought = loads((dq_hbm, dk_hbm, dv_hbm, xt_hbm), (dq_ref, dk_ref, dv_ref, xt_ref), load_sem)

        def remote(source, target, send, recv, which, other):
            return pltpu.make_async_remote_copy(
                src_ref=source, dst_ref=target, send_sem=send.at[which], recv_sem=recv.at[which], device_id=other, device_id_type=MESH
            )

        def own_copy(which):
            target = got.at[:, pl.ds(pl.multiple_of(which * TILE, TILE), TILE)]
            return remote(sent.at[which], target, own_send, own_recv, which, (me, across))

        def early_copy(which):
            return remote(early.at[which, across], early_in.at[which], early_send, early_recv, which, (me, across))

        def near_copy(which):
            return remote(early_in.at[which, 1], near_in.at[which], near_send, near_recv, which, (ring.partner, side))

        def far_copy(which):
            return remote(early_in.at[which, 0], far_in.at[which], far_send, far_recv, which, (before, side))

        @pl.when(step == 0)
        def _():
            for copy in brought:
                copy.start()
            ring.barrier(((me, across), (later, side), (before, side)))
            ring.begin()
            for copy in brought[:3]:
                copy.wait()

        @pl.when(step == tiles)
        def _():
            brought[3].wait()

        @pl.when(step < tiles)
        def _():
            w_key, w_value = w_ref[:, columns : 2 * columns], w_ref[:, 2 * columns :]
            part = dot_nt(dq_ref[...], w_ref[:, :columns])
            part += dot_nt(dk_ref[2 * m :, :], w_key) + dot_nt(dv_ref[2 * m :, :], w_value)
            low = part.astype(BF)
            sent[step] = low
            sent_ref[...] = low
            for block in range(2):
                span = slice(block * m, (block + 1) * m)
                part = (dot_nt(dk_ref[span, :], w_key) + dot_nt(dv_ref[span, :], w_value)).astype(BF)
                for number in range(2):
                    early[step, number, block] = part[number * half : (number + 1) * half]
            early_copy(step).start()

        number = step - tiles

        @pl.when((number >= 0) & (number < tiles))
        def _():
            own_copy(number).start()
            early_copy(number).wait_recv()
            early_in[number] = (early_in[number].astype(F32) + early[number, side].astype(F32)).astype(BF)
            near_copy(number).start()

        @pl.when((number >= 1) & (number <= tiles))
        def _():
            which = number - 1
            near_copy(which).wait_recv()
            early_in[which, 0] = (early_in[which, 0].astype(F32) + near_in[which].astype(F32) * share).astype(BF)

            @pl.when(me >= 2)
            def _():
                far_copy(which).start()

        @pl.when((number >= 0) & (number < per))
        def _():
            here = pl.ds(pl.multiple_of(number * TILE, TILE), TILE)
            grad_ref[...] = dot_nn(xt_ref[:, 2 * m :], dq_ref[:, here]).astype(BF)

        @pl.when((number >= per) & (number < 2 * per))
        def _():
            here = pl.ds(pl.multiple_of((number - per) * TILE, TILE), TILE)
            grad_ref[...] = dot_nn(xt_ref[...], dk_ref[:, here]).astype(BF)

        @pl.when(number >= 2 * per)
        def _():
            here = pl.ds(pl.multiple_of((number - 2 * per) * TILE, TILE), TILE)
            grad_ref[...] = dot_nn(xt_ref[...], dv_ref[:, here]).astype(BF)

        ring.pace(step, [(tiles, 5), (3 * per, 4)])

        @pl.when(step == total - 1)
        def _():
            for which in range(tiles):
                here = slice(which * TILE, (which + 1) * TILE)
                add_ref[:, here] = (near_in[which].astype(F32) * (1.0 - share)).astype(BF)

                @pl.when(me < devices - 2)
                def _():
                    far_copy(which).wait_recv()
                    add_ref[:, here] = (add_ref[:, here].astype(F32) + far_in[which].astype(F32)).astype(BF)

                @pl.when(me >= 2)
                def _():
                    far_copy(which).wait_send()

                near_copy(which).wait_send()
                early_copy(which).wait_send()
                own_copy(which).wait()
            ring.finish()

    any_space = pl.BlockSpec(memory_space=pl.ANY)
    dma = pltpu.SemaphoreType.DMA

    def second(i):
        return jnp.minimum(i, tiles - 1)

    return pl.pallas_call(
        kernel,
        grid=(total,),
        out_shape=[
            jax.ShapeDtypeStruct((width, 3 * columns), BF),
            jax.ShapeDtypeStruct((m, width), BF),
            jax.ShapeDtypeStruct((m, width), BF),
            jax.ShapeDtypeStruct((half, width), BF),
            jax.ShapeDtypeStruct((rows, out_width), F32),
            jax.ShapeDtypeStruct((rows, columns), F32),
        ],
        in_specs=[
            any_space, any_space, any_space, any_space,
            pl.BlockSpec((TILE, 3 * columns), lambda i: (second(i), 0)),
            any_space, any_space,
        ],
        out_specs=[
            pl.BlockSpec((width, TILE), lambda i: (0, jnp.maximum(i - tiles, 0))),
            pl.BlockSpec((m, TILE), lambda i: (0, second(i))),
            any_space,
            single((half, width)),
            single((rows, out_width)),
            single((rows, columns)),
        ],
        scratch_shapes=[
            pltpu.VMEM((width, reach), BF),
            pltpu.VMEM((m, columns), BF),
            pltpu.VMEM((reach, columns), BF),
            pltpu.VMEM((reach, columns), BF),
            dma((4,)),
            pltpu.VMEM((tiles, m, TILE), BF),
            pltpu.VMEM((tiles, 2, 2, half, TILE), BF),
            pltpu.VMEM((tiles, 2, half, TILE), BF),
            pltpu.VMEM((tiles, half, TILE), BF),
            pltpu.VMEM((tiles, half, TILE), BF),
            *[dma((tiles,))] * 8,
            *Ring.scratch(devices, shapes),
        ],
        compiler_params=pltpu.CompilerParams(vmem_limit_bytes=VMEM, collective_id=identity, has_side_effects=True),
        cost_estimate=cost(4 * (m + 2 * reach) * width * columns, 12 * width * columns),
        name="qkv_back",
    )(x_t, d_query, d_key, d_value, w_attn, up_part, out_part)


def tiles_of(width):
    return width // TILE


def root_of(rows):
    return lax.rsqrt(jnp.mean(rows * rows, axis=-1, keepdims=True) + EPS)


def norm_grad(rows, gain, grad):
    root = root_of(rows)
    pushed = grad * gain
    inner = jnp.mean(pushed * rows, axis=-1, keepdims=True)
    return root * pushed - rows * (root * root * root * inner), jnp.sum(grad * rows * root, axis=0, keepdims=True)


def first_norm(far, near, tokens, gain):
    m, width = tokens.shape
    steps = m // ROWS

    def kernel(far_ref, near_ref, x_ref, g_ref, o_ref, t_ref):
        step = pl.program_id(0)
        me = lax.axis_index("dp")

        def normed(ref):
            rows = ref[...].astype(F32)
            return (rows * root_of(rows) * g_ref[...]).astype(BF)

        def earlier(ref, there):
            @pl.when(there)
            def _():
                made = normed(ref)
                o_ref[...] = made
                t_ref[...] = made.T

            @pl.when(jnp.logical_not(there))
            def _():
                o_ref[...] = jnp.zeros_like(o_ref)
                t_ref[...] = jnp.zeros_like(t_ref)

        @pl.when(step < steps)
        def _():
            earlier(far_ref, me >= 2)

        @pl.when((step >= steps) & (step < 2 * steps))
        def _():
            earlier(near_ref, me >= 1)

        @pl.when(step >= 2 * steps)
        def _():
            made = normed(x_ref)
            o_ref[...] = made
            t_ref[...] = made.T

    def part(which):
        return pl.BlockSpec((ROWS, width), lambda i: (jnp.clip(i - which * steps, 0, steps - 1), 0))

    return pl.pallas_call(
        kernel,
        grid=(3 * steps,),
        out_shape=[jax.ShapeDtypeStruct((3 * m, width), BF), jax.ShapeDtypeStruct((width, 3 * m), BF)],
        in_specs=[part(0), part(1), part(2), whole_spec((1, width))],
        out_specs=[
            pl.BlockSpec((ROWS, width), lambda i: (i, 0)),
            pl.BlockSpec((width, ROWS), lambda i: (0, i)),
        ],
        compiler_params=pltpu.CompilerParams(vmem_limit_bytes=VMEM),
        cost_estimate=cost(24 * m * width, 14 * m * width),
        name="first_norm",
    )(far, near, tokens, gain)


def out_norm(mixed, w_attn, place, tokens, gain, identity):
    m, columns = mixed.shape
    width = tokens.shape[1]
    steps = m // ROWS
    sides = lax.axis_size("tensor")

    def kernel(x_ref, w_ref, r_ref, g_ref, hidden_ref, normed_ref, turned_ref, sent, got, send, recv):
        step = pl.program_id(0)
        other = (lax.axis_index("dp"), lax.rem(lax.axis_index("tensor") + 1, sides))

        @pl.when(step == 0)
        def _():
            semaphore = pltpu.get_barrier_semaphore()
            pl.semaphore_signal(semaphore, inc=1, device_id=other, device_id_type=MESH)
            pl.semaphore_wait(semaphore, 1)

        def across(which):
            return pltpu.make_async_remote_copy(
                src_ref=sent.at[which], dst_ref=got.at[which], send_sem=send.at[which], recv_sem=recv.at[which],
                device_id=other, device_id_type=MESH,
            )

        @pl.when(step < steps)
        def _():
            sent[step] = dot_nt(x_ref[...], w_ref[...]).astype(BF)
            across(step).start()

        @pl.when(step >= steps)
        def _():
            which = step - steps
            across(which).wait()
            hidden = r_ref[...].astype(F32) + (sent[which].astype(F32) + got[which].astype(F32))
            normed = (hidden * root_of(hidden) * g_ref[...]).astype(BF)
            hidden_ref[...] = hidden
            normed_ref[...] = normed
            turned_ref[...] = normed.T

    def late(i):
        return jnp.maximum(i - steps, 0)

    late_rows = pl.BlockSpec((ROWS, width), lambda i: (late(i), 0))
    dma = pltpu.SemaphoreType.DMA
    return pl.pallas_call(
        kernel,
        grid=(2 * steps,),
        out_shape=[
            jax.ShapeDtypeStruct((m, width), F32),
            jax.ShapeDtypeStruct((m, width), BF),
            jax.ShapeDtypeStruct((width, m), BF),
        ],
        in_specs=[
            pl.BlockSpec((ROWS, columns), lambda i: (jnp.minimum(i, steps - 1), 0)),
            pl.BlockSpec((width, columns), lambda i: (0, place), pipeline_mode=pl.Buffered(1)),
            late_rows,
            single((1, width)),
        ],
        out_specs=[late_rows, late_rows, pl.BlockSpec((width, ROWS), lambda i: (0, late(i)))],
        scratch_shapes=[pltpu.VMEM((steps, ROWS, width), BF), pltpu.VMEM((steps, ROWS, width), BF), dma((steps,)), dma((steps,))],
        compiler_params=pltpu.CompilerParams(vmem_limit_bytes=VMEM, collective_id=identity, has_side_effects=True),
        cost_estimate=cost(2 * m * width * columns, 12 * m * width),
        name="out_norm",
    )(mixed, w_attn, tokens, gain)


def last_pass(tokens, gain, grad, grad_other, grad_add, d_hidden, hidden, act_early, act_late, w_ffn, rest, gain_ffn_grad, flip, qkv_part, lanes, identity):
    m, width = tokens.shape
    devices, rows, all_columns = qkv_part.shape
    columns = all_columns // 3
    chips = devices // 2
    size = ROWS // 2
    steps = m // size
    total = tiles_of(width) + steps + chips
    names = 3
    half = m // 2
    tiles = tiles_of(width)
    some, late = act_early.shape[1], act_late.shape[1]
    sides = lax.axis_size("tensor")
    assert chips >= tiles

    def kernel(x_ref, g_ref, dn_ref, do_ref, add_hbm, dh_ref, h_ref, a_hbm, al_hbm, w_ref, rest_ref, gf_ref, flip_hbm, source, grad_ref, layer_ref, flipped_ref, q_ref, k_ref, v_ref, gains_ref, a_ref, al_ref, flip_ref, add, load_sem, add_send, add_recv, gain_sum, gain_source, sent, got, y_send, y_recv, *scratch):
        step = pl.program_id(0)
        ring = Ring(
            devices, [(source, number * columns, columns) for number in range(names)], [(q_ref, 0), (k_ref, 0), (v_ref, 0)],
            [[0], [1], [2]], scratch[: 3 * names + 5],
        )
        gain_ring = Ring(devices, [(gain_source, 0, lanes)], [(gains_ref, 0)], [[0]], scratch[3 * names + 5 :])
        other = (ring.me, lax.rem(ring.side + 1, sides))
        brought = loads((a_hbm, al_hbm, flip_hbm, add_hbm), (a_ref, al_ref, flip_ref, add.at[ring.side]), load_sem)
        add_copy = pltpu.make_async_remote_copy(
            src_ref=add_hbm, dst_ref=add.at[ring.side], send_sem=add_send, recv_sem=add_recv, device_id=other, device_id_type=MESH
        )
        row_step = step - tiles
        end_step = step - tiles - steps

        def across(which):
            return pltpu.make_async_remote_copy(
                src_ref=sent.at[which], dst_ref=got.at[which], send_sem=y_send.at[which], recv_sem=y_recv.at[which],
                device_id=other, device_id_type=MESH,
            )

        @pl.when(step == 0)
        def _():
            for copy in brought:
                copy.start()
            ring.barrier((other,))
            add_copy.start()
            ring.begin()
            for copy in brought:
                copy.wait()
            flipped_ref[...] = flip_ref[...].T

        @pl.when(row_step == 0)
        def _():
            add_copy.wait()

        @pl.when(step < tiles)
        def _():
            sent[step] = (dot_nt(a_ref[...], w_ref[...]) + dot_nt(al_ref[...], rest_ref[...])).astype(BF)
            across(step).start()

        @pl.when((row_step >= 0) & (row_step < steps))
        def _():
            which = row_step * size // half
            here = pl.ds(pl.multiple_of(row_step * size - which * half, size), size)
            grad_rows = dn_ref[...].astype(F32) + do_ref[...].astype(F32) + add[which, here, :].astype(F32)
            change, gain_part = norm_grad(x_ref[...].astype(F32), g_ref[...], grad_rows)
            grad_ref[...] = dh_ref[...] + change

            @pl.when(row_step == 0)
            def _():
                gain_sum[...] = gain_part

            @pl.when(row_step > 0)
            def _():
                gain_sum[...] += gain_part

        @pl.when(row_step == steps - 1)
        def _():
            gain_source[...] = jnp.zeros_like(gain_source)
            for device in range(devices):
                span = slice(device * rows, (device + 1) * rows)
                gain_source[device, :16, :rows] = jnp.broadcast_to(gain_sum[:, span], (16, rows)).astype(BF)
                gain_source[device, 16:, :rows] = jnp.broadcast_to(gf_ref[:, span], (16, rows)).astype(BF)
            gain_ring.begin()

        ring.pace(step, [(tiles, 4), (steps, 3), (chips, 3)])

        @pl.when(end_step >= 0)
        def _():
            gain_ring.run(end_step, jnp.minimum(end_step + 1, gain_ring.events))

        @pl.when((end_step >= 0) & (end_step < tiles))
        def _():
            across(end_step).wait()
            layer_ref[...] = (h_ref[...] + (sent[end_step].astype(F32) + got[end_step].astype(F32))).astype(BF)

        @pl.when(step == total - 1)
        def _():
            ring.finish()
            gain_ring.finish()

    def early(i):
        return jnp.minimum(i, tiles - 1)

    rows_spec = pl.BlockSpec((size, width), lambda i: (jnp.clip(i - tiles, 0, steps - 1), 0))
    tile_spec = pl.BlockSpec((m, TILE), lambda i: (0, jnp.clip(i - tiles - steps, 0, tiles - 1)))
    dma = pltpu.SemaphoreType.DMA
    sums = jax.ShapeDtypeStruct((rows, columns), F32)
    return pl.pallas_call(
        kernel,
        grid=(total,),
        out_shape=[
            jax.ShapeDtypeStruct((m, width), F32),
            jax.ShapeDtypeStruct((m, width), BF),
            jax.ShapeDtypeStruct((flip.shape[1], flip.shape[0]), F32),
            sums, sums, sums,
            jax.ShapeDtypeStruct((32, lanes), F32),
        ],
        in_specs=[
            rows_spec, single((1, width)), rows_spec, rows_spec, pl.BlockSpec(memory_space=pl.ANY), rows_spec, tile_spec, pl.BlockSpec(memory_space=pl.ANY), pl.BlockSpec(memory_space=pl.ANY),
            pl.BlockSpec((TILE, some), lambda i: (early(i), 2)), pl.BlockSpec((TILE, late), lambda i: (early(i), 2)), single((1, width)),
            pl.BlockSpec(memory_space=pl.ANY), pl.BlockSpec(memory_space=pl.ANY),
        ],
        out_specs=[
            rows_spec, tile_spec, single((flip.shape[1], flip.shape[0])),
            single(sums.shape), single(sums.shape), single(sums.shape), single((32, lanes)),
        ],
        scratch_shapes=[
            pltpu.VMEM((m, some), BF),
            pltpu.VMEM((m, late), BF),
            pltpu.VMEM(flip.shape, F32),
            pltpu.VMEM((2, half, width), BF),
            dma((4,)),
            dma,
            dma,
            pltpu.VMEM((1, width), F32),
            pltpu.VMEM((devices, 32, lanes), BF),
            pltpu.VMEM((tiles, m, TILE), BF),
            pltpu.VMEM((tiles, m, TILE), BF),
            dma((tiles,)),
            dma((tiles,)),
            *Ring.scratch(devices, [(rows, columns)] * names),
            *Ring.scratch(devices, [(32, lanes)]),
        ],
        compiler_params=pltpu.CompilerParams(vmem_limit_bytes=VMEM, collective_id=identity, has_side_effects=True),
        cost_estimate=cost(20 * m * width, 24 * m * width),
        name="last_pass",
    )(tokens, gain, grad, grad_other, grad_add, d_hidden, hidden, act_early, act_late, w_ffn, rest, gain_ffn_grad, flip, qkv_part)


def feed_tile(x_ref, dy_ref, dyt_ref, g_ref, u_ref, d_ref, act_ref, both_ref, down_ref):
    gate = dot_nn(x_ref[...], g_ref[...])
    up = dot_nn(x_ref[...], u_ref[...])
    d_act = dot_nn(dy_ref[...], d_ref[...])
    soft = 1.0 / (1.0 + jnp.exp(-gate))
    silu = gate * soft
    act = (silu * up).astype(BF)
    act_ref[...] = act
    both_ref[0] = (d_act * up * (soft * (1.0 + gate * (1.0 - soft)))).astype(BF)
    both_ref[1] = (d_act * silu).astype(BF)
    down_ref[...] = dot_nn(dyt_ref[...], act).astype(BF)


def feed(x, dy, dy_t, w, block, tiles, identity):
    m, k = x.shape
    early = tiles - LATE
    devices = lax.axis_size("dp")
    width = block.shape[1] // 2

    def kernel(x_hbm, dy_hbm, dyt_hbm, g_ref, u_ref, d_ref, block_ref, act_ref, both_ref, down_ref, rest_ref, x_ref, dy_ref, dyt_ref, load_sem, *scratch):
        step = pl.program_id(0)
        brought = loads((x_hbm, dy_hbm, dyt_hbm), (x_ref, dy_ref, dyt_ref), load_sem)
        spread = Spread(devices, [(block_ref, rest_ref, 0, width), (block_ref, rest_ref, width, width)], scratch)

        @pl.when(step == 0)
        def _():
            for copy in brought:
                copy.start()
            spread.barrier()
            spread.begin()
            for copy in brought:
                copy.wait()

        feed_tile(x_ref, dy_ref, dyt_ref, g_ref, u_ref, d_ref, act_ref, both_ref, down_ref)
        spread.pace(step, early)

        @pl.when(step == early - 1)
        def _():
            spread.finish()

    any_space = pl.BlockSpec(memory_space=pl.ANY)
    return pl.pallas_call(
        kernel,
        grid=(early,),
        out_shape=[
            jax.ShapeDtypeStruct((m, early * TILE), BF),
            jax.ShapeDtypeStruct((2, m, early * TILE), BF),
            jax.ShapeDtypeStruct((k, early * TILE), BF),
            jax.ShapeDtypeStruct((k, block.shape[1]), BF),
        ],
        in_specs=[
            any_space, any_space, any_space,
            pl.BlockSpec((k, TILE), lambda i: (0, i)),
            pl.BlockSpec((k, TILE), lambda i: (0, i + early)),
            pl.BlockSpec((k, TILE), lambda i: (0, i + 2 * early)),
            any_space,
        ],
        out_specs=[
            pl.BlockSpec((m, TILE), lambda i: (0, i)),
            pl.BlockSpec((2, m, TILE), lambda i: (0, 0, i)),
            pl.BlockSpec((k, TILE), lambda i: (0, i)),
            any_space,
        ],
        scratch_shapes=[
            pltpu.VMEM((m, k), BF), pltpu.VMEM((m, k), BF), pltpu.VMEM((k, m), BF), pltpu.SemaphoreType.DMA((3,)),
            *Spread.scratch(devices, 2),
        ],
        compiler_params=pltpu.CompilerParams(vmem_limit_bytes=VMEM, collective_id=identity, has_side_effects=True),
        cost_estimate=cost(8 * m * k * early * TILE, 8 * (m + k) * early * TILE, m * early * TILE),
        name="feed",
    )(x, dy, dy_t, w, w, w, block)


def ffn_back(x, x_t, dy, dy_t, d_early, w_ffn, rest, down_early, identity):
    m, width = x.shape
    devices, rows, some = down_early.shape
    late = LATE * TILE
    padded = some + late
    early_tiles = some // TILE
    tiles = width // TILE
    grads = 2 * (early_tiles + LATE)
    total = LATE + tiles + grads
    sides = lax.axis_size("tensor")
    pieces = [(rows, some // 2)] * 2

    def kernel(x_hbm, xt_hbm, dy_hbm, dyt_hbm, rg_ref, ru_ref, rd_ref, d_hbm, tile_ref, wg_ref, wu_ref, lg_ref, lu_ref, source, act_ref, grad_ref, sent_ref, got, sum_ref, x_ref, xt_ref, dy_ref, dyt_ref, d_ref, load_sem, d_late, down_late, down_tile, both_tile, sent, y_send, y_recv, *scratch):
        step = pl.program_id(0)
        brought = loads((x_hbm, dy_hbm, dyt_hbm, d_hbm, xt_hbm), (x_ref, dy_ref, dyt_ref, d_ref, xt_ref), load_sem)
        ring = Ring(devices, [(source, 0, some // 2), (source, some // 2, some // 2)], [(sum_ref, 0), (sum_ref, some // 2)], [[0], [1]], scratch[:11])
        late_ring = Ring(devices, [(down_late, 0, late)], [(sum_ref, some)], [[0]], scratch[11:])
        other = (ring.me, lax.rem(ring.side + 1, sides))

        def across(which):
            return pltpu.make_async_remote_copy(
                src_ref=sent.at[which], dst_ref=got.at[:, pl.ds(pl.multiple_of(which * TILE, TILE), TILE)],
                send_sem=y_send.at[which], recv_sem=y_recv.at[which], device_id=other, device_id_type=MESH,
            )

        @pl.when(step == 0)
        def _():
            for copy in brought:
                copy.start()
            ring.barrier((other,))
            ring.begin()
            for copy in brought[:3]:
                copy.wait()

        @pl.when(step == LATE)
        def _():
            brought[3].wait()

        @pl.when(step == LATE + tiles)
        def _():
            brought[4].wait()

        @pl.when(step < LATE)
        def _():
            feed_tile(x_ref, dy_ref, dyt_ref, rg_ref, ru_ref, rd_ref, act_ref, both_tile, down_tile)
            here = pl.ds(pl.multiple_of(step * TILE, TILE), TILE)
            d_late[:, :, here] = both_tile[...]
            down_late[:, :, here] = down_tile[...].reshape(devices, rows, TILE)

        @pl.when(step == LATE - 1)
        def _():
            late_ring.begin()

        @pl.when((step >= LATE) & (step < LATE + tiles))
        def _():
            which = step - LATE
            part = dot_nt(d_ref[0], wg_ref[...]) + dot_nt(d_ref[1], wu_ref[...])
            part += dot_nt(d_late[0], lg_ref[...]) + dot_nt(d_late[1], lu_ref[...])
            low = part.astype(BF)
            sent[which] = low
            sent_ref[...] = low
            across(which).start()

        @pl.when((step >= LATE + tiles) & (step < LATE + tiles + 2 * early_tiles))
        def _():
            grad_ref[0] = dot_nn(xt_ref[...], tile_ref[0]).astype(BF)

        @pl.when(step >= LATE + tiles + 2 * early_tiles)
        def _():
            number = step - (LATE + tiles + 2 * early_tiles)
            here = pl.ds(pl.multiple_of(lax.rem(number, LATE) * TILE, TILE), TILE)
            grad_ref[0] = dot_nn(xt_ref[...], d_late[number // LATE, :, here]).astype(BF)

        ring.pace(step, [(LATE, 12), (tiles, 8), (grads, 4)])
        late_ring.pace(step, [(LATE, 0), (tiles, 8), (grads, 4)])

        @pl.when(step == total - 1)
        def _():
            for which in range(tiles):
                across(which).wait()
            ring.finish()
            late_ring.finish()

    def first(i):
        return jnp.minimum(i, LATE - 1)

    def second(i):
        return jnp.clip(i - LATE, 0, tiles - 1)

    def third(i):
        at = jnp.clip(i - LATE - tiles, 0, 2 * early_tiles - 1)
        return (at // early_tiles, 0, at % early_tiles)

    def grad_at(i):
        at = jnp.maximum(i - LATE - tiles, 0)
        more = jnp.maximum(at - 2 * early_tiles, 0)
        is_late = at // (2 * early_tiles)
        return (
            (1 - is_late) * (at // early_tiles) + is_late * (more // LATE),
            0,
            (1 - is_late) * (at % early_tiles) + is_late * (early_tiles + more % LATE),
        )

    assert LATE <= early_tiles
    any_space = pl.BlockSpec(memory_space=pl.ANY)
    dma = pltpu.SemaphoreType.DMA

    def rest_tile(which):
        return pl.BlockSpec((width, TILE), lambda i: (0, first(i) + which * LATE))

    return pl.pallas_call(
        kernel,
        grid=(total,),
        out_shape=[
            jax.ShapeDtypeStruct((m, late), BF),
            jax.ShapeDtypeStruct((2, width, padded), BF),
            jax.ShapeDtypeStruct((m, width), BF),
            jax.ShapeDtypeStruct((m, width), BF),
            jax.ShapeDtypeStruct((rows, padded), F32),
        ],
        in_specs=[
            any_space, any_space, any_space, any_space,
            rest_tile(0), rest_tile(1), rest_tile(2),
            any_space,
            pl.BlockSpec((1, m, TILE), third),
            pl.BlockSpec((TILE, some), lambda i: (second(i), 0)),
            pl.BlockSpec((TILE, some), lambda i: (second(i), 1)),
            pl.BlockSpec((TILE, late), lambda i: (second(i), 0)),
            pl.BlockSpec((TILE, late), lambda i: (second(i), 1)),
            any_space,
        ],
        out_specs=[
            pl.BlockSpec((m, TILE), lambda i: (0, first(i))),
            pl.BlockSpec((1, width, TILE), grad_at),
            pl.BlockSpec((m, TILE), lambda i: (0, second(i))),
            any_space,
            single((rows, padded)),
        ],
        scratch_shapes=[
            pltpu.VMEM((m, width), BF),
            pltpu.VMEM((width, m), BF),
            pltpu.VMEM((m, width), BF),
            pltpu.VMEM((width, m), BF),
            pltpu.VMEM((2, m, some), BF),
            dma((5,)),
            pltpu.VMEM((2, m, late), BF),
            pltpu.VMEM((devices, rows, late), BF),
            pltpu.VMEM((width, TILE), BF),
            pltpu.VMEM((2, m, TILE), BF),
            pltpu.VMEM((tiles, m, TILE), BF),
            dma((tiles,)),
            dma((tiles,)),
            *Ring.scratch(devices, pieces),
            *Ring.scratch(devices, [(rows, late)]),
        ],
        compiler_params=pltpu.CompilerParams(vmem_limit_bytes=VMEM, collective_id=identity, has_side_effects=True),
        cost_estimate=cost(8 * m * width * padded + 8 * m * width * late, 10 * width * padded),
        name="ffn_back",
    )(x, x_t, dy, dy_t, rest, rest, rest, d_early, d_early, w_ffn, w_ffn, rest, rest, down_early)


def shards(tokens, positions, attn_gain, w_query, w_key, w_value, w_out, ffn_gain, w_gate, w_up, w_down, cotangent):
    devices = lax.axis_size("dp")
    span = tokens.shape[0]
    assert 2 * span == WINDOW
    own_rows = w_query.shape[0]
    width = tokens.shape[1]
    head_columns = w_query.shape[1]
    heads = head_columns // E
    hidden_units = w_gate.shape[1]
    tiles = (hidden_units + TILE - 1) // TILE
    padded = tiles * TILE

    attn_pack = jnp.concatenate([w_query, w_key, w_value, w_out.T], axis=1)
    lanes = max(128, own_rows)
    gains = jnp.zeros((32, lanes), BF).at[0, :own_rows].set(attn_gain).at[16, :own_rows].set(ffn_gain)
    w_attn, all_gains, near, far = ring_gather((attn_pack, gains), (2, 1), tokens, 0)

    def wide(matrix):
        return jnp.pad(matrix, ((0, 0), (0, padded - hidden_units)))

    ffn_parts = [wide(w_gate), wide(w_up), wide(w_down.T)]
    some = padded - LATE * TILE
    ffn_pack = jnp.concatenate([part[:, :some] for part in ffn_parts], axis=1)
    rest_pack = jnp.concatenate([part[:, some:] for part in ffn_parts], axis=1)
    w_attn, all_gains, ffn_pack = lax.optimization_barrier((w_attn, all_gains, ffn_pack))
    w_ffn = lax.all_gather(ffn_pack, "dp", axis=0, tiled=True)
    all_gains = all_gains.reshape(devices, 32, lanes)
    gain_attn = all_gains[:, 0, :own_rows].reshape(1, width).astype(F32)
    gain_ffn = all_gains[:, 16, :own_rows].reshape(1, width).astype(F32)

    frequency = THETA ** (-(jnp.arange(E // 2, dtype=F32) * 2.0 / E))
    earlier = positions[0] - WINDOW + jnp.arange(WINDOW, dtype=jnp.int32)
    angles = jnp.concatenate([earlier, positions]).astype(F32)[:, None] * frequency[None, :]
    cosine_half, sine_half = jnp.cos(angles), jnp.sin(angles)
    cosine = jnp.concatenate([cosine_half, cosine_half], axis=1)
    sine = jnp.concatenate([-sine_half, sine_half], axis=1)

    normed_attn, normed_attn_t = first_norm(far, near, tokens, gain_attn)
    query, kv = project(normed_attn, w_attn, cosine, sine, span, heads)
    mixed, probs = attend(query, kv, positions[None, :], heads)
    hidden, normed_ffn, normed_ffn_t = out_norm(mixed, w_attn, 3, tokens, gain_ffn, 5)

    cotangent_t = cotangent.T
    act_early, d_early, down_early, rest = feed(normed_ffn, cotangent, cotangent_t, w_ffn, rest_pack, tiles, 6)
    act_late, both_part, d_normed_ffn, d_normed_other, down_grad = ffn_back(
        normed_ffn, normed_ffn_t, cotangent, cotangent_t, d_early, w_ffn, rest, down_early.reshape(devices, own_rows, some), 1
    )
    both_part = both_part.reshape(2, devices, own_rows, padded)

    d_query, d_key, d_value, out_part, gate_grad, w_down_grad, d_hidden, gain_ffn_grad = attend_back(
        query, kv, probs, mixed, w_attn, hidden, gain_ffn, d_normed_ffn, d_normed_other, cotangent, cosine, sine, down_grad, both_part, heads, hidden_units, 2
    )
    qkv_part, d_normed_attn, d_attn_other, d_attn_add, up_grad, out_grad = qkv_back(
        normed_attn_t, d_query, d_key, d_value, w_attn, both_part, out_part.reshape(devices, own_rows, head_columns), hidden_units, 3
    )
    tokens_grad, layer_out, w_out_grad, query_grad, key_grad, value_grad, gain_grads = last_pass(
        tokens, gain_attn, d_normed_attn, d_attn_other, d_attn_add, d_hidden, hidden, act_early, act_late, w_ffn, rest, gain_ffn_grad, out_grad,
        qkv_part.reshape(devices, own_rows, 3 * head_columns), lanes, 4,
    )
    return (
        layer_out,
        tokens_grad,
        gain_grads[0, :own_rows],
        query_grad,
        key_grad,
        value_grad,
        w_out_grad,
        gain_grads[16, :own_rows],
        gate_grad,
        up_grad,
        w_down_grad,
    )


def solution(mesh):
    by_rows, by_both, turned_both, line = P("dp", None), P("dp", "tensor"), P("tensor", "dp"), P("dp")
    return jax.shard_map(
        shards,
        mesh=mesh,
        in_specs=(by_rows, line, line, by_both, by_both, by_both, turned_both, line, by_both, by_both, turned_both, by_rows),
        out_specs=(by_rows, by_rows, line, by_both, by_both, by_both, turned_both, line, by_both, by_both, turned_both),
        check_vma=False,
    )
```

```python
import functools

import jax
import jax.numpy as jnp
from jax import lax
from jax.experimental import pallas as pl
from jax.experimental.pallas import tpu as pltpu
from jax.sharding import PartitionSpec as P

E = 128
WINDOW = 1024
EPS = 1e-06
THETA = 10000.0
LOG2E = 1.4426950408889634
MESH = pl.DeviceIdType.MESH
BF = jnp.bfloat16
F32 = jnp.float32
QB = 256
KB = WINDOW + QB
TILE = 256
ROWS = 128
SOON = 2
LATE = 3
VMEM = 59 * 1024 * 1024


def whole_spec(shape):
    return pl.BlockSpec(shape, lambda i: (0,) * len(shape))


def single(shape):
    return pl.BlockSpec(shape, lambda i: (0,) * len(shape), pipeline_mode=pl.Buffered(1))


def loads(sources, targets, semaphores):
    return [pltpu.make_async_copy(s, t, semaphores.at[i]) for i, (s, t) in enumerate(zip(sources, targets))]


def cost(flops, nbytes, special=0):
    return pl.CostEstimate(flops=flops, bytes_accessed=nbytes, transcendentals=special)


def ring_chip(place, chips):
    place = lax.rem(place + 2 * chips, chips)
    late = place // (chips // 2)
    return (1 - late) * 2 * place + late * (2 * (chips - 1 - place) + 1)


def ring_place(chip, chips):
    column = lax.rem(chip, 2)
    row = chip // 2
    return (1 - column) * row + column * (chips - 1 - row)


class Spread:
    def __init__(self, devices, pieces, scratch):
        self.devices, self.chips, self.pieces = devices, devices // 2, pieces
        self.local_sem, self.send_sem, self.recv_sem, self.give_sem, self.take_sem = scratch
        self.me = lax.axis_index("dp")
        self.side = lax.axis_index("tensor")
        self.core = lax.rem(self.me, 2)
        self.place = ring_place(self.me // 2, self.chips)
        self.partner = self.me + 1 - 2 * self.core
        self.next = (
            ring_chip(self.place + 1, self.chips) * 2 + self.core,
            ring_chip(self.place - 1, self.chips) * 2 + self.core,
        )
        self.events = (self.chips - 1) * len(pieces)

    @staticmethod
    def scratch(devices, count):
        dma = pltpu.SemaphoreType.DMA
        chips = devices // 2
        return [dma((count,))] + [dma((count, amount, 2)) for amount in (chips - 1, chips - 1, chips, chips)]

    def barrier(self, others=()):
        semaphore = pltpu.get_barrier_semaphore()
        everyone = [(self.next[0], self.side), (self.next[1], self.side), (self.partner, self.side), *others]
        for other in everyone:
            pl.semaphore_signal(semaphore, inc=1, device_id=other, device_id_type=MESH)
        pl.semaphore_wait(semaphore, len(everyone))

    def block(self, index, stage, half):
        source, _, whole, column, width = self.pieces[index]
        rows = source.shape[0]
        owner = ring_chip(self.place - stage if half == 0 else self.place + stage, self.chips) * 2 + self.core
        return whole.at[pl.ds(pl.multiple_of(owner * rows + half * (rows // 2), 16), rows // 2), pl.ds(column, width)]

    def first(self, index, half):
        source, column, _, _, width = self.pieces[index]
        rows = source.shape[0]
        return source.at[pl.ds(half * (rows // 2), rows // 2), pl.ds(column, width)]

    def local(self, index):
        source, start, whole, column, width = self.pieces[index]
        rows = source.shape[0]
        span = pl.ds(pl.multiple_of(self.me * rows, 16), rows)
        return pltpu.make_async_copy(
            source.at[:, pl.ds(start, width)], whole.at[span, pl.ds(column, width)], self.local_sem.at[index]
        )

    def copy(self, index, stage, half, start, across):
        block = self.block(index, stage, half)
        send, recv = (self.give_sem, self.take_sem) if across else (self.send_sem, self.recv_sem)
        return pltpu.make_async_remote_copy(
            src_ref=self.first(index, half) if start else block,
            dst_ref=block,
            send_sem=send.at[index, stage, half],
            recv_sem=recv.at[index, stage, half],
            device_id=(self.partner if across else self.next[half], self.side),
            device_id_type=MESH,
        )

    def each(self):
        return [(index, half) for index in range(len(self.pieces)) for half in range(2)]

    def begin(self):
        for index, half in self.each():
            self.copy(index, 0, half, True, False).start()
        for index, half in self.each():
            self.copy(index, 0, half, True, True).start()
        for index in range(len(self.pieces)):
            self.local(index).start()

    def stage(self, stage, index):
        for half in range(2):
            self.copy(index, stage - 1, half, False, False).wait_recv()

            @pl.when(stage < self.chips - 1)
            def _():
                self.copy(index, stage, half, False, False).start()

            self.copy(index, stage, half, False, True).start()

    def pace(self, step, total):
        count = len(self.pieces)

        def one(event, carry):
            for index in range(count):
                pl.when(lax.rem(event, count) == index)(functools.partial(self.stage, event // count + 1, index))
            return carry

        lax.fori_loop(step * self.events // total, (step + 1) * self.events // total, one, 0)

    def finish(self):
        for index in range(len(self.pieces)):
            self.local(index).wait()
        for index, half in self.each():
            self.copy(index, 0, half, True, False).wait_send()
            self.copy(index, 0, half, True, True).wait()

        def sent(stage, carry):
            for index, half in self.each():
                self.copy(index, stage, half, False, False).wait_send()
            return carry

        lax.fori_loop(1, self.chips - 1, sent, 0)

        def gave(stage, carry):
            for index, half in self.each():
                self.copy(index, stage, half, False, True).wait()
            return carry

        lax.fori_loop(1, self.chips, gave, 0)


def first_gather(w_query, w_key, w_value, w_out, gains, tokens, w_gate_t, w_up_t, w_down, identity):
    devices = lax.axis_size("dp")
    sides = lax.axis_size("tensor")
    rows, columns = w_query.shape
    units = w_down.shape[0]
    tiles = (units + TILE - 1) // TILE
    padded, late = tiles * TILE, LATE * TILE
    some = padded - late
    span = tokens.shape[0] // 2

    def kernel(q_ref, k_ref, v_ref, o_hbm, gains_ref, tokens_ref, gate_hbm, up_hbm, down_hbm, attn_ref, all_ref, near, far, early_hbm, late_hbm, o_in, o_turned, gate_in, up_in, down_in, early_pack, late_pack, load_sem, store_sem, far_send, far_recv, near_send, near_recv, *scratch):
        pieces = [(ref, 0, attn_ref, number * columns, columns) for number, ref in enumerate((q_ref, k_ref, v_ref, o_turned))]
        spread = Spread(devices, [*pieces, (gains_ref, 0, all_ref, 0, gains_ref.shape[1])], scratch)
        me, side, core = spread.me, spread.side, spread.core
        across = lax.rem(side + 1, sides)
        later, before = lax.rem(me + 2, devices), lax.rem(me + devices - 2, devices)
        parts = (gate_in, up_in, down_in)
        brought = loads(
            (o_hbm, gate_hbm, up_hbm, down_hbm), (o_in, *[part.at[pl.ds(0, units)] for part in parts]), load_sem
        )
        stored = loads((early_pack, late_pack), (early_hbm, late_hbm), store_sem)
        for copy in brought:
            copy.start()
        spread.barrier(((me, across), (later, side), (before, side)))

        def described(source, target, send, recv, other):
            return pltpu.make_async_remote_copy(
                src_ref=source, dst_ref=target, send_sem=send, recv_sem=recv, device_id=other, device_id_type=MESH
            )

        def half_rows(ref, which):
            return ref.at[pl.ds(pl.multiple_of(which * span, span), span)]

        far_copy = described(half_rows(tokens_ref, side), half_rows(far, side), far_send.at[0], far_recv.at[0], (later, side))
        cross_copy = described(half_rows(far, side), half_rows(far, side), far_send.at[1], far_recv.at[1], (me, across))

        def near_copy(source, which, slot):
            return described(half_rows(source, which), half_rows(near, which), near_send.at[slot], near_recv.at[slot], (spread.partner, side))

        own_near = [near_copy(tokens_ref, which, which) for which in range(2)]
        far_near = [near_copy(far, which, slot) for slot, which in enumerate((side, across))]

        brought[0].wait()
        o_turned[...] = o_in[...].T
        spread.begin()

        @pl.when(me < devices - 2)
        def _():
            far_copy.start()

        @pl.when(core == 0)
        def _():
            for copy in own_near:
                copy.start()

        for number, part in enumerate(parts):
            brought[1 + number].wait()
            part[units:, :] = jnp.zeros((padded - units, rows), BF)
            made = part[...].T
            early_pack[:, number * some : (number + 1) * some] = made[:, :some]
            late_pack[:, number * late : (number + 1) * late] = made[:, some:]
        for copy in stored:
            copy.start()

        def one(stage, carry):
            for index in range(len(pieces) + 1):
                spread.stage(stage, index)

            @pl.when((stage == spread.chips // 2) & (me >= 2))
            def _():
                far_copy.wait_recv()
                cross_copy.start()

                @pl.when(core == 1)
                def _():
                    far_near[0].start()

            @pl.when((stage == spread.chips - 2) & (me >= 2))
            def _():
                cross_copy.wait_recv()

                @pl.when(core == 1)
                def _():
                    far_near[1].start()

            return carry

        lax.fori_loop(1, spread.chips, one, 0)
        for copy in stored:
            copy.wait()
        spread.finish()

        @pl.when(me < devices - 2)
        def _():
            far_copy.wait_send()

        @pl.when(me >= 2)
        def _():
            cross_copy.wait_send()

            @pl.when(core == 1)
            def _():
                for copy in far_near:
                    copy.wait_send()

        @pl.when(core == 0)
        def _():
            for copy in own_near:
                copy.wait_send()

        @pl.when((core == 1) | (me >= 2))
        def _():
            for copy in own_near:
                copy.wait_recv()

    dma = pltpu.SemaphoreType.DMA
    any_space = pl.BlockSpec(memory_space=pl.ANY)
    low = functools.partial(jax.ShapeDtypeStruct, dtype=BF)
    return pl.pallas_call(
        kernel,
        out_shape=[
            low((rows * devices, 4 * columns)),
            low((gains.shape[0] * devices, gains.shape[1])),
            low(tokens.shape),
            low(tokens.shape),
            low((rows, 3 * some)),
            low((rows, 3 * late)),
        ],
        in_specs=[any_space] * 9,
        out_specs=[any_space] * 6,
        scratch_shapes=[
            pltpu.VMEM(w_out.shape, BF),
            pltpu.VMEM((rows, columns), BF),
            *[pltpu.VMEM((padded, rows), BF)] * 3,
            pltpu.VMEM((rows, 3 * some), BF),
            pltpu.VMEM((rows, 3 * late), BF),
            dma((4,)),
            dma((2,)),
            dma((2,)),
            dma((2,)),
            dma((2,)),
            dma((2,)),
            *Spread.scratch(devices, 5),
        ],
        compiler_params=pltpu.CompilerParams(vmem_limit_bytes=VMEM, collective_id=identity, has_side_effects=True),
        name="first_gather",
    )(w_query, w_key, w_value, w_out, gains, tokens, w_gate_t, w_up_t, w_down)


class Ring:
    AHEAD = 3

    def __init__(self, devices, terms, goals, groups, scratch):
        self.devices, self.chips = devices, devices // 2
        self.terms, self.goals, self.groups = terms, goals, groups
        count = len(terms)
        self.mine, self.taken, self.inbox = scratch[0 : 3 * count : 3], scratch[1 : 3 * count : 3], scratch[2 : 3 * count : 3]
        self.own_sem, self.give_sem, self.take_sem, self.send_sem, self.recv_sem = scratch[3 * count : 3 * count + 5]
        self.me = lax.axis_index("dp")
        self.side = lax.axis_index("tensor")
        self.core = lax.rem(self.me, 2)
        self.place = ring_place(self.me // 2, self.chips)
        self.partner = self.me + 1 - 2 * self.core
        self.next = (
            ring_chip(self.place + 1, self.chips) * 2 + self.core,
            ring_chip(self.place - 1, self.chips) * 2 + self.core,
        )
        self.events = (self.chips - 1) * len(groups)

    @staticmethod
    def scratch(devices, shapes):
        chips, count = devices // 2, len(shapes)
        dma = pltpu.SemaphoreType.DMA
        buffers = []
        for rows, width in shapes:
            buffers += [pltpu.VMEM((amount, 2, rows // 2, width), BF) for amount in (chips, chips, chips - 1)]
        return buffers + [dma((count, amount, 2)) for amount in (chips, chips, chips, chips - 1, chips - 1)]

    def barrier(self, others=()):
        semaphore = pltpu.get_barrier_semaphore()
        everyone = [(self.next[0], self.side), (self.next[1], self.side), (self.partner, self.side), *others]
        for other in everyone:
            pl.semaphore_signal(semaphore, inc=1, device_id=other, device_id_type=MESH)
        pl.semaphore_wait(semaphore, len(everyone))

    def block(self, index, stage, half, core):
        at = self.place - 1 - stage if half == 0 else self.place + 1 + stage
        size = self.mine[index].shape[2]
        source, column, width = self.terms[index]
        return source.at[ring_chip(at, self.chips) * 2 + core, pl.ds(half * size, size), pl.ds(column, width)]

    def own(self, index, stage, half):
        return pltpu.make_async_copy(
            self.block(index, stage, half, self.core), self.mine[index].at[stage, half], self.own_sem.at[index, stage, half]
        )

    def given(self, index, stage, half):
        return pltpu.make_async_remote_copy(
            src_ref=self.block(index, stage, half, 1 - self.core),
            dst_ref=self.taken[index].at[stage, half],
            send_sem=self.give_sem.at[index, stage, half],
            recv_sem=self.take_sem.at[index, stage, half],
            device_id=(self.partner, self.side),
            device_id_type=MESH,
        )

    def hop(self, index, stage, half, first):
        source = self.mine[index].at[0, half] if first else self.inbox[index].at[stage - 1, half]
        return pltpu.make_async_remote_copy(
            src_ref=source,
            dst_ref=self.inbox[index].at[stage, half],
            send_sem=self.send_sem.at[index, stage, half],
            recv_sem=self.recv_sem.at[index, stage, half],
            device_id=(self.next[half], self.side),
            device_id_type=MESH,
        )

    def each(self, group=None):
        members = range(len(self.terms)) if group is None else self.groups[group]
        return [(index, half) for index in members for half in range(2)]

    def fetch(self, stage, group):
        for index, half in self.each(group):
            self.given(index, stage, half).start()
            self.own(index, stage, half).start()

    def begin(self):
        for group in range(len(self.groups)):
            self.fetch(0, group)
        for index, half in self.each():
            self.mine[index][0, half] = self.chip_term(index, 0, half).astype(BF)
            self.hop(index, 0, half, True).start()
        for stage in range(1, self.AHEAD + 1):
            for group in range(len(self.groups)):
                self.fetch(stage, group)

    def chip_term(self, index, stage, half):
        self.own(index, stage, half).wait()
        self.given(index, stage, half).wait_recv()
        return self.mine[index][stage, half].astype(F32) + self.taken[index][stage, half].astype(F32)

    def stage(self, stage, group):
        last = self.chips - 1

        @pl.when(stage < last)
        def _():
            for index, half in self.each(group):
                self.hop(index, stage - 1, half, True).wait_recv()
                came = self.inbox[index][stage - 1, half].astype(F32)
                self.inbox[index][stage - 1, half] = (came + self.chip_term(index, stage, half)).astype(BF)
                self.hop(index, stage, half, False).start()

        @pl.when(stage + self.AHEAD < self.chips)
        def _():
            self.fetch(stage + self.AHEAD, group)

        @pl.when(stage == last)
        def _():
            for index, half in self.each(group):
                self.hop(index, last - 1, half, True).wait_recv()
                came = self.inbox[index][last - 1, half].astype(F32)
                size = came.shape[0]
                total = came + self.chip_term(index, last, half)
                goal, column = self.goals[index]
                width = min(goal.shape[1] - column, total.shape[1])
                goal[half * size : (half + 1) * size, column : column + width] = total[:, :width]

    def run(self, first, stop):
        count = len(self.groups)

        def one(event, carry):
            for group in range(count):
                if count == 1:
                    self.stage(event + 1, 0)
                else:
                    pl.when(lax.rem(event, count) == group)(functools.partial(self.stage, event // count + 1, group))
            return carry

        lax.fori_loop(first, stop, one, 0)

    def pace(self, step, costs):
        whole = sum(steps * each for steps, each in costs)

        def done(at):
            spent, before = 0, 0
            for steps, each in costs:
                spent = spent + jnp.minimum(jnp.maximum(at - before, 0), steps) * each
                before += steps
            return spent * self.events // whole

        self.run(done(step), done(step + 1))

    def finish(self):
        for index, half in self.each():
            self.hop(index, 0, half, True).wait_send()

        def sent(stage, carry):
            for index, half in self.each():
                self.hop(index, stage, half, False).wait_send()
            return carry

        lax.fori_loop(1, self.chips - 1, sent, 0)

        def gave(stage, carry):
            for index, half in self.each():
                self.given(index, stage, half).wait_send()
            return carry

        lax.fori_loop(0, self.chips, gave, 0)


def dot_nn(a, b):
    return jnp.dot(a, b, preferred_element_type=F32)


def dot_nt(a, b):
    return lax.dot_general(a, b, (((1,), (1,)), ((), ())), preferred_element_type=F32)


def turned(block, cosine, sine, back):
    other = pltpu.roll(block, E // 2, 1)
    if back:
        return block * cosine - other * sine
    return block * cosine + other * sine


def project(x, w, cosine, sine, own, heads):
    m, k = x.shape
    per = TILE // E
    some = heads // per

    def kernel(x_ref, w_ref, c_ref, s_ref, q_ref, kv_ref):
        step = pl.program_id(0)

        def rotate_to(ref, made, rows):
            for part in range(per):
                piece = slice(part * E, (part + 1) * E)
                ref[:, piece] = turned(made[:, piece], c_ref[rows, :], s_ref[rows, :], False).astype(BF)

        @pl.when(step < some)
        def _():
            rows = slice(m - own, m)
            rotate_to(q_ref, dot_nn(x_ref[rows, :], w_ref[...]), rows)

        @pl.when((step >= some) & (step < 2 * some))
        def _():
            rotate_to(kv_ref, dot_nn(x_ref[...], w_ref[...]), slice(0, m))

        @pl.when(step >= 2 * some)
        def _():
            kv_ref[...] = dot_nn(x_ref[...], w_ref[...]).astype(BF)

    return pl.pallas_call(
        kernel,
        grid=(3 * some,),
        out_shape=[jax.ShapeDtypeStruct((own, heads * E), BF), jax.ShapeDtypeStruct((m, 2 * heads * E), BF)],
        in_specs=[single((m, k)), pl.BlockSpec((k, TILE), lambda i: (0, i)), single((m, E)), single((m, E))],
        out_specs=[
            pl.BlockSpec((own, TILE), lambda i: (0, jnp.minimum(i, some - 1))),
            pl.BlockSpec((m, TILE), lambda i: (0, jnp.maximum(i - some, 0))),
        ],
        compiler_params=pltpu.CompilerParams(vmem_limit_bytes=VMEM),
        cost_estimate=cost(2 * (own + 2 * m) * k * heads * E, 2 * (m * k + 3 * (m + k) * heads * E)),
        name="project",
    )(x, w, cosine, sine)


def attend(query, kv, places, heads):
    m = query.shape[0]
    blocks = m // QB
    factor = E ** (-0.5) * LOG2E

    def kernel(q_ref, k_ref, v_ref, p_ref, o_ref, probs_ref, bias):
        @pl.when(pl.program_id(0) == 0)
        def _():
            for block in range(blocks):
                key = lax.broadcasted_iota(jnp.int32, (KB, QB), 0) + block * QB
                query = lax.broadcasted_iota(jnp.int32, (KB, QB), 1) + block * QB
                place = p_ref[:, block * QB : (block + 1) * QB]
                allowed = (key <= query + WINDOW) & (key > query) & (key >= query + WINDOW - place)
                bias[block] = jnp.where(allowed, 0.0, -1e30)

        values_t = v_ref[...].T
        for block in range(blocks):
            span = slice(block * QB, block * QB + KB)
            scores = dot_nt(k_ref[span, :], q_ref[block * QB : (block + 1) * QB, :]) * factor + bias[block]
            largest = jnp.max(scores, axis=0, keepdims=True)
            grown = jnp.exp2(scores - largest)
            inverse = 1.0 / jnp.sum(grown, axis=0, keepdims=True)
            probs = (grown * inverse).astype(BF)
            probs_ref[0, block] = probs
            mixed_t = dot_nn(values_t[:, span], probs)
            o_ref[block * QB : (block + 1) * QB, :] = mixed_t.T.astype(BF)

    head = pl.BlockSpec((m, E), lambda i: (0, i))
    reach = kv.shape[0]

    return pl.pallas_call(
        kernel,
        grid=(heads,),
        out_shape=[
            jax.ShapeDtypeStruct((m, heads * E), BF),
            jax.ShapeDtypeStruct((heads, blocks, KB, QB), BF),
        ],
        in_specs=[
            head,
            pl.BlockSpec((reach, E), lambda i: (0, i)),
            pl.BlockSpec((reach, E), lambda i: (0, i + heads)),
            whole_spec((1, m)),
        ],
        out_specs=[head, pl.BlockSpec((1, blocks, KB, QB), lambda i: (i, 0, 0, 0))],
        scratch_shapes=[pltpu.VMEM((blocks, KB, QB), F32)],
        compiler_params=pltpu.CompilerParams(vmem_limit_bytes=VMEM),
        cost_estimate=cost(4 * heads * m * KB * E * 2, 2 * heads * m * KB, heads * m * KB),
        name="attend",
    )(query, kv, kv, places)


def attend_back(query, kv, probs, mixed, w_attn, hidden, gain, d_normed, d_normed_other, cotangent, cosine, sine, flip, act_early, act_late, w_ffn, rest, ring_source, heads, out_width, identity):
    m, width = hidden.shape
    firsts = m // ROWS
    devices, rows, ring_width = ring_source.shape[1:]
    blocks = m // QB
    factor = E ** (-0.5)
    reach = WINDOW + m
    columns = heads * E
    some, late = act_early.shape[1], act_late.shape[1]
    sides = lax.axis_size("tensor")

    def kernel(q_ref, k_ref, v_ref, p_ref, x_ref, w_ref, h_ref, gain_ref, dn_ref, do_ref, y_ref, c_hbm, s_hbm, flip_hbm, ae_hbm, al_hbm, wd_ref, rd_ref, source, dq_ref, dk_ref, dv_ref, out_ref, sum_ref, flipped_ref, dh_ref, gain_out, sent_ref, got, c_ref, s_ref, flip_ref, ae_ref, al_ref, load_sem, sent, y_send, y_recv, g_ref, gt_ref, keys_sum, values_sum, *scratch):
        step = pl.program_id(0)
        half = ring_width // 2
        ring = Ring(devices, [(source.at[0], 0, half), (source.at[0], half, half)], [(sum_ref, 0), (sum_ref, half)], [[0], [1]], scratch)
        brought = loads((c_hbm, s_hbm, flip_hbm, ae_hbm, al_hbm), (c_ref, s_ref, flip_ref, ae_ref, al_ref), load_sem)
        other = (ring.me, lax.rem(ring.side + 1, sides))

        def across(which):
            return pltpu.make_async_remote_copy(
                src_ref=sent.at[which], dst_ref=got.at[:, pl.ds(pl.multiple_of(which * TILE, TILE), TILE)],
                send_sem=y_send.at[which], recv_sem=y_recv.at[which], device_id=other, device_id_type=MESH,
            )

        turns = [(firsts + 2 * heads, 1)]

        @pl.when(step == 0)
        def _():
            for copy in brought:
                copy.start()
            ring.barrier((other,))
            ring.begin()

        @pl.when(step == firsts)
        def _():
            for copy in brought:
                copy.wait()

        @pl.when(step < firsts)
        def _():
            change, gain_part = norm_grad(h_ref[...], gain_ref[...], dn_ref[...].astype(F32) + do_ref[...].astype(F32))
            total = y_ref[...].astype(F32) + change
            low = total.astype(BF)
            dh_ref[...] = total
            here = pl.ds(pl.multiple_of(step * ROWS, ROWS), ROWS)
            g_ref[here, :] = low
            gt_ref[:, here] = low.T

            @pl.when(step == 0)
            def _():
                gain_out[...] = gain_part

            @pl.when(step > 0)
            def _():
                gain_out[...] += gain_part

            ring.pace(step, turns)

        @pl.when(step >= firsts)
        def _():
            head = step - firsts

            @pl.when(head < SOON)
            def _():
                down = (dot_nt(ae_ref[...], wd_ref[...]) + dot_nt(al_ref[...], rd_ref[...])).astype(BF)
                sent[head] = down
                sent_ref[...] = down
                across(head).start()

            grad_all = dot_nn(g_ref[...], w_ref[...]).astype(BF)
            out_ref[...] = dot_nn(gt_ref[...], x_ref[...]).astype(BF)
            keys_t = k_ref[...].T
            keys_sum[...] = jnp.zeros_like(keys_sum)
            values_sum[...] = jnp.zeros_like(values_sum)
            for block in range(blocks):
                span = slice(block * QB, block * QB + KB)
                here = slice(block * QB, (block + 1) * QB)
                there = slice(WINDOW + block * QB, WINDOW + (block + 1) * QB)
                low = p_ref[0, block]
                grad = grad_all[here, :]
                d_probs = dot_nt(v_ref[span, :], grad)
                weighted = low.astype(F32) * d_probs
                total = jnp.sum(weighted, axis=0, keepdims=True)
                d_scores = (weighted - low.astype(F32) * total).astype(BF)
                values_sum[span, :] += dot_nn(low, grad)
                keys_sum[span, :] += dot_nn(d_scores, q_ref[here, :])
                d_query = dot_nn(keys_t[:, span], d_scores).T * factor
                dq_ref[here, :] = turned(d_query, c_ref[there, :], s_ref[there, :], True).astype(BF)
                if block == 0:
                    ring.pace(firsts + 2 * head, turns)
            dk_ref[...] = turned(keys_sum[...] * factor, c_ref[...], s_ref[...], True).astype(BF)
            dv_ref[...] = values_sum[...].astype(BF)
            ring.pace(firsts + 2 * head + 1, turns)

            @pl.when(head == 1)
            def _():
                flipped_ref[...] = flip_ref[...].T[: flipped_ref.shape[0]]

            @pl.when(head == heads - 1)
            def _():
                for which in range(SOON):
                    across(which).wait()
                ring.finish()

    def at(i):
        return jnp.maximum(i - firsts, 0)

    head_spec = pl.BlockSpec((m, E), lambda i: (0, at(i)))
    long_spec = pl.BlockSpec((reach, E), lambda i: (0, at(i)))
    rows_spec = pl.BlockSpec((ROWS, width), lambda i: (jnp.minimum(i, firsts - 1), 0))
    dma = pltpu.SemaphoreType.DMA

    def soon(i):
        return jnp.minimum(at(i), SOON - 1)

    any_space = pl.BlockSpec(memory_space=pl.ANY)
    return pl.pallas_call(
        kernel,
        grid=(firsts + heads,),
        out_shape=[
            jax.ShapeDtypeStruct((m, columns), BF),
            jax.ShapeDtypeStruct((reach, columns), BF),
            jax.ShapeDtypeStruct((reach, columns), BF),
            jax.ShapeDtypeStruct((width, columns), BF),
            jax.ShapeDtypeStruct((rows, out_width), F32),
            jax.ShapeDtypeStruct((out_width, rows), F32),
            jax.ShapeDtypeStruct((m, width), F32),
            jax.ShapeDtypeStruct((1, width), F32),
            jax.ShapeDtypeStruct((m, SOON * TILE), BF),
            jax.ShapeDtypeStruct((m, SOON * TILE), BF),
        ],
        in_specs=[
            head_spec,
            long_spec,
            pl.BlockSpec((reach, E), lambda i: (0, at(i) + heads)),
            pl.BlockSpec((1, blocks, KB, QB), lambda i: (at(i), 0, 0, 0)),
            head_spec,
            pl.BlockSpec((width, E), lambda i: (0, at(i) + 3 * heads)),
            rows_spec,
            single((1, width)),
            rows_spec,
            rows_spec,
            rows_spec,
            any_space, any_space, any_space, any_space, any_space,
            pl.BlockSpec((TILE, some), lambda i: (soon(i), 2)),
            pl.BlockSpec((TILE, late), lambda i: (soon(i), 2)),
            any_space,
        ],
        out_specs=[
            head_spec,
            long_spec,
            long_spec,
            pl.BlockSpec((width, E), lambda i: (0, at(i))),
            single((rows, out_width)),
            single((out_width, rows)),
            rows_spec,
            single((1, width)),
            pl.BlockSpec((m, TILE), lambda i: (0, soon(i))),
            any_space,
        ],
        scratch_shapes=[
            pltpu.VMEM((reach, E), F32), pltpu.VMEM((reach, E), F32), pltpu.VMEM(flip.shape, F32),
            pltpu.VMEM((m, some), BF), pltpu.VMEM((m, late), BF), dma((5,)),
            pltpu.VMEM((SOON, m, TILE), BF), dma((SOON,)), dma((SOON,)),
            pltpu.VMEM((m, width), BF), pltpu.VMEM((width, m), BF),
            pltpu.VMEM((reach, E), F32), pltpu.VMEM((reach, E), F32),
            *Ring.scratch(devices, [(rows, ring_width // 2)] * 2),
        ],
        compiler_params=pltpu.CompilerParams(vmem_limit_bytes=VMEM, collective_id=identity, has_side_effects=True),
        cost_estimate=cost(8 * heads * m * KB * E * 2, 2 * heads * m * KB),
        name="attend_back",
    )(query, kv, kv, probs, mixed, w_attn, hidden, gain, d_normed, d_normed_other, cotangent, cosine, sine, flip, act_early, act_late, w_ffn, rest, ring_source)


def qkv_back(x_t, d_query, d_key, d_value, w_attn, up_part, out_part, out_width, identity):
    width, reach = x_t.shape
    m, columns = d_query.shape
    devices, rows, up_width = up_part.shape[1:]
    tiles = width // TILE
    per = columns // TILE
    total = tiles + 3 * per
    sides = lax.axis_size("tensor")
    half = m // 2
    piece = up_width // 2
    shapes = [(rows, piece), (rows, piece), (rows, columns)]
    assert 3 * per > tiles and reach == 3 * m

    def kernel(xt_hbm, dq_hbm, dk_hbm, dv_hbm, w_ref, up_ref, out_ref, grad_ref, sent_ref, got, add_ref, up_sum, out_sum, xt_ref, dq_ref, dk_ref, dv_ref, load_sem, sent, early, early_in, near_in, far_in, own_send, own_recv, early_send, early_recv, near_send, near_recv, far_send, far_recv, *scratch):
        step = pl.program_id(0)
        source = up_ref.at[1]
        ring = Ring(
            devices, [(source, 0, piece), (source, piece, piece), (out_ref, 0, columns)], [(up_sum, 0), (up_sum, piece), (out_sum, 0)],
            [[0], [1], [2]], scratch,
        )
        me, side = ring.me, ring.side
        across = lax.rem(side + 1, sides)
        later, before = lax.rem(me + 2, devices), lax.rem(me + devices - 2, devices)
        share = ring.core.astype(F32)
        brought = loads((dq_hbm, dk_hbm, dv_hbm, xt_hbm), (dq_ref, dk_ref, dv_ref, xt_ref), load_sem)

        def remote(source, target, send, recv, which, other):
            return pltpu.make_async_remote_copy(
                src_ref=source, dst_ref=target, send_sem=send.at[which], recv_sem=recv.at[which], device_id=other, device_id_type=MESH
            )

        def own_copy(which):
            target = got.at[:, pl.ds(pl.multiple_of(which * TILE, TILE), TILE)]
            return remote(sent.at[which], target, own_send, own_recv, which, (me, across))

        def early_copy(which):
            return remote(early.at[which, across], early_in.at[which], early_send, early_recv, which, (me, across))

        def near_copy(which):
            return remote(early_in.at[which, 1], near_in.at[which], near_send, near_recv, which, (ring.partner, side))

        def far_copy(which):
            return remote(early_in.at[which, 0], far_in.at[which], far_send, far_recv, which, (before, side))

        @pl.when(step == 0)
        def _():
            for copy in brought:
                copy.start()
            ring.barrier(((me, across), (later, side), (before, side)))
            ring.begin()
            for copy in brought[:3]:
                copy.wait()

        @pl.when(step == tiles)
        def _():
            brought[3].wait()

        @pl.when(step < tiles)
        def _():
            w_key, w_value = w_ref[:, columns : 2 * columns], w_ref[:, 2 * columns :]
            part = dot_nt(dq_ref[...], w_ref[:, :columns])
            part += dot_nt(dk_ref[2 * m :, :], w_key) + dot_nt(dv_ref[2 * m :, :], w_value)
            low = part.astype(BF)
            sent[step] = low
            sent_ref[...] = low
            for block in range(2):
                span = slice(block * m, (block + 1) * m)
                part = (dot_nt(dk_ref[span, :], w_key) + dot_nt(dv_ref[span, :], w_value)).astype(BF)
                for number in range(2):
                    early[step, number, block] = part[number * half : (number + 1) * half]
            early_copy(step).start()

        number = step - tiles

        @pl.when((number >= 0) & (number < tiles))
        def _():
            own_copy(number).start()
            early_copy(number).wait_recv()
            early_in[number] = (early_in[number].astype(F32) + early[number, side].astype(F32)).astype(BF)
            near_copy(number).start()

        @pl.when((number >= 1) & (number <= tiles))
        def _():
            which = number - 1
            near_copy(which).wait_recv()
            early_in[which, 0] = (early_in[which, 0].astype(F32) + near_in[which].astype(F32) * share).astype(BF)

            @pl.when(me >= 2)
            def _():
                far_copy(which).start()

        @pl.when((number >= 0) & (number < per))
        def _():
            here = pl.ds(pl.multiple_of(number * TILE, TILE), TILE)
            grad_ref[...] = dot_nn(xt_ref[:, 2 * m :], dq_ref[:, here]).astype(BF)

        @pl.when((number >= per) & (number < 2 * per))
        def _():
            here = pl.ds(pl.multiple_of((number - per) * TILE, TILE), TILE)
            grad_ref[...] = dot_nn(xt_ref[...], dk_ref[:, here]).astype(BF)

        @pl.when(number >= 2 * per)
        def _():
            here = pl.ds(pl.multiple_of((number - 2 * per) * TILE, TILE), TILE)
            grad_ref[...] = dot_nn(xt_ref[...], dv_ref[:, here]).astype(BF)

        ring.pace(step, [(tiles, 5), (3 * per, 4)])

        @pl.when(step == total - 1)
        def _():
            for which in range(tiles):
                here = slice(which * TILE, (which + 1) * TILE)
                add_ref[:, here] = (near_in[which].astype(F32) * (1.0 - share)).astype(BF)

                @pl.when(me < devices - 2)
                def _():
                    far_copy(which).wait_recv()
                    add_ref[:, here] = (add_ref[:, here].astype(F32) + far_in[which].astype(F32)).astype(BF)

                @pl.when(me >= 2)
                def _():
                    far_copy(which).wait_send()

                near_copy(which).wait_send()
                early_copy(which).wait_send()
                own_copy(which).wait()
            ring.finish()

    any_space = pl.BlockSpec(memory_space=pl.ANY)
    dma = pltpu.SemaphoreType.DMA

    def second(i):
        return jnp.minimum(i, tiles - 1)

    return pl.pallas_call(
        kernel,
        grid=(total,),
        out_shape=[
            jax.ShapeDtypeStruct((width, 3 * columns), BF),
            jax.ShapeDtypeStruct((m, width), BF),
            jax.ShapeDtypeStruct((m, width), BF),
            jax.ShapeDtypeStruct((half, width), BF),
            jax.ShapeDtypeStruct((rows, out_width), F32),
            jax.ShapeDtypeStruct((rows, columns), F32),
        ],
        in_specs=[
            any_space, any_space, any_space, any_space,
            pl.BlockSpec((TILE, 3 * columns), lambda i: (second(i), 0)),
            any_space, any_space,
        ],
        out_specs=[
            pl.BlockSpec((width, TILE), lambda i: (0, jnp.maximum(i - tiles, 0))),
            pl.BlockSpec((m, TILE), lambda i: (0, second(i))),
            any_space,
            single((half, width)),
            single((rows, out_width)),
            single((rows, columns)),
        ],
        scratch_shapes=[
            pltpu.VMEM((width, reach), BF),
            pltpu.VMEM((m, columns), BF),
            pltpu.VMEM((reach, columns), BF),
            pltpu.VMEM((reach, columns), BF),
            dma((4,)),
            pltpu.VMEM((tiles, m, TILE), BF),
            pltpu.VMEM((tiles, 2, 2, half, TILE), BF),
            pltpu.VMEM((tiles, 2, half, TILE), BF),
            pltpu.VMEM((tiles, half, TILE), BF),
            pltpu.VMEM((tiles, half, TILE), BF),
            *[dma((tiles,))] * 8,
            *Ring.scratch(devices, shapes),
        ],
        compiler_params=pltpu.CompilerParams(vmem_limit_bytes=VMEM, collective_id=identity, has_side_effects=True),
        cost_estimate=cost(4 * (m + 2 * reach) * width * columns, 12 * width * columns),
        name="qkv_back",
    )(x_t, d_query, d_key, d_value, w_attn, up_part, out_part)


def tiles_of(width):
    return width // TILE


def root_of(rows):
    return lax.rsqrt(jnp.mean(rows * rows, axis=-1, keepdims=True) + EPS)


def norm_grad(rows, gain, grad):
    root = root_of(rows)
    pushed = grad * gain
    inner = jnp.mean(pushed * rows, axis=-1, keepdims=True)
    return root * pushed - rows * (root * root * root * inner), jnp.sum(grad * rows * root, axis=0, keepdims=True)


def first_norm(far, near, tokens, gain):
    m, width = tokens.shape
    steps = m // ROWS

    def kernel(far_ref, near_ref, x_ref, g_ref, o_ref, t_ref):
        step = pl.program_id(0)
        me = lax.axis_index("dp")

        def normed(ref):
            rows = ref[...].astype(F32)
            return (rows * root_of(rows) * g_ref[...]).astype(BF)

        def earlier(ref, there):
            @pl.when(there)
            def _():
                made = normed(ref)
                o_ref[...] = made
                t_ref[...] = made.T

            @pl.when(jnp.logical_not(there))
            def _():
                o_ref[...] = jnp.zeros_like(o_ref)
                t_ref[...] = jnp.zeros_like(t_ref)

        @pl.when(step < steps)
        def _():
            earlier(far_ref, me >= 2)

        @pl.when((step >= steps) & (step < 2 * steps))
        def _():
            earlier(near_ref, me >= 1)

        @pl.when(step >= 2 * steps)
        def _():
            made = normed(x_ref)
            o_ref[...] = made
            t_ref[...] = made.T

    def part(which):
        return pl.BlockSpec((ROWS, width), lambda i: (jnp.clip(i - which * steps, 0, steps - 1), 0))

    return pl.pallas_call(
        kernel,
        grid=(3 * steps,),
        out_shape=[jax.ShapeDtypeStruct((3 * m, width), BF), jax.ShapeDtypeStruct((width, 3 * m), BF)],
        in_specs=[part(0), part(1), part(2), whole_spec((1, width))],
        out_specs=[
            pl.BlockSpec((ROWS, width), lambda i: (i, 0)),
            pl.BlockSpec((width, ROWS), lambda i: (0, i)),
        ],
        compiler_params=pltpu.CompilerParams(vmem_limit_bytes=VMEM),
        cost_estimate=cost(24 * m * width, 14 * m * width),
        name="first_norm",
    )(far, near, tokens, gain)


def out_norm(mixed, w_attn, place, tokens, gain, identity):
    m, columns = mixed.shape
    width = tokens.shape[1]
    steps = m // ROWS
    sides = lax.axis_size("tensor")

    def kernel(x_ref, w_ref, r_ref, g_ref, hidden_ref, normed_ref, turned_ref, sent, got, send, recv):
        step = pl.program_id(0)
        other = (lax.axis_index("dp"), lax.rem(lax.axis_index("tensor") + 1, sides))

        @pl.when(step == 0)
        def _():
            semaphore = pltpu.get_barrier_semaphore()
            pl.semaphore_signal(semaphore, inc=1, device_id=other, device_id_type=MESH)
            pl.semaphore_wait(semaphore, 1)

        def across(which):
            return pltpu.make_async_remote_copy(
                src_ref=sent.at[which], dst_ref=got.at[which], send_sem=send.at[which], recv_sem=recv.at[which],
                device_id=other, device_id_type=MESH,
            )

        @pl.when(step < steps)
        def _():
            sent[step] = dot_nt(x_ref[...], w_ref[...]).astype(BF)
            across(step).start()

        @pl.when(step >= steps)
        def _():
            which = step - steps
            across(which).wait()
            hidden = r_ref[...].astype(F32) + (sent[which].astype(F32) + got[which].astype(F32))
            normed = (hidden * root_of(hidden) * g_ref[...]).astype(BF)
            hidden_ref[...] = hidden
            normed_ref[...] = normed
            turned_ref[...] = normed.T

    def late(i):
        return jnp.maximum(i - steps, 0)

    late_rows = pl.BlockSpec((ROWS, width), lambda i: (late(i), 0))
    dma = pltpu.SemaphoreType.DMA
    return pl.pallas_call(
        kernel,
        grid=(2 * steps,),
        out_shape=[
            jax.ShapeDtypeStruct((m, width), F32),
            jax.ShapeDtypeStruct((m, width), BF),
            jax.ShapeDtypeStruct((width, m), BF),
        ],
        in_specs=[
            pl.BlockSpec((ROWS, columns), lambda i: (jnp.minimum(i, steps - 1), 0)),
            pl.BlockSpec((width, columns), lambda i: (0, place), pipeline_mode=pl.Buffered(1)),
            late_rows,
            single((1, width)),
        ],
        out_specs=[late_rows, late_rows, pl.BlockSpec((width, ROWS), lambda i: (0, late(i)))],
        scratch_shapes=[pltpu.VMEM((steps, ROWS, width), BF), pltpu.VMEM((steps, ROWS, width), BF), dma((steps,)), dma((steps,))],
        compiler_params=pltpu.CompilerParams(vmem_limit_bytes=VMEM, collective_id=identity, has_side_effects=True),
        cost_estimate=cost(2 * m * width * columns, 12 * m * width),
        name="out_norm",
    )(mixed, w_attn, tokens, gain)


def last_pass(tokens, gain, grad, grad_other, grad_add, d_hidden, hidden, ffn_part, ffn_other, act_early, act_late, w_ffn, rest, gain_ffn_grad, flip, qkv_part, lanes, identity):
    m, width = tokens.shape
    devices, rows, all_columns = qkv_part.shape
    columns = all_columns // 3
    chips = devices // 2
    size = ROWS // 2
    steps = m // size
    downs = tiles_of(width) - SOON
    total = downs + steps + chips
    names = 3
    half = m // 2
    tiles = tiles_of(width)
    some, late = act_early.shape[1], act_late.shape[1]
    sides = lax.axis_size("tensor")
    assert chips >= tiles

    def kernel(x_ref, g_ref, dn_ref, do_ref, add_hbm, dh_ref, h_ref, fp_ref, fo_ref, a_hbm, al_hbm, w_ref, rest_ref, gf_ref, flip_hbm, source, grad_ref, layer_ref, flipped_ref, q_ref, k_ref, v_ref, gains_ref, a_ref, al_ref, flip_ref, add, load_sem, add_send, add_recv, gain_sum, gain_source, gain_in, gain_send, gain_recv, sent, got, y_send, y_recv, *scratch):
        step = pl.program_id(0)
        ring = Ring(
            devices, [(source, number * columns, columns) for number in range(names)], [(q_ref, 0), (k_ref, 0), (v_ref, 0)],
            [[0], [1], [2]], scratch,
        )

        def gain_copy(away):
            owner = lax.rem(ring.me + away, devices)
            return pltpu.make_async_remote_copy(
                src_ref=gain_source.at[owner], dst_ref=gain_in.at[away], send_sem=gain_send.at[away], recv_sem=gain_recv.at[away],
                device_id=(owner, ring.side), device_id_type=MESH,
            )

        other = (ring.me, lax.rem(ring.side + 1, sides))
        brought = loads((a_hbm, al_hbm, flip_hbm, add_hbm), (a_ref, al_ref, flip_ref, add.at[ring.side]), load_sem)
        add_copy = pltpu.make_async_remote_copy(
            src_ref=add_hbm, dst_ref=add.at[ring.side], send_sem=add_send, recv_sem=add_recv, device_id=other, device_id_type=MESH
        )
        row_step = step - downs
        end_step = step - downs - steps

        def across(which):
            return pltpu.make_async_remote_copy(
                src_ref=sent.at[which], dst_ref=got.at[which], send_sem=y_send.at[which], recv_sem=y_recv.at[which],
                device_id=other, device_id_type=MESH,
            )

        @pl.when(step == 0)
        def _():
            for copy in brought:
                copy.start()
            ring.barrier((other, *[(lax.rem(ring.me + away, devices), ring.side) for away in range(1, devices)]))
            add_copy.start()
            ring.begin()
            for copy in brought:
                copy.wait()
            flipped_ref[...] = flip_ref[...].T

        @pl.when(row_step == 0)
        def _():
            add_copy.wait()

        @pl.when(step < downs)
        def _():
            sent[step] = (dot_nt(a_ref[...], w_ref[...]) + dot_nt(al_ref[...], rest_ref[...])).astype(BF)
            across(step).start()

        @pl.when((row_step >= 0) & (row_step < steps))
        def _():
            which = row_step * size // half
            here = pl.ds(pl.multiple_of(row_step * size - which * half, size), size)
            grad_rows = dn_ref[...].astype(F32) + do_ref[...].astype(F32) + add[which, here, :].astype(F32)
            change, gain_part = norm_grad(x_ref[...].astype(F32), g_ref[...], grad_rows)
            grad_ref[...] = dh_ref[...] + change

            @pl.when(row_step == 0)
            def _():
                gain_sum[...] = gain_part

            @pl.when(row_step > 0)
            def _():
                gain_sum[...] += gain_part

        @pl.when(row_step == steps - 1)
        def _():
            gain_source[...] = jnp.zeros_like(gain_source)
            for device in range(devices):
                span = slice(device * rows, (device + 1) * rows)
                gain_source[device, :16, :rows] = jnp.broadcast_to(gain_sum[:, span], (16, rows)).astype(BF)
                gain_source[device, 16:, :rows] = jnp.broadcast_to(gf_ref[:, span], (16, rows)).astype(BF)

            def send(away, carry):
                gain_copy(away).start()
                return carry

            lax.fori_loop(1, devices, send, 0)

        ring.pace(step, [(downs, 5), (steps, 3), (chips, 3)])

        @pl.when((end_step >= 0) & (end_step < SOON))
        def _():
            layer_ref[...] = (h_ref[...] + (fp_ref[...].astype(F32) + fo_ref[...].astype(F32))).astype(BF)

        @pl.when((end_step >= SOON) & (end_step < tiles))
        def _():
            which = end_step - SOON
            across(which).wait()
            layer_ref[...] = (h_ref[...] + (sent[which].astype(F32) + got[which].astype(F32))).astype(BF)

        @pl.when(step == total - 1)
        def _():
            ring.finish()

            def take(away, total):
                gain_copy(away).wait()
                return total + gain_in[away].astype(F32)

            gains_ref[...] = lax.fori_loop(1, devices, take, gain_source[ring.me].astype(F32))

    def early(i):
        return jnp.minimum(i, downs - 1) + SOON

    def ending(i):
        return jnp.clip(i - downs - steps, 0, tiles - 1)

    rows_spec = pl.BlockSpec((size, width), lambda i: (jnp.clip(i - downs, 0, steps - 1), 0))
    tile_spec = pl.BlockSpec((m, TILE), lambda i: (0, ending(i)))
    soon_spec = pl.BlockSpec((m, TILE), lambda i: (0, jnp.minimum(ending(i), SOON - 1)))
    dma = pltpu.SemaphoreType.DMA
    sums = jax.ShapeDtypeStruct((rows, columns), F32)
    return pl.pallas_call(
        kernel,
        grid=(total,),
        out_shape=[
            jax.ShapeDtypeStruct((m, width), F32),
            jax.ShapeDtypeStruct((m, width), BF),
            jax.ShapeDtypeStruct((flip.shape[1], flip.shape[0]), F32),
            sums, sums, sums,
            jax.ShapeDtypeStruct((32, lanes), F32),
        ],
        in_specs=[
            rows_spec, single((1, width)), rows_spec, rows_spec, pl.BlockSpec(memory_space=pl.ANY), rows_spec, tile_spec, soon_spec, soon_spec, pl.BlockSpec(memory_space=pl.ANY), pl.BlockSpec(memory_space=pl.ANY),
            pl.BlockSpec((TILE, some), lambda i: (early(i), 2)), pl.BlockSpec((TILE, late), lambda i: (early(i), 2)), single((1, width)),
            pl.BlockSpec(memory_space=pl.ANY), pl.BlockSpec(memory_space=pl.ANY),
        ],
        out_specs=[
            rows_spec, tile_spec, single((flip.shape[1], flip.shape[0])),
            single(sums.shape), single(sums.shape), single(sums.shape), single((32, lanes)),
        ],
        scratch_shapes=[
            pltpu.VMEM((m, some), BF),
            pltpu.VMEM((m, late), BF),
            pltpu.VMEM(flip.shape, F32),
            pltpu.VMEM((2, half, width), BF),
            dma((4,)),
            dma,
            dma,
            pltpu.VMEM((1, width), F32),
            pltpu.VMEM((devices, 32, lanes), BF),
            pltpu.VMEM((devices, 32, lanes), BF),
            dma((devices,)),
            dma((devices,)),
            pltpu.VMEM((downs, m, TILE), BF),
            pltpu.VMEM((downs, m, TILE), BF),
            dma((downs,)),
            dma((downs,)),
            *Ring.scratch(devices, [(rows, columns)] * names),
        ],
        compiler_params=pltpu.CompilerParams(vmem_limit_bytes=VMEM, collective_id=identity, has_side_effects=True),
        cost_estimate=cost(20 * m * width, 24 * m * width),
        name="last_pass",
    )(tokens, gain, grad, grad_other, grad_add, d_hidden, hidden, ffn_part, ffn_other, act_early, act_late, w_ffn, rest, gain_ffn_grad, flip, qkv_part)


def feed_tile(x_ref, dy_ref, dyt_ref, g_ref, u_ref, d_ref, act_ref, both_ref, down_ref):
    gate = dot_nn(x_ref[...], g_ref[...])
    up = dot_nn(x_ref[...], u_ref[...])
    d_act = dot_nn(dy_ref[...], d_ref[...])
    soft = 1.0 / (1.0 + jnp.exp(-gate))
    silu = gate * soft
    act = (silu * up).astype(BF)
    act_ref[...] = act
    both_ref[0] = (d_act * up * (soft * (1.0 + gate * (1.0 - soft)))).astype(BF)
    both_ref[1] = (d_act * silu).astype(BF)
    down_ref[...] = dot_nn(dyt_ref[...], act).astype(BF)


def feed(x, dy, dy_t, w, block, tiles, identity):
    m, k = x.shape
    early = tiles - LATE
    devices = lax.axis_size("dp")
    width = block.shape[1] // 2

    def kernel(x_hbm, dy_hbm, dyt_hbm, g_ref, u_ref, d_ref, block_ref, act_ref, both_ref, down_ref, rest_ref, x_ref, dy_ref, dyt_ref, load_sem, *scratch):
        step = pl.program_id(0)
        brought = loads((x_hbm, dy_hbm, dyt_hbm), (x_ref, dy_ref, dyt_ref), load_sem)
        spread = Spread(devices, [(block_ref, 0, rest_ref, 0, width), (block_ref, width, rest_ref, width, width)], scratch)

        @pl.when(step == 0)
        def _():
            for copy in brought:
                copy.start()
            spread.barrier()
            spread.begin()
            for copy in brought:
                copy.wait()

        feed_tile(x_ref, dy_ref, dyt_ref, g_ref, u_ref, d_ref, act_ref, both_ref, down_ref)
        spread.pace(step, early)

        @pl.when(step == early - 1)
        def _():
            spread.finish()

    any_space = pl.BlockSpec(memory_space=pl.ANY)
    return pl.pallas_call(
        kernel,
        grid=(early,),
        out_shape=[
            jax.ShapeDtypeStruct((m, early * TILE), BF),
            jax.ShapeDtypeStruct((2, m, early * TILE), BF),
            jax.ShapeDtypeStruct((k, early * TILE), BF),
            jax.ShapeDtypeStruct((k, block.shape[1]), BF),
        ],
        in_specs=[
            any_space, any_space, any_space,
            pl.BlockSpec((k, TILE), lambda i: (0, i)),
            pl.BlockSpec((k, TILE), lambda i: (0, i + early)),
            pl.BlockSpec((k, TILE), lambda i: (0, i + 2 * early)),
            any_space,
        ],
        out_specs=[
            pl.BlockSpec((m, TILE), lambda i: (0, i)),
            pl.BlockSpec((2, m, TILE), lambda i: (0, 0, i)),
            pl.BlockSpec((k, TILE), lambda i: (0, i)),
            any_space,
        ],
        scratch_shapes=[
            pltpu.VMEM((m, k), BF), pltpu.VMEM((m, k), BF), pltpu.VMEM((k, m), BF), pltpu.SemaphoreType.DMA((3,)),
            *Spread.scratch(devices, 2),
        ],
        compiler_params=pltpu.CompilerParams(vmem_limit_bytes=VMEM, collective_id=identity, has_side_effects=True),
        cost_estimate=cost(8 * m * k * early * TILE, 8 * (m + k) * early * TILE, m * early * TILE),
        name="feed",
    )(x, dy, dy_t, w, w, w, block)


def ffn_back(x, x_t, dy, dy_t, d_early, w_ffn, rest, down_early, identity):
    m, width = x.shape
    devices, rows, some = down_early.shape
    late = LATE * TILE
    padded = some + late
    tiles = width // TILE
    wide = 2 * TILE
    early_wide, late_wide = some // wide, (late + wide - 1) // wide
    grads = 2 * (early_wide + late_wide)
    total = LATE + tiles + grads
    sides = lax.axis_size("tensor")
    pieces = [(rows, some // 2)] * 2

    def kernel(x_hbm, xt_hbm, dy_hbm, dyt_hbm, rg_ref, ru_ref, rd_ref, d_hbm, tile_ref, wg_ref, wu_ref, lg_ref, lu_ref, source, act_ref, grad_ref, sent_ref, got, sum_ref, x_ref, xt_ref, dy_ref, dyt_ref, d_ref, load_sem, d_late, down_late, down_tile, both_tile, sent, y_send, y_recv, *scratch):
        step = pl.program_id(0)
        brought = loads((x_hbm, dy_hbm, dyt_hbm, d_hbm, xt_hbm), (x_ref, dy_ref, dyt_ref, d_ref, xt_ref), load_sem)
        ring = Ring(devices, [(source, 0, some // 2), (source, some // 2, some // 2)], [(sum_ref, 0), (sum_ref, some // 2)], [[0], [1]], scratch[:11])
        late_ring = Ring(devices, [(down_late, 0, late)], [(sum_ref, some)], [[0]], scratch[11:])
        other = (ring.me, lax.rem(ring.side + 1, sides))

        def across(which):
            return pltpu.make_async_remote_copy(
                src_ref=sent.at[which], dst_ref=got.at[:, pl.ds(pl.multiple_of(which * TILE, TILE), TILE)],
                send_sem=y_send.at[which], recv_sem=y_recv.at[which], device_id=other, device_id_type=MESH,
            )

        @pl.when(step == 0)
        def _():
            for copy in brought:
                copy.start()
            ring.barrier((other,))
            ring.begin()
            for copy in brought[:3]:
                copy.wait()

        @pl.when(step == LATE)
        def _():
            brought[3].wait()

        @pl.when(step == LATE + tiles)
        def _():
            brought[4].wait()

        @pl.when(step < LATE)
        def _():
            feed_tile(x_ref, dy_ref, dyt_ref, rg_ref, ru_ref, rd_ref, act_ref, both_tile, down_tile)
            here = pl.ds(pl.multiple_of(step * TILE, TILE), TILE)
            d_late[:, :, here] = both_tile[...]
            down_late[:, :, here] = down_tile[...].reshape(devices, rows, TILE)

        @pl.when(step == LATE - 1)
        def _():
            late_ring.begin()

        @pl.when((step >= LATE) & (step < LATE + tiles))
        def _():
            which = step - LATE
            part = dot_nt(d_ref[0], wg_ref[...]) + dot_nt(d_ref[1], wu_ref[...])
            part += dot_nt(d_late[0], lg_ref[...]) + dot_nt(d_late[1], lu_ref[...])
            low = part.astype(BF)
            sent[which] = low
            sent_ref[...] = low
            across(which).start()

        @pl.when((step >= LATE + tiles) & (step < LATE + tiles + 2 * early_wide))
        def _():
            grad_ref[0] = dot_nn(xt_ref[...], tile_ref[0]).astype(BF)

        number = step - (LATE + tiles + 2 * early_wide)
        for part in range(late_wide):
            several = min(wide, late - part * wide)

            @pl.when((number >= 0) & (lax.rem(number, late_wide) == part))
            def _():
                piece = d_late[number // late_wide, :, part * wide : part * wide + several]
                grad_ref[0, :, :several] = dot_nn(xt_ref[...], piece).astype(BF)

        ring.pace(step, [(LATE, 12), (tiles, 8), (grads, 7)])
        late_ring.pace(step, [(LATE, 0), (tiles, 8), (grads, 7)])

        @pl.when(step == total - 1)
        def _():
            for which in range(tiles):
                across(which).wait()
            ring.finish()
            late_ring.finish()

    def first(i):
        return jnp.minimum(i, LATE - 1)

    def second(i):
        return jnp.clip(i - LATE, 0, tiles - 1)

    def third(i):
        at = jnp.clip(i - LATE - tiles, 0, 2 * early_wide - 1)
        return (at // early_wide, 0, at % early_wide)

    def grad_at(i):
        at = jnp.maximum(i - LATE - tiles, 0)
        more = jnp.maximum(at - 2 * early_wide, 0)
        is_late = at // (2 * early_wide)
        return (
            (1 - is_late) * (at // early_wide) + is_late * (more // late_wide),
            0,
            (1 - is_late) * (at % early_wide) + is_late * (early_wide + more % late_wide),
        )

    assert late_wide <= early_wide and some % wide == 0
    any_space = pl.BlockSpec(memory_space=pl.ANY)
    dma = pltpu.SemaphoreType.DMA

    def rest_tile(which):
        return pl.BlockSpec((width, TILE), lambda i: (0, first(i) + which * LATE))

    return pl.pallas_call(
        kernel,
        grid=(total,),
        out_shape=[
            jax.ShapeDtypeStruct((m, late), BF),
            jax.ShapeDtypeStruct((2, width, padded), BF),
            jax.ShapeDtypeStruct((m, width), BF),
            jax.ShapeDtypeStruct((m, width), BF),
            jax.ShapeDtypeStruct((rows, padded), F32),
        ],
        in_specs=[
            any_space, any_space, any_space, any_space,
            rest_tile(0), rest_tile(1), rest_tile(2),
            any_space,
            pl.BlockSpec((1, m, wide), third),
            pl.BlockSpec((TILE, some), lambda i: (second(i), 0)),
            pl.BlockSpec((TILE, some), lambda i: (second(i), 1)),
            pl.BlockSpec((TILE, late), lambda i: (second(i), 0)),
            pl.BlockSpec((TILE, late), lambda i: (second(i), 1)),
            any_space,
        ],
        out_specs=[
            pl.BlockSpec((m, TILE), lambda i: (0, first(i))),
            pl.BlockSpec((1, width, wide), grad_at),
            pl.BlockSpec((m, TILE), lambda i: (0, second(i))),
            any_space,
            single((rows, padded)),
        ],
        scratch_shapes=[
            pltpu.VMEM((m, width), BF),
            pltpu.VMEM((width, m), BF),
            pltpu.VMEM((m, width), BF),
            pltpu.VMEM((width, m), BF),
            pltpu.VMEM((2, m, some), BF),
            dma((5,)),
            pltpu.VMEM((2, m, late), BF),
            pltpu.VMEM((devices, rows, late), BF),
            pltpu.VMEM((width, TILE), BF),
            pltpu.VMEM((2, m, TILE), BF),
            pltpu.VMEM((tiles, m, TILE), BF),
            dma((tiles,)),
            dma((tiles,)),
            *Ring.scratch(devices, pieces),
            *Ring.scratch(devices, [(rows, late)]),
        ],
        compiler_params=pltpu.CompilerParams(vmem_limit_bytes=VMEM, collective_id=identity, has_side_effects=True),
        cost_estimate=cost(8 * m * width * padded + 8 * m * width * late, 10 * width * padded),
        name="ffn_back",
    )(x, x_t, dy, dy_t, rest, rest, rest, d_early, d_early, w_ffn, w_ffn, rest, rest, down_early)


def shards(tokens, positions, attn_gain, w_query, w_key, w_value, w_out, ffn_gain, w_gate, w_up, w_down, cotangent):
    devices = lax.axis_size("dp")
    span = tokens.shape[0]
    assert 2 * span == WINDOW
    own_rows = w_query.shape[0]
    width = tokens.shape[1]
    head_columns = w_query.shape[1]
    heads = head_columns // E
    hidden_units = w_gate.shape[1]
    tiles = (hidden_units + TILE - 1) // TILE
    padded = tiles * TILE

    some = padded - LATE * TILE
    lanes = max(128, own_rows)
    gains = jnp.zeros((32, lanes), BF).at[0, :own_rows].set(attn_gain).at[16, :own_rows].set(ffn_gain)
    w_attn, all_gains, near, far, ffn_pack, rest_pack = first_gather(
        w_query, w_key, w_value, w_out, gains, tokens, w_gate.T, w_up.T, w_down, 0
    )
    w_ffn = lax.all_gather(ffn_pack, "dp", axis=0, tiled=True)
    all_gains = all_gains.reshape(devices, 32, lanes)
    gain_attn = all_gains[:, 0, :own_rows].reshape(1, width).astype(F32)
    gain_ffn = all_gains[:, 16, :own_rows].reshape(1, width).astype(F32)

    frequency = THETA ** (-(jnp.arange(E // 2, dtype=F32) * 2.0 / E))
    earlier = positions[0] - WINDOW + jnp.arange(WINDOW, dtype=jnp.int32)
    angles = jnp.concatenate([earlier, positions]).astype(F32)[:, None] * frequency[None, :]
    cosine_half, sine_half = jnp.cos(angles), jnp.sin(angles)
    cosine = jnp.concatenate([cosine_half, cosine_half], axis=1)
    sine = jnp.concatenate([-sine_half, sine_half], axis=1)

    normed_attn, normed_attn_t = first_norm(far, near, tokens, gain_attn)
    query, kv = project(normed_attn, w_attn, cosine, sine, span, heads)
    mixed, probs = attend(query, kv, positions[None, :], heads)
    hidden, normed_ffn, normed_ffn_t = out_norm(mixed, w_attn, 3, tokens, gain_ffn, 5)

    cotangent_t = cotangent.T
    act_early, d_early, down_early, rest = feed(normed_ffn, cotangent, cotangent_t, w_ffn, rest_pack, tiles, 6)
    act_late, both_part, d_normed_ffn, d_normed_other, down_grad = ffn_back(
        normed_ffn, normed_ffn_t, cotangent, cotangent_t, d_early, w_ffn, rest, down_early.reshape(devices, own_rows, some), 1
    )
    both_part = both_part.reshape(2, devices, own_rows, padded)

    d_query, d_key, d_value, out_part, gate_grad, w_down_grad, d_hidden, gain_ffn_grad, ffn_part, ffn_other = attend_back(
        query, kv, probs, mixed, w_attn, hidden, gain_ffn, d_normed_ffn, d_normed_other, cotangent, cosine, sine, down_grad, act_early, act_late, w_ffn, rest,
        both_part, heads, hidden_units, 2,
    )
    qkv_part, d_normed_attn, d_attn_other, d_attn_add, up_grad, out_grad = qkv_back(
        normed_attn_t, d_query, d_key, d_value, w_attn, both_part, out_part.reshape(devices, own_rows, head_columns), hidden_units, 3
    )
    tokens_grad, layer_out, w_out_grad, query_grad, key_grad, value_grad, gain_grads = last_pass(
        tokens, gain_attn, d_normed_attn, d_attn_other, d_attn_add, d_hidden, hidden, ffn_part, ffn_other, act_early, act_late, w_ffn, rest, gain_ffn_grad, out_grad,
        qkv_part.reshape(devices, own_rows, 3 * head_columns), lanes, 4,
    )
    return (
        layer_out,
        tokens_grad,
        gain_grads[0, :own_rows],
        query_grad,
        key_grad,
        value_grad,
        w_out_grad,
        gain_grads[16, :own_rows],
        gate_grad,
        up_grad,
        w_down_grad,
    )


def solution(mesh):
    by_rows, by_both, turned_both, line = P("dp", None), P("dp", "tensor"), P("tensor", "dp"), P("dp")
    return jax.shard_map(
        shards,
        mesh=mesh,
        in_specs=(by_rows, line, line, by_both, by_both, by_both, turned_both, line, by_both, by_both, turned_both, by_rows),
        out_specs=(by_rows, by_rows, line, by_both, by_both, by_both, turned_both, line, by_both, by_both, turned_both),
        check_vma=False,
    )
```

```python
import functools

import jax
import jax.numpy as jnp
import numpy as np
from jax import lax
from jax.experimental import pallas as pl
from jax.experimental.pallas import tpu as pltpu
from jax.sharding import PartitionSpec as P

E = 128
WINDOW = 1024
EPS = 1e-06
THETA = 10000.0
LOG2E = 1.4426950408889634
MESH = pl.DeviceIdType.MESH
BF = jnp.bfloat16
F32 = jnp.float32
QB = 256
KB = WINDOW + QB
TILE = 256
ROWS = 128
SOON = 2
LATE = 3
VMEM = 59 * 1024 * 1024


def whole_spec(shape):
    return pl.BlockSpec(shape, lambda i: (0,) * len(shape))


def single(shape):
    return pl.BlockSpec(shape, lambda i: (0,) * len(shape), pipeline_mode=pl.Buffered(1))


def loads(sources, targets, semaphores):
    return [pltpu.make_async_copy(s, t, semaphores.at[i]) for i, (s, t) in enumerate(zip(sources, targets))]


def cost(flops, nbytes, special=0):
    return pl.CostEstimate(flops=flops, bytes_accessed=nbytes, transcendentals=special)


def ring_chip(place, chips):
    place = lax.rem(place + 2 * chips, chips)
    late = place // (chips // 2)
    return (1 - late) * 2 * place + late * (2 * (chips - 1 - place) + 1)


def ring_place(chip, chips):
    column = lax.rem(chip, 2)
    row = chip // 2
    return (1 - column) * row + column * (chips - 1 - row)


def paced(at, costs, events):
    spent, before = 0, 0
    for steps, each in costs:
        spent = spent + jnp.minimum(jnp.maximum(at - before, 0), steps) * each
        before += steps
    return spent * events // sum(steps * each for steps, each in costs)


class Spread:
    def __init__(self, devices, pieces, scratch):
        self.devices, self.chips, self.pieces = devices, devices // 2, pieces
        self.local_sem, self.send_sem, self.recv_sem, self.give_sem, self.take_sem = scratch
        self.me = lax.axis_index("dp")
        self.side = lax.axis_index("tensor")
        self.core = lax.rem(self.me, 2)
        self.place = ring_place(self.me // 2, self.chips)
        self.partner = self.me + 1 - 2 * self.core
        self.next = (
            ring_chip(self.place + 1, self.chips) * 2 + self.core,
            ring_chip(self.place - 1, self.chips) * 2 + self.core,
        )
        self.events = (self.chips - 1) * len(pieces)

    @staticmethod
    def scratch(devices, count):
        dma = pltpu.SemaphoreType.DMA
        chips = devices // 2
        return [dma((count,))] + [dma((count, amount, 2)) for amount in (chips - 1, chips - 1, chips, chips)]

    def barrier(self, others=()):
        semaphore = pltpu.get_barrier_semaphore()
        everyone = [(self.next[0], self.side), (self.next[1], self.side), (self.partner, self.side), *others]
        for other in everyone:
            pl.semaphore_signal(semaphore, inc=1, device_id=other, device_id_type=MESH)
        pl.semaphore_wait(semaphore, len(everyone))

    def block(self, index, stage, half):
        source, _, whole, column, width = self.pieces[index]
        rows = source.shape[0]
        owner = ring_chip(self.place - stage if half == 0 else self.place + stage, self.chips) * 2 + self.core
        return whole.at[pl.ds(pl.multiple_of(owner * rows + half * (rows // 2), 16), rows // 2), pl.ds(column, width)]

    def first(self, index, half):
        source, column, _, _, width = self.pieces[index]
        rows = source.shape[0]
        return source.at[pl.ds(half * (rows // 2), rows // 2), pl.ds(column, width)]

    def local(self, index):
        source, start, whole, column, width = self.pieces[index]
        rows = source.shape[0]
        span = pl.ds(pl.multiple_of(self.me * rows, 16), rows)
        return pltpu.make_async_copy(
            source.at[:, pl.ds(start, width)], whole.at[span, pl.ds(column, width)], self.local_sem.at[index]
        )

    def copy(self, index, stage, half, start, across):
        block = self.block(index, stage, half)
        send, recv = (self.give_sem, self.take_sem) if across else (self.send_sem, self.recv_sem)
        return pltpu.make_async_remote_copy(
            src_ref=self.first(index, half) if start else block,
            dst_ref=block,
            send_sem=send.at[index, stage, half],
            recv_sem=recv.at[index, stage, half],
            device_id=(self.partner if across else self.next[half], self.side),
            device_id_type=MESH,
        )

    def each(self):
        return [(index, half) for index in range(len(self.pieces)) for half in range(2)]

    def begin(self):
        for index, half in self.each():
            self.copy(index, 0, half, True, False).start()
        for index, half in self.each():
            self.copy(index, 0, half, True, True).start()
        for index in range(len(self.pieces)):
            self.local(index).start()

    def stage(self, stage, index):
        for half in range(2):
            self.copy(index, stage - 1, half, False, False).wait_recv()

            @pl.when(stage < self.chips - 1)
            def _():
                self.copy(index, stage, half, False, False).start()

            self.copy(index, stage, half, False, True).start()

    def pace(self, step, costs):
        count = len(self.pieces)

        def one(event, carry):
            for index in range(count):
                pl.when(lax.rem(event, count) == index)(functools.partial(self.stage, event // count + 1, index))
            return carry

        lax.fori_loop(paced(step, costs, self.events), paced(step + 1, costs, self.events), one, 0)

    def finish(self):
        for index in range(len(self.pieces)):
            self.local(index).wait()
        for index, half in self.each():
            self.copy(index, 0, half, True, False).wait_send()
            self.copy(index, 0, half, True, True).wait()

        def sent(stage, carry):
            for index, half in self.each():
                self.copy(index, stage, half, False, False).wait_send()
            return carry

        lax.fori_loop(1, self.chips - 1, sent, 0)

        def gave(stage, carry):
            for index, half in self.each():
                self.copy(index, stage, half, False, True).wait()
            return carry

        lax.fori_loop(1, self.chips, gave, 0)


def first_gather(w_query, w_key, w_value, w_out, gains, tokens, w_gate_t, w_up_t, w_down, cotangent, places, identity):
    devices = lax.axis_size("dp")
    sides = lax.axis_size("tensor")
    rows, columns = w_query.shape
    units = w_down.shape[0]
    tiles = (units + TILE - 1) // TILE
    padded, late = tiles * TILE, LATE * TILE
    some = padded - late
    m, width = tokens.shape
    span = m // 2
    reach = WINDOW + m
    rates = THETA ** (-(np.arange(E // 2, dtype=np.float32) * 2.0 / E))
    rates = jnp.asarray(np.concatenate([rates, rates])[None, :], F32)

    def kernel(q_ref, k_ref, v_ref, o_hbm, gains_ref, tokens_ref, gate_hbm, up_hbm, down_hbm, dy_hbm, places_ref, rates_ref, attn_ref, all_ref, near, far, early_hbm, late_hbm, dyt_hbm, cos_hbm, sin_hbm, o_in, o_turned, gate_in, up_in, down_in, early_pack, late_pack, dy_in, dyt, cosine, sine, load_sem, store_sem, far_send, far_recv, near_send, near_recv, *scratch):
        pieces = [(ref, 0, attn_ref, number * columns, columns) for number, ref in enumerate((q_ref, k_ref, v_ref, o_turned))]
        spread = Spread(devices, [*pieces, (gains_ref, 0, all_ref, 0, gains_ref.shape[1])], scratch)
        me, side, core = spread.me, spread.side, spread.core
        across = lax.rem(side + 1, sides)
        later, before = lax.rem(me + 2, devices), lax.rem(me + devices - 2, devices)
        parts = (gate_in, up_in, down_in)
        brought = loads(
            (o_hbm, gate_hbm, up_hbm, down_hbm, dy_hbm), (o_in, *[part.at[pl.ds(0, units)] for part in parts], dy_in), load_sem
        )
        stored = loads((early_pack, late_pack, dyt, cosine, sine), (early_hbm, late_hbm, dyt_hbm, cos_hbm, sin_hbm), store_sem)

        def tables(first, made):
            angles = made * rates_ref[...]
            lane = lax.broadcasted_iota(jnp.int32, (E, E), 1)
            cosine[first : first + E, :] = jnp.cos(angles)
            turn = jnp.sin(angles)
            sine[first : first + E, :] = jnp.where(lane < E // 2, -turn, turn)

        def own_tables():
            for first in range(0, m, E):
                row = places_ref[:, first : first + E].astype(F32)
                tables(WINDOW + first, jnp.broadcast_to(row, (E, E)).T)

        def earlier_tables(begin, end):
            for first in range(begin, end, E):
                row = lax.broadcasted_iota(jnp.int32, (E, E), 0) + (first - WINDOW)
                tables(first, (row + places_ref[:, :1]).astype(F32))

        for copy in brought:
            copy.start()
        spread.barrier(((me, across), (later, side), (before, side)))

        def described(source, target, send, recv, other):
            return pltpu.make_async_remote_copy(
                src_ref=source, dst_ref=target, send_sem=send, recv_sem=recv, device_id=other, device_id_type=MESH
            )

        def half_rows(ref, which):
            return ref.at[pl.ds(pl.multiple_of(which * span, span), span)]

        far_copy = described(half_rows(tokens_ref, side), half_rows(far, side), far_send.at[0], far_recv.at[0], (later, side))
        cross_copy = described(half_rows(far, side), half_rows(far, side), far_send.at[1], far_recv.at[1], (me, across))

        def near_copy(source, which, slot):
            return described(half_rows(source, which), half_rows(near, which), near_send.at[slot], near_recv.at[slot], (spread.partner, side))

        own_near = [near_copy(tokens_ref, which, which) for which in range(2)]
        far_near = [near_copy(far, which, slot) for slot, which in enumerate((side, across))]

        brought[0].wait()
        o_turned[...] = o_in[...].T
        spread.begin()

        @pl.when(me < devices - 2)
        def _():
            far_copy.start()

        @pl.when(core == 0)
        def _():
            for copy in own_near:
                copy.start()

        for number, part in enumerate(parts):
            brought[1 + number].wait()
            part[units:, :] = jnp.zeros((padded - units, rows), BF)
            made = part[...].T
            early_pack[:, number * some : (number + 1) * some] = made[:, :some]
            late_pack[:, number * late : (number + 1) * late] = made[:, some:]
        for copy in stored[:2]:
            copy.start()

        def one(stage, carry):
            for index in range(len(pieces) + 1):
                spread.stage(stage, index)

            pl.when(stage == 1)(own_tables)
            pl.when(stage == 2)(functools.partial(earlier_tables, 0, WINDOW // 2))
            pl.when(stage == 3)(functools.partial(earlier_tables, WINDOW // 2, WINDOW))

            @pl.when(stage == 4)
            def _():
                brought[4].wait()
                dyt[...] = dy_in[...].T
                for copy in stored[2:]:
                    copy.start()

            @pl.when((stage == spread.chips // 2) & (me >= 2))
            def _():
                far_copy.wait_recv()
                cross_copy.start()

                @pl.when(core == 1)
                def _():
                    far_near[0].start()

            @pl.when((stage == spread.chips - 2) & (me >= 2))
            def _():
                cross_copy.wait_recv()

                @pl.when(core == 1)
                def _():
                    far_near[1].start()

            return carry

        lax.fori_loop(1, spread.chips, one, 0)
        for copy in stored:
            copy.wait()
        spread.finish()

        @pl.when(me < devices - 2)
        def _():
            far_copy.wait_send()

        @pl.when(me >= 2)
        def _():
            cross_copy.wait_send()

            @pl.when(core == 1)
            def _():
                for copy in far_near:
                    copy.wait_send()

        @pl.when(core == 0)
        def _():
            for copy in own_near:
                copy.wait_send()

        @pl.when((core == 1) | (me >= 2))
        def _():
            for copy in own_near:
                copy.wait_recv()

    dma = pltpu.SemaphoreType.DMA
    any_space = pl.BlockSpec(memory_space=pl.ANY)
    low = functools.partial(jax.ShapeDtypeStruct, dtype=BF)
    return pl.pallas_call(
        kernel,
        out_shape=[
            low((rows * devices, 4 * columns)),
            low((gains.shape[0] * devices, gains.shape[1])),
            low(tokens.shape),
            low(tokens.shape),
            low((rows, 3 * some)),
            low((rows, 3 * late)),
            low((width, m)),
            jax.ShapeDtypeStruct((reach, E), F32),
            jax.ShapeDtypeStruct((reach, E), F32),
        ],
        in_specs=[any_space] * 10 + [pl.BlockSpec(memory_space=pltpu.VMEM)] * 2,
        out_specs=[any_space] * 9,
        scratch_shapes=[
            pltpu.VMEM(w_out.shape, BF),
            pltpu.VMEM((rows, columns), BF),
            *[pltpu.VMEM((padded, rows), BF)] * 3,
            pltpu.VMEM((rows, 3 * some), BF),
            pltpu.VMEM((rows, 3 * late), BF),
            pltpu.VMEM((m, width), BF),
            pltpu.VMEM((width, m), BF),
            pltpu.VMEM((reach, E), F32),
            pltpu.VMEM((reach, E), F32),
            dma((5,)),
            dma((5,)),
            dma((2,)),
            dma((2,)),
            dma((2,)),
            dma((2,)),
            *Spread.scratch(devices, 5),
        ],
        compiler_params=pltpu.CompilerParams(vmem_limit_bytes=VMEM, collective_id=identity, has_side_effects=True),
        name="first_gather",
    )(w_query, w_key, w_value, w_out, gains, tokens, w_gate_t, w_up_t, w_down, cotangent, places, rates)


class Ring:
    AHEAD = 3

    def __init__(self, devices, terms, goals, groups, scratch):
        self.devices, self.chips = devices, devices // 2
        self.terms, self.goals, self.groups = terms, goals, groups
        count = len(terms)
        self.mine, self.taken, self.inbox = scratch[0 : 3 * count : 3], scratch[1 : 3 * count : 3], scratch[2 : 3 * count : 3]
        self.own_sem, self.give_sem, self.take_sem, self.send_sem, self.recv_sem = scratch[3 * count : 3 * count + 5]
        self.me = lax.axis_index("dp")
        self.side = lax.axis_index("tensor")
        self.core = lax.rem(self.me, 2)
        self.place = ring_place(self.me // 2, self.chips)
        self.partner = self.me + 1 - 2 * self.core
        self.next = (
            ring_chip(self.place + 1, self.chips) * 2 + self.core,
            ring_chip(self.place - 1, self.chips) * 2 + self.core,
        )
        self.events = (self.chips - 1) * len(groups)

    @staticmethod
    def scratch(devices, shapes):
        chips, count = devices // 2, len(shapes)
        dma = pltpu.SemaphoreType.DMA
        buffers = []
        for rows, width in shapes:
            buffers += [pltpu.VMEM((amount, 2, rows // 2, width), BF) for amount in (chips, chips, chips - 1)]
        return buffers + [dma((count, amount, 2)) for amount in (chips, chips, chips, chips - 1, chips - 1)]

    def barrier(self, others=()):
        semaphore = pltpu.get_barrier_semaphore()
        everyone = [(self.next[0], self.side), (self.next[1], self.side), (self.partner, self.side), *others]
        for other in everyone:
            pl.semaphore_signal(semaphore, inc=1, device_id=other, device_id_type=MESH)
        pl.semaphore_wait(semaphore, len(everyone))

    def block(self, index, stage, half, core):
        at = self.place - 1 - stage if half == 0 else self.place + 1 + stage
        size = self.mine[index].shape[2]
        source, column, width = self.terms[index]
        return source.at[ring_chip(at, self.chips) * 2 + core, pl.ds(half * size, size), pl.ds(column, width)]

    def own(self, index, stage, half):
        return pltpu.make_async_copy(
            self.block(index, stage, half, self.core), self.mine[index].at[stage, half], self.own_sem.at[index, stage, half]
        )

    def given(self, index, stage, half):
        return pltpu.make_async_remote_copy(
            src_ref=self.block(index, stage, half, 1 - self.core),
            dst_ref=self.taken[index].at[stage, half],
            send_sem=self.give_sem.at[index, stage, half],
            recv_sem=self.take_sem.at[index, stage, half],
            device_id=(self.partner, self.side),
            device_id_type=MESH,
        )

    def hop(self, index, stage, half, first):
        source = self.mine[index].at[0, half] if first else self.inbox[index].at[stage - 1, half]
        return pltpu.make_async_remote_copy(
            src_ref=source,
            dst_ref=self.inbox[index].at[stage, half],
            send_sem=self.send_sem.at[index, stage, half],
            recv_sem=self.recv_sem.at[index, stage, half],
            device_id=(self.next[half], self.side),
            device_id_type=MESH,
        )

    def each(self, group=None):
        members = range(len(self.terms)) if group is None else self.groups[group]
        return [(index, half) for index in members for half in range(2)]

    def fetch(self, stage, group):
        for index, half in self.each(group):
            self.given(index, stage, half).start()
            self.own(index, stage, half).start()

    def begin(self):
        for group in range(len(self.groups)):
            self.fetch(0, group)
        for index, half in self.each():
            self.mine[index][0, half] = self.chip_term(index, 0, half).astype(BF)
            self.hop(index, 0, half, True).start()
        for stage in range(1, self.AHEAD + 1):
            for group in range(len(self.groups)):
                self.fetch(stage, group)

    def chip_term(self, index, stage, half):
        self.own(index, stage, half).wait()
        self.given(index, stage, half).wait_recv()
        return self.mine[index][stage, half].astype(F32) + self.taken[index][stage, half].astype(F32)

    def stage(self, stage, group):
        last = self.chips - 1

        @pl.when(stage < last)
        def _():
            for index, half in self.each(group):
                self.hop(index, stage - 1, half, True).wait_recv()
                came = self.inbox[index][stage - 1, half].astype(F32)
                self.inbox[index][stage - 1, half] = (came + self.chip_term(index, stage, half)).astype(BF)
                self.hop(index, stage, half, False).start()

        @pl.when(stage + self.AHEAD < self.chips)
        def _():
            self.fetch(stage + self.AHEAD, group)

        @pl.when(stage == last)
        def _():
            for index, half in self.each(group):
                self.hop(index, last - 1, half, True).wait_recv()
                came = self.inbox[index][last - 1, half].astype(F32)
                size = came.shape[0]
                total = came + self.chip_term(index, last, half)
                goal, column = self.goals[index]
                width = min(goal.shape[1] - column, total.shape[1])
                goal[half * size : (half + 1) * size, column : column + width] = total[:, :width]

    def run(self, first, stop):
        count = len(self.groups)

        def one(event, carry):
            for group in range(count):
                if count == 1:
                    self.stage(event + 1, 0)
                else:
                    pl.when(lax.rem(event, count) == group)(functools.partial(self.stage, event // count + 1, group))
            return carry

        lax.fori_loop(first, stop, one, 0)

    def pace(self, step, costs):
        self.run(paced(step, costs, self.events), paced(step + 1, costs, self.events))

    def finish(self):
        for index, half in self.each():
            self.hop(index, 0, half, True).wait_send()

        def sent(stage, carry):
            for index, half in self.each():
                self.hop(index, stage, half, False).wait_send()
            return carry

        lax.fori_loop(1, self.chips - 1, sent, 0)

        def gave(stage, carry):
            for index, half in self.each():
                self.given(index, stage, half).wait_send()
            return carry

        lax.fori_loop(0, self.chips, gave, 0)


def dot_nn(a, b):
    return jnp.dot(a, b, preferred_element_type=F32)


def dot_nt(a, b):
    return lax.dot_general(a, b, (((1,), (1,)), ((), ())), preferred_element_type=F32)


def turned(block, cosine, sine, back):
    other = pltpu.roll(block, E // 2, 1)
    if back:
        return block * cosine - other * sine
    return block * cosine + other * sine


def attend_back(query, kv, probs, mixed, w_attn, hidden, gain, d_normed, d_normed_other, cotangent, cosine, sine, flip, act_early, act_late, w_ffn, rest, ring_source, heads, out_width, identity):
    m, width = hidden.shape
    firsts = m // ROWS
    devices, rows, ring_width = ring_source.shape[1:]
    blocks = m // QB
    factor = E ** (-0.5)
    reach = WINDOW + m
    columns = heads * E
    some, late = act_early.shape[1], act_late.shape[1]
    sides = lax.axis_size("tensor")

    def kernel(q_ref, k_ref, v_ref, p_ref, x_ref, w_ref, h_ref, gain_ref, dn_ref, do_ref, y_ref, c_hbm, s_hbm, flip_hbm, ae_hbm, al_hbm, wd_ref, rd_ref, source, dq_ref, dk_ref, dv_ref, out_ref, sum_ref, flipped_ref, dh_ref, gain_out, sent_ref, got, c_ref, s_ref, flip_ref, ae_ref, al_ref, load_sem, sent, y_send, y_recv, g_ref, gt_ref, keys_sum, values_sum, *scratch):
        step = pl.program_id(0)
        half = ring_width // 2
        ring = Ring(devices, [(source.at[0], 0, half), (source.at[0], half, half)], [(sum_ref, 0), (sum_ref, half)], [[0], [1]], scratch)
        brought = loads((c_hbm, s_hbm, flip_hbm, ae_hbm, al_hbm), (c_ref, s_ref, flip_ref, ae_ref, al_ref), load_sem)
        other = (ring.me, lax.rem(ring.side + 1, sides))

        def across(which):
            return pltpu.make_async_remote_copy(
                src_ref=sent.at[which], dst_ref=got.at[:, pl.ds(pl.multiple_of(which * TILE, TILE), TILE)],
                send_sem=y_send.at[which], recv_sem=y_recv.at[which], device_id=other, device_id_type=MESH,
            )

        turns = [(firsts + 2 * heads, 1)]

        @pl.when(step == 0)
        def _():
            for copy in brought:
                copy.start()
            ring.barrier((other,))
            ring.begin()

        @pl.when(step == firsts)
        def _():
            for copy in brought:
                copy.wait()

        @pl.when(step < firsts)
        def _():
            change, gain_part = norm_grad(h_ref[...], gain_ref[...], dn_ref[...].astype(F32) + do_ref[...].astype(F32))
            total = y_ref[...].astype(F32) + change
            low = total.astype(BF)
            dh_ref[...] = total
            here = pl.ds(pl.multiple_of(step * ROWS, ROWS), ROWS)
            g_ref[here, :] = low
            gt_ref[:, here] = low.T

            @pl.when(step == 0)
            def _():
                gain_out[...] = gain_part

            @pl.when(step > 0)
            def _():
                gain_out[...] += gain_part

            ring.pace(step, turns)

        @pl.when(step >= firsts)
        def _():
            head = step - firsts

            @pl.when(head < SOON)
            def _():
                down = (dot_nt(ae_ref[...], wd_ref[...]) + dot_nt(al_ref[...], rd_ref[...])).astype(BF)
                sent[head] = down
                sent_ref[...] = down
                across(head).start()

            grad_all = dot_nn(g_ref[...], w_ref[...]).astype(BF)
            out_ref[...] = dot_nn(gt_ref[...], x_ref[...]).astype(BF)
            keys_t = k_ref[...].T
            keys_sum[...] = jnp.zeros_like(keys_sum)
            values_sum[...] = jnp.zeros_like(values_sum)
            for block in range(blocks):
                span = slice(block * QB, block * QB + KB)
                here = slice(block * QB, (block + 1) * QB)
                there = slice(WINDOW + block * QB, WINDOW + (block + 1) * QB)
                low = p_ref[0, block]
                grad = grad_all[here, :]
                d_probs = dot_nt(v_ref[span, :], grad)
                weighted = low.astype(F32) * d_probs
                total = jnp.sum(weighted, axis=0, keepdims=True)
                d_scores = (weighted - low.astype(F32) * total).astype(BF)
                values_sum[span, :] += dot_nn(low, grad)
                keys_sum[span, :] += dot_nn(d_scores, q_ref[here, :])
                d_query = dot_nn(keys_t[:, span], d_scores).T * factor
                dq_ref[here, :] = turned(d_query, c_ref[there, :], s_ref[there, :], True).astype(BF)
                if block == 0:
                    ring.pace(firsts + 2 * head, turns)
            dk_ref[...] = turned(keys_sum[...] * factor, c_ref[...], s_ref[...], True).astype(BF)
            dv_ref[...] = values_sum[...].astype(BF)
            ring.pace(firsts + 2 * head + 1, turns)

            @pl.when(head == 1)
            def _():
                flipped_ref[...] = flip_ref[...].T[: flipped_ref.shape[0]]

            @pl.when(head == heads - 1)
            def _():
                for which in range(SOON):
                    across(which).wait()
                ring.finish()

    def at(i):
        return jnp.maximum(i - firsts, 0)

    head_spec = pl.BlockSpec((m, E), lambda i: (0, at(i)))
    long_spec = pl.BlockSpec((reach, E), lambda i: (0, at(i)))
    rows_spec = pl.BlockSpec((ROWS, width), lambda i: (jnp.minimum(i, firsts - 1), 0))
    dma = pltpu.SemaphoreType.DMA

    def soon(i):
        return jnp.minimum(at(i), SOON - 1)

    any_space = pl.BlockSpec(memory_space=pl.ANY)
    return pl.pallas_call(
        kernel,
        grid=(firsts + heads,),
        out_shape=[
            jax.ShapeDtypeStruct((m, columns), BF),
            jax.ShapeDtypeStruct((reach, columns), BF),
            jax.ShapeDtypeStruct((reach, columns), BF),
            jax.ShapeDtypeStruct((width, columns), BF),
            jax.ShapeDtypeStruct((rows, out_width), F32),
            jax.ShapeDtypeStruct((out_width, rows), F32),
            jax.ShapeDtypeStruct((m, width), F32),
            jax.ShapeDtypeStruct((1, width), F32),
            jax.ShapeDtypeStruct((m, SOON * TILE), BF),
            jax.ShapeDtypeStruct((m, SOON * TILE), BF),
        ],
        in_specs=[
            head_spec,
            long_spec,
            pl.BlockSpec((reach, E), lambda i: (0, at(i) + heads)),
            pl.BlockSpec((1, blocks, KB, QB), lambda i: (at(i), 0, 0, 0)),
            head_spec,
            pl.BlockSpec((width, E), lambda i: (0, at(i) + 3 * heads)),
            rows_spec,
            single((1, width)),
            rows_spec,
            rows_spec,
            rows_spec,
            any_space, any_space, any_space, any_space, any_space,
            pl.BlockSpec((TILE, some), lambda i: (soon(i), 2)),
            pl.BlockSpec((TILE, late), lambda i: (soon(i), 2)),
            any_space,
        ],
        out_specs=[
            head_spec,
            long_spec,
            long_spec,
            pl.BlockSpec((width, E), lambda i: (0, at(i))),
            single((rows, out_width)),
            single((out_width, rows)),
            rows_spec,
            single((1, width)),
            pl.BlockSpec((m, TILE), lambda i: (0, soon(i))),
            any_space,
        ],
        scratch_shapes=[
            pltpu.VMEM((reach, E), F32), pltpu.VMEM((reach, E), F32), pltpu.VMEM(flip.shape, F32),
            pltpu.VMEM((m, some), BF), pltpu.VMEM((m, late), BF), dma((5,)),
            pltpu.VMEM((SOON, m, TILE), BF), dma((SOON,)), dma((SOON,)),
            pltpu.VMEM((m, width), BF), pltpu.VMEM((width, m), BF),
            pltpu.VMEM((reach, E), F32), pltpu.VMEM((reach, E), F32),
            *Ring.scratch(devices, [(rows, ring_width // 2)] * 2),
        ],
        compiler_params=pltpu.CompilerParams(vmem_limit_bytes=VMEM, collective_id=identity, has_side_effects=True),
        cost_estimate=cost(8 * heads * m * KB * E * 2, 2 * heads * m * KB),
        name="attend_back",
    )(query, kv, kv, probs, mixed, w_attn, hidden, gain, d_normed, d_normed_other, cotangent, cosine, sine, flip, act_early, act_late, w_ffn, rest, ring_source)


def qkv_back(x_t, d_query, d_key, d_value, w_attn, up_part, out_part, out_width, identity):
    width, reach = x_t.shape
    m, columns = d_query.shape
    devices, rows, up_width = up_part.shape[1:]
    tiles = width // TILE
    per = columns // TILE
    total = tiles + 3 * per
    sides = lax.axis_size("tensor")
    half = m // 2
    piece = up_width // 2
    shapes = [(rows, piece), (rows, piece), (rows, columns)]
    assert 3 * per > tiles and reach == 3 * m

    def kernel(xt_hbm, dq_hbm, dk_hbm, dv_hbm, w_ref, up_ref, out_ref, grad_ref, sent_ref, got, add_ref, up_sum, out_sum, xt_ref, dq_ref, dk_ref, dv_ref, load_sem, sent, early, early_in, near_in, far_in, own_send, own_recv, early_send, early_recv, near_send, near_recv, far_send, far_recv, *scratch):
        step = pl.program_id(0)
        source = up_ref.at[1]
        ring = Ring(
            devices, [(source, 0, piece), (source, piece, piece), (out_ref, 0, columns)], [(up_sum, 0), (up_sum, piece), (out_sum, 0)],
            [[0], [1], [2]], scratch,
        )
        me, side = ring.me, ring.side
        across = lax.rem(side + 1, sides)
        later, before = lax.rem(me + 2, devices), lax.rem(me + devices - 2, devices)
        share = ring.core.astype(F32)
        brought = loads((dq_hbm, dk_hbm, dv_hbm, xt_hbm), (dq_ref, dk_ref, dv_ref, xt_ref), load_sem)

        def remote(source, target, send, recv, which, other):
            return pltpu.make_async_remote_copy(
                src_ref=source, dst_ref=target, send_sem=send.at[which], recv_sem=recv.at[which], device_id=other, device_id_type=MESH
            )

        def own_copy(which):
            target = got.at[:, pl.ds(pl.multiple_of(which * TILE, TILE), TILE)]
            return remote(sent.at[which], target, own_send, own_recv, which, (me, across))

        def early_copy(which):
            return remote(early.at[which, across], early_in.at[which], early_send, early_recv, which, (me, across))

        def near_copy(which):
            return remote(early_in.at[which, 1], near_in.at[which], near_send, near_recv, which, (ring.partner, side))

        def far_copy(which):
            return remote(early_in.at[which, 0], far_in.at[which], far_send, far_recv, which, (before, side))

        @pl.when(step == 0)
        def _():
            for copy in brought:
                copy.start()
            ring.barrier(((me, across), (later, side), (before, side)))
            ring.begin()
            for copy in brought[:3]:
                copy.wait()

        @pl.when(step == tiles)
        def _():
            brought[3].wait()

        @pl.when(step < tiles)
        def _():
            w_key, w_value = w_ref[:, columns : 2 * columns], w_ref[:, 2 * columns :]
            part = dot_nt(dq_ref[...], w_ref[:, :columns])
            part += dot_nt(dk_ref[2 * m :, :], w_key) + dot_nt(dv_ref[2 * m :, :], w_value)
            low = part.astype(BF)
            sent[step] = low
            sent_ref[...] = low
            for block in range(2):
                span = slice(block * m, (block + 1) * m)
                part = (dot_nt(dk_ref[span, :], w_key) + dot_nt(dv_ref[span, :], w_value)).astype(BF)
                for number in range(2):
                    early[step, number, block] = part[number * half : (number + 1) * half]
            early_copy(step).start()

        number = step - tiles

        @pl.when((number >= 0) & (number < tiles))
        def _():
            own_copy(number).start()
            early_copy(number).wait_recv()
            early_in[number] = (early_in[number].astype(F32) + early[number, side].astype(F32)).astype(BF)
            near_copy(number).start()

        @pl.when((number >= 1) & (number <= tiles))
        def _():
            which = number - 1
            near_copy(which).wait_recv()
            early_in[which, 0] = (early_in[which, 0].astype(F32) + near_in[which].astype(F32) * share).astype(BF)

            @pl.when(me >= 2)
            def _():
                far_copy(which).start()

        @pl.when((number >= 0) & (number < per))
        def _():
            here = pl.ds(pl.multiple_of(number * TILE, TILE), TILE)
            grad_ref[...] = dot_nn(xt_ref[:, 2 * m :], dq_ref[:, here]).astype(BF)

        @pl.when((number >= per) & (number < 2 * per))
        def _():
            here = pl.ds(pl.multiple_of((number - per) * TILE, TILE), TILE)
            grad_ref[...] = dot_nn(xt_ref[...], dk_ref[:, here]).astype(BF)

        @pl.when(number >= 2 * per)
        def _():
            here = pl.ds(pl.multiple_of((number - 2 * per) * TILE, TILE), TILE)
            grad_ref[...] = dot_nn(xt_ref[...], dv_ref[:, here]).astype(BF)

        ring.pace(step, [(tiles, 5), (3 * per, 4)])

        @pl.when(step == total - 1)
        def _():
            for which in range(tiles):
                here = slice(which * TILE, (which + 1) * TILE)
                add_ref[:, here] = (near_in[which].astype(F32) * (1.0 - share)).astype(BF)

                @pl.when(me < devices - 2)
                def _():
                    far_copy(which).wait_recv()
                    add_ref[:, here] = (add_ref[:, here].astype(F32) + far_in[which].astype(F32)).astype(BF)

                @pl.when(me >= 2)
                def _():
                    far_copy(which).wait_send()

                near_copy(which).wait_send()
                early_copy(which).wait_send()
                own_copy(which).wait()
            ring.finish()

    any_space = pl.BlockSpec(memory_space=pl.ANY)
    dma = pltpu.SemaphoreType.DMA

    def second(i):
        return jnp.minimum(i, tiles - 1)

    return pl.pallas_call(
        kernel,
        grid=(total,),
        out_shape=[
            jax.ShapeDtypeStruct((width, 3 * columns), BF),
            jax.ShapeDtypeStruct((m, width), BF),
            jax.ShapeDtypeStruct((m, width), BF),
            jax.ShapeDtypeStruct((half, width), BF),
            jax.ShapeDtypeStruct((rows, out_width), F32),
            jax.ShapeDtypeStruct((rows, columns), F32),
        ],
        in_specs=[
            any_space, any_space, any_space, any_space,
            pl.BlockSpec((TILE, 3 * columns), lambda i: (second(i), 0)),
            any_space, any_space,
        ],
        out_specs=[
            pl.BlockSpec((width, TILE), lambda i: (0, jnp.maximum(i - tiles, 0))),
            pl.BlockSpec((m, TILE), lambda i: (0, second(i))),
            any_space,
            single((half, width)),
            single((rows, out_width)),
            single((rows, columns)),
        ],
        scratch_shapes=[
            pltpu.VMEM((width, reach), BF),
            pltpu.VMEM((m, columns), BF),
            pltpu.VMEM((reach, columns), BF),
            pltpu.VMEM((reach, columns), BF),
            dma((4,)),
            pltpu.VMEM((tiles, m, TILE), BF),
            pltpu.VMEM((tiles, 2, 2, half, TILE), BF),
            pltpu.VMEM((tiles, 2, half, TILE), BF),
            pltpu.VMEM((tiles, half, TILE), BF),
            pltpu.VMEM((tiles, half, TILE), BF),
            *[dma((tiles,))] * 8,
            *Ring.scratch(devices, shapes),
        ],
        compiler_params=pltpu.CompilerParams(vmem_limit_bytes=VMEM, collective_id=identity, has_side_effects=True),
        cost_estimate=cost(4 * (m + 2 * reach) * width * columns, 12 * width * columns),
        name="qkv_back",
    )(x_t, d_query, d_key, d_value, w_attn, up_part, out_part)


def tiles_of(width):
    return width // TILE


def root_of(rows):
    return lax.rsqrt(jnp.mean(rows * rows, axis=-1, keepdims=True) + EPS)


def norm_grad(rows, gain, grad):
    root = root_of(rows)
    pushed = grad * gain
    inner = jnp.mean(pushed * rows, axis=-1, keepdims=True)
    return root * pushed - rows * (root * root * root * inner), jnp.sum(grad * rows * root, axis=0, keepdims=True)


def forward(far, near, tokens, gain, w_attn, cosine, sine, places, gain_ffn, block, heads, identity):
    m, width = tokens.shape
    reach = 3 * m
    columns = heads * E
    devices = lax.axis_size("dp")
    sides = lax.axis_size("tensor")
    part_steps = m // ROWS
    per = TILE // E
    some = heads // per
    blocks = m // QB
    factor = E ** (-0.5) * LOG2E
    counts = (3 * part_steps, some, 2 * some, heads, part_steps, part_steps)
    starts = [sum(counts[:number]) for number in range(len(counts) + 1)]
    total = starts[-1]
    piece = block.shape[1] // 4

    def kernel(far_ref, near_ref, x_ref, again_ref, g_ref, w_ref, c_ref, s_ref, places_ref, gf_ref, w_hbm, block_ref, nt_ref, q_out, kv_out, mixed_out, probs_ref, hidden_ref, normed_ref, turned_ref, whole_ref, normed, q_all, kv_all, mixed_all, w_out, bias, sent, got, load_sem, y_send, y_recv, *scratch):
        step = pl.program_id(0)
        spread = Spread(devices, [(block_ref, number * piece, whole_ref, number * piece, piece) for number in range(4)], scratch)
        me, side = spread.me, spread.side
        other = (me, lax.rem(side + 1, sides))
        brought = loads((w_hbm.at[:, pl.ds(3 * columns, columns)],), (w_out,), load_sem)

        def across(which):
            return pltpu.make_async_remote_copy(
                src_ref=sent.at[which], dst_ref=got.at[which], send_sem=y_send.at[which], recv_sem=y_recv.at[which],
                device_id=other, device_id_type=MESH,
            )

        def phase(number):
            return pl.when((step >= starts[number]) & (step < starts[number + 1]))

        @pl.when(step == 0)
        def _():
            brought[0].start()
            spread.barrier((other,))
            spread.begin()

        @phase(0)
        def _():
            here = pl.ds(pl.multiple_of(step * ROWS, ROWS), ROWS)

            def put(ref):
                rows = ref[...].astype(F32)
                made = (rows * root_of(rows) * g_ref[...]).astype(BF)
                normed[here, :] = made
                nt_ref[...] = made.T

            def earlier(ref, there):
                pl.when(there)(functools.partial(put, ref))

                @pl.when(jnp.logical_not(there))
                def _():
                    normed[here, :] = jnp.zeros((ROWS, width), BF)
                    nt_ref[...] = jnp.zeros((width, ROWS), BF)

            pl.when(step < part_steps)(functools.partial(earlier, far_ref, me >= 2))
            pl.when((step >= part_steps) & (step < 2 * part_steps))(functools.partial(earlier, near_ref, me >= 1))
            pl.when(step >= 2 * part_steps)(functools.partial(put, x_ref))

        def rotated(made, rows):
            pieces = [turned(made[:, part * E : (part + 1) * E], c_ref[rows, :], s_ref[rows, :], False) for part in range(per)]
            return jnp.concatenate(pieces, axis=1).astype(BF)

        @phase(1)
        def _():
            rows = slice(reach - m, reach)
            made = rotated(dot_nn(normed[rows, :], w_ref[...]), rows)
            q_out[...] = made
            q_all[:, pl.ds(pl.multiple_of((step - starts[1]) * TILE, TILE), TILE)] = made

        @phase(2)
        def _():
            number = step - starts[2]

            def put(made):
                kv_out[...] = made
                kv_all[:, pl.ds(pl.multiple_of(number * TILE, TILE), TILE)] = made

            @pl.when(number < some)
            def _():
                put(rotated(dot_nn(normed[...], w_ref[...]), slice(0, reach)))

            @pl.when(number >= some)
            def _():
                put(dot_nn(normed[...], w_ref[...]).astype(BF))

        @pl.when(step == starts[3])
        def _():
            for number in range(blocks):
                key = lax.broadcasted_iota(jnp.int32, (KB, QB), 0) + number * QB
                query = lax.broadcasted_iota(jnp.int32, (KB, QB), 1) + number * QB
                place = places_ref[:, number * QB : (number + 1) * QB]
                allowed = (key <= query + WINDOW) & (key > query) & (key >= query + WINDOW - place)
                bias[number] = jnp.where(allowed, 0.0, -1e30)

        @phase(3)
        def _():
            head = step - starts[3]
            lanes = pl.ds(pl.multiple_of(head * E, E), E)
            queries = q_all[:, lanes]
            keys = kv_all[:, lanes]
            values_t = kv_all[:, pl.ds(pl.multiple_of(columns + head * E, E), E)].T
            for number in range(blocks):
                span = slice(number * QB, number * QB + KB)
                here = slice(number * QB, (number + 1) * QB)
                scores = dot_nt(keys[span], queries[here]) * factor + bias[number]
                largest = jnp.max(scores, axis=0, keepdims=True)
                grown = jnp.exp2(scores - largest)
                inverse = 1.0 / jnp.sum(grown, axis=0, keepdims=True)
                probs = (grown * inverse).astype(BF)
                probs_ref[0, number] = probs
                made = dot_nn(values_t[:, span], probs).T.astype(BF)
                mixed_out[here, :] = made
                mixed_all[here, lanes] = made

        @pl.when(step == starts[4])
        def _():
            brought[0].wait()

        @phase(4)
        def _():
            which = step - starts[4]
            here = pl.ds(pl.multiple_of(which * ROWS, ROWS), ROWS)
            sent[which] = dot_nt(mixed_all[here, :], w_out[...]).astype(BF)
            across(which).start()

        @phase(5)
        def _():
            which = step - starts[5]
            across(which).wait()
            hidden = again_ref[...].astype(F32) + (sent[which].astype(F32) + got[which].astype(F32))
            made = (hidden * root_of(hidden) * gf_ref[...]).astype(BF)
            hidden_ref[...] = hidden
            normed_ref[...] = made
            turned_ref[...] = made.T

        spread.pace(step, list(zip(counts, (2, 2, 5, 5, 5, 20))))

        @pl.when(step == total - 1)
        def _():
            spread.finish()

    def within(number, i, length):
        return jnp.clip(i - starts[number], 0, length - 1)

    def rows_at(first):
        return pl.BlockSpec((ROWS, width), lambda i: (jnp.clip(i - first, 0, part_steps - 1), 0))

    any_space = pl.BlockSpec(memory_space=pl.ANY)
    dma = pltpu.SemaphoreType.DMA
    low = functools.partial(jax.ShapeDtypeStruct, dtype=BF)
    return pl.pallas_call(
        kernel,
        grid=(total,),
        out_shape=[
            low((width, reach)),
            low((m, columns)),
            low((reach, 2 * columns)),
            low((m, columns)),
            low((heads, blocks, KB, QB)),
            jax.ShapeDtypeStruct((m, width), F32),
            low((m, width)),
            low((width, m)),
            low((block.shape[0] * devices, block.shape[1])),
        ],
        in_specs=[
            rows_at(0), rows_at(part_steps), rows_at(2 * part_steps), rows_at(starts[5]),
            single((1, width)),
            pl.BlockSpec((width, TILE), lambda i: (0, within(1, i, 3 * some))),
            single((reach, E)),
            single((reach, E)),
            single((1, m)),
            single((1, width)),
            any_space,
            any_space,
        ],
        out_specs=[
            pl.BlockSpec((width, ROWS), lambda i: (0, within(0, i, 3 * part_steps))),
            pl.BlockSpec((m, TILE), lambda i: (0, within(1, i, some))),
            pl.BlockSpec((reach, TILE), lambda i: (0, within(2, i, 2 * some))),
            pl.BlockSpec((m, E), lambda i: (0, within(3, i, heads))),
            pl.BlockSpec((1, blocks, KB, QB), lambda i: (within(3, i, heads), 0, 0, 0)),
            rows_at(starts[5]),
            rows_at(starts[5]),
            pl.BlockSpec((width, ROWS), lambda i: (0, within(5, i, part_steps))),
            any_space,
        ],
        scratch_shapes=[
            pltpu.VMEM((reach, width), BF),
            pltpu.VMEM((m, columns), BF),
            pltpu.VMEM((reach, 2 * columns), BF),
            pltpu.VMEM((m, columns), BF),
            pltpu.VMEM((width, columns), BF),
            pltpu.VMEM((blocks, KB, QB), F32),
            pltpu.VMEM((part_steps, ROWS, width), BF),
            pltpu.VMEM((part_steps, ROWS, width), BF),
            dma((1,)),
            dma((part_steps,)),
            dma((part_steps,)),
            *Spread.scratch(devices, 4),
        ],
        compiler_params=pltpu.CompilerParams(vmem_limit_bytes=VMEM, collective_id=identity, has_side_effects=True),
        cost_estimate=cost(2 * (m + 2 * reach) * width * columns, 8 * reach * width, heads * m * KB),
        name="forward",
    )(far, near, tokens, tokens, gain, w_attn, cosine, sine, places, gain_ffn, w_attn, block)


def last_pass(tokens, gain, grad, grad_other, grad_add, d_hidden, hidden, ffn_part, ffn_other, act_early, act_late, w_ffn, rest, gain_ffn_grad, flip, qkv_part, lanes, identity):
    m, width = tokens.shape
    devices, rows, all_columns = qkv_part.shape
    columns = all_columns // 3
    chips = devices // 2
    size = ROWS // 2
    steps = m // size
    downs = tiles_of(width) - SOON
    total = downs + steps + chips
    names = 3
    half = m // 2
    tiles = tiles_of(width)
    some, late = act_early.shape[1], act_late.shape[1]
    sides = lax.axis_size("tensor")
    assert chips >= tiles

    def kernel(x_ref, g_ref, dn_ref, do_ref, add_hbm, dh_ref, h_ref, fp_ref, fo_ref, a_hbm, al_hbm, w_ref, rest_ref, gf_ref, flip_hbm, source, grad_ref, layer_ref, flipped_ref, q_ref, k_ref, v_ref, gains_ref, a_ref, al_ref, flip_ref, add, load_sem, add_send, add_recv, gain_sum, gain_source, gain_in, gain_send, gain_recv, sent, got, y_send, y_recv, *scratch):
        step = pl.program_id(0)
        ring = Ring(
            devices, [(source, number * columns, columns) for number in range(names)], [(q_ref, 0), (k_ref, 0), (v_ref, 0)],
            [[0], [1], [2]], scratch,
        )

        def gain_copy(away):
            owner = lax.rem(ring.me + away, devices)
            return pltpu.make_async_remote_copy(
                src_ref=gain_source.at[owner], dst_ref=gain_in.at[away], send_sem=gain_send.at[away], recv_sem=gain_recv.at[away],
                device_id=(owner, ring.side), device_id_type=MESH,
            )

        other = (ring.me, lax.rem(ring.side + 1, sides))
        brought = loads((a_hbm, al_hbm, flip_hbm, add_hbm), (a_ref, al_ref, flip_ref, add.at[ring.side]), load_sem)
        add_copy = pltpu.make_async_remote_copy(
            src_ref=add_hbm, dst_ref=add.at[ring.side], send_sem=add_send, recv_sem=add_recv, device_id=other, device_id_type=MESH
        )
        row_step = step - downs
        end_step = step - downs - steps

        def across(which):
            return pltpu.make_async_remote_copy(
                src_ref=sent.at[which], dst_ref=got.at[which], send_sem=y_send.at[which], recv_sem=y_recv.at[which],
                device_id=other, device_id_type=MESH,
            )

        @pl.when(step == 0)
        def _():
            for copy in brought:
                copy.start()
            ring.barrier((other, *[(lax.rem(ring.me + away, devices), ring.side) for away in range(1, devices)]))
            add_copy.start()
            ring.begin()
            for copy in brought:
                copy.wait()
            flipped_ref[...] = flip_ref[...].T

        @pl.when(row_step == 0)
        def _():
            add_copy.wait()

        @pl.when(step < downs)
        def _():
            sent[step] = (dot_nt(a_ref[...], w_ref[...]) + dot_nt(al_ref[...], rest_ref[...])).astype(BF)
            across(step).start()

        @pl.when((row_step >= 0) & (row_step < steps))
        def _():
            which = row_step * size // half
            here = pl.ds(pl.multiple_of(row_step * size - which * half, size), size)
            grad_rows = dn_ref[...].astype(F32) + do_ref[...].astype(F32) + add[which, here, :].astype(F32)
            change, gain_part = norm_grad(x_ref[...].astype(F32), g_ref[...], grad_rows)
            grad_ref[...] = dh_ref[...] + change

            @pl.when(row_step == 0)
            def _():
                gain_sum[...] = gain_part

            @pl.when(row_step > 0)
            def _():
                gain_sum[...] += gain_part

        @pl.when(row_step == steps - 1)
        def _():
            gain_source[...] = jnp.zeros_like(gain_source)
            for device in range(devices):
                span = slice(device * rows, (device + 1) * rows)
                gain_source[device, :16, :rows] = jnp.broadcast_to(gain_sum[:, span], (16, rows)).astype(BF)
                gain_source[device, 16:, :rows] = jnp.broadcast_to(gf_ref[:, span], (16, rows)).astype(BF)

            def send(away, carry):
                gain_copy(away).start()
                return carry

            lax.fori_loop(1, devices, send, 0)

        ring.pace(step, [(downs, 5), (steps, 3), (chips, 3)])

        @pl.when((end_step >= 0) & (end_step < SOON))
        def _():
            layer_ref[...] = (h_ref[...] + (fp_ref[...].astype(F32) + fo_ref[...].astype(F32))).astype(BF)

        @pl.when((end_step >= SOON) & (end_step < tiles))
        def _():
            which = end_step - SOON
            across(which).wait()
            layer_ref[...] = (h_ref[...] + (sent[which].astype(F32) + got[which].astype(F32))).astype(BF)

        @pl.when(step == total - 1)
        def _():
            ring.finish()

            def take(away, total):
                gain_copy(away).wait()
                return total + gain_in[away].astype(F32)

            gains_ref[...] = lax.fori_loop(1, devices, take, gain_source[ring.me].astype(F32))

    def early(i):
        return jnp.minimum(i, downs - 1) + SOON

    def ending(i):
        return jnp.clip(i - downs - steps, 0, tiles - 1)

    rows_spec = pl.BlockSpec((size, width), lambda i: (jnp.clip(i - downs, 0, steps - 1), 0))
    tile_spec = pl.BlockSpec((m, TILE), lambda i: (0, ending(i)))
    soon_spec = pl.BlockSpec((m, TILE), lambda i: (0, jnp.minimum(ending(i), SOON - 1)))
    dma = pltpu.SemaphoreType.DMA
    sums = jax.ShapeDtypeStruct((rows, columns), F32)
    return pl.pallas_call(
        kernel,
        grid=(total,),
        out_shape=[
            jax.ShapeDtypeStruct((m, width), F32),
            jax.ShapeDtypeStruct((m, width), BF),
            jax.ShapeDtypeStruct((flip.shape[1], flip.shape[0]), F32),
            sums, sums, sums,
            jax.ShapeDtypeStruct((32, lanes), F32),
        ],
        in_specs=[
            rows_spec, single((1, width)), rows_spec, rows_spec, pl.BlockSpec(memory_space=pl.ANY), rows_spec, tile_spec, soon_spec, soon_spec, pl.BlockSpec(memory_space=pl.ANY), pl.BlockSpec(memory_space=pl.ANY),
            pl.BlockSpec((TILE, some), lambda i: (early(i), 2)), pl.BlockSpec((TILE, late), lambda i: (early(i), 2)), single((1, width)),
            pl.BlockSpec(memory_space=pl.ANY), pl.BlockSpec(memory_space=pl.ANY),
        ],
        out_specs=[
            rows_spec, tile_spec, single((flip.shape[1], flip.shape[0])),
            single(sums.shape), single(sums.shape), single(sums.shape), single((32, lanes)),
        ],
        scratch_shapes=[
            pltpu.VMEM((m, some), BF),
            pltpu.VMEM((m, late), BF),
            pltpu.VMEM(flip.shape, F32),
            pltpu.VMEM((2, half, width), BF),
            dma((4,)),
            dma,
            dma,
            pltpu.VMEM((1, width), F32),
            pltpu.VMEM((devices, 32, lanes), BF),
            pltpu.VMEM((devices, 32, lanes), BF),
            dma((devices,)),
            dma((devices,)),
            pltpu.VMEM((downs, m, TILE), BF),
            pltpu.VMEM((downs, m, TILE), BF),
            dma((downs,)),
            dma((downs,)),
            *Ring.scratch(devices, [(rows, columns)] * names),
        ],
        compiler_params=pltpu.CompilerParams(vmem_limit_bytes=VMEM, collective_id=identity, has_side_effects=True),
        cost_estimate=cost(20 * m * width, 24 * m * width),
        name="last_pass",
    )(tokens, gain, grad, grad_other, grad_add, d_hidden, hidden, ffn_part, ffn_other, act_early, act_late, w_ffn, rest, gain_ffn_grad, flip, qkv_part)


def feed_tile(x_ref, dy_ref, dyt_ref, g_ref, u_ref, d_ref, act_ref, both_ref, down_ref):
    gate = dot_nn(x_ref[...], g_ref[...])
    up = dot_nn(x_ref[...], u_ref[...])
    d_act = dot_nn(dy_ref[...], d_ref[...])
    soft = 1.0 / (1.0 + jnp.exp(-gate))
    silu = gate * soft
    act = (silu * up).astype(BF)
    act_ref[...] = act
    both_ref[0] = (d_act * up * (soft * (1.0 + gate * (1.0 - soft)))).astype(BF)
    both_ref[1] = (d_act * silu).astype(BF)
    down_ref[...] = dot_nn(dyt_ref[...], act).astype(BF)


def feed(x, dy, dy_t, w, block, tiles, identity):
    m, k = x.shape
    early = tiles - LATE
    devices = lax.axis_size("dp")
    width = block.shape[1] // 2

    def kernel(x_hbm, dy_hbm, dyt_hbm, g_ref, u_ref, d_ref, block_ref, act_ref, both_ref, down_ref, rest_ref, x_ref, dy_ref, dyt_ref, load_sem, *scratch):
        step = pl.program_id(0)
        brought = loads((x_hbm, dy_hbm, dyt_hbm), (x_ref, dy_ref, dyt_ref), load_sem)
        spread = Spread(devices, [(block_ref, 0, rest_ref, 0, width), (block_ref, width, rest_ref, width, width)], scratch)

        @pl.when(step == 0)
        def _():
            for copy in brought:
                copy.start()
            spread.barrier()
            spread.begin()
            for copy in brought:
                copy.wait()

        feed_tile(x_ref, dy_ref, dyt_ref, g_ref, u_ref, d_ref, act_ref, both_ref, down_ref)
        spread.pace(step, [(early, 1)])

        @pl.when(step == early - 1)
        def _():
            spread.finish()

    any_space = pl.BlockSpec(memory_space=pl.ANY)
    return pl.pallas_call(
        kernel,
        grid=(early,),
        out_shape=[
            jax.ShapeDtypeStruct((m, early * TILE), BF),
            jax.ShapeDtypeStruct((2, m, early * TILE), BF),
            jax.ShapeDtypeStruct((k, early * TILE), BF),
            jax.ShapeDtypeStruct((k, block.shape[1]), BF),
        ],
        in_specs=[
            any_space, any_space, any_space,
            pl.BlockSpec((k, TILE), lambda i: (0, i)),
            pl.BlockSpec((k, TILE), lambda i: (0, i + early)),
            pl.BlockSpec((k, TILE), lambda i: (0, i + 2 * early)),
            any_space,
        ],
        out_specs=[
            pl.BlockSpec((m, TILE), lambda i: (0, i)),
            pl.BlockSpec((2, m, TILE), lambda i: (0, 0, i)),
            pl.BlockSpec((k, TILE), lambda i: (0, i)),
            any_space,
        ],
        scratch_shapes=[
            pltpu.VMEM((m, k), BF), pltpu.VMEM((m, k), BF), pltpu.VMEM((k, m), BF), pltpu.SemaphoreType.DMA((3,)),
            *Spread.scratch(devices, 2),
        ],
        compiler_params=pltpu.CompilerParams(vmem_limit_bytes=VMEM, collective_id=identity, has_side_effects=True),
        cost_estimate=cost(8 * m * k * early * TILE, 8 * (m + k) * early * TILE, m * early * TILE),
        name="feed",
    )(x, dy, dy_t, w, w, w, block)


def ffn_back(x, x_t, dy, dy_t, d_early, w_ffn, rest, down_early, identity):
    m, width = x.shape
    devices, rows, some = down_early.shape
    late = LATE * TILE
    padded = some + late
    tiles = width // TILE
    wide = 2 * TILE
    early_wide, late_wide = some // wide, (late + wide - 1) // wide
    grads = 2 * (early_wide + late_wide)
    total = LATE + tiles + grads
    sides = lax.axis_size("tensor")
    pieces = [(rows, some // 2)] * 2

    def kernel(x_hbm, xt_hbm, dy_hbm, dyt_hbm, rg_ref, ru_ref, rd_ref, d_hbm, tile_ref, wg_ref, wu_ref, lg_ref, lu_ref, source, act_ref, grad_ref, sent_ref, got, sum_ref, x_ref, xt_ref, dy_ref, dyt_ref, d_ref, load_sem, d_late, down_late, down_tile, both_tile, sent, y_send, y_recv, *scratch):
        step = pl.program_id(0)
        brought = loads((x_hbm, dy_hbm, dyt_hbm, d_hbm, xt_hbm), (x_ref, dy_ref, dyt_ref, d_ref, xt_ref), load_sem)
        ring = Ring(devices, [(source, 0, some // 2), (source, some // 2, some // 2)], [(sum_ref, 0), (sum_ref, some // 2)], [[0], [1]], scratch[:11])
        late_ring = Ring(devices, [(down_late, 0, late)], [(sum_ref, some)], [[0]], scratch[11:])
        other = (ring.me, lax.rem(ring.side + 1, sides))

        def across(which):
            return pltpu.make_async_remote_copy(
                src_ref=sent.at[which], dst_ref=got.at[:, pl.ds(pl.multiple_of(which * TILE, TILE), TILE)],
                send_sem=y_send.at[which], recv_sem=y_recv.at[which], device_id=other, device_id_type=MESH,
            )

        @pl.when(step == 0)
        def _():
            for copy in brought:
                copy.start()
            ring.barrier((other,))
            ring.begin()
            for copy in brought[:3]:
                copy.wait()

        @pl.when(step == LATE)
        def _():
            brought[3].wait()

        @pl.when(step == LATE + tiles)
        def _():
            brought[4].wait()

        @pl.when(step < LATE)
        def _():
            feed_tile(x_ref, dy_ref, dyt_ref, rg_ref, ru_ref, rd_ref, act_ref, both_tile, down_tile)
            here = pl.ds(pl.multiple_of(step * TILE, TILE), TILE)
            d_late[:, :, here] = both_tile[...]
            down_late[:, :, here] = down_tile[...].reshape(devices, rows, TILE)

        @pl.when(step == LATE - 1)
        def _():
            late_ring.begin()

        @pl.when((step >= LATE) & (step < LATE + tiles))
        def _():
            which = step - LATE
            part = dot_nt(d_ref[0], wg_ref[...]) + dot_nt(d_ref[1], wu_ref[...])
            part += dot_nt(d_late[0], lg_ref[...]) + dot_nt(d_late[1], lu_ref[...])
            low = part.astype(BF)
            sent[which] = low
            sent_ref[...] = low
            across(which).start()

        @pl.when((step >= LATE + tiles) & (step < LATE + tiles + 2 * early_wide))
        def _():
            grad_ref[0] = dot_nn(xt_ref[...], tile_ref[0]).astype(BF)

        number = step - (LATE + tiles + 2 * early_wide)
        for part in range(late_wide):
            several = min(wide, late - part * wide)

            @pl.when((number >= 0) & (lax.rem(number, late_wide) == part))
            def _():
                piece = d_late[number // late_wide, :, part * wide : part * wide + several]
                grad_ref[0, :, :several] = dot_nn(xt_ref[...], piece).astype(BF)

        ring.pace(step, [(LATE, 12), (tiles, 8), (grads, 7)])
        late_ring.pace(step, [(LATE, 0), (tiles, 8), (grads, 7)])

        @pl.when(step == total - 1)
        def _():
            for which in range(tiles):
                across(which).wait()
            ring.finish()
            late_ring.finish()

    def first(i):
        return jnp.minimum(i, LATE - 1)

    def second(i):
        return jnp.clip(i - LATE, 0, tiles - 1)

    def third(i):
        at = jnp.clip(i - LATE - tiles, 0, 2 * early_wide - 1)
        return (at // early_wide, 0, at % early_wide)

    def grad_at(i):
        at = jnp.maximum(i - LATE - tiles, 0)
        more = jnp.maximum(at - 2 * early_wide, 0)
        is_late = at // (2 * early_wide)
        return (
            (1 - is_late) * (at // early_wide) + is_late * (more // late_wide),
            0,
            (1 - is_late) * (at % early_wide) + is_late * (early_wide + more % late_wide),
        )

    assert late_wide <= early_wide and some % wide == 0
    any_space = pl.BlockSpec(memory_space=pl.ANY)
    dma = pltpu.SemaphoreType.DMA

    def rest_tile(which):
        return pl.BlockSpec((width, TILE), lambda i: (0, first(i) + which * LATE))

    return pl.pallas_call(
        kernel,
        grid=(total,),
        out_shape=[
            jax.ShapeDtypeStruct((m, late), BF),
            jax.ShapeDtypeStruct((2, width, padded), BF),
            jax.ShapeDtypeStruct((m, width), BF),
            jax.ShapeDtypeStruct((m, width), BF),
            jax.ShapeDtypeStruct((rows, padded), F32),
        ],
        in_specs=[
            any_space, any_space, any_space, any_space,
            rest_tile(0), rest_tile(1), rest_tile(2),
            any_space,
            pl.BlockSpec((1, m, wide), third),
            pl.BlockSpec((TILE, some), lambda i: (second(i), 0)),
            pl.BlockSpec((TILE, some), lambda i: (second(i), 1)),
            pl.BlockSpec((TILE, late), lambda i: (second(i), 0)),
            pl.BlockSpec((TILE, late), lambda i: (second(i), 1)),
            any_space,
        ],
        out_specs=[
            pl.BlockSpec((m, TILE), lambda i: (0, first(i))),
            pl.BlockSpec((1, width, wide), grad_at),
            pl.BlockSpec((m, TILE), lambda i: (0, second(i))),
            any_space,
            single((rows, padded)),
        ],
        scratch_shapes=[
            pltpu.VMEM((m, width), BF),
            pltpu.VMEM((width, m), BF),
            pltpu.VMEM((m, width), BF),
            pltpu.VMEM((width, m), BF),
            pltpu.VMEM((2, m, some), BF),
            dma((5,)),
            pltpu.VMEM((2, m, late), BF),
            pltpu.VMEM((devices, rows, late), BF),
            pltpu.VMEM((width, TILE), BF),
            pltpu.VMEM((2, m, TILE), BF),
            pltpu.VMEM((tiles, m, TILE), BF),
            dma((tiles,)),
            dma((tiles,)),
            *Ring.scratch(devices, pieces),
            *Ring.scratch(devices, [(rows, late)]),
        ],
        compiler_params=pltpu.CompilerParams(vmem_limit_bytes=VMEM, collective_id=identity, has_side_effects=True),
        cost_estimate=cost(8 * m * width * padded + 8 * m * width * late, 10 * width * padded),
        name="ffn_back",
    )(x, x_t, dy, dy_t, rest, rest, rest, d_early, d_early, w_ffn, w_ffn, rest, rest, down_early)


def shards(tokens, positions, attn_gain, w_query, w_key, w_value, w_out, ffn_gain, w_gate, w_up, w_down, cotangent):
    devices = lax.axis_size("dp")
    span = tokens.shape[0]
    assert 2 * span == WINDOW
    own_rows = w_query.shape[0]
    width = tokens.shape[1]
    head_columns = w_query.shape[1]
    heads = head_columns // E
    hidden_units = w_gate.shape[1]
    tiles = (hidden_units + TILE - 1) // TILE
    padded = tiles * TILE

    some = padded - LATE * TILE
    lanes = max(128, own_rows)
    gains = jnp.zeros((32, lanes), BF).at[0, :own_rows].set(attn_gain).at[16, :own_rows].set(ffn_gain)
    places = positions[None, :]
    w_attn, all_gains, near, far, ffn_pack, rest_pack, cotangent_t, cosine, sine = first_gather(
        w_query, w_key, w_value, w_out, gains, tokens, w_gate.T, w_up.T, w_down, cotangent, places, 0
    )
    all_gains = all_gains.reshape(devices, 32, lanes)
    gain_attn = all_gains[:, 0, :own_rows].reshape(1, width).astype(F32)
    gain_ffn = all_gains[:, 16, :own_rows].reshape(1, width).astype(F32)

    normed_attn_t, query, kv, mixed, probs, hidden, normed_ffn, normed_ffn_t, w_ffn = forward(
        far, near, tokens, gain_attn, w_attn, cosine, sine, places, gain_ffn, ffn_pack, heads, 5
    )

    act_early, d_early, down_early, rest = feed(normed_ffn, cotangent, cotangent_t, w_ffn, rest_pack, tiles, 6)
    act_late, both_part, d_normed_ffn, d_normed_other, down_grad = ffn_back(
        normed_ffn, normed_ffn_t, cotangent, cotangent_t, d_early, w_ffn, rest, down_early.reshape(devices, own_rows, some), 1
    )
    both_part = both_part.reshape(2, devices, own_rows, padded)

    d_query, d_key, d_value, out_part, gate_grad, w_down_grad, d_hidden, gain_ffn_grad, ffn_part, ffn_other = attend_back(
        query, kv, probs, mixed, w_attn, hidden, gain_ffn, d_normed_ffn, d_normed_other, cotangent, cosine, sine, down_grad, act_early, act_late, w_ffn, rest,
        both_part, heads, hidden_units, 2,
    )
    qkv_part, d_normed_attn, d_attn_other, d_attn_add, up_grad, out_grad = qkv_back(
        normed_attn_t, d_query, d_key, d_value, w_attn, both_part, out_part.reshape(devices, own_rows, head_columns), hidden_units, 3
    )
    tokens_grad, layer_out, w_out_grad, query_grad, key_grad, value_grad, gain_grads = last_pass(
        tokens, gain_attn, d_normed_attn, d_attn_other, d_attn_add, d_hidden, hidden, ffn_part, ffn_other, act_early, act_late, w_ffn, rest, gain_ffn_grad, out_grad,
        qkv_part.reshape(devices, own_rows, 3 * head_columns), lanes, 4,
    )
    return (
        layer_out,
        tokens_grad,
        gain_grads[0, :own_rows],
        query_grad,
        key_grad,
        value_grad,
        w_out_grad,
        gain_grads[16, :own_rows],
        gate_grad,
        up_grad,
        w_down_grad,
    )


def solution(mesh):
    by_rows, by_both, turned_both, line = P("dp", None), P("dp", "tensor"), P("tensor", "dp"), P("dp")
    return jax.shard_map(
        shards,
        mesh=mesh,
        in_specs=(by_rows, line, line, by_both, by_both, by_both, turned_both, line, by_both, by_both, turned_both, by_rows),
        out_specs=(by_rows, by_rows, line, by_both, by_both, by_both, turned_both, line, by_both, by_both, turned_both),
        check_vma=False,
    )
```

```python
import functools

import jax
import jax.numpy as jnp
import numpy as np
from jax import lax
from jax.experimental import pallas as pl
from jax.experimental.pallas import tpu as pltpu
from jax.sharding import PartitionSpec as P

E = 128
WINDOW = 1024
EPS = 1e-06
THETA = 10000.0
LOG2E = 1.4426950408889634
MESH = pl.DeviceIdType.MESH
BF = jnp.bfloat16
F32 = jnp.float32
QB = 256
KB = WINDOW + QB
TILE = 256
ROWS = 128
SOON = 2
LATE = 3
VMEM = 59 * 1024 * 1024


def whole_spec(shape):
    return pl.BlockSpec(shape, lambda i: (0,) * len(shape))


def single(shape):
    return pl.BlockSpec(shape, lambda i: (0,) * len(shape), pipeline_mode=pl.Buffered(1))


def loads(sources, targets, semaphores):
    return [pltpu.make_async_copy(s, t, semaphores.at[i]) for i, (s, t) in enumerate(zip(sources, targets))]


def cost(flops, nbytes, special=0):
    return pl.CostEstimate(flops=flops, bytes_accessed=nbytes, transcendentals=special)


def ring_chip(place, chips):
    place = lax.rem(place + 2 * chips, chips)
    late = place // (chips // 2)
    return (1 - late) * 2 * place + late * (2 * (chips - 1 - place) + 1)


def ring_place(chip, chips):
    column = lax.rem(chip, 2)
    row = chip // 2
    return (1 - column) * row + column * (chips - 1 - row)


def paced(at, costs, events):
    spent, before = 0, 0
    for steps, each in costs:
        spent = spent + jnp.minimum(jnp.maximum(at - before, 0), steps) * each
        before += steps
    return spent * events // sum(steps * each for steps, each in costs)


class Spread:
    def __init__(self, devices, pieces, scratch):
        self.devices, self.chips, self.pieces = devices, devices // 2, pieces
        self.local_sem, self.send_sem, self.recv_sem, self.give_sem, self.take_sem = scratch
        self.me = lax.axis_index("dp")
        self.side = lax.axis_index("tensor")
        self.core = lax.rem(self.me, 2)
        self.place = ring_place(self.me // 2, self.chips)
        self.partner = self.me + 1 - 2 * self.core
        self.next = (
            ring_chip(self.place + 1, self.chips) * 2 + self.core,
            ring_chip(self.place - 1, self.chips) * 2 + self.core,
        )
        self.events = (self.chips - 1) * len(pieces)

    @staticmethod
    def scratch(devices, count):
        dma = pltpu.SemaphoreType.DMA
        chips = devices // 2
        return [dma((count,))] + [dma((count, amount, 2)) for amount in (chips - 1, chips - 1, chips, chips)]

    def barrier(self, others=()):
        semaphore = pltpu.get_barrier_semaphore()
        everyone = [(self.next[0], self.side), (self.next[1], self.side), (self.partner, self.side), *others]
        for other in everyone:
            pl.semaphore_signal(semaphore, inc=1, device_id=other, device_id_type=MESH)
        pl.semaphore_wait(semaphore, len(everyone))

    def block(self, index, stage, half):
        source, _, whole, column, width = self.pieces[index]
        rows = source.shape[0]
        owner = ring_chip(self.place - stage if half == 0 else self.place + stage, self.chips) * 2 + self.core
        return whole.at[pl.ds(pl.multiple_of(owner * rows + half * (rows // 2), 16), rows // 2), pl.ds(column, width)]

    def first(self, index, half):
        source, column, _, _, width = self.pieces[index]
        rows = source.shape[0]
        return source.at[pl.ds(half * (rows // 2), rows // 2), pl.ds(column, width)]

    def local(self, index):
        source, start, whole, column, width = self.pieces[index]
        rows = source.shape[0]
        span = pl.ds(pl.multiple_of(self.me * rows, 16), rows)
        return pltpu.make_async_copy(
            source.at[:, pl.ds(start, width)], whole.at[span, pl.ds(column, width)], self.local_sem.at[index]
        )

    def copy(self, index, stage, half, start, across):
        block = self.block(index, stage, half)
        send, recv = (self.give_sem, self.take_sem) if across else (self.send_sem, self.recv_sem)
        return pltpu.make_async_remote_copy(
            src_ref=self.first(index, half) if start else block,
            dst_ref=block,
            send_sem=send.at[index, stage, half],
            recv_sem=recv.at[index, stage, half],
            device_id=(self.partner if across else self.next[half], self.side),
            device_id_type=MESH,
        )

    def each(self):
        return [(index, half) for index in range(len(self.pieces)) for half in range(2)]

    def begin(self):
        for index, half in self.each():
            self.copy(index, 0, half, True, False).start()
        for index, half in self.each():
            self.copy(index, 0, half, True, True).start()
        for index in range(len(self.pieces)):
            self.local(index).start()

    def stage(self, stage, index):
        for half in range(2):
            self.copy(index, stage - 1, half, False, False).wait_recv()

            @pl.when(stage < self.chips - 1)
            def _():
                self.copy(index, stage, half, False, False).start()

            self.copy(index, stage, half, False, True).start()

    def pace(self, step, costs):
        count = len(self.pieces)

        def one(event, carry):
            for index in range(count):
                pl.when(lax.rem(event, count) == index)(functools.partial(self.stage, event // count + 1, index))
            return carry

        lax.fori_loop(paced(step, costs, self.events), paced(step + 1, costs, self.events), one, 0)

    def finish(self):
        for index in range(len(self.pieces)):
            self.local(index).wait()
        for index, half in self.each():
            self.copy(index, 0, half, True, False).wait_send()
            self.copy(index, 0, half, True, True).wait()

        def sent(stage, carry):
            for index, half in self.each():
                self.copy(index, stage, half, False, False).wait_send()
            return carry

        lax.fori_loop(1, self.chips - 1, sent, 0)

        def gave(stage, carry):
            for index, half in self.each():
                self.copy(index, stage, half, False, True).wait()
            return carry

        lax.fori_loop(1, self.chips, gave, 0)


def first_gather(w_query, w_key, w_value, w_out, attn_gain, ffn_gain, tokens, w_gate_t, w_up_t, w_down, cotangent, places, identity):
    devices = lax.axis_size("dp")
    sides = lax.axis_size("tensor")
    rows, columns = w_query.shape
    units = w_down.shape[0]
    tiles = (units + TILE - 1) // TILE
    padded, late = tiles * TILE, LATE * TILE
    some = padded - late
    m, width = tokens.shape
    span = m // 2
    reach = WINDOW + m
    rates = THETA ** (-(np.arange(E // 2, dtype=np.float32) * 2.0 / E))
    rates = jnp.asarray(np.concatenate([rates, rates])[None, :], F32)

    lanes = max(128, rows)

    def kernel(q_ref, k_ref, v_ref, o_hbm, tokens_ref, gate_hbm, up_hbm, down_hbm, dy_hbm, ag_ref, fg_ref, places_ref, rates_ref, attn_ref, all_ref, near, far, early_hbm, late_hbm, dyt_hbm, cos_hbm, sin_hbm, o_in, o_turned, gate_in, up_in, down_in, early_pack, late_pack, dy_in, dyt, cosine, sine, gains_ref, load_sem, store_sem, far_send, far_recv, near_send, near_recv, *scratch):
        pieces = [(ref, 0, attn_ref, number * columns, columns) for number, ref in enumerate((q_ref, k_ref, v_ref, o_turned))]
        spread = Spread(devices, [*pieces, (gains_ref, 0, all_ref, 0, lanes)], scratch)
        me, side, core = spread.me, spread.side, spread.core
        across = lax.rem(side + 1, sides)
        later, before = lax.rem(me + 2, devices), lax.rem(me + devices - 2, devices)
        parts = (gate_in, up_in, down_in)
        brought = loads(
            (o_hbm, gate_hbm, up_hbm, down_hbm, dy_hbm), (o_in, *[part.at[pl.ds(0, units)] for part in parts], dy_in), load_sem
        )
        stored = loads((early_pack, late_pack, dyt, cosine, sine), (early_hbm, late_hbm, dyt_hbm, cos_hbm, sin_hbm), store_sem)

        def tables(first, made):
            angles = made * rates_ref[...]
            lane = lax.broadcasted_iota(jnp.int32, (E, E), 1)
            cosine[first : first + E, :] = jnp.cos(angles)
            turn = jnp.sin(angles)
            sine[first : first + E, :] = jnp.where(lane < E // 2, -turn, turn)

        def own_tables():
            for first in range(0, m, E):
                row = places_ref[:, first : first + E].astype(F32)
                tables(WINDOW + first, jnp.broadcast_to(row, (E, E)).T)

        def earlier_tables(begin, end):
            for first in range(begin, end, E):
                row = lax.broadcasted_iota(jnp.int32, (E, E), 0) + (first - WINDOW)
                tables(first, (row + places_ref[:, :1]).astype(F32))

        for copy in brought:
            copy.start()
        spread.barrier(((me, across), (later, side), (before, side)))

        def described(source, target, send, recv, other):
            return pltpu.make_async_remote_copy(
                src_ref=source, dst_ref=target, send_sem=send, recv_sem=recv, device_id=other, device_id_type=MESH
            )

        def half_rows(ref, which):
            return ref.at[pl.ds(pl.multiple_of(which * span, span), span)]

        far_copy = described(half_rows(tokens_ref, side), half_rows(far, side), far_send.at[0], far_recv.at[0], (later, side))
        cross_copy = described(half_rows(far, side), half_rows(far, side), far_send.at[1], far_recv.at[1], (me, across))

        def near_copy(source, which, slot):
            return described(half_rows(source, which), half_rows(near, which), near_send.at[slot], near_recv.at[slot], (spread.partner, side))

        own_near = [near_copy(tokens_ref, which, which) for which in range(2)]
        far_near = [near_copy(far, which, slot) for slot, which in enumerate((side, across))]

        gains_ref[...] = jnp.zeros_like(gains_ref)
        gains_ref[:16, :rows] = jnp.broadcast_to(ag_ref[...], (16, rows))
        gains_ref[16:, :rows] = jnp.broadcast_to(fg_ref[...], (16, rows))
        brought[0].wait()
        o_turned[...] = o_in[...].T
        spread.begin()

        @pl.when(me < devices - 2)
        def _():
            far_copy.start()

        @pl.when(core == 0)
        def _():
            for copy in own_near:
                copy.start()

        for number, part in enumerate(parts):
            brought[1 + number].wait()
            part[units:, :] = jnp.zeros((padded - units, rows), BF)
            made = part[...].T
            early_pack[:, number * some : (number + 1) * some] = made[:, :some]
            late_pack[:, number * late : (number + 1) * late] = made[:, some:]
        for copy in stored[:2]:
            copy.start()

        def one(stage, carry):
            for index in range(len(pieces) + 1):
                spread.stage(stage, index)

            pl.when(stage == 1)(own_tables)
            pl.when(stage == 2)(functools.partial(earlier_tables, 0, WINDOW // 2))
            pl.when(stage == 3)(functools.partial(earlier_tables, WINDOW // 2, WINDOW))

            @pl.when(stage == 4)
            def _():
                brought[4].wait()
                dyt[...] = dy_in[...].T
                for copy in stored[2:]:
                    copy.start()

            @pl.when((stage == spread.chips // 2) & (me >= 2))
            def _():
                far_copy.wait_recv()
                cross_copy.start()

                @pl.when(core == 1)
                def _():
                    far_near[0].start()

            @pl.when((stage == spread.chips - 2) & (me >= 2))
            def _():
                cross_copy.wait_recv()

                @pl.when(core == 1)
                def _():
                    far_near[1].start()

            return carry

        lax.fori_loop(1, spread.chips, one, 0)
        for copy in stored:
            copy.wait()
        spread.finish()

        @pl.when(me < devices - 2)
        def _():
            far_copy.wait_send()

        @pl.when(me >= 2)
        def _():
            cross_copy.wait_send()

            @pl.when(core == 1)
            def _():
                for copy in far_near:
                    copy.wait_send()

        @pl.when(core == 0)
        def _():
            for copy in own_near:
                copy.wait_send()

        @pl.when((core == 1) | (me >= 2))
        def _():
            for copy in own_near:
                copy.wait_recv()

    dma = pltpu.SemaphoreType.DMA
    any_space = pl.BlockSpec(memory_space=pl.ANY)
    low = functools.partial(jax.ShapeDtypeStruct, dtype=BF)
    return pl.pallas_call(
        kernel,
        out_shape=[
            low((rows * devices, 4 * columns)),
            low((32 * devices, lanes)),
            low(tokens.shape),
            low(tokens.shape),
            low((rows, 3 * some)),
            low((rows, 3 * late)),
            low((width, m)),
            jax.ShapeDtypeStruct((reach, E), F32),
            jax.ShapeDtypeStruct((reach, E), F32),
        ],
        in_specs=[any_space] * 9 + [pl.BlockSpec(memory_space=pltpu.VMEM)] * 4,
        out_specs=[any_space] * 9,
        scratch_shapes=[
            pltpu.VMEM(w_out.shape, BF),
            pltpu.VMEM((rows, columns), BF),
            *[pltpu.VMEM((padded, rows), BF)] * 3,
            pltpu.VMEM((rows, 3 * some), BF),
            pltpu.VMEM((rows, 3 * late), BF),
            pltpu.VMEM((m, width), BF),
            pltpu.VMEM((width, m), BF),
            pltpu.VMEM((reach, E), F32),
            pltpu.VMEM((reach, E), F32),
            pltpu.VMEM((32, lanes), BF),
            dma((5,)),
            dma((5,)),
            dma((2,)),
            dma((2,)),
            dma((2,)),
            dma((2,)),
            *Spread.scratch(devices, 5),
        ],
        compiler_params=pltpu.CompilerParams(vmem_limit_bytes=VMEM, collective_id=identity, has_side_effects=True),
        name="first_gather",
    )(w_query, w_key, w_value, w_out, tokens, w_gate_t, w_up_t, w_down, cotangent, attn_gain[None, :], ffn_gain[None, :], places, rates)


class Ring:
    AHEAD = 3

    def __init__(self, devices, terms, goals, groups, scratch):
        self.devices, self.chips = devices, devices // 2
        self.terms, self.goals, self.groups = terms, goals, groups
        count = len(terms)
        self.mine, self.taken, self.inbox = scratch[0 : 3 * count : 3], scratch[1 : 3 * count : 3], scratch[2 : 3 * count : 3]
        self.own_sem, self.give_sem, self.take_sem, self.send_sem, self.recv_sem = scratch[3 * count : 3 * count + 5]
        self.me = lax.axis_index("dp")
        self.side = lax.axis_index("tensor")
        self.core = lax.rem(self.me, 2)
        self.place = ring_place(self.me // 2, self.chips)
        self.partner = self.me + 1 - 2 * self.core
        self.next = (
            ring_chip(self.place + 1, self.chips) * 2 + self.core,
            ring_chip(self.place - 1, self.chips) * 2 + self.core,
        )
        self.events = (self.chips - 1) * len(groups)

    @staticmethod
    def scratch(devices, shapes):
        chips, count = devices // 2, len(shapes)
        dma = pltpu.SemaphoreType.DMA
        buffers = []
        for rows, width in shapes:
            buffers += [pltpu.VMEM((amount, 2, rows // 2, width), BF) for amount in (chips, chips, chips - 1)]
        return buffers + [dma((count, amount, 2)) for amount in (chips, chips, chips, chips - 1, chips - 1)]

    def barrier(self, others=()):
        semaphore = pltpu.get_barrier_semaphore()
        everyone = [(self.next[0], self.side), (self.next[1], self.side), (self.partner, self.side), *others]
        for other in everyone:
            pl.semaphore_signal(semaphore, inc=1, device_id=other, device_id_type=MESH)
        pl.semaphore_wait(semaphore, len(everyone))

    def block(self, index, stage, half, core):
        at = self.place - 1 - stage if half == 0 else self.place + 1 + stage
        size = self.mine[index].shape[2]
        source, column, width = self.terms[index]
        return source.at[ring_chip(at, self.chips) * 2 + core, pl.ds(half * size, size), pl.ds(column, width)]

    def own(self, index, stage, half):
        return pltpu.make_async_copy(
            self.block(index, stage, half, self.core), self.mine[index].at[stage, half], self.own_sem.at[index, stage, half]
        )

    def given(self, index, stage, half):
        return pltpu.make_async_remote_copy(
            src_ref=self.block(index, stage, half, 1 - self.core),
            dst_ref=self.taken[index].at[stage, half],
            send_sem=self.give_sem.at[index, stage, half],
            recv_sem=self.take_sem.at[index, stage, half],
            device_id=(self.partner, self.side),
            device_id_type=MESH,
        )

    def hop(self, index, stage, half, first):
        source = self.mine[index].at[0, half] if first else self.inbox[index].at[stage - 1, half]
        return pltpu.make_async_remote_copy(
            src_ref=source,
            dst_ref=self.inbox[index].at[stage, half],
            send_sem=self.send_sem.at[index, stage, half],
            recv_sem=self.recv_sem.at[index, stage, half],
            device_id=(self.next[half], self.side),
            device_id_type=MESH,
        )

    def each(self, group=None):
        members = range(len(self.terms)) if group is None else self.groups[group]
        return [(index, half) for index in members for half in range(2)]

    def fetch(self, stage, group):
        for index, half in self.each(group):
            self.given(index, stage, half).start()
            self.own(index, stage, half).start()

    def begin(self):
        for group in range(len(self.groups)):
            self.fetch(0, group)
        for index, half in self.each():
            self.mine[index][0, half] = self.chip_term(index, 0, half).astype(BF)
            self.hop(index, 0, half, True).start()
        for stage in range(1, self.AHEAD + 1):
            for group in range(len(self.groups)):
                self.fetch(stage, group)

    def chip_term(self, index, stage, half):
        self.own(index, stage, half).wait()
        self.given(index, stage, half).wait_recv()
        return self.mine[index][stage, half].astype(F32) + self.taken[index][stage, half].astype(F32)

    def stage(self, stage, group):
        last = self.chips - 1

        @pl.when(stage < last)
        def _():
            for index, half in self.each(group):
                self.hop(index, stage - 1, half, True).wait_recv()
                came = self.inbox[index][stage - 1, half].astype(F32)
                self.inbox[index][stage - 1, half] = (came + self.chip_term(index, stage, half)).astype(BF)
                self.hop(index, stage, half, False).start()

        @pl.when(stage + self.AHEAD < self.chips)
        def _():
            self.fetch(stage + self.AHEAD, group)

        @pl.when(stage == last)
        def _():
            for index, half in self.each(group):
                self.hop(index, last - 1, half, True).wait_recv()
                came = self.inbox[index][last - 1, half].astype(F32)
                size = came.shape[0]
                total = came + self.chip_term(index, last, half)
                goal, column = self.goals[index]
                width = min(goal.shape[1] - column, total.shape[1])
                goal[half * size : (half + 1) * size, column : column + width] = total[:, :width]

    def run(self, first, stop):
        count = len(self.groups)

        def one(event, carry):
            for group in range(count):
                if count == 1:
                    self.stage(event + 1, 0)
                else:
                    pl.when(lax.rem(event, count) == group)(functools.partial(self.stage, event // count + 1, group))
            return carry

        lax.fori_loop(first, stop, one, 0)

    def pace(self, step, costs):
        self.run(paced(step, costs, self.events), paced(step + 1, costs, self.events))

    def finish(self):
        for index, half in self.each():
            self.hop(index, 0, half, True).wait_send()

        def sent(stage, carry):
            for index, half in self.each():
                self.hop(index, stage, half, False).wait_send()
            return carry

        lax.fori_loop(1, self.chips - 1, sent, 0)

        def gave(stage, carry):
            for index, half in self.each():
                self.given(index, stage, half).wait_send()
            return carry

        lax.fori_loop(0, self.chips, gave, 0)


def dot_nn(a, b):
    return jnp.dot(a, b, preferred_element_type=F32)


def dot_nt(a, b):
    return lax.dot_general(a, b, (((1,), (1,)), ((), ())), preferred_element_type=F32)


def turned(block, cosine, sine, back):
    other = pltpu.roll(block, E // 2, 1)
    if back:
        return block * cosine - other * sine
    return block * cosine + other * sine


def attend_back(query, kv, probs, mixed, w_attn, hidden, gain, d_normed, d_normed_other, cotangent, cosine, sine, flip, act_early, act_late, w_ffn, rest, ring_source, heads, out_width, identity):
    m, width = hidden.shape
    firsts = m // ROWS
    devices, rows, ring_width = ring_source.shape[1:]
    blocks = m // QB
    factor = E ** (-0.5)
    reach = WINDOW + m
    columns = heads * E
    some, late = act_early.shape[1], act_late.shape[1]
    sides = lax.axis_size("tensor")

    def kernel(q_ref, k_ref, v_ref, p_ref, x_ref, w_ref, h_ref, gain_ref, dn_ref, do_ref, y_ref, c_hbm, s_hbm, flip_hbm, ae_hbm, al_hbm, wd_ref, rd_ref, source, dq_ref, dk_ref, dv_ref, out_ref, sum_ref, flipped_ref, dh_ref, gain_out, sent_ref, got, c_ref, s_ref, flip_ref, ae_ref, al_ref, load_sem, sent, y_send, y_recv, g_ref, gt_ref, keys_sum, values_sum, *scratch):
        step = pl.program_id(0)
        half = ring_width // 2
        ring = Ring(devices, [(source.at[0], 0, half), (source.at[0], half, half)], [(sum_ref, 0), (sum_ref, half)], [[0], [1]], scratch)
        brought = loads((c_hbm, s_hbm, flip_hbm, ae_hbm, al_hbm), (c_ref, s_ref, flip_ref, ae_ref, al_ref), load_sem)
        other = (ring.me, lax.rem(ring.side + 1, sides))

        def across(which):
            return pltpu.make_async_remote_copy(
                src_ref=sent.at[which], dst_ref=got.at[:, pl.ds(pl.multiple_of(which * TILE, TILE), TILE)],
                send_sem=y_send.at[which], recv_sem=y_recv.at[which], device_id=other, device_id_type=MESH,
            )

        turns = [(firsts + 2 * heads, 1)]

        @pl.when(step == 0)
        def _():
            for copy in brought:
                copy.start()
            ring.barrier((other,))
            ring.begin()

        @pl.when(step == firsts)
        def _():
            for copy in brought:
                copy.wait()

        @pl.when(step < firsts)
        def _():
            change, gain_part = norm_grad(h_ref[...], gain_ref[...], dn_ref[...].astype(F32) + do_ref[...].astype(F32))
            total = y_ref[...].astype(F32) + change
            low = total.astype(BF)
            dh_ref[...] = total
            here = pl.ds(pl.multiple_of(step * ROWS, ROWS), ROWS)
            g_ref[here, :] = low
            gt_ref[:, here] = low.T

            @pl.when(step == 0)
            def _():
                gain_out[...] = gain_part

            @pl.when(step > 0)
            def _():
                gain_out[...] += gain_part

            ring.pace(step, turns)

        @pl.when(step >= firsts)
        def _():
            head = step - firsts

            @pl.when(head < SOON)
            def _():
                down = (dot_nt(ae_ref[...], wd_ref[...]) + dot_nt(al_ref[...], rd_ref[...])).astype(BF)
                sent[head] = down
                sent_ref[...] = down
                across(head).start()

            grad_all = dot_nn(g_ref[...], w_ref[...]).astype(BF)
            out_ref[...] = dot_nn(gt_ref[...], x_ref[...]).astype(BF)
            keys_t = k_ref[...].T
            keys_sum[...] = jnp.zeros_like(keys_sum)
            values_sum[...] = jnp.zeros_like(values_sum)
            for block in range(blocks):
                span = slice(block * QB, block * QB + KB)
                here = slice(block * QB, (block + 1) * QB)
                there = slice(WINDOW + block * QB, WINDOW + (block + 1) * QB)
                low = p_ref[0, block]
                grad = grad_all[here, :]
                d_probs = dot_nt(v_ref[span, :], grad)
                weighted = low.astype(F32) * d_probs
                total = jnp.sum(weighted, axis=0, keepdims=True)
                d_scores = (weighted - low.astype(F32) * total).astype(BF)
                values_sum[span, :] += dot_nn(low, grad)
                keys_sum[span, :] += dot_nn(d_scores, q_ref[here, :])
                d_query = dot_nn(keys_t[:, span], d_scores).T * factor
                dq_ref[here, :] = turned(d_query, c_ref[there, :], s_ref[there, :], True).astype(BF)
                if block == 0:
                    ring.pace(firsts + 2 * head, turns)
            dk_ref[...] = turned(keys_sum[...] * factor, c_ref[...], s_ref[...], True).astype(BF)
            dv_ref[...] = values_sum[...].astype(BF)
            ring.pace(firsts + 2 * head + 1, turns)

            @pl.when(head == 1)
            def _():
                flipped_ref[...] = flip_ref[...].T[: flipped_ref.shape[0]]

            @pl.when(head == heads - 1)
            def _():
                for which in range(SOON):
                    across(which).wait()
                ring.finish()

    def at(i):
        return jnp.maximum(i - firsts, 0)

    head_spec = pl.BlockSpec((m, E), lambda i: (0, at(i)))
    long_spec = pl.BlockSpec((reach, E), lambda i: (0, at(i)))
    rows_spec = pl.BlockSpec((ROWS, width), lambda i: (jnp.minimum(i, firsts - 1), 0))
    dma = pltpu.SemaphoreType.DMA

    def soon(i):
        return jnp.minimum(at(i), SOON - 1)

    any_space = pl.BlockSpec(memory_space=pl.ANY)
    return pl.pallas_call(
        kernel,
        grid=(firsts + heads,),
        out_shape=[
            jax.ShapeDtypeStruct((m, columns), BF),
            jax.ShapeDtypeStruct((reach, columns), BF),
            jax.ShapeDtypeStruct((reach, columns), BF),
            jax.ShapeDtypeStruct((width, columns), BF),
            jax.ShapeDtypeStruct((rows, out_width), F32),
            jax.ShapeDtypeStruct((out_width, rows), F32),
            jax.ShapeDtypeStruct((m, width), F32),
            jax.ShapeDtypeStruct((1, width), F32),
            jax.ShapeDtypeStruct((m, SOON * TILE), BF),
            jax.ShapeDtypeStruct((m, SOON * TILE), BF),
        ],
        in_specs=[
            head_spec,
            long_spec,
            pl.BlockSpec((reach, E), lambda i: (0, at(i) + heads)),
            pl.BlockSpec((1, blocks, KB, QB), lambda i: (at(i), 0, 0, 0)),
            head_spec,
            pl.BlockSpec((width, E), lambda i: (0, at(i) + 3 * heads)),
            rows_spec,
            single((1, width)),
            rows_spec,
            rows_spec,
            rows_spec,
            any_space, any_space, any_space, any_space, any_space,
            pl.BlockSpec((TILE, some), lambda i: (soon(i), 2)),
            pl.BlockSpec((TILE, late), lambda i: (soon(i), 2)),
            any_space,
        ],
        out_specs=[
            head_spec,
            long_spec,
            long_spec,
            pl.BlockSpec((width, E), lambda i: (0, at(i))),
            single((rows, out_width)),
            single((out_width, rows)),
            rows_spec,
            single((1, width)),
            pl.BlockSpec((m, TILE), lambda i: (0, soon(i))),
            any_space,
        ],
        scratch_shapes=[
            pltpu.VMEM((reach, E), F32), pltpu.VMEM((reach, E), F32), pltpu.VMEM(flip.shape, F32),
            pltpu.VMEM((m, some), BF), pltpu.VMEM((m, late), BF), dma((5,)),
            pltpu.VMEM((SOON, m, TILE), BF), dma((SOON,)), dma((SOON,)),
            pltpu.VMEM((m, width), BF), pltpu.VMEM((width, m), BF),
            pltpu.VMEM((reach, E), F32), pltpu.VMEM((reach, E), F32),
            *Ring.scratch(devices, [(rows, ring_width // 2)] * 2),
        ],
        compiler_params=pltpu.CompilerParams(vmem_limit_bytes=VMEM, collective_id=identity, has_side_effects=True),
        cost_estimate=cost(8 * heads * m * KB * E * 2, 2 * heads * m * KB),
        name="attend_back",
    )(query, kv, kv, probs, mixed, w_attn, hidden, gain, d_normed, d_normed_other, cotangent, cosine, sine, flip, act_early, act_late, w_ffn, rest, ring_source)


def qkv_back(x_t, d_query, d_key, d_value, w_attn, up_part, out_part, out_width, identity):
    width, reach = x_t.shape
    m, columns = d_query.shape
    devices, rows, up_width = up_part.shape[1:]
    tiles = width // TILE
    per = columns // TILE
    total = tiles + 3 * per
    sides = lax.axis_size("tensor")
    half = m // 2
    piece = up_width // 2
    shapes = [(rows, piece), (rows, piece), (rows, columns)]
    assert 3 * per > tiles and reach == 3 * m

    def kernel(xt_hbm, dq_hbm, dk_hbm, dv_hbm, w_ref, up_ref, out_ref, grad_ref, sent_ref, got, add_ref, up_sum, out_sum, xt_ref, dq_ref, dk_ref, dv_ref, load_sem, sent, early, early_in, near_in, far_in, own_send, own_recv, early_send, early_recv, near_send, near_recv, far_send, far_recv, *scratch):
        step = pl.program_id(0)
        source = up_ref.at[1]
        ring = Ring(
            devices, [(source, 0, piece), (source, piece, piece), (out_ref, 0, columns)], [(up_sum, 0), (up_sum, piece), (out_sum, 0)],
            [[0], [1], [2]], scratch,
        )
        me, side = ring.me, ring.side
        across = lax.rem(side + 1, sides)
        later, before = lax.rem(me + 2, devices), lax.rem(me + devices - 2, devices)
        share = ring.core.astype(F32)
        brought = loads((dq_hbm, dk_hbm, dv_hbm, xt_hbm), (dq_ref, dk_ref, dv_ref, xt_ref), load_sem)

        def remote(source, target, send, recv, which, other):
            return pltpu.make_async_remote_copy(
                src_ref=source, dst_ref=target, send_sem=send.at[which], recv_sem=recv.at[which], device_id=other, device_id_type=MESH
            )

        def own_copy(which):
            target = got.at[:, pl.ds(pl.multiple_of(which * TILE, TILE), TILE)]
            return remote(sent.at[which], target, own_send, own_recv, which, (me, across))

        def early_copy(which):
            return remote(early.at[which, across], early_in.at[which], early_send, early_recv, which, (me, across))

        def near_copy(which):
            return remote(early_in.at[which, 1], near_in.at[which], near_send, near_recv, which, (ring.partner, side))

        def far_copy(which):
            return remote(early_in.at[which, 0], far_in.at[which], far_send, far_recv, which, (before, side))

        @pl.when(step == 0)
        def _():
            for copy in brought:
                copy.start()
            ring.barrier(((me, across), (later, side), (before, side)))
            ring.begin()
            for copy in brought[:3]:
                copy.wait()

        @pl.when(step == tiles)
        def _():
            brought[3].wait()

        @pl.when(step < tiles)
        def _():
            w_key, w_value = w_ref[:, columns : 2 * columns], w_ref[:, 2 * columns :]
            part = dot_nt(dq_ref[...], w_ref[:, :columns])
            part += dot_nt(dk_ref[2 * m :, :], w_key) + dot_nt(dv_ref[2 * m :, :], w_value)
            low = part.astype(BF)
            sent[step] = low
            sent_ref[...] = low
            for block in range(2):
                span = slice(block * m, (block + 1) * m)
                part = (dot_nt(dk_ref[span, :], w_key) + dot_nt(dv_ref[span, :], w_value)).astype(BF)
                for number in range(2):
                    early[step, number, block] = part[number * half : (number + 1) * half]
            early_copy(step).start()

        number = step - tiles

        @pl.when((number >= 0) & (number < tiles))
        def _():
            own_copy(number).start()
            early_copy(number).wait_recv()
            early_in[number] = (early_in[number].astype(F32) + early[number, side].astype(F32)).astype(BF)
            near_copy(number).start()

        @pl.when((number >= 1) & (number <= tiles))
        def _():
            which = number - 1
            near_copy(which).wait_recv()
            early_in[which, 0] = (early_in[which, 0].astype(F32) + near_in[which].astype(F32) * share).astype(BF)

            @pl.when(me >= 2)
            def _():
                far_copy(which).start()

        @pl.when((number >= 0) & (number < per))
        def _():
            here = pl.ds(pl.multiple_of(number * TILE, TILE), TILE)
            grad_ref[...] = dot_nn(xt_ref[:, 2 * m :], dq_ref[:, here]).astype(BF)

        @pl.when((number >= per) & (number < 2 * per))
        def _():
            here = pl.ds(pl.multiple_of((number - per) * TILE, TILE), TILE)
            grad_ref[...] = dot_nn(xt_ref[...], dk_ref[:, here]).astype(BF)

        @pl.when(number >= 2 * per)
        def _():
            here = pl.ds(pl.multiple_of((number - 2 * per) * TILE, TILE), TILE)
            grad_ref[...] = dot_nn(xt_ref[...], dv_ref[:, here]).astype(BF)

        ring.pace(step, [(tiles, 5), (3 * per, 4)])

        @pl.when(step == total - 1)
        def _():
            for which in range(tiles):
                here = slice(which * TILE, (which + 1) * TILE)
                add_ref[:, here] = (near_in[which].astype(F32) * (1.0 - share)).astype(BF)

                @pl.when(me < devices - 2)
                def _():
                    far_copy(which).wait_recv()
                    add_ref[:, here] = (add_ref[:, here].astype(F32) + far_in[which].astype(F32)).astype(BF)

                @pl.when(me >= 2)
                def _():
                    far_copy(which).wait_send()

                near_copy(which).wait_send()
                early_copy(which).wait_send()
                own_copy(which).wait()
            ring.finish()

    any_space = pl.BlockSpec(memory_space=pl.ANY)
    dma = pltpu.SemaphoreType.DMA

    def second(i):
        return jnp.minimum(i, tiles - 1)

    return pl.pallas_call(
        kernel,
        grid=(total,),
        out_shape=[
            jax.ShapeDtypeStruct((width, 3 * columns), BF),
            jax.ShapeDtypeStruct((m, width), BF),
            jax.ShapeDtypeStruct((m, width), BF),
            jax.ShapeDtypeStruct((half, width), BF),
            jax.ShapeDtypeStruct((rows, out_width), F32),
            jax.ShapeDtypeStruct((rows, columns), F32),
        ],
        in_specs=[
            any_space, any_space, any_space, any_space,
            pl.BlockSpec((TILE, 3 * columns), lambda i: (second(i), 0)),
            any_space, any_space,
        ],
        out_specs=[
            pl.BlockSpec((width, TILE), lambda i: (0, jnp.maximum(i - tiles, 0))),
            pl.BlockSpec((m, TILE), lambda i: (0, second(i))),
            any_space,
            single((half, width)),
            single((rows, out_width)),
            single((rows, columns)),
        ],
        scratch_shapes=[
            pltpu.VMEM((width, reach), BF),
            pltpu.VMEM((m, columns), BF),
            pltpu.VMEM((reach, columns), BF),
            pltpu.VMEM((reach, columns), BF),
            dma((4,)),
            pltpu.VMEM((tiles, m, TILE), BF),
            pltpu.VMEM((tiles, 2, 2, half, TILE), BF),
            pltpu.VMEM((tiles, 2, half, TILE), BF),
            pltpu.VMEM((tiles, half, TILE), BF),
            pltpu.VMEM((tiles, half, TILE), BF),
            *[dma((tiles,))] * 8,
            *Ring.scratch(devices, shapes),
        ],
        compiler_params=pltpu.CompilerParams(vmem_limit_bytes=VMEM, collective_id=identity, has_side_effects=True),
        cost_estimate=cost(4 * (m + 2 * reach) * width * columns, 12 * width * columns),
        name="qkv_back",
    )(x_t, d_query, d_key, d_value, w_attn, up_part, out_part)


def tiles_of(width):
    return width // TILE


def root_of(rows):
    return lax.rsqrt(jnp.mean(rows * rows, axis=-1, keepdims=True) + EPS)


def norm_grad(rows, gain, grad):
    root = root_of(rows)
    pushed = grad * gain
    inner = jnp.mean(pushed * rows, axis=-1, keepdims=True)
    return root * pushed - rows * (root * root * root * inner), jnp.sum(grad * rows * root, axis=0, keepdims=True)


def forward(far, near, tokens, gains, w_attn, cosine, sine, places, block, heads, identity):
    m, width = tokens.shape
    reach = 3 * m
    columns = heads * E
    devices = lax.axis_size("dp")
    sides = lax.axis_size("tensor")
    part_steps = m // ROWS
    per = TILE // E
    some = heads // per
    blocks = m // QB
    factor = E ** (-0.5) * LOG2E
    counts = (3 * part_steps, some, 2 * some, heads, part_steps, part_steps)
    starts = [sum(counts[:number]) for number in range(len(counts) + 1)]
    total = starts[-1]
    piece = block.shape[1] // 4

    own = width // devices

    def kernel(far_ref, near_ref, x_ref, again_ref, gains_ref, w_ref, c_ref, s_ref, places_ref, w_hbm, block_ref, nt_ref, q_out, kv_out, mixed_out, probs_ref, hidden_ref, normed_ref, turned_ref, whole_ref, g_ref, gf_ref, normed, q_all, kv_all, mixed_all, w_out, bias, sent, got, load_sem, y_send, y_recv, *scratch):
        step = pl.program_id(0)
        spread = Spread(devices, [(block_ref, number * piece, whole_ref, number * piece, piece) for number in range(4)], scratch)
        me, side = spread.me, spread.side
        other = (me, lax.rem(side + 1, sides))
        brought = loads((w_hbm.at[:, pl.ds(3 * columns, columns)],), (w_out,), load_sem)

        def across(which):
            return pltpu.make_async_remote_copy(
                src_ref=sent.at[which], dst_ref=got.at[which], send_sem=y_send.at[which], recv_sem=y_recv.at[which],
                device_id=other, device_id_type=MESH,
            )

        def phase(number):
            return pl.when((step >= starts[number]) & (step < starts[number + 1]))

        @pl.when(step == 0)
        def _():
            brought[0].start()
            spread.barrier((other,))
            spread.begin()
            for device in range(devices):
                span = slice(device * own, (device + 1) * own)
                g_ref[:, span] = gains_ref[device * 32 : device * 32 + 1, :own].astype(F32)
                gf_ref[:, span] = gains_ref[device * 32 + 16 : device * 32 + 17, :own].astype(F32)

        @phase(0)
        def _():
            here = pl.ds(pl.multiple_of(step * ROWS, ROWS), ROWS)

            def put(ref):
                rows = ref[...].astype(F32)
                made = (rows * root_of(rows) * g_ref[...]).astype(BF)
                normed[here, :] = made
                nt_ref[...] = made.T

            def earlier(ref, there):
                pl.when(there)(functools.partial(put, ref))

                @pl.when(jnp.logical_not(there))
                def _():
                    normed[here, :] = jnp.zeros((ROWS, width), BF)
                    nt_ref[...] = jnp.zeros((width, ROWS), BF)

            pl.when(step < part_steps)(functools.partial(earlier, far_ref, me >= 2))
            pl.when((step >= part_steps) & (step < 2 * part_steps))(functools.partial(earlier, near_ref, me >= 1))
            pl.when(step >= 2 * part_steps)(functools.partial(put, x_ref))

        def rotated(made, rows):
            pieces = [turned(made[:, part * E : (part + 1) * E], c_ref[rows, :], s_ref[rows, :], False) for part in range(per)]
            return jnp.concatenate(pieces, axis=1).astype(BF)

        @phase(1)
        def _():
            rows = slice(reach - m, reach)
            made = rotated(dot_nn(normed[rows, :], w_ref[...]), rows)
            q_out[...] = made
            q_all[:, pl.ds(pl.multiple_of((step - starts[1]) * TILE, TILE), TILE)] = made

        @phase(2)
        def _():
            number = step - starts[2]

            def put(made):
                kv_out[...] = made
                kv_all[:, pl.ds(pl.multiple_of(number * TILE, TILE), TILE)] = made

            @pl.when(number < some)
            def _():
                put(rotated(dot_nn(normed[...], w_ref[...]), slice(0, reach)))

            @pl.when(number >= some)
            def _():
                put(dot_nn(normed[...], w_ref[...]).astype(BF))

        @pl.when(step == starts[3])
        def _():
            for number in range(blocks):
                key = lax.broadcasted_iota(jnp.int32, (KB, QB), 0) + number * QB
                query = lax.broadcasted_iota(jnp.int32, (KB, QB), 1) + number * QB
                place = places_ref[:, number * QB : (number + 1) * QB]
                allowed = (key <= query + WINDOW) & (key > query) & (key >= query + WINDOW - place)
                bias[number] = jnp.where(allowed, 0.0, -1e30)

        @phase(3)
        def _():
            head = step - starts[3]
            lanes = pl.ds(pl.multiple_of(head * E, E), E)
            queries = q_all[:, lanes]
            keys = kv_all[:, lanes]
            values_t = kv_all[:, pl.ds(pl.multiple_of(columns + head * E, E), E)].T
            for number in range(blocks):
                span = slice(number * QB, number * QB + KB)
                here = slice(number * QB, (number + 1) * QB)
                scores = dot_nt(keys[span], queries[here]) * factor + bias[number]
                largest = jnp.max(scores, axis=0, keepdims=True)
                grown = jnp.exp2(scores - largest)
                inverse = 1.0 / jnp.sum(grown, axis=0, keepdims=True)
                probs = (grown * inverse).astype(BF)
                probs_ref[0, number] = probs
                made = dot_nn(values_t[:, span], probs).T.astype(BF)
                mixed_out[here, :] = made
                mixed_all[here, lanes] = made

        @pl.when(step == starts[4])
        def _():
            brought[0].wait()

        @phase(4)
        def _():
            which = step - starts[4]
            here = pl.ds(pl.multiple_of(which * ROWS, ROWS), ROWS)
            sent[which] = dot_nt(mixed_all[here, :], w_out[...]).astype(BF)
            across(which).start()

        @phase(5)
        def _():
            which = step - starts[5]
            across(which).wait()
            hidden = again_ref[...].astype(F32) + (sent[which].astype(F32) + got[which].astype(F32))
            made = (hidden * root_of(hidden) * gf_ref[...]).astype(BF)
            hidden_ref[...] = hidden
            normed_ref[...] = made
            turned_ref[...] = made.T

        spread.pace(step, list(zip(counts, (2, 2, 5, 5, 5, 20))))

        @pl.when(step == total - 1)
        def _():
            spread.finish()

    def within(number, i, length):
        return jnp.clip(i - starts[number], 0, length - 1)

    def rows_at(first):
        return pl.BlockSpec((ROWS, width), lambda i: (jnp.clip(i - first, 0, part_steps - 1), 0))

    any_space = pl.BlockSpec(memory_space=pl.ANY)
    dma = pltpu.SemaphoreType.DMA
    low = functools.partial(jax.ShapeDtypeStruct, dtype=BF)
    return pl.pallas_call(
        kernel,
        grid=(total,),
        out_shape=[
            low((width, reach)),
            low((m, columns)),
            low((reach, 2 * columns)),
            low((m, columns)),
            low((heads, blocks, KB, QB)),
            jax.ShapeDtypeStruct((m, width), F32),
            low((m, width)),
            low((width, m)),
            low((block.shape[0] * devices, block.shape[1])),
            jax.ShapeDtypeStruct((1, width), F32),
            jax.ShapeDtypeStruct((1, width), F32),
        ],
        in_specs=[
            rows_at(0), rows_at(part_steps), rows_at(2 * part_steps), rows_at(starts[5]),
            single(gains.shape),
            pl.BlockSpec((width, TILE), lambda i: (0, within(1, i, 3 * some))),
            single((reach, E)),
            single((reach, E)),
            single((1, m)),
            any_space,
            any_space,
        ],
        out_specs=[
            pl.BlockSpec((width, ROWS), lambda i: (0, within(0, i, 3 * part_steps))),
            pl.BlockSpec((m, TILE), lambda i: (0, within(1, i, some))),
            pl.BlockSpec((reach, TILE), lambda i: (0, within(2, i, 2 * some))),
            pl.BlockSpec((m, E), lambda i: (0, within(3, i, heads))),
            pl.BlockSpec((1, blocks, KB, QB), lambda i: (within(3, i, heads), 0, 0, 0)),
            rows_at(starts[5]),
            rows_at(starts[5]),
            pl.BlockSpec((width, ROWS), lambda i: (0, within(5, i, part_steps))),
            any_space,
            single((1, width)),
            single((1, width)),
        ],
        scratch_shapes=[
            pltpu.VMEM((reach, width), BF),
            pltpu.VMEM((m, columns), BF),
            pltpu.VMEM((reach, 2 * columns), BF),
            pltpu.VMEM((m, columns), BF),
            pltpu.VMEM((width, columns), BF),
            pltpu.VMEM((blocks, KB, QB), F32),
            pltpu.VMEM((part_steps, ROWS, width), BF),
            pltpu.VMEM((part_steps, ROWS, width), BF),
            dma((1,)),
            dma((part_steps,)),
            dma((part_steps,)),
            *Spread.scratch(devices, 4),
        ],
        compiler_params=pltpu.CompilerParams(vmem_limit_bytes=VMEM, collective_id=identity, has_side_effects=True),
        cost_estimate=cost(2 * (m + 2 * reach) * width * columns, 8 * reach * width, heads * m * KB),
        name="forward",
    )(far, near, tokens, tokens, gains, w_attn, cosine, sine, places, w_attn, block)


def last_pass(tokens, gain, grad, grad_other, grad_add, d_hidden, hidden, ffn_part, ffn_other, act_early, act_late, w_ffn, rest, gain_ffn_grad, flip, qkv_part, lanes, identity):
    m, width = tokens.shape
    devices, rows, all_columns = qkv_part.shape
    columns = all_columns // 3
    chips = devices // 2
    size = ROWS // 2
    steps = m // size
    downs = tiles_of(width) - SOON
    total = downs + steps + chips
    names = 3
    half = m // 2
    tiles = tiles_of(width)
    some, late = act_early.shape[1], act_late.shape[1]
    sides = lax.axis_size("tensor")
    assert chips >= tiles

    def kernel(x_ref, g_ref, dn_ref, do_ref, add_hbm, dh_ref, h_ref, fp_ref, fo_ref, a_hbm, al_hbm, w_ref, rest_ref, gf_ref, flip_hbm, source, grad_ref, layer_ref, flipped_ref, q_ref, k_ref, v_ref, gains_ref, a_ref, al_ref, flip_ref, add, load_sem, add_send, add_recv, gain_sum, gain_source, gain_in, gain_send, gain_recv, sent, got, y_send, y_recv, *scratch):
        step = pl.program_id(0)
        ring = Ring(
            devices, [(source, number * columns, columns) for number in range(names)], [(q_ref, 0), (k_ref, 0), (v_ref, 0)],
            [[0], [1], [2]], scratch,
        )

        def gain_copy(away):
            owner = lax.rem(ring.me + away, devices)
            return pltpu.make_async_remote_copy(
                src_ref=gain_source.at[owner], dst_ref=gain_in.at[away], send_sem=gain_send.at[away], recv_sem=gain_recv.at[away],
                device_id=(owner, ring.side), device_id_type=MESH,
            )

        other = (ring.me, lax.rem(ring.side + 1, sides))
        brought = loads((a_hbm, al_hbm, flip_hbm, add_hbm), (a_ref, al_ref, flip_ref, add.at[ring.side]), load_sem)
        add_copy = pltpu.make_async_remote_copy(
            src_ref=add_hbm, dst_ref=add.at[ring.side], send_sem=add_send, recv_sem=add_recv, device_id=other, device_id_type=MESH
        )
        row_step = step - downs
        end_step = step - downs - steps

        def across(which):
            return pltpu.make_async_remote_copy(
                src_ref=sent.at[which], dst_ref=got.at[which], send_sem=y_send.at[which], recv_sem=y_recv.at[which],
                device_id=other, device_id_type=MESH,
            )

        @pl.when(step == 0)
        def _():
            for copy in brought:
                copy.start()
            ring.barrier((other, *[(lax.rem(ring.me + away, devices), ring.side) for away in range(1, devices)]))
            add_copy.start()
            ring.begin()
            for copy in brought:
                copy.wait()
            flipped_ref[...] = flip_ref[...].T

        @pl.when(row_step == 0)
        def _():
            add_copy.wait()

        @pl.when(step < downs)
        def _():
            sent[step] = (dot_nt(a_ref[...], w_ref[...]) + dot_nt(al_ref[...], rest_ref[...])).astype(BF)
            across(step).start()

        @pl.when((row_step >= 0) & (row_step < steps))
        def _():
            which = row_step * size // half
            here = pl.ds(pl.multiple_of(row_step * size - which * half, size), size)
            grad_rows = dn_ref[...].astype(F32) + do_ref[...].astype(F32) + add[which, here, :].astype(F32)
            change, gain_part = norm_grad(x_ref[...].astype(F32), g_ref[...], grad_rows)
            grad_ref[...] = dh_ref[...] + change

            @pl.when(row_step == 0)
            def _():
                gain_sum[...] = gain_part

            @pl.when(row_step > 0)
            def _():
                gain_sum[...] += gain_part

        @pl.when(row_step == steps - 1)
        def _():
            gain_source[...] = jnp.zeros_like(gain_source)
            for device in range(devices):
                span = slice(device * rows, (device + 1) * rows)
                gain_source[device, :16, :rows] = jnp.broadcast_to(gain_sum[:, span], (16, rows)).astype(BF)
                gain_source[device, 16:, :rows] = jnp.broadcast_to(gf_ref[:, span], (16, rows)).astype(BF)

            def send(away, carry):
                gain_copy(away).start()
                return carry

            lax.fori_loop(1, devices, send, 0)

        ring.pace(step, [(downs, 5), (steps, 3), (chips, 3)])

        @pl.when((end_step >= 0) & (end_step < SOON))
        def _():
            layer_ref[...] = (h_ref[...] + (fp_ref[...].astype(F32) + fo_ref[...].astype(F32))).astype(BF)

        @pl.when((end_step >= SOON) & (end_step < tiles))
        def _():
            which = end_step - SOON
            across(which).wait()
            layer_ref[...] = (h_ref[...] + (sent[which].astype(F32) + got[which].astype(F32))).astype(BF)

        @pl.when(step == total - 1)
        def _():
            ring.finish()

            def take(away, total):
                gain_copy(away).wait()
                return total + gain_in[away].astype(F32)

            gains_ref[...] = lax.fori_loop(1, devices, take, gain_source[ring.me].astype(F32))

    def early(i):
        return jnp.minimum(i, downs - 1) + SOON

    def ending(i):
        return jnp.clip(i - downs - steps, 0, tiles - 1)

    rows_spec = pl.BlockSpec((size, width), lambda i: (jnp.clip(i - downs, 0, steps - 1), 0))
    tile_spec = pl.BlockSpec((m, TILE), lambda i: (0, ending(i)))
    soon_spec = pl.BlockSpec((m, TILE), lambda i: (0, jnp.minimum(ending(i), SOON - 1)))
    dma = pltpu.SemaphoreType.DMA
    sums = jax.ShapeDtypeStruct((rows, columns), F32)
    return pl.pallas_call(
        kernel,
        grid=(total,),
        out_shape=[
            jax.ShapeDtypeStruct((m, width), F32),
            jax.ShapeDtypeStruct((m, width), BF),
            jax.ShapeDtypeStruct((flip.shape[1], flip.shape[0]), F32),
            sums, sums, sums,
            jax.ShapeDtypeStruct((32, lanes), F32),
        ],
        in_specs=[
            rows_spec, single((1, width)), rows_spec, rows_spec, pl.BlockSpec(memory_space=pl.ANY), rows_spec, tile_spec, soon_spec, soon_spec, pl.BlockSpec(memory_space=pl.ANY), pl.BlockSpec(memory_space=pl.ANY),
            pl.BlockSpec((TILE, some), lambda i: (early(i), 2)), pl.BlockSpec((TILE, late), lambda i: (early(i), 2)), single((1, width)),
            pl.BlockSpec(memory_space=pl.ANY), pl.BlockSpec(memory_space=pl.ANY),
        ],
        out_specs=[
            rows_spec, tile_spec, single((flip.shape[1], flip.shape[0])),
            single(sums.shape), single(sums.shape), single(sums.shape), single((32, lanes)),
        ],
        scratch_shapes=[
            pltpu.VMEM((m, some), BF),
            pltpu.VMEM((m, late), BF),
            pltpu.VMEM(flip.shape, F32),
            pltpu.VMEM((2, half, width), BF),
            dma((4,)),
            dma,
            dma,
            pltpu.VMEM((1, width), F32),
            pltpu.VMEM((devices, 32, lanes), BF),
            pltpu.VMEM((devices, 32, lanes), BF),
            dma((devices,)),
            dma((devices,)),
            pltpu.VMEM((downs, m, TILE), BF),
            pltpu.VMEM((downs, m, TILE), BF),
            dma((downs,)),
            dma((downs,)),
            *Ring.scratch(devices, [(rows, columns)] * names),
        ],
        compiler_params=pltpu.CompilerParams(vmem_limit_bytes=VMEM, collective_id=identity, has_side_effects=True),
        cost_estimate=cost(20 * m * width, 24 * m * width),
        name="last_pass",
    )(tokens, gain, grad, grad_other, grad_add, d_hidden, hidden, ffn_part, ffn_other, act_early, act_late, w_ffn, rest, gain_ffn_grad, flip, qkv_part)


def feed_tile(x_ref, dy_ref, dyt_ref, g_ref, u_ref, d_ref, act_ref, both_ref, down_ref):
    gate = dot_nn(x_ref[...], g_ref[...])
    up = dot_nn(x_ref[...], u_ref[...])
    d_act = dot_nn(dy_ref[...], d_ref[...])
    soft = 1.0 / (1.0 + jnp.exp(-gate))
    silu = gate * soft
    act = (silu * up).astype(BF)
    act_ref[...] = act
    both_ref[0] = (d_act * up * (soft * (1.0 + gate * (1.0 - soft)))).astype(BF)
    both_ref[1] = (d_act * silu).astype(BF)
    down_ref[...] = dot_nn(dyt_ref[...], act).astype(BF)


def feed(x, dy, dy_t, w, block, tiles, identity):
    m, k = x.shape
    early = tiles - LATE
    devices = lax.axis_size("dp")
    width = block.shape[1] // 2

    def kernel(x_hbm, dy_hbm, dyt_hbm, g_ref, u_ref, d_ref, block_ref, act_ref, both_ref, down_ref, rest_ref, x_ref, dy_ref, dyt_ref, load_sem, *scratch):
        step = pl.program_id(0)
        brought = loads((x_hbm, dy_hbm, dyt_hbm), (x_ref, dy_ref, dyt_ref), load_sem)
        spread = Spread(devices, [(block_ref, 0, rest_ref, 0, width), (block_ref, width, rest_ref, width, width)], scratch)

        @pl.when(step == 0)
        def _():
            for copy in brought:
                copy.start()
            spread.barrier()
            spread.begin()
            for copy in brought:
                copy.wait()

        feed_tile(x_ref, dy_ref, dyt_ref, g_ref, u_ref, d_ref, act_ref, both_ref, down_ref)
        spread.pace(step, [(early, 1)])

        @pl.when(step == early - 1)
        def _():
            spread.finish()

    any_space = pl.BlockSpec(memory_space=pl.ANY)
    return pl.pallas_call(
        kernel,
        grid=(early,),
        out_shape=[
            jax.ShapeDtypeStruct((m, early * TILE), BF),
            jax.ShapeDtypeStruct((2, m, early * TILE), BF),
            jax.ShapeDtypeStruct((k, early * TILE), BF),
            jax.ShapeDtypeStruct((k, block.shape[1]), BF),
        ],
        in_specs=[
            any_space, any_space, any_space,
            pl.BlockSpec((k, TILE), lambda i: (0, i)),
            pl.BlockSpec((k, TILE), lambda i: (0, i + early)),
            pl.BlockSpec((k, TILE), lambda i: (0, i + 2 * early)),
            any_space,
        ],
        out_specs=[
            pl.BlockSpec((m, TILE), lambda i: (0, i)),
            pl.BlockSpec((2, m, TILE), lambda i: (0, 0, i)),
            pl.BlockSpec((k, TILE), lambda i: (0, i)),
            any_space,
        ],
        scratch_shapes=[
            pltpu.VMEM((m, k), BF), pltpu.VMEM((m, k), BF), pltpu.VMEM((k, m), BF), pltpu.SemaphoreType.DMA((3,)),
            *Spread.scratch(devices, 2),
        ],
        compiler_params=pltpu.CompilerParams(vmem_limit_bytes=VMEM, collective_id=identity, has_side_effects=True),
        cost_estimate=cost(8 * m * k * early * TILE, 8 * (m + k) * early * TILE, m * early * TILE),
        name="feed",
    )(x, dy, dy_t, w, w, w, block)


def ffn_back(x, x_t, dy, dy_t, d_early, w_ffn, rest, down_early, identity):
    m, width = x.shape
    devices, rows, some = down_early.shape
    late = LATE * TILE
    padded = some + late
    tiles = width // TILE
    wide = 2 * TILE
    early_wide, late_wide = some // wide, (late + wide - 1) // wide
    grads = 2 * (early_wide + late_wide)
    total = LATE + tiles + grads
    sides = lax.axis_size("tensor")
    pieces = [(rows, some // 2)] * 2

    def kernel(x_hbm, xt_hbm, dy_hbm, dyt_hbm, rg_ref, ru_ref, rd_ref, d_hbm, tile_ref, wg_ref, wu_ref, lg_ref, lu_ref, source, act_ref, grad_ref, sent_ref, got, sum_ref, x_ref, xt_ref, dy_ref, dyt_ref, d_ref, load_sem, d_late, down_late, down_tile, both_tile, sent, y_send, y_recv, *scratch):
        step = pl.program_id(0)
        brought = loads((x_hbm, dy_hbm, dyt_hbm, d_hbm, xt_hbm), (x_ref, dy_ref, dyt_ref, d_ref, xt_ref), load_sem)
        ring = Ring(devices, [(source, 0, some // 2), (source, some // 2, some // 2)], [(sum_ref, 0), (sum_ref, some // 2)], [[0], [1]], scratch[:11])
        late_ring = Ring(devices, [(down_late, 0, late)], [(sum_ref, some)], [[0]], scratch[11:])
        other = (ring.me, lax.rem(ring.side + 1, sides))

        def across(which):
            return pltpu.make_async_remote_copy(
                src_ref=sent.at[which], dst_ref=got.at[:, pl.ds(pl.multiple_of(which * TILE, TILE), TILE)],
                send_sem=y_send.at[which], recv_sem=y_recv.at[which], device_id=other, device_id_type=MESH,
            )

        @pl.when(step == 0)
        def _():
            for copy in brought:
                copy.start()
            ring.barrier((other,))
            ring.begin()
            for copy in brought[:3]:
                copy.wait()

        @pl.when(step == LATE)
        def _():
            brought[3].wait()

        @pl.when(step == LATE + tiles)
        def _():
            brought[4].wait()

        @pl.when(step < LATE)
        def _():
            feed_tile(x_ref, dy_ref, dyt_ref, rg_ref, ru_ref, rd_ref, act_ref, both_tile, down_tile)
            here = pl.ds(pl.multiple_of(step * TILE, TILE), TILE)
            d_late[:, :, here] = both_tile[...]
            down_late[:, :, here] = down_tile[...].reshape(devices, rows, TILE)

        @pl.when(step == LATE - 1)
        def _():
            late_ring.begin()

        @pl.when((step >= LATE) & (step < LATE + tiles))
        def _():
            which = step - LATE
            part = dot_nt(d_ref[0], wg_ref[...]) + dot_nt(d_ref[1], wu_ref[...])
            part += dot_nt(d_late[0], lg_ref[...]) + dot_nt(d_late[1], lu_ref[...])
            low = part.astype(BF)
            sent[which] = low
            sent_ref[...] = low
            across(which).start()

        @pl.when((step >= LATE + tiles) & (step < LATE + tiles + 2 * early_wide))
        def _():
            grad_ref[0] = dot_nn(xt_ref[...], tile_ref[0]).astype(BF)

        number = step - (LATE + tiles + 2 * early_wide)
        for part in range(late_wide):
            several = min(wide, late - part * wide)

            @pl.when((number >= 0) & (lax.rem(number, late_wide) == part))
            def _():
                piece = d_late[number // late_wide, :, part * wide : part * wide + several]
                grad_ref[0, :, :several] = dot_nn(xt_ref[...], piece).astype(BF)

        ring.pace(step, [(LATE, 12), (tiles, 8), (grads, 7)])
        late_ring.pace(step, [(LATE, 0), (tiles, 8), (grads, 7)])

        @pl.when(step == total - 1)
        def _():
            for which in range(tiles):
                across(which).wait()
            ring.finish()
            late_ring.finish()

    def first(i):
        return jnp.minimum(i, LATE - 1)

    def second(i):
        return jnp.clip(i - LATE, 0, tiles - 1)

    def third(i):
        at = jnp.clip(i - LATE - tiles, 0, 2 * early_wide - 1)
        return (at // early_wide, 0, at % early_wide)

    def grad_at(i):
        at = jnp.maximum(i - LATE - tiles, 0)
        more = jnp.maximum(at - 2 * early_wide, 0)
        is_late = at // (2 * early_wide)
        return (
            (1 - is_late) * (at // early_wide) + is_late * (more // late_wide),
            0,
            (1 - is_late) * (at % early_wide) + is_late * (early_wide + more % late_wide),
        )

    assert late_wide <= early_wide and some % wide == 0
    any_space = pl.BlockSpec(memory_space=pl.ANY)
    dma = pltpu.SemaphoreType.DMA

    def rest_tile(which):
        return pl.BlockSpec((width, TILE), lambda i: (0, first(i) + which * LATE))

    return pl.pallas_call(
        kernel,
        grid=(total,),
        out_shape=[
            jax.ShapeDtypeStruct((m, late), BF),
            jax.ShapeDtypeStruct((2, width, padded), BF),
            jax.ShapeDtypeStruct((m, width), BF),
            jax.ShapeDtypeStruct((m, width), BF),
            jax.ShapeDtypeStruct((rows, padded), F32),
        ],
        in_specs=[
            any_space, any_space, any_space, any_space,
            rest_tile(0), rest_tile(1), rest_tile(2),
            any_space,
            pl.BlockSpec((1, m, wide), third),
            pl.BlockSpec((TILE, some), lambda i: (second(i), 0)),
            pl.BlockSpec((TILE, some), lambda i: (second(i), 1)),
            pl.BlockSpec((TILE, late), lambda i: (second(i), 0)),
            pl.BlockSpec((TILE, late), lambda i: (second(i), 1)),
            any_space,
        ],
        out_specs=[
            pl.BlockSpec((m, TILE), lambda i: (0, first(i))),
            pl.BlockSpec((1, width, wide), grad_at),
            pl.BlockSpec((m, TILE), lambda i: (0, second(i))),
            any_space,
            single((rows, padded)),
        ],
        scratch_shapes=[
            pltpu.VMEM((m, width), BF),
            pltpu.VMEM((width, m), BF),
            pltpu.VMEM((m, width), BF),
            pltpu.VMEM((width, m), BF),
            pltpu.VMEM((2, m, some), BF),
            dma((5,)),
            pltpu.VMEM((2, m, late), BF),
            pltpu.VMEM((devices, rows, late), BF),
            pltpu.VMEM((width, TILE), BF),
            pltpu.VMEM((2, m, TILE), BF),
            pltpu.VMEM((tiles, m, TILE), BF),
            dma((tiles,)),
            dma((tiles,)),
            *Ring.scratch(devices, pieces),
            *Ring.scratch(devices, [(rows, late)]),
        ],
        compiler_params=pltpu.CompilerParams(vmem_limit_bytes=VMEM, collective_id=identity, has_side_effects=True),
        cost_estimate=cost(8 * m * width * padded + 8 * m * width * late, 10 * width * padded),
        name="ffn_back",
    )(x, x_t, dy, dy_t, rest, rest, rest, d_early, d_early, w_ffn, w_ffn, rest, rest, down_early)


def shards(tokens, positions, attn_gain, w_query, w_key, w_value, w_out, ffn_gain, w_gate, w_up, w_down, cotangent):
    devices = lax.axis_size("dp")
    span = tokens.shape[0]
    assert 2 * span == WINDOW
    own_rows = w_query.shape[0]
    width = tokens.shape[1]
    head_columns = w_query.shape[1]
    heads = head_columns // E
    hidden_units = w_gate.shape[1]
    tiles = (hidden_units + TILE - 1) // TILE
    padded = tiles * TILE

    some = padded - LATE * TILE
    lanes = max(128, own_rows)
    places = positions[None, :]
    w_attn, all_gains, near, far, ffn_pack, rest_pack, cotangent_t, cosine, sine = first_gather(
        w_query, w_key, w_value, w_out, attn_gain, ffn_gain, tokens, w_gate.T, w_up.T, w_down, cotangent, places, 0
    )
    normed_attn_t, query, kv, mixed, probs, hidden, normed_ffn, normed_ffn_t, w_ffn, gain_attn, gain_ffn = forward(
        far, near, tokens, all_gains, w_attn, cosine, sine, places, ffn_pack, heads, 5
    )

    act_early, d_early, down_early, rest = feed(normed_ffn, cotangent, cotangent_t, w_ffn, rest_pack, tiles, 6)
    act_late, both_part, d_normed_ffn, d_normed_other, down_grad = ffn_back(
        normed_ffn, normed_ffn_t, cotangent, cotangent_t, d_early, w_ffn, rest, down_early.reshape(devices, own_rows, some), 1
    )
    both_part = both_part.reshape(2, devices, own_rows, padded)

    d_query, d_key, d_value, out_part, gate_grad, w_down_grad, d_hidden, gain_ffn_grad, ffn_part, ffn_other = attend_back(
        query, kv, probs, mixed, w_attn, hidden, gain_ffn, d_normed_ffn, d_normed_other, cotangent, cosine, sine, down_grad, act_early, act_late, w_ffn, rest,
        both_part, heads, hidden_units, 2,
    )
    qkv_part, d_normed_attn, d_attn_other, d_attn_add, up_grad, out_grad = qkv_back(
        normed_attn_t, d_query, d_key, d_value, w_attn, both_part, out_part.reshape(devices, own_rows, head_columns), hidden_units, 3
    )
    tokens_grad, layer_out, w_out_grad, query_grad, key_grad, value_grad, gain_grads = last_pass(
        tokens, gain_attn, d_normed_attn, d_attn_other, d_attn_add, d_hidden, hidden, ffn_part, ffn_other, act_early, act_late, w_ffn, rest, gain_ffn_grad, out_grad,
        qkv_part.reshape(devices, own_rows, 3 * head_columns), lanes, 4,
    )
    return (
        layer_out,
        tokens_grad,
        gain_grads[0, :own_rows],
        query_grad,
        key_grad,
        value_grad,
        w_out_grad,
        gain_grads[16, :own_rows],
        gate_grad,
        up_grad,
        w_down_grad,
    )


def solution(mesh):
    by_rows, by_both, turned_both, line = P("dp", None), P("dp", "tensor"), P("tensor", "dp"), P("dp")
    return jax.shard_map(
        shards,
        mesh=mesh,
        in_specs=(by_rows, line, line, by_both, by_both, by_both, turned_both, line, by_both, by_both, turned_both, by_rows),
        out_specs=(by_rows, by_rows, line, by_both, by_both, by_both, turned_both, line, by_both, by_both, turned_both),
        check_vma=False,
    )
```

```python
import functools

import jax
import jax.numpy as jnp
import numpy as np
from jax import lax
from jax.experimental import pallas as pl
from jax.experimental.pallas import tpu as pltpu
from jax.sharding import PartitionSpec as P

E = 128
WINDOW = 1024
EPS = 1e-06
THETA = 10000.0
LOG2E = 1.4426950408889634
MESH = pl.DeviceIdType.MESH
BF = jnp.bfloat16
F32 = jnp.float32
QB = 256
KB = WINDOW + QB
TILE = 256
ROWS = 128
SOON = 3
LATE = 3
VMEM = 59 * 1024 * 1024


def whole_spec(shape):
    return pl.BlockSpec(shape, lambda i: (0,) * len(shape))


def single(shape):
    return pl.BlockSpec(shape, lambda i: (0,) * len(shape), pipeline_mode=pl.Buffered(1))


def loads(sources, targets, semaphores):
    return [pltpu.make_async_copy(s, t, semaphores.at[i]) for i, (s, t) in enumerate(zip(sources, targets))]


def cost(flops, nbytes, special=0):
    return pl.CostEstimate(flops=flops, bytes_accessed=nbytes, transcendentals=special)


def ring_chip(place, chips):
    place = lax.rem(place + 2 * chips, chips)
    late = place // (chips // 2)
    return (1 - late) * 2 * place + late * (2 * (chips - 1 - place) + 1)


def ring_place(chip, chips):
    column = lax.rem(chip, 2)
    row = chip // 2
    return (1 - column) * row + column * (chips - 1 - row)


def paced(at, costs, events):
    spent, before = 0, 0
    for steps, each in costs:
        spent = spent + jnp.minimum(jnp.maximum(at - before, 0), steps) * each
        before += steps
    return spent * events // sum(steps * each for steps, each in costs)


class Spread:
    def __init__(self, devices, pieces, scratch):
        self.devices, self.chips, self.pieces = devices, devices // 2, pieces
        self.local_sem, self.send_sem, self.recv_sem, self.give_sem, self.take_sem = scratch
        self.me = lax.axis_index("dp")
        self.side = lax.axis_index("tensor")
        self.core = lax.rem(self.me, 2)
        self.place = ring_place(self.me // 2, self.chips)
        self.partner = self.me + 1 - 2 * self.core
        self.next = (
            ring_chip(self.place + 1, self.chips) * 2 + self.core,
            ring_chip(self.place - 1, self.chips) * 2 + self.core,
        )
        self.events = (self.chips - 1) * len(pieces)

    @staticmethod
    def scratch(devices, count):
        dma = pltpu.SemaphoreType.DMA
        chips = devices // 2
        return [dma((count,))] + [dma((count, amount, 2)) for amount in (chips - 1, chips - 1, chips, chips)]

    def barrier(self, others=()):
        semaphore = pltpu.get_barrier_semaphore()
        everyone = [(self.next[0], self.side), (self.next[1], self.side), (self.partner, self.side), *others]
        for other in everyone:
            pl.semaphore_signal(semaphore, inc=1, device_id=other, device_id_type=MESH)
        pl.semaphore_wait(semaphore, len(everyone))

    def block(self, index, stage, half):
        source, _, whole, column, width = self.pieces[index]
        rows = source.shape[0]
        owner = ring_chip(self.place - stage if half == 0 else self.place + stage, self.chips) * 2 + self.core
        return whole.at[pl.ds(pl.multiple_of(owner * rows + half * (rows // 2), 16), rows // 2), pl.ds(column, width)]

    def first(self, index, half):
        source, column, _, _, width = self.pieces[index]
        rows = source.shape[0]
        return source.at[pl.ds(half * (rows // 2), rows // 2), pl.ds(column, width)]

    def local(self, index):
        source, start, whole, column, width = self.pieces[index]
        rows = source.shape[0]
        span = pl.ds(pl.multiple_of(self.me * rows, 16), rows)
        return pltpu.make_async_copy(
            source.at[:, pl.ds(start, width)], whole.at[span, pl.ds(column, width)], self.local_sem.at[index]
        )

    def copy(self, index, stage, half, start, across):
        block = self.block(index, stage, half)
        send, recv = (self.give_sem, self.take_sem) if across else (self.send_sem, self.recv_sem)
        return pltpu.make_async_remote_copy(
            src_ref=self.first(index, half) if start else block,
            dst_ref=block,
            send_sem=send.at[index, stage, half],
            recv_sem=recv.at[index, stage, half],
            device_id=(self.partner if across else self.next[half], self.side),
            device_id_type=MESH,
        )

    def each(self):
        return [(index, half) for index in range(len(self.pieces)) for half in range(2)]

    def begin(self):
        for index, half in self.each():
            self.copy(index, 0, half, True, False).start()
        for index, half in self.each():
            self.copy(index, 0, half, True, True).start()
        for index in range(len(self.pieces)):
            self.local(index).start()

    def stage(self, stage, index):
        for half in range(2):
            self.copy(index, stage - 1, half, False, False).wait_recv()

            @pl.when(stage < self.chips - 1)
            def _():
                self.copy(index, stage, half, False, False).start()

            self.copy(index, stage, half, False, True).start()

    def pace(self, step, costs):
        count = len(self.pieces)

        def one(event, carry):
            for index in range(count):
                pl.when(lax.rem(event, count) == index)(functools.partial(self.stage, event // count + 1, index))
            return carry

        lax.fori_loop(paced(step, costs, self.events), paced(step + 1, costs, self.events), one, 0)

    def finish(self):
        for index in range(len(self.pieces)):
            self.local(index).wait()
        for index, half in self.each():
            self.copy(index, 0, half, True, False).wait_send()
            self.copy(index, 0, half, True, True).wait()

        def sent(stage, carry):
            for index, half in self.each():
                self.copy(index, stage, half, False, False).wait_send()
            return carry

        lax.fori_loop(1, self.chips - 1, sent, 0)

        def gave(stage, carry):
            for index, half in self.each():
                self.copy(index, stage, half, False, True).wait()
            return carry

        lax.fori_loop(1, self.chips, gave, 0)


def first_gather(w_query, w_key, w_value, w_out, attn_gain, ffn_gain, tokens, w_gate_t, w_up_t, w_down, cotangent, places, identity):
    devices = lax.axis_size("dp")
    sides = lax.axis_size("tensor")
    rows, columns = w_query.shape
    units = w_down.shape[0]
    tiles = (units + TILE - 1) // TILE
    padded, late = tiles * TILE, LATE * TILE
    some = padded - late
    m, width = tokens.shape
    span = m // 2
    reach = WINDOW + m
    rates = THETA ** (-(np.arange(E // 2, dtype=np.float32) * 2.0 / E))
    rates = jnp.asarray(np.concatenate([rates, rates])[None, :], F32)

    lanes = max(128, rows)

    def kernel(q_ref, k_ref, v_ref, o_hbm, tokens_ref, gate_hbm, up_hbm, down_hbm, dy_hbm, ag_ref, fg_ref, places_ref, rates_ref, attn_ref, all_ref, near, far, early_hbm, late_hbm, dyt_hbm, cos_hbm, sin_hbm, o_in, o_turned, gate_in, up_in, down_in, early_pack, late_pack, dy_in, dyt, cosine, sine, gains_ref, load_sem, store_sem, far_send, far_recv, near_send, near_recv, *scratch):
        pieces = [(ref, 0, attn_ref, number * columns, columns) for number, ref in enumerate((q_ref, k_ref, v_ref, o_turned))]
        spread = Spread(devices, [*pieces, (gains_ref, 0, all_ref, 0, lanes)], scratch)
        me, side, core = spread.me, spread.side, spread.core
        across = lax.rem(side + 1, sides)
        later, before = lax.rem(me + 2, devices), lax.rem(me + devices - 2, devices)
        parts = (gate_in, up_in, down_in)
        brought = loads(
            (o_hbm, gate_hbm, up_hbm, down_hbm, dy_hbm), (o_in, *[part.at[pl.ds(0, units)] for part in parts], dy_in), load_sem
        )
        stored = loads((early_pack, late_pack, dyt, cosine, sine), (early_hbm, late_hbm, dyt_hbm, cos_hbm, sin_hbm), store_sem)

        def tables(first, made):
            angles = made * rates_ref[...]
            lane = lax.broadcasted_iota(jnp.int32, (E, E), 1)
            cosine[first : first + E, :] = jnp.cos(angles)
            turn = jnp.sin(angles)
            sine[first : first + E, :] = jnp.where(lane < E // 2, -turn, turn)

        def own_tables():
            for first in range(0, m, E):
                row = places_ref[:, first : first + E].astype(F32)
                tables(WINDOW + first, jnp.broadcast_to(row, (E, E)).T)

        def earlier_tables(begin, end):
            for first in range(begin, end, E):
                row = lax.broadcasted_iota(jnp.int32, (E, E), 0) + (first - WINDOW)
                tables(first, (row + places_ref[:, :1]).astype(F32))

        for copy in brought:
            copy.start()
        spread.barrier(((me, across), (later, side), (before, side)))

        def described(source, target, send, recv, other):
            return pltpu.make_async_remote_copy(
                src_ref=source, dst_ref=target, send_sem=send, recv_sem=recv, device_id=other, device_id_type=MESH
            )

        def half_rows(ref, which):
            return ref.at[pl.ds(pl.multiple_of(which * span, span), span)]

        far_copy = described(half_rows(tokens_ref, side), half_rows(far, side), far_send.at[0], far_recv.at[0], (later, side))
        cross_copy = described(half_rows(far, side), half_rows(far, side), far_send.at[1], far_recv.at[1], (me, across))

        def near_copy(source, which, slot):
            return described(half_rows(source, which), half_rows(near, which), near_send.at[slot], near_recv.at[slot], (spread.partner, side))

        own_near = [near_copy(tokens_ref, which, which) for which in range(2)]
        far_near = [near_copy(far, which, slot) for slot, which in enumerate((side, across))]

        gains_ref[...] = jnp.zeros_like(gains_ref)
        gains_ref[:16, :rows] = jnp.broadcast_to(ag_ref[...], (16, rows))
        gains_ref[16:, :rows] = jnp.broadcast_to(fg_ref[...], (16, rows))
        brought[0].wait()
        o_turned[...] = o_in[...].T
        spread.begin()

        @pl.when(me < devices - 2)
        def _():
            far_copy.start()

        @pl.when(core == 0)
        def _():
            for copy in own_near:
                copy.start()

        for number, part in enumerate(parts):
            brought[1 + number].wait()
            part[units:, :] = jnp.zeros((padded - units, rows), BF)
            made = part[...].T
            early_pack[:, number * some : (number + 1) * some] = made[:, :some]
            late_pack[:, number * late : (number + 1) * late] = made[:, some:]
        for copy in stored[:2]:
            copy.start()

        def one(stage, carry):
            for index in range(len(pieces) + 1):
                spread.stage(stage, index)

            pl.when(stage == 1)(own_tables)
            pl.when(stage == 2)(functools.partial(earlier_tables, 0, WINDOW // 2))
            pl.when(stage == 3)(functools.partial(earlier_tables, WINDOW // 2, WINDOW))

            @pl.when(stage == 4)
            def _():
                brought[4].wait()
                dyt[...] = dy_in[...].T
                for copy in stored[2:]:
                    copy.start()

            @pl.when((stage == spread.chips // 2) & (me >= 2))
            def _():
                far_copy.wait_recv()
                cross_copy.start()

                @pl.when(core == 1)
                def _():
                    far_near[0].start()

            @pl.when((stage == spread.chips - 2) & (me >= 2))
            def _():
                cross_copy.wait_recv()

                @pl.when(core == 1)
                def _():
                    far_near[1].start()

            return carry

        lax.fori_loop(1, spread.chips, one, 0)
        for copy in stored:
            copy.wait()
        spread.finish()

        @pl.when(me < devices - 2)
        def _():
            far_copy.wait_send()

        @pl.when(me >= 2)
        def _():
            cross_copy.wait_send()

            @pl.when(core == 1)
            def _():
                for copy in far_near:
                    copy.wait_send()

        @pl.when(core == 0)
        def _():
            for copy in own_near:
                copy.wait_send()

        @pl.when((core == 1) | (me >= 2))
        def _():
            for copy in own_near:
                copy.wait_recv()

    dma = pltpu.SemaphoreType.DMA
    any_space = pl.BlockSpec(memory_space=pl.ANY)
    low = functools.partial(jax.ShapeDtypeStruct, dtype=BF)
    return pl.pallas_call(
        kernel,
        out_shape=[
            low((rows * devices, 4 * columns)),
            low((32 * devices, lanes)),
            low(tokens.shape),
            low(tokens.shape),
            low((rows, 3 * some)),
            low((rows, 3 * late)),
            low((width, m)),
            jax.ShapeDtypeStruct((reach, E), F32),
            jax.ShapeDtypeStruct((reach, E), F32),
        ],
        in_specs=[any_space] * 9 + [pl.BlockSpec(memory_space=pltpu.VMEM)] * 4,
        out_specs=[any_space] * 9,
        scratch_shapes=[
            pltpu.VMEM(w_out.shape, BF),
            pltpu.VMEM((rows, columns), BF),
            *[pltpu.VMEM((padded, rows), BF)] * 3,
            pltpu.VMEM((rows, 3 * some), BF),
            pltpu.VMEM((rows, 3 * late), BF),
            pltpu.VMEM((m, width), BF),
            pltpu.VMEM((width, m), BF),
            pltpu.VMEM((reach, E), F32),
            pltpu.VMEM((reach, E), F32),
            pltpu.VMEM((32, lanes), BF),
            dma((5,)),
            dma((5,)),
            dma((2,)),
            dma((2,)),
            dma((2,)),
            dma((2,)),
            *Spread.scratch(devices, 5),
        ],
        compiler_params=pltpu.CompilerParams(vmem_limit_bytes=VMEM, collective_id=identity, has_side_effects=True),
        name="first_gather",
    )(w_query, w_key, w_value, w_out, tokens, w_gate_t, w_up_t, w_down, cotangent, attn_gain[None, :], ffn_gain[None, :], places, rates)


class Ring:
    AHEAD = 3

    def __init__(self, devices, terms, goals, groups, scratch):
        self.devices, self.chips = devices, devices // 2
        self.terms, self.goals, self.groups = terms, goals, groups
        count = len(terms)
        self.mine, self.taken, self.inbox = scratch[0 : 3 * count : 3], scratch[1 : 3 * count : 3], scratch[2 : 3 * count : 3]
        self.own_sem, self.give_sem, self.take_sem, self.send_sem, self.recv_sem = scratch[3 * count : 3 * count + 5]
        self.me = lax.axis_index("dp")
        self.side = lax.axis_index("tensor")
        self.core = lax.rem(self.me, 2)
        self.place = ring_place(self.me // 2, self.chips)
        self.partner = self.me + 1 - 2 * self.core
        self.next = (
            ring_chip(self.place + 1, self.chips) * 2 + self.core,
            ring_chip(self.place - 1, self.chips) * 2 + self.core,
        )
        self.events = (self.chips - 1) * len(groups)

    @staticmethod
    def scratch(devices, shapes):
        chips, count = devices // 2, len(shapes)
        dma = pltpu.SemaphoreType.DMA
        buffers = []
        for rows, width in shapes:
            buffers += [pltpu.VMEM((amount, 2, rows // 2, width), BF) for amount in (chips, chips, chips - 1)]
        return buffers + [dma((count, amount, 2)) for amount in (chips, chips, chips, chips - 1, chips - 1)]

    def barrier(self, others=()):
        semaphore = pltpu.get_barrier_semaphore()
        everyone = [(self.next[0], self.side), (self.next[1], self.side), (self.partner, self.side), *others]
        for other in everyone:
            pl.semaphore_signal(semaphore, inc=1, device_id=other, device_id_type=MESH)
        pl.semaphore_wait(semaphore, len(everyone))

    def block(self, index, stage, half, core):
        at = self.place - 1 - stage if half == 0 else self.place + 1 + stage
        size = self.mine[index].shape[2]
        source, column, width = self.terms[index]
        return source.at[ring_chip(at, self.chips) * 2 + core, pl.ds(half * size, size), pl.ds(column, width)]

    def own(self, index, stage, half):
        return pltpu.make_async_copy(
            self.block(index, stage, half, self.core), self.mine[index].at[stage, half], self.own_sem.at[index, stage, half]
        )

    def given(self, index, stage, half):
        return pltpu.make_async_remote_copy(
            src_ref=self.block(index, stage, half, 1 - self.core),
            dst_ref=self.taken[index].at[stage, half],
            send_sem=self.give_sem.at[index, stage, half],
            recv_sem=self.take_sem.at[index, stage, half],
            device_id=(self.partner, self.side),
            device_id_type=MESH,
        )

    def hop(self, index, stage, half, first):
        source = self.mine[index].at[0, half] if first else self.inbox[index].at[stage - 1, half]
        return pltpu.make_async_remote_copy(
            src_ref=source,
            dst_ref=self.inbox[index].at[stage, half],
            send_sem=self.send_sem.at[index, stage, half],
            recv_sem=self.recv_sem.at[index, stage, half],
            device_id=(self.next[half], self.side),
            device_id_type=MESH,
        )

    def each(self, group=None):
        members = range(len(self.terms)) if group is None else self.groups[group]
        return [(index, half) for index in members for half in range(2)]

    def fetch(self, stage, group):
        for index, half in self.each(group):
            self.given(index, stage, half).start()
            self.own(index, stage, half).start()

    def begin(self):
        for group in range(len(self.groups)):
            self.fetch(0, group)
        for index, half in self.each():
            self.mine[index][0, half] = self.chip_term(index, 0, half).astype(BF)
            self.hop(index, 0, half, True).start()
        for stage in range(1, self.AHEAD + 1):
            for group in range(len(self.groups)):
                self.fetch(stage, group)

    def chip_term(self, index, stage, half):
        self.own(index, stage, half).wait()
        self.given(index, stage, half).wait_recv()
        return self.mine[index][stage, half].astype(F32) + self.taken[index][stage, half].astype(F32)

    def stage(self, stage, group):
        last = self.chips - 1

        @pl.when(stage < last)
        def _():
            for index, half in self.each(group):
                self.hop(index, stage - 1, half, True).wait_recv()
                came = self.inbox[index][stage - 1, half].astype(F32)
                self.inbox[index][stage - 1, half] = (came + self.chip_term(index, stage, half)).astype(BF)
                self.hop(index, stage, half, False).start()

        @pl.when(stage + self.AHEAD < self.chips)
        def _():
            self.fetch(stage + self.AHEAD, group)

        @pl.when(stage == last)
        def _():
            for index, half in self.each(group):
                self.hop(index, last - 1, half, True).wait_recv()
                came = self.inbox[index][last - 1, half].astype(F32)
                size = came.shape[0]
                total = came + self.chip_term(index, last, half)
                goal, column = self.goals[index]
                width = min(goal.shape[1] - column, total.shape[1])
                goal[half * size : (half + 1) * size, column : column + width] = total[:, :width]

    def run(self, first, stop):
        count = len(self.groups)

        def one(event, carry):
            for group in range(count):
                if count == 1:
                    self.stage(event + 1, 0)
                else:
                    pl.when(lax.rem(event, count) == group)(functools.partial(self.stage, event // count + 1, group))
            return carry

        lax.fori_loop(first, stop, one, 0)

    def pace(self, step, costs):
        self.run(paced(step, costs, self.events), paced(step + 1, costs, self.events))

    def finish(self):
        for index, half in self.each():
            self.hop(index, 0, half, True).wait_send()

        def sent(stage, carry):
            for index, half in self.each():
                self.hop(index, stage, half, False).wait_send()
            return carry

        lax.fori_loop(1, self.chips - 1, sent, 0)

        def gave(stage, carry):
            for index, half in self.each():
                self.given(index, stage, half).wait_send()
            return carry

        lax.fori_loop(0, self.chips, gave, 0)


def dot_nn(a, b):
    return jnp.dot(a, b, preferred_element_type=F32)


def dot_nt(a, b):
    return lax.dot_general(a, b, (((1,), (1,)), ((), ())), preferred_element_type=F32)


def turned(block, cosine, sine, back):
    other = pltpu.roll(block, E // 2, 1)
    if back:
        return block * cosine - other * sine
    return block * cosine + other * sine


def attend_back(query, kv, probs, mixed, w_attn, hidden, gain, d_normed, d_normed_other, cotangent, cosine, sine, flip, act_early, act_late, w_ffn, rest, ring_source, heads, out_width, identity):
    m, width = hidden.shape
    firsts = m // ROWS
    devices, rows, ring_width = ring_source.shape[1:]
    blocks = m // QB
    factor = E ** (-0.5)
    reach = WINDOW + m
    columns = heads * E
    some, late = act_early.shape[1], act_late.shape[1]
    sides = lax.axis_size("tensor")

    def kernel(q_ref, k_ref, v_ref, p_ref, x_ref, w_ref, h_ref, gain_ref, dn_ref, do_ref, y_ref, c_hbm, s_hbm, flip_hbm, ae_hbm, al_hbm, wd_ref, rd_ref, source, dq_ref, dk_ref, dv_ref, out_ref, sum_ref, flipped_ref, dh_ref, gain_out, sent_ref, got, c_ref, s_ref, flip_ref, ae_ref, al_ref, load_sem, sent, y_send, y_recv, g_ref, gt_ref, keys_sum, values_sum, *scratch):
        step = pl.program_id(0)
        half = ring_width // 2
        ring = Ring(devices, [(source.at[0], 0, half), (source.at[0], half, half)], [(sum_ref, 0), (sum_ref, half)], [[0], [1]], scratch)
        brought = loads((c_hbm, s_hbm, flip_hbm, ae_hbm, al_hbm), (c_ref, s_ref, flip_ref, ae_ref, al_ref), load_sem)
        other = (ring.me, lax.rem(ring.side + 1, sides))

        def across(which):
            return pltpu.make_async_remote_copy(
                src_ref=sent.at[which], dst_ref=got.at[:, pl.ds(pl.multiple_of(which * TILE, TILE), TILE)],
                send_sem=y_send.at[which], recv_sem=y_recv.at[which], device_id=other, device_id_type=MESH,
            )

        turns = [(firsts + 2 * heads, 1)]

        @pl.when(step == 0)
        def _():
            for copy in brought:
                copy.start()
            ring.barrier((other,))
            ring.begin()

        @pl.when(step == firsts)
        def _():
            for copy in brought:
                copy.wait()

        @pl.when(step < firsts)
        def _():
            change, gain_part = norm_grad(h_ref[...], gain_ref[...], dn_ref[...].astype(F32) + do_ref[...].astype(F32))
            total = y_ref[...].astype(F32) + change
            low = total.astype(BF)
            dh_ref[...] = total
            here = pl.ds(pl.multiple_of(step * ROWS, ROWS), ROWS)
            g_ref[here, :] = low
            gt_ref[:, here] = low.T

            @pl.when(step == 0)
            def _():
                gain_out[...] = gain_part

            @pl.when(step > 0)
            def _():
                gain_out[...] += gain_part

            ring.pace(step, turns)

        @pl.when(step >= firsts)
        def _():
            head = step - firsts

            @pl.when(head < SOON)
            def _():
                down = (dot_nt(ae_ref[...], wd_ref[...]) + dot_nt(al_ref[...], rd_ref[...])).astype(BF)
                sent[head] = down
                sent_ref[...] = down
                across(head).start()

            grad_all = dot_nn(g_ref[...], w_ref[...]).astype(BF)
            out_ref[...] = dot_nn(gt_ref[...], x_ref[...]).astype(BF)
            keys_t = k_ref[...].T
            keys_sum[...] = jnp.zeros_like(keys_sum)
            values_sum[...] = jnp.zeros_like(values_sum)
            for block in range(blocks):
                span = slice(block * QB, block * QB + KB)
                here = slice(block * QB, (block + 1) * QB)
                there = slice(WINDOW + block * QB, WINDOW + (block + 1) * QB)
                low = p_ref[0, block]
                grad = grad_all[here, :]
                d_probs = dot_nt(v_ref[span, :], grad)
                weighted = low.astype(F32) * d_probs
                total = jnp.sum(weighted, axis=0, keepdims=True)
                d_scores = (weighted - low.astype(F32) * total).astype(BF)
                values_sum[span, :] += dot_nn(low, grad)
                keys_sum[span, :] += dot_nn(d_scores, q_ref[here, :])
                d_query = dot_nn(keys_t[:, span], d_scores).T * factor
                dq_ref[here, :] = turned(d_query, c_ref[there, :], s_ref[there, :], True).astype(BF)
                if block == 0:
                    ring.pace(firsts + 2 * head, turns)
            dk_ref[...] = turned(keys_sum[...] * factor, c_ref[...], s_ref[...], True).astype(BF)
            dv_ref[...] = values_sum[...].astype(BF)
            ring.pace(firsts + 2 * head + 1, turns)

            @pl.when(head == 1)
            def _():
                flipped_ref[...] = flip_ref[...].T[: flipped_ref.shape[0]]

            @pl.when(head == heads - 1)
            def _():
                for which in range(SOON):
                    across(which).wait()
                ring.finish()

    def at(i):
        return jnp.maximum(i - firsts, 0)

    head_spec = pl.BlockSpec((m, E), lambda i: (0, at(i)))
    long_spec = pl.BlockSpec((reach, E), lambda i: (0, at(i)))
    rows_spec = pl.BlockSpec((ROWS, width), lambda i: (jnp.minimum(i, firsts - 1), 0))
    dma = pltpu.SemaphoreType.DMA

    def soon(i):
        return jnp.minimum(at(i), SOON - 1)

    any_space = pl.BlockSpec(memory_space=pl.ANY)
    return pl.pallas_call(
        kernel,
        grid=(firsts + heads,),
        out_shape=[
            jax.ShapeDtypeStruct((m, columns), BF),
            jax.ShapeDtypeStruct((reach, columns), BF),
            jax.ShapeDtypeStruct((reach, columns), BF),
            jax.ShapeDtypeStruct((width, columns), BF),
            jax.ShapeDtypeStruct((rows, out_width), F32),
            jax.ShapeDtypeStruct((out_width, rows), F32),
            jax.ShapeDtypeStruct((m, width), F32),
            jax.ShapeDtypeStruct((1, width), F32),
            jax.ShapeDtypeStruct((m, SOON * TILE), BF),
            jax.ShapeDtypeStruct((m, SOON * TILE), BF),
        ],
        in_specs=[
            head_spec,
            long_spec,
            pl.BlockSpec((reach, E), lambda i: (0, at(i) + heads)),
            pl.BlockSpec((1, blocks, KB, QB), lambda i: (at(i), 0, 0, 0)),
            head_spec,
            pl.BlockSpec((width, E), lambda i: (0, at(i) + 3 * heads)),
            rows_spec,
            single((1, width)),
            rows_spec,
            rows_spec,
            rows_spec,
            any_space, any_space, any_space, any_space, any_space,
            pl.BlockSpec((TILE, some), lambda i: (soon(i), 2)),
            pl.BlockSpec((TILE, late), lambda i: (soon(i), 2)),
            any_space,
        ],
        out_specs=[
            head_spec,
            long_spec,
            long_spec,
            pl.BlockSpec((width, E), lambda i: (0, at(i))),
            single((rows, out_width)),
            single((out_width, rows)),
            rows_spec,
            single((1, width)),
            pl.BlockSpec((m, TILE), lambda i: (0, soon(i))),
            any_space,
        ],
        scratch_shapes=[
            pltpu.VMEM((reach, E), F32), pltpu.VMEM((reach, E), F32), pltpu.VMEM(flip.shape, F32),
            pltpu.VMEM((m, some), BF), pltpu.VMEM((m, late), BF), dma((5,)),
            pltpu.VMEM((SOON, m, TILE), BF), dma((SOON,)), dma((SOON,)),
            pltpu.VMEM((m, width), BF), pltpu.VMEM((width, m), BF),
            pltpu.VMEM((reach, E), F32), pltpu.VMEM((reach, E), F32),
            *Ring.scratch(devices, [(rows, ring_width // 2)] * 2),
        ],
        compiler_params=pltpu.CompilerParams(vmem_limit_bytes=VMEM, collective_id=identity, has_side_effects=True),
        cost_estimate=cost(8 * heads * m * KB * E * 2, 2 * heads * m * KB),
        name="attend_back",
    )(query, kv, kv, probs, mixed, w_attn, hidden, gain, d_normed, d_normed_other, cotangent, cosine, sine, flip, act_early, act_late, w_ffn, rest, ring_source)


def qkv_back(x_t, d_query, d_key, d_value, w_attn, up_part, out_part, out_width, identity):
    width, reach = x_t.shape
    m, columns = d_query.shape
    devices, rows, up_width = up_part.shape[1:]
    tiles = width // TILE
    per = columns // TILE
    total = tiles + 3 * per
    sides = lax.axis_size("tensor")
    half = m // 2
    piece = up_width // 2
    shapes = [(rows, piece), (rows, piece), (rows, columns)]
    assert 3 * per > tiles and reach == 3 * m

    def kernel(xt_hbm, dq_hbm, dk_hbm, dv_hbm, w_ref, up_ref, out_ref, grad_ref, sent_ref, got, add_ref, up_sum, out_sum, xt_ref, dq_ref, dk_ref, dv_ref, load_sem, sent, early, early_in, near_in, far_in, own_send, own_recv, early_send, early_recv, near_send, near_recv, far_send, far_recv, *scratch):
        step = pl.program_id(0)
        source = up_ref.at[1]
        ring = Ring(
            devices, [(source, 0, piece), (source, piece, piece), (out_ref, 0, columns)], [(up_sum, 0), (up_sum, piece), (out_sum, 0)],
            [[0], [1], [2]], scratch,
        )
        me, side = ring.me, ring.side
        across = lax.rem(side + 1, sides)
        later, before = lax.rem(me + 2, devices), lax.rem(me + devices - 2, devices)
        share = ring.core.astype(F32)
        brought = loads((dq_hbm, dk_hbm, dv_hbm, xt_hbm), (dq_ref, dk_ref, dv_ref, xt_ref), load_sem)

        def remote(source, target, send, recv, which, other):
            return pltpu.make_async_remote_copy(
                src_ref=source, dst_ref=target, send_sem=send.at[which], recv_sem=recv.at[which], device_id=other, device_id_type=MESH
            )

        def own_copy(which):
            target = got.at[:, pl.ds(pl.multiple_of(which * TILE, TILE), TILE)]
            return remote(sent.at[which], target, own_send, own_recv, which, (me, across))

        def early_copy(which):
            return remote(early.at[which, across], early_in.at[which], early_send, early_recv, which, (me, across))

        def near_copy(which):
            return remote(early_in.at[which, 1], near_in.at[which], near_send, near_recv, which, (ring.partner, side))

        def far_copy(which):
            return remote(early_in.at[which, 0], far_in.at[which], far_send, far_recv, which, (before, side))

        @pl.when(step == 0)
        def _():
            for copy in brought:
                copy.start()
            ring.barrier(((me, across), (later, side), (before, side)))
            ring.begin()
            for copy in brought[:3]:
                copy.wait()

        @pl.when(step == tiles)
        def _():
            brought[3].wait()

        @pl.when(step < tiles)
        def _():
            w_key, w_value = w_ref[:, columns : 2 * columns], w_ref[:, 2 * columns :]
            part = dot_nt(dq_ref[...], w_ref[:, :columns])
            part += dot_nt(dk_ref[2 * m :, :], w_key) + dot_nt(dv_ref[2 * m :, :], w_value)
            low = part.astype(BF)
            sent[step] = low
            sent_ref[...] = low
            for block in range(2):
                span = slice(block * m, (block + 1) * m)
                part = (dot_nt(dk_ref[span, :], w_key) + dot_nt(dv_ref[span, :], w_value)).astype(BF)
                for number in range(2):
                    early[step, number, block] = part[number * half : (number + 1) * half]
            early_copy(step).start()

        number = step - tiles

        @pl.when((number >= 0) & (number < tiles))
        def _():
            own_copy(number).start()
            early_copy(number).wait_recv()
            early_in[number] = (early_in[number].astype(F32) + early[number, side].astype(F32)).astype(BF)
            near_copy(number).start()

        @pl.when((number >= 1) & (number <= tiles))
        def _():
            which = number - 1
            near_copy(which).wait_recv()
            early_in[which, 0] = (early_in[which, 0].astype(F32) + near_in[which].astype(F32) * share).astype(BF)

            @pl.when(me >= 2)
            def _():
                far_copy(which).start()

        @pl.when((number >= 0) & (number < per))
        def _():
            here = pl.ds(pl.multiple_of(number * TILE, TILE), TILE)
            grad_ref[...] = dot_nn(xt_ref[:, 2 * m :], dq_ref[:, here]).astype(BF)

        @pl.when((number >= per) & (number < 2 * per))
        def _():
            here = pl.ds(pl.multiple_of((number - per) * TILE, TILE), TILE)
            grad_ref[...] = dot_nn(xt_ref[...], dk_ref[:, here]).astype(BF)

        @pl.when(number >= 2 * per)
        def _():
            here = pl.ds(pl.multiple_of((number - 2 * per) * TILE, TILE), TILE)
            grad_ref[...] = dot_nn(xt_ref[...], dv_ref[:, here]).astype(BF)

        ring.pace(step, [(tiles, 5), (3 * per, 4)])

        @pl.when(step == total - 1)
        def _():
            for which in range(tiles):
                here = slice(which * TILE, (which + 1) * TILE)
                add_ref[:, here] = (near_in[which].astype(F32) * (1.0 - share)).astype(BF)

                @pl.when(me < devices - 2)
                def _():
                    far_copy(which).wait_recv()
                    add_ref[:, here] = (add_ref[:, here].astype(F32) + far_in[which].astype(F32)).astype(BF)

                @pl.when(me >= 2)
                def _():
                    far_copy(which).wait_send()

                near_copy(which).wait_send()
                early_copy(which).wait_send()
                own_copy(which).wait()
            ring.finish()

    any_space = pl.BlockSpec(memory_space=pl.ANY)
    dma = pltpu.SemaphoreType.DMA

    def second(i):
        return jnp.minimum(i, tiles - 1)

    return pl.pallas_call(
        kernel,
        grid=(total,),
        out_shape=[
            jax.ShapeDtypeStruct((width, 3 * columns), BF),
            jax.ShapeDtypeStruct((m, width), BF),
            jax.ShapeDtypeStruct((m, width), BF),
            jax.ShapeDtypeStruct((half, width), BF),
            jax.ShapeDtypeStruct((rows, out_width), F32),
            jax.ShapeDtypeStruct((rows, columns), F32),
        ],
        in_specs=[
            any_space, any_space, any_space, any_space,
            pl.BlockSpec((TILE, 3 * columns), lambda i: (second(i), 0)),
            any_space, any_space,
        ],
        out_specs=[
            pl.BlockSpec((width, TILE), lambda i: (0, jnp.maximum(i - tiles, 0))),
            pl.BlockSpec((m, TILE), lambda i: (0, second(i))),
            any_space,
            single((half, width)),
            single((rows, out_width)),
            single((rows, columns)),
        ],
        scratch_shapes=[
            pltpu.VMEM((width, reach), BF),
            pltpu.VMEM((m, columns), BF),
            pltpu.VMEM((reach, columns), BF),
            pltpu.VMEM((reach, columns), BF),
            dma((4,)),
            pltpu.VMEM((tiles, m, TILE), BF),
            pltpu.VMEM((tiles, 2, 2, half, TILE), BF),
            pltpu.VMEM((tiles, 2, half, TILE), BF),
            pltpu.VMEM((tiles, half, TILE), BF),
            pltpu.VMEM((tiles, half, TILE), BF),
            *[dma((tiles,))] * 8,
            *Ring.scratch(devices, shapes),
        ],
        compiler_params=pltpu.CompilerParams(vmem_limit_bytes=VMEM, collective_id=identity, has_side_effects=True),
        cost_estimate=cost(4 * (m + 2 * reach) * width * columns, 12 * width * columns),
        name="qkv_back",
    )(x_t, d_query, d_key, d_value, w_attn, up_part, out_part)


def tiles_of(width):
    return width // TILE


def root_of(rows):
    return lax.rsqrt(jnp.mean(rows * rows, axis=-1, keepdims=True) + EPS)


def norm_grad(rows, gain, grad):
    root = root_of(rows)
    pushed = grad * gain
    inner = jnp.mean(pushed * rows, axis=-1, keepdims=True)
    return root * pushed - rows * (root * root * root * inner), jnp.sum(grad * rows * root, axis=0, keepdims=True)


def forward(far, near, tokens, gains, w_attn, cosine, sine, places, block, heads, identity):
    m, width = tokens.shape
    reach = 3 * m
    columns = heads * E
    devices = lax.axis_size("dp")
    sides = lax.axis_size("tensor")
    part_steps = m // ROWS
    per = TILE // E
    some = heads // per
    blocks = m // QB
    factor = E ** (-0.5) * LOG2E
    counts = (3 * part_steps, some, 2 * some, heads, part_steps, part_steps)
    starts = [sum(counts[:number]) for number in range(len(counts) + 1)]
    total = starts[-1]
    piece = block.shape[1] // 4

    own = width // devices

    def kernel(far_ref, near_ref, x_ref, again_ref, gains_ref, w_ref, c_ref, s_ref, places_ref, w_hbm, block_ref, nt_ref, q_out, kv_out, mixed_out, probs_ref, hidden_ref, normed_ref, turned_ref, whole_ref, g_ref, gf_ref, normed, q_all, kv_all, mixed_all, w_out, bias, sent, got, load_sem, y_send, y_recv, *scratch):
        step = pl.program_id(0)
        spread = Spread(devices, [(block_ref, number * piece, whole_ref, number * piece, piece) for number in range(4)], scratch)
        me, side = spread.me, spread.side
        other = (me, lax.rem(side + 1, sides))
        brought = loads((w_hbm.at[:, pl.ds(3 * columns, columns)],), (w_out,), load_sem)

        def across(which):
            return pltpu.make_async_remote_copy(
                src_ref=sent.at[which], dst_ref=got.at[which], send_sem=y_send.at[which], recv_sem=y_recv.at[which],
                device_id=other, device_id_type=MESH,
            )

        def phase(number):
            return pl.when((step >= starts[number]) & (step < starts[number + 1]))

        @pl.when(step == 0)
        def _():
            brought[0].start()
            spread.barrier((other,))
            spread.begin()
            for device in range(devices):
                span = slice(device * own, (device + 1) * own)
                g_ref[:, span] = gains_ref[device * 32 : device * 32 + 1, :own].astype(F32)
                gf_ref[:, span] = gains_ref[device * 32 + 16 : device * 32 + 17, :own].astype(F32)

        @phase(0)
        def _():
            here = pl.ds(pl.multiple_of(step * ROWS, ROWS), ROWS)

            def put(ref):
                rows = ref[...].astype(F32)
                made = (rows * root_of(rows) * g_ref[...]).astype(BF)
                normed[here, :] = made
                nt_ref[...] = made.T

            def earlier(ref, there):
                pl.when(there)(functools.partial(put, ref))

                @pl.when(jnp.logical_not(there))
                def _():
                    normed[here, :] = jnp.zeros((ROWS, width), BF)
                    nt_ref[...] = jnp.zeros((width, ROWS), BF)

            pl.when(step < part_steps)(functools.partial(earlier, far_ref, me >= 2))
            pl.when((step >= part_steps) & (step < 2 * part_steps))(functools.partial(earlier, near_ref, me >= 1))
            pl.when(step >= 2 * part_steps)(functools.partial(put, x_ref))

        def rotated(made, rows):
            pieces = [turned(made[:, part * E : (part + 1) * E], c_ref[rows, :], s_ref[rows, :], False) for part in range(per)]
            return jnp.concatenate(pieces, axis=1).astype(BF)

        @phase(1)
        def _():
            rows = slice(reach - m, reach)
            made = rotated(dot_nn(normed[rows, :], w_ref[...]), rows)
            q_out[...] = made
            q_all[:, pl.ds(pl.multiple_of((step - starts[1]) * TILE, TILE), TILE)] = made

        @phase(2)
        def _():
            number = step - starts[2]

            def put(made):
                kv_out[...] = made
                kv_all[:, pl.ds(pl.multiple_of(number * TILE, TILE), TILE)] = made

            @pl.when(number < some)
            def _():
                put(rotated(dot_nn(normed[...], w_ref[...]), slice(0, reach)))

            @pl.when(number >= some)
            def _():
                put(dot_nn(normed[...], w_ref[...]).astype(BF))

        @pl.when(step == starts[3])
        def _():
            for number in range(blocks):
                key = lax.broadcasted_iota(jnp.int32, (KB, QB), 0) + number * QB
                query = lax.broadcasted_iota(jnp.int32, (KB, QB), 1) + number * QB
                place = places_ref[:, number * QB : (number + 1) * QB]
                allowed = (key <= query + WINDOW) & (key > query) & (key >= query + WINDOW - place)
                bias[number] = jnp.where(allowed, 0.0, -1e30)

        @phase(3)
        def _():
            head = step - starts[3]
            lanes = pl.ds(pl.multiple_of(head * E, E), E)
            queries = q_all[:, lanes]
            keys = kv_all[:, lanes]
            values_t = kv_all[:, pl.ds(pl.multiple_of(columns + head * E, E), E)].T
            for number in range(blocks):
                span = slice(number * QB, number * QB + KB)
                here = slice(number * QB, (number + 1) * QB)
                scores = dot_nt(keys[span], queries[here]) * factor + bias[number]
                largest = jnp.max(scores, axis=0, keepdims=True)
                grown = jnp.exp2(scores - largest)
                inverse = 1.0 / jnp.sum(grown, axis=0, keepdims=True)
                probs = (grown * inverse).astype(BF)
                probs_ref[0, number] = probs
                made = dot_nn(values_t[:, span], probs).T.astype(BF)
                mixed_out[here, :] = made
                mixed_all[here, lanes] = made

        @pl.when(step == starts[4])
        def _():
            brought[0].wait()

        @phase(4)
        def _():
            which = step - starts[4]
            here = pl.ds(pl.multiple_of(which * ROWS, ROWS), ROWS)
            sent[which] = dot_nt(mixed_all[here, :], w_out[...]).astype(BF)
            across(which).start()

        @phase(5)
        def _():
            which = step - starts[5]
            across(which).wait()
            hidden = again_ref[...].astype(F32) + (sent[which].astype(F32) + got[which].astype(F32))
            made = (hidden * root_of(hidden) * gf_ref[...]).astype(BF)
            hidden_ref[...] = hidden
            normed_ref[...] = made
            turned_ref[...] = made.T

        spread.pace(step, list(zip(counts, (2, 2, 5, 5, 5, 20))))

        @pl.when(step == total - 1)
        def _():
            spread.finish()

    def within(number, i, length):
        return jnp.clip(i - starts[number], 0, length - 1)

    def rows_at(first):
        return pl.BlockSpec((ROWS, width), lambda i: (jnp.clip(i - first, 0, part_steps - 1), 0))

    any_space = pl.BlockSpec(memory_space=pl.ANY)
    dma = pltpu.SemaphoreType.DMA
    low = functools.partial(jax.ShapeDtypeStruct, dtype=BF)
    return pl.pallas_call(
        kernel,
        grid=(total,),
        out_shape=[
            low((width, reach)),
            low((m, columns)),
            low((reach, 2 * columns)),
            low((m, columns)),
            low((heads, blocks, KB, QB)),
            jax.ShapeDtypeStruct((m, width), F32),
            low((m, width)),
            low((width, m)),
            low((block.shape[0] * devices, block.shape[1])),
            jax.ShapeDtypeStruct((1, width), F32),
            jax.ShapeDtypeStruct((1, width), F32),
        ],
        in_specs=[
            rows_at(0), rows_at(part_steps), rows_at(2 * part_steps), rows_at(starts[5]),
            single(gains.shape),
            pl.BlockSpec((width, TILE), lambda i: (0, within(1, i, 3 * some))),
            single((reach, E)),
            single((reach, E)),
            single((1, m)),
            any_space,
            any_space,
        ],
        out_specs=[
            pl.BlockSpec((width, ROWS), lambda i: (0, within(0, i, 3 * part_steps))),
            pl.BlockSpec((m, TILE), lambda i: (0, within(1, i, some))),
            pl.BlockSpec((reach, TILE), lambda i: (0, within(2, i, 2 * some))),
            pl.BlockSpec((m, E), lambda i: (0, within(3, i, heads))),
            pl.BlockSpec((1, blocks, KB, QB), lambda i: (within(3, i, heads), 0, 0, 0)),
            rows_at(starts[5]),
            rows_at(starts[5]),
            pl.BlockSpec((width, ROWS), lambda i: (0, within(5, i, part_steps))),
            any_space,
            single((1, width)),
            single((1, width)),
        ],
        scratch_shapes=[
            pltpu.VMEM((reach, width), BF),
            pltpu.VMEM((m, columns), BF),
            pltpu.VMEM((reach, 2 * columns), BF),
            pltpu.VMEM((m, columns), BF),
            pltpu.VMEM((width, columns), BF),
            pltpu.VMEM((blocks, KB, QB), F32),
            pltpu.VMEM((part_steps, ROWS, width), BF),
            pltpu.VMEM((part_steps, ROWS, width), BF),
            dma((1,)),
            dma((part_steps,)),
            dma((part_steps,)),
            *Spread.scratch(devices, 4),
        ],
        compiler_params=pltpu.CompilerParams(vmem_limit_bytes=VMEM, collective_id=identity, has_side_effects=True),
        cost_estimate=cost(2 * (m + 2 * reach) * width * columns, 8 * reach * width, heads * m * KB),
        name="forward",
    )(far, near, tokens, tokens, gains, w_attn, cosine, sine, places, w_attn, block)


def last_pass(tokens, gain, grad, grad_other, grad_add, d_hidden, hidden, ffn_part, ffn_other, act_early, act_late, w_ffn, rest, gain_ffn_grad, flip, qkv_part, lanes, identity):
    m, width = tokens.shape
    devices, rows, all_columns = qkv_part.shape
    columns = all_columns // 3
    chips = devices // 2
    size = ROWS // 2
    steps = m // size
    downs = tiles_of(width) - SOON
    total = downs + steps + chips
    names = 3
    half = m // 2
    tiles = tiles_of(width)
    some, late = act_early.shape[1], act_late.shape[1]
    sides = lax.axis_size("tensor")
    assert chips >= tiles

    def kernel(x_ref, g_ref, dn_ref, do_ref, add_hbm, dh_ref, h_ref, fp_ref, fo_ref, a_hbm, al_hbm, w_ref, rest_ref, gf_ref, flip_hbm, source, grad_ref, layer_ref, flipped_ref, q_ref, k_ref, v_ref, gains_ref, a_ref, al_ref, flip_ref, add, load_sem, add_send, add_recv, gain_sum, gain_source, gain_in, gain_send, gain_recv, sent, got, y_send, y_recv, *scratch):
        step = pl.program_id(0)
        ring = Ring(
            devices, [(source, number * columns, columns) for number in range(names)], [(q_ref, 0), (k_ref, 0), (v_ref, 0)],
            [[0], [1], [2]], scratch,
        )

        def gain_copy(away):
            owner = lax.rem(ring.me + away, devices)
            return pltpu.make_async_remote_copy(
                src_ref=gain_source.at[owner], dst_ref=gain_in.at[away], send_sem=gain_send.at[away], recv_sem=gain_recv.at[away],
                device_id=(owner, ring.side), device_id_type=MESH,
            )

        other = (ring.me, lax.rem(ring.side + 1, sides))
        brought = loads((a_hbm, al_hbm, flip_hbm, add_hbm), (a_ref, al_ref, flip_ref, add.at[ring.side]), load_sem)
        add_copy = pltpu.make_async_remote_copy(
            src_ref=add_hbm, dst_ref=add.at[ring.side], send_sem=add_send, recv_sem=add_recv, device_id=other, device_id_type=MESH
        )
        row_step = step - downs
        end_step = step - downs - steps

        def across(which):
            return pltpu.make_async_remote_copy(
                src_ref=sent.at[which], dst_ref=got.at[which], send_sem=y_send.at[which], recv_sem=y_recv.at[which],
                device_id=other, device_id_type=MESH,
            )

        @pl.when(step == 0)
        def _():
            for copy in brought:
                copy.start()
            ring.barrier((other, *[(lax.rem(ring.me + away, devices), ring.side) for away in range(1, devices)]))
            add_copy.start()
            ring.begin()
            for copy in brought:
                copy.wait()
            flipped_ref[...] = flip_ref[...].T

        @pl.when(row_step == 0)
        def _():
            add_copy.wait()

        @pl.when(step < downs)
        def _():
            sent[step] = (dot_nt(a_ref[...], w_ref[...]) + dot_nt(al_ref[...], rest_ref[...])).astype(BF)
            across(step).start()

        @pl.when((row_step >= 0) & (row_step < steps))
        def _():
            which = row_step * size // half
            here = pl.ds(pl.multiple_of(row_step * size - which * half, size), size)
            grad_rows = dn_ref[...].astype(F32) + do_ref[...].astype(F32) + add[which, here, :].astype(F32)
            change, gain_part = norm_grad(x_ref[...].astype(F32), g_ref[...], grad_rows)
            grad_ref[...] = dh_ref[...] + change

            @pl.when(row_step == 0)
            def _():
                gain_sum[...] = gain_part

            @pl.when(row_step > 0)
            def _():
                gain_sum[...] += gain_part

        @pl.when(row_step == steps - 1)
        def _():
            gain_source[...] = jnp.zeros_like(gain_source)
            for device in range(devices):
                span = slice(device * rows, (device + 1) * rows)
                gain_source[device, :16, :rows] = jnp.broadcast_to(gain_sum[:, span], (16, rows)).astype(BF)
                gain_source[device, 16:, :rows] = jnp.broadcast_to(gf_ref[:, span], (16, rows)).astype(BF)

            def send(away, carry):
                gain_copy(away).start()
                return carry

            lax.fori_loop(1, devices, send, 0)

        ring.pace(step, [(downs, 5), (steps, 3), (chips, 3)])

        @pl.when((end_step >= 0) & (end_step < SOON))
        def _():
            layer_ref[...] = (h_ref[...] + (fp_ref[...].astype(F32) + fo_ref[...].astype(F32))).astype(BF)

        @pl.when((end_step >= SOON) & (end_step < tiles))
        def _():
            which = end_step - SOON
            across(which).wait()
            layer_ref[...] = (h_ref[...] + (sent[which].astype(F32) + got[which].astype(F32))).astype(BF)

        @pl.when(step == total - 1)
        def _():
            ring.finish()

            def take(away, total):
                gain_copy(away).wait()
                return total + gain_in[away].astype(F32)

            gains_ref[...] = lax.fori_loop(1, devices, take, gain_source[ring.me].astype(F32))

    def early(i):
        return jnp.minimum(i, downs - 1) + SOON

    def ending(i):
        return jnp.clip(i - downs - steps, 0, tiles - 1)

    rows_spec = pl.BlockSpec((size, width), lambda i: (jnp.clip(i - downs, 0, steps - 1), 0))
    tile_spec = pl.BlockSpec((m, TILE), lambda i: (0, ending(i)))
    soon_spec = pl.BlockSpec((m, TILE), lambda i: (0, jnp.minimum(ending(i), SOON - 1)))
    dma = pltpu.SemaphoreType.DMA
    sums = jax.ShapeDtypeStruct((rows, columns), F32)
    return pl.pallas_call(
        kernel,
        grid=(total,),
        out_shape=[
            jax.ShapeDtypeStruct((m, width), F32),
            jax.ShapeDtypeStruct((m, width), BF),
            jax.ShapeDtypeStruct((flip.shape[1], flip.shape[0]), F32),
            sums, sums, sums,
            jax.ShapeDtypeStruct((32, lanes), F32),
        ],
        in_specs=[
            rows_spec, single((1, width)), rows_spec, rows_spec, pl.BlockSpec(memory_space=pl.ANY), rows_spec, tile_spec, soon_spec, soon_spec, pl.BlockSpec(memory_space=pl.ANY), pl.BlockSpec(memory_space=pl.ANY),
            pl.BlockSpec((TILE, some), lambda i: (early(i), 2)), pl.BlockSpec((TILE, late), lambda i: (early(i), 2)), single((1, width)),
            pl.BlockSpec(memory_space=pl.ANY), pl.BlockSpec(memory_space=pl.ANY),
        ],
        out_specs=[
            rows_spec, tile_spec, single((flip.shape[1], flip.shape[0])),
            single(sums.shape), single(sums.shape), single(sums.shape), single((32, lanes)),
        ],
        scratch_shapes=[
            pltpu.VMEM((m, some), BF),
            pltpu.VMEM((m, late), BF),
            pltpu.VMEM(flip.shape, F32),
            pltpu.VMEM((2, half, width), BF),
            dma((4,)),
            dma,
            dma,
            pltpu.VMEM((1, width), F32),
            pltpu.VMEM((devices, 32, lanes), BF),
            pltpu.VMEM((devices, 32, lanes), BF),
            dma((devices,)),
            dma((devices,)),
            pltpu.VMEM((downs, m, TILE), BF),
            pltpu.VMEM((downs, m, TILE), BF),
            dma((downs,)),
            dma((downs,)),
            *Ring.scratch(devices, [(rows, columns)] * names),
        ],
        compiler_params=pltpu.CompilerParams(vmem_limit_bytes=VMEM, collective_id=identity, has_side_effects=True),
        cost_estimate=cost(20 * m * width, 24 * m * width),
        name="last_pass",
    )(tokens, gain, grad, grad_other, grad_add, d_hidden, hidden, ffn_part, ffn_other, act_early, act_late, w_ffn, rest, gain_ffn_grad, flip, qkv_part)


def feed_tile(x_ref, dy_ref, dyt_ref, g_ref, u_ref, d_ref, act_ref, both_ref, down_ref):
    gate = dot_nn(x_ref[...], g_ref[...])
    up = dot_nn(x_ref[...], u_ref[...])
    d_act = dot_nn(dy_ref[...], d_ref[...])
    soft = 1.0 / (1.0 + jnp.exp(-gate))
    silu = gate * soft
    act = (silu * up).astype(BF)
    act_ref[...] = act
    both_ref[0] = (d_act * up * (soft * (1.0 + gate * (1.0 - soft)))).astype(BF)
    both_ref[1] = (d_act * silu).astype(BF)
    down_ref[...] = dot_nn(dyt_ref[...], act).astype(BF)


def feed(x, dy, dy_t, w, block, tiles, identity):
    m, k = x.shape
    early = tiles - LATE
    devices = lax.axis_size("dp")
    width = block.shape[1] // 2

    def kernel(x_hbm, dy_hbm, dyt_hbm, g_ref, u_ref, d_ref, block_ref, act_ref, both_ref, down_ref, rest_ref, x_ref, dy_ref, dyt_ref, load_sem, *scratch):
        step = pl.program_id(0)
        brought = loads((x_hbm, dy_hbm, dyt_hbm), (x_ref, dy_ref, dyt_ref), load_sem)
        spread = Spread(devices, [(block_ref, 0, rest_ref, 0, width), (block_ref, width, rest_ref, width, width)], scratch)

        @pl.when(step == 0)
        def _():
            for copy in brought:
                copy.start()
            spread.barrier()
            spread.begin()
            for copy in brought:
                copy.wait()

        feed_tile(x_ref, dy_ref, dyt_ref, g_ref, u_ref, d_ref, act_ref, both_ref, down_ref)
        spread.pace(step, [(early, 1)])

        @pl.when(step == early - 1)
        def _():
            spread.finish()

    any_space = pl.BlockSpec(memory_space=pl.ANY)
    return pl.pallas_call(
        kernel,
        grid=(early,),
        out_shape=[
            jax.ShapeDtypeStruct((m, early * TILE), BF),
            jax.ShapeDtypeStruct((2, m, early * TILE), BF),
            jax.ShapeDtypeStruct((k, early * TILE), BF),
            jax.ShapeDtypeStruct((k, block.shape[1]), BF),
        ],
        in_specs=[
            any_space, any_space, any_space,
            pl.BlockSpec((k, TILE), lambda i: (0, i)),
            pl.BlockSpec((k, TILE), lambda i: (0, i + early)),
            pl.BlockSpec((k, TILE), lambda i: (0, i + 2 * early)),
            any_space,
        ],
        out_specs=[
            pl.BlockSpec((m, TILE), lambda i: (0, i)),
            pl.BlockSpec((2, m, TILE), lambda i: (0, 0, i)),
            pl.BlockSpec((k, TILE), lambda i: (0, i)),
            any_space,
        ],
        scratch_shapes=[
            pltpu.VMEM((m, k), BF), pltpu.VMEM((m, k), BF), pltpu.VMEM((k, m), BF), pltpu.SemaphoreType.DMA((3,)),
            *Spread.scratch(devices, 2),
        ],
        compiler_params=pltpu.CompilerParams(vmem_limit_bytes=VMEM, collective_id=identity, has_side_effects=True),
        cost_estimate=cost(8 * m * k * early * TILE, 8 * (m + k) * early * TILE, m * early * TILE),
        name="feed",
    )(x, dy, dy_t, w, w, w, block)


def ffn_back(x, x_t, dy, dy_t, d_early, w_ffn, rest, down_early, identity):
    m, width = x.shape
    devices, rows, some = down_early.shape
    late = LATE * TILE
    padded = some + late
    tiles = width // TILE
    wide = 2 * TILE
    early_wide, late_wide = some // wide, (late + wide - 1) // wide
    grads = 2 * (early_wide + late_wide)
    total = LATE + tiles + grads
    sides = lax.axis_size("tensor")
    pieces = [(rows, some // 2)] * 2

    def kernel(x_hbm, xt_hbm, dy_hbm, dyt_hbm, rg_ref, ru_ref, rd_ref, d_hbm, tile_ref, wg_ref, wu_ref, lg_ref, lu_ref, source, act_ref, grad_ref, sent_ref, got, sum_ref, x_ref, xt_ref, dy_ref, dyt_ref, d_ref, load_sem, d_late, down_late, down_tile, both_tile, sent, y_send, y_recv, *scratch):
        step = pl.program_id(0)
        brought = loads((x_hbm, dy_hbm, dyt_hbm, d_hbm, xt_hbm), (x_ref, dy_ref, dyt_ref, d_ref, xt_ref), load_sem)
        ring = Ring(devices, [(source, 0, some // 2), (source, some // 2, some // 2)], [(sum_ref, 0), (sum_ref, some // 2)], [[0], [1]], scratch[:11])
        late_ring = Ring(devices, [(down_late, 0, late)], [(sum_ref, some)], [[0]], scratch[11:])
        other = (ring.me, lax.rem(ring.side + 1, sides))

        def across(which):
            return pltpu.make_async_remote_copy(
                src_ref=sent.at[which], dst_ref=got.at[:, pl.ds(pl.multiple_of(which * TILE, TILE), TILE)],
                send_sem=y_send.at[which], recv_sem=y_recv.at[which], device_id=other, device_id_type=MESH,
            )

        @pl.when(step == 0)
        def _():
            for copy in brought:
                copy.start()
            ring.barrier((other,))
            ring.begin()
            for copy in brought[:3]:
                copy.wait()

        @pl.when(step == LATE)
        def _():
            brought[3].wait()

        @pl.when(step == LATE + tiles)
        def _():
            brought[4].wait()

        @pl.when(step < LATE)
        def _():
            feed_tile(x_ref, dy_ref, dyt_ref, rg_ref, ru_ref, rd_ref, act_ref, both_tile, down_tile)
            here = pl.ds(pl.multiple_of(step * TILE, TILE), TILE)
            d_late[:, :, here] = both_tile[...]
            down_late[:, :, here] = down_tile[...].reshape(devices, rows, TILE)

        @pl.when(step == LATE - 1)
        def _():
            late_ring.begin()

        @pl.when((step >= LATE) & (step < LATE + tiles))
        def _():
            which = step - LATE
            part = dot_nt(d_ref[0], wg_ref[...]) + dot_nt(d_ref[1], wu_ref[...])
            part += dot_nt(d_late[0], lg_ref[...]) + dot_nt(d_late[1], lu_ref[...])
            low = part.astype(BF)
            sent[which] = low
            sent_ref[...] = low
            across(which).start()

        @pl.when((step >= LATE + tiles) & (step < LATE + tiles + 2 * early_wide))
        def _():
            grad_ref[0] = dot_nn(xt_ref[...], tile_ref[0]).astype(BF)

        number = step - (LATE + tiles + 2 * early_wide)
        for part in range(late_wide):
            several = min(wide, late - part * wide)

            @pl.when((number >= 0) & (lax.rem(number, late_wide) == part))
            def _():
                piece = d_late[number // late_wide, :, part * wide : part * wide + several]
                grad_ref[0, :, :several] = dot_nn(xt_ref[...], piece).astype(BF)

        ring.pace(step, [(LATE, 12), (tiles, 8), (grads, 7)])
        late_ring.pace(step, [(LATE, 0), (tiles, 8), (grads, 7)])

        @pl.when(step == total - 1)
        def _():
            for which in range(tiles):
                across(which).wait()
            ring.finish()
            late_ring.finish()

    def first(i):
        return jnp.minimum(i, LATE - 1)

    def second(i):
        return jnp.clip(i - LATE, 0, tiles - 1)

    def third(i):
        at = jnp.clip(i - LATE - tiles, 0, 2 * early_wide - 1)
        return (at // early_wide, 0, at % early_wide)

    def grad_at(i):
        at = jnp.maximum(i - LATE - tiles, 0)
        more = jnp.maximum(at - 2 * early_wide, 0)
        is_late = at // (2 * early_wide)
        return (
            (1 - is_late) * (at // early_wide) + is_late * (more // late_wide),
            0,
            (1 - is_late) * (at % early_wide) + is_late * (early_wide + more % late_wide),
        )

    assert late_wide <= early_wide and some % wide == 0
    any_space = pl.BlockSpec(memory_space=pl.ANY)
    dma = pltpu.SemaphoreType.DMA

    def rest_tile(which):
        return pl.BlockSpec((width, TILE), lambda i: (0, first(i) + which * LATE))

    return pl.pallas_call(
        kernel,
        grid=(total,),
        out_shape=[
            jax.ShapeDtypeStruct((m, late), BF),
            jax.ShapeDtypeStruct((2, width, padded), BF),
            jax.ShapeDtypeStruct((m, width), BF),
            jax.ShapeDtypeStruct((m, width), BF),
            jax.ShapeDtypeStruct((rows, padded), F32),
        ],
        in_specs=[
            any_space, any_space, any_space, any_space,
            rest_tile(0), rest_tile(1), rest_tile(2),
            any_space,
            pl.BlockSpec((1, m, wide), third),
            pl.BlockSpec((TILE, some), lambda i: (second(i), 0)),
            pl.BlockSpec((TILE, some), lambda i: (second(i), 1)),
            pl.BlockSpec((TILE, late), lambda i: (second(i), 0)),
            pl.BlockSpec((TILE, late), lambda i: (second(i), 1)),
            any_space,
        ],
        out_specs=[
            pl.BlockSpec((m, TILE), lambda i: (0, first(i))),
            pl.BlockSpec((1, width, wide), grad_at),
            pl.BlockSpec((m, TILE), lambda i: (0, second(i))),
            any_space,
            single((rows, padded)),
        ],
        scratch_shapes=[
            pltpu.VMEM((m, width), BF),
            pltpu.VMEM((width, m), BF),
            pltpu.VMEM((m, width), BF),
            pltpu.VMEM((width, m), BF),
            pltpu.VMEM((2, m, some), BF),
            dma((5,)),
            pltpu.VMEM((2, m, late), BF),
            pltpu.VMEM((devices, rows, late), BF),
            pltpu.VMEM((width, TILE), BF),
            pltpu.VMEM((2, m, TILE), BF),
            pltpu.VMEM((tiles, m, TILE), BF),
            dma((tiles,)),
            dma((tiles,)),
            *Ring.scratch(devices, pieces),
            *Ring.scratch(devices, [(rows, late)]),
        ],
        compiler_params=pltpu.CompilerParams(vmem_limit_bytes=VMEM, collective_id=identity, has_side_effects=True),
        cost_estimate=cost(8 * m * width * padded + 8 * m * width * late, 10 * width * padded),
        name="ffn_back",
    )(x, x_t, dy, dy_t, rest, rest, rest, d_early, d_early, w_ffn, w_ffn, rest, rest, down_early)


def shards(tokens, positions, attn_gain, w_query, w_key, w_value, w_out, ffn_gain, w_gate, w_up, w_down, cotangent):
    devices = lax.axis_size("dp")
    span = tokens.shape[0]
    assert 2 * span == WINDOW
    own_rows = w_query.shape[0]
    width = tokens.shape[1]
    head_columns = w_query.shape[1]
    heads = head_columns // E
    hidden_units = w_gate.shape[1]
    tiles = (hidden_units + TILE - 1) // TILE
    padded = tiles * TILE

    some = padded - LATE * TILE
    lanes = max(128, own_rows)
    places = positions[None, :]
    w_attn, all_gains, near, far, ffn_pack, rest_pack, cotangent_t, cosine, sine = first_gather(
        w_query, w_key, w_value, w_out, attn_gain, ffn_gain, tokens, w_gate.T, w_up.T, w_down, cotangent, places, 0
    )
    normed_attn_t, query, kv, mixed, probs, hidden, normed_ffn, normed_ffn_t, w_ffn, gain_attn, gain_ffn = forward(
        far, near, tokens, all_gains, w_attn, cosine, sine, places, ffn_pack, heads, 5
    )

    act_early, d_early, down_early, rest = feed(normed_ffn, cotangent, cotangent_t, w_ffn, rest_pack, tiles, 6)
    act_late, both_part, d_normed_ffn, d_normed_other, down_grad = ffn_back(
        normed_ffn, normed_ffn_t, cotangent, cotangent_t, d_early, w_ffn, rest, down_early.reshape(devices, own_rows, some), 1
    )
    both_part = both_part.reshape(2, devices, own_rows, padded)

    d_query, d_key, d_value, out_part, gate_grad, w_down_grad, d_hidden, gain_ffn_grad, ffn_part, ffn_other = attend_back(
        query, kv, probs, mixed, w_attn, hidden, gain_ffn, d_normed_ffn, d_normed_other, cotangent, cosine, sine, down_grad, act_early, act_late, w_ffn, rest,
        both_part, heads, hidden_units, 2,
    )
    qkv_part, d_normed_attn, d_attn_other, d_attn_add, up_grad, out_grad = qkv_back(
        normed_attn_t, d_query, d_key, d_value, w_attn, both_part, out_part.reshape(devices, own_rows, head_columns), hidden_units, 3
    )
    tokens_grad, layer_out, w_out_grad, query_grad, key_grad, value_grad, gain_grads = last_pass(
        tokens, gain_attn, d_normed_attn, d_attn_other, d_attn_add, d_hidden, hidden, ffn_part, ffn_other, act_early, act_late, w_ffn, rest, gain_ffn_grad, out_grad,
        qkv_part.reshape(devices, own_rows, 3 * head_columns), lanes, 4,
    )
    return (
        layer_out,
        tokens_grad,
        gain_grads[0, :own_rows],
        query_grad,
        key_grad,
        value_grad,
        w_out_grad,
        gain_grads[16, :own_rows],
        gate_grad,
        up_grad,
        w_down_grad,
    )


def solution(mesh):
    by_rows, by_both, turned_both, line = P("dp", None), P("dp", "tensor"), P("tensor", "dp"), P("dp")
    return jax.shard_map(
        shards,
        mesh=mesh,
        in_specs=(by_rows, line, line, by_both, by_both, by_both, turned_both, line, by_both, by_both, turned_both, by_rows),
        out_specs=(by_rows, by_rows, line, by_both, by_both, by_both, turned_both, line, by_both, by_both, turned_both),
        check_vma=False,
    )
```
